32 devices in a mesh: pb: 4 (over y, core), pa: 8 (over z, x).
Axes of the slice: x: 2, y: 2, z: 4, core: 2. Of those that a mesh axis runs over, the one named last changes fastest.
Arguments:
- enc_in: bfloat16 [32768, 768], P(('pb', 'pa')), may hold values from -6 to 6
- dec_in: bfloat16 [192, 768], P('pb'), may hold values from -6 to 6
- question_of: int32 [64], P(('pb', 'pa')), may hold values from 0 to 1, as said below
- lengths: int32 [64], P(('pb', 'pa')), may hold values from 64 to 512, as said below
- enc_gain_attn: bfloat16 [768], replicated, may hold values from 0.5 to 1.5
- enc_query: bfloat16 [768, 768], replicated, may hold values from -0.21875 to 0.21875
- enc_key: bfloat16 [768, 768], replicated, may hold values from -0.21875 to 0.21875
- enc_value: bfloat16 [768, 768], replicated, may hold values from -0.21875 to 0.21875
- enc_output: bfloat16 [768, 768], replicated, may hold values from -3.5 to 3.5
- enc_bias: bfloat16 [32, 12], replicated, may hold values from -4 to 4
- enc_gain_ffn: bfloat16 [768], replicated, may hold values from 0.5 to 1.5
- enc_ff_in: bfloat16 [768, 3072], replicated, may hold values from -0.21875 to 0.21875
- enc_ff_out: bfloat16 [3072, 768], replicated, may hold values from -0.109375 to 0.109375
- enc_gain_final: bfloat16 [768], replicated, may hold values from 0.5 to 1.5
- cross_key: bfloat16 [768, 768], replicated, may hold values from -0.21875 to 0.21875
- cross_value: bfloat16 [768, 768], replicated, may hold values from -0.21875 to 0.21875
- dec_gain_self: bfloat16 [768], replicated, may hold values from 0.5 to 1.5
- dec_query: bfloat16 [768, 768], replicated, may hold values from -0.21875 to 0.21875
- dec_key: bfloat16 [768, 768], replicated, may hold values from -0.21875 to 0.21875
- dec_value: bfloat16 [768, 768], replicated, may hold values from -0.21875 to 0.21875
- dec_output: bfloat16 [768, 768], replicated, may hold values from -0.625 to 0.625
- dec_bias: bfloat16 [32, 12], replicated, may hold values from -4 to 4
- dec_gain_cross: bfloat16 [768], replicated, may hold values from 0.5 to 1.5
- cross_query: bfloat16 [768, 768], replicated, may hold values from -0.21875 to 0.21875
- cross_output: bfloat16 [768, 768], replicated, may hold values from -9 to 9
- dec_gain_ffn: bfloat16 [768], replicated, may hold values from 0.5 to 1.5
- dec_ff_in: bfloat16 [768, 3072], replicated, may hold values from -0.21875 to 0.21875
- dec_ff_out: bfloat16 [3072, 768], replicated, may hold values from -0.109375 to 0.109375
- enc_cot: bfloat16 [32768, 768], P(('pb', 'pa')), may hold values from -6 to 6
- dec_cot: bfloat16 [192, 768], P('pb'), may hold values from -6 to 6
Outputs:
- enc_out: bfloat16 [32768, 768], P(('pb', 'pa'))
- dec_out: bfloat16 [192, 768], P('pb')
- enc_in_grad: float32 [32768, 768], P(('pb', 'pa'))
- dec_in_grad: float32 [192, 768], P('pb')
- enc_gain_attn_grad: float32 [768], P(('pb', 'pa'))
- enc_query_grad: float32 [768, 768], P(('pb', 'pa'))
- enc_key_grad: float32 [768, 768], P(('pb', 'pa'))
- enc_value_grad: float32 [768, 768], P(('pb', 'pa'))
- enc_output_grad: float32 [768, 768], P(('pb', 'pa'))
- enc_bias_grad: float32 [384], P(('pb', 'pa'))
- enc_gain_ffn_grad: float32 [768], P(('pb', 'pa'))
- enc_ff_in_grad: float32 [768, 3072], P(('pb', 'pa'))
- enc_ff_out_grad: float32 [3072, 768], P(('pb', 'pa'))
- enc_gain_final_grad: float32 [768], P(('pb', 'pa'))
- cross_key_grad: float32 [768, 768], P(('pb', 'pa'))
- cross_value_grad: float32 [768, 768], P(('pb', 'pa'))
- dec_gain_self_grad: float32 [768], P(('pb', 'pa'))
- dec_query_grad: float32 [768, 768], P(('pb', 'pa'))
- dec_key_grad: float32 [768, 768], P(('pb', 'pa'))
- dec_value_grad: float32 [768, 768], P(('pb', 'pa'))
- dec_output_grad: float32 [768, 768], P(('pb', 'pa'))
- dec_bias_grad: float32 [384], P(('pb', 'pa'))
- dec_gain_cross_grad: float32 [768], P(('pb', 'pa'))
- cross_query_grad: float32 [768, 768], P(('pb', 'pa'))
- cross_output_grad: float32 [768, 768], P(('pb', 'pa'))
- dec_gain_ffn_grad: float32 [768], P(('pb', 'pa'))
- dec_ff_in_grad: float32 [768, 3072], P(('pb', 'pa'))
- dec_ff_out_grad: float32 [3072, 768], P(('pb', 'pa'))
The draws below stay inside these ranges and needn't reach their ends.
Inputs may be any that keep to these rules, and one draw needn't show every extreme that they name: question_of[n] names a question of the passage's group (the 2 questions whose answers are rows g * 2 * 24 onward of dec_in for group g); every question of every group has at least one passage. A passage's tokens fill the first lengths[n] of its 512 slots, the rest is padding; some passage holds exactly 512 tokens.
All inputs are finite; a program needn't handle non-finite values.
Results may differ from the reference program's by a relative error of at most 0.017.
Values sent between devices are 32-bit elements; how exact they have to be, the bound alone decides.
A program may use at most 384 MiB of HBM per device.

```python
import math
import jax
import jax.numpy as jnp
import numpy as np
from jax import lax

D = 768
HEADS = 12
HEAD = 64
FF = 3072
BUCKETS = 32
PL = 512
P_DEV = 2
QD = 2
ANS = 24
TOK_DEV = 1024
TOKENS = 32768
PASSAGES = 64
QUESTIONS = 8
DROWS = 192
N_PB = 4
N_PA = 8


def draw_question_of(key, part):
    groups = QUESTIONS // QD
    per_group = PASSAGES // groups
    key_one, key_two = jax.random.split(key)
    chosen = jax.random.randint(key_one, (groups, per_group), 0, QD)
    orders = jax.vmap(lambda single_key: jax.random.permutation(single_key, per_group))(jax.random.split(key_two, groups))
    group_index = jnp.arange(groups)[:, None]
    chosen = chosen.at[group_index, orders[:, :QD]].set(jnp.arange(QD, dtype=jnp.int32)[None, :])
    return chosen.reshape(PASSAGES).astype(jnp.int32)


def draw_lengths(key, part):
    key_one, key_two = jax.random.split(key)
    shortest = max(1, PL // 8)
    drawn = jax.random.randint(key_one, (PASSAGES,), shortest, PL + 1)
    full_place = jax.random.randint(key_two, (), 0, PASSAGES)
    drawn = drawn.at[full_place].set(PL)
    drawn = drawn.at[(full_place + 1) % PASSAGES].set(shortest)
    return drawn.astype(jnp.int32)


def levels(stream_key, extent, shards, smallest, largest):
    loudness = 1.0
    for dim, parts in shards:
        heights = jax.random.uniform(jax.random.fold_in(jax.random.fold_in(stream_key, 6), dim), (parts,), jnp.float32, smallest / len(shards), largest / len(shards))
        loudness = loudness * jnp.repeat(jnp.exp(heights), extent[dim] // parts).reshape((-1,) + (1,) * (len(extent) - 1 - dim))
    return loudness


def noise(own_key, shape, scale, reach, cuts=(), kind=jnp.bfloat16):
    values = jax.random.normal(own_key, shape, jnp.float32) * scale
    if len(cuts) > 0:
        values = levels(own_key, shape, cuts, -0.22, 0.18) * values
    return jnp.clip(values, min=-reach, max=reach).astype(kind)


def setup_inputs(seed: int = 0) -> dict:
    key_list = jax.random.split(jax.random.key(seed), 31)
    return {
        "enc_in": noise(key_list[0], (TOKENS, D), 1.0, 6.0, ((0, 32),)),
        "dec_in": noise(key_list[1], (DROWS, D), 1.0, 6.0, ((0, 4),)),
        "question_of": draw_question_of(jax.random.fold_in(key_list[30], 71), 0),
        "lengths": draw_lengths(jax.random.fold_in(key_list[30], 71), 0),
        "enc_gain_attn": jnp.clip(1.0 + 0.1 * jax.random.normal(key_list[4], (D,), jnp.float32), 0.5, 1.5).astype(jnp.bfloat16),
        "enc_query": noise(key_list[5], (D, D), D ** -0.5, 0.21875),
        "enc_key": noise(key_list[6], (D, D), D ** -0.5, 0.21875),
        "enc_value": noise(key_list[7], (D, D), D ** -0.5, 0.21875),
        "enc_output": noise(key_list[8], (D, D), (max(1, D // 256)) ** -0.5, 3.5),
        "enc_bias": noise(key_list[9], (BUCKETS, HEADS), 1.0, 4.0),
        "enc_gain_ffn": jnp.clip(1.0 + 0.1 * jax.random.normal(key_list[10], (D,), jnp.float32), 0.5, 1.5).astype(jnp.bfloat16),
        "enc_ff_in": noise(key_list[11], (D, FF), D ** -0.5, 0.21875),
        "enc_ff_out": noise(key_list[12], (FF, D), FF ** -0.5, 0.109375),
        "enc_gain_final": jnp.clip(1.0 + 0.1 * jax.random.normal(key_list[13], (D,), jnp.float32), 0.5, 1.5).astype(jnp.bfloat16),
        "cross_key": noise(key_list[14], (D, D), D ** -0.5, 0.21875),
        "cross_value": noise(key_list[15], (D, D), D ** -0.5, 0.21875),
        "dec_gain_self": jnp.clip(1.0 + 0.1 * jax.random.normal(key_list[16], (D,), jnp.float32), 0.5, 1.5).astype(jnp.bfloat16),
        "dec_query": noise(key_list[17], (D, D), D ** -0.5, 0.21875),
        "dec_key": noise(key_list[18], (D, D), D ** -0.5, 0.21875),
        "dec_value": noise(key_list[19], (D, D), D ** -0.5, 0.21875),
        "dec_output": noise(key_list[20], (D, D), (max(1, D // 8)) ** -0.5, 0.625),
        "dec_bias": noise(key_list[21], (BUCKETS, HEADS), 1.0, 4.0),
        "dec_gain_cross": jnp.clip(1.0 + 0.1 * jax.random.normal(key_list[22], (D,), jnp.float32), 0.5, 1.5).astype(jnp.bfloat16),
        "cross_query": noise(key_list[23], (D, D), D ** -0.5, 0.21875),
        "cross_output": noise(key_list[24], (D, D), 1.5, 9.0),
        "dec_gain_ffn": jnp.clip(1.0 + 0.1 * jax.random.normal(key_list[25], (D,), jnp.float32), 0.5, 1.5).astype(jnp.bfloat16),
        "dec_ff_in": noise(key_list[26], (D, FF), D ** -0.5, 0.21875),
        "dec_ff_out": noise(key_list[27], (FF, D), FF ** -0.5, 0.109375),
        "enc_cot": noise(key_list[28], (TOKENS, D), 1.0, 6.0, ((0, 32),)),
        "dec_cot": noise(key_list[29], (DROWS, D), 1.0, 6.0, ((0, 4),)),
    }


far_distance = 128
epsilon = 1e-06
highest = lax.Precision.HIGHEST

@jax.custom_vjp
def low(v):
    return lax.optimization_barrier(v.astype(jnp.bfloat16)).astype(jnp.float32)

@jax.custom_vjp
def low_back(v):
    return v

def low_keep(v):
    return (low(v), None)

def low_pass(kept, grad):
    return (grad,)

def back_keep(v):
    return (v, None)

def back_low(kept, grad):
    return (low(grad),)
low.defvjp(low_keep, low_pass)
low_back.defvjp(back_keep, back_low)

def smooth_unit(values):
    return jax.nn.gelu(values, approximate=True)

def bucket_of(offset, bidirectional):
    if bidirectional:
        halves = BUCKETS // 2
        base_bucket = halves if offset > 0 else 0
        distance = abs(offset)
    else:
        halves = BUCKETS
        base_bucket = 0
        distance = max(-offset, 0)
    exact_count = halves // 2
    if distance < exact_count:
        return base_bucket + distance
    scaled = math.log(distance / exact_count) / math.log(far_distance / exact_count) * (halves - exact_count)
    return base_bucket + min(exact_count + int(scaled), halves - 1)

def offset_onehot(length):
    table = np.zeros((2 * length - 1, BUCKETS), np.float32)
    for offset in range(-(length - 1), length):
        table[offset + length - 1, bucket_of(offset, True)] = 1.0
    return table

def causal_onehot(length):
    table = np.zeros((length * length, BUCKETS), np.float32)
    for query_pos in range(length):
        for key_pos in range(length):
            table[query_pos * length + key_pos, bucket_of(key_pos - query_pos, False)] = 1.0
    return table

def rms_norm(values, gain):
    return values * lax.rsqrt(lax.optimization_barrier(jnp.mean(values * values, axis=-1, keepdims=True)) + epsilon) * gain

def matmul(left, right):
    return jnp.dot(left, right, precision=highest)

def both_ways(values):
    return low_back(low(values))

def encoder_bias(bias_table):
    per_offset = jnp.dot(jnp.asarray(offset_onehot(PL)), bias_table, precision=highest)
    index = np.arange(PL)[None, :] - np.arange(PL)[:, None] + PL - 1
    return jnp.transpose(per_offset[index], (2, 0, 1))

def decoder_bias(bias_table):
    return jnp.dot(jnp.asarray(causal_onehot(ANS)), bias_table, precision=highest).T.reshape(HEADS, ANS, ANS)

def encode_block(params, block_in, block_lengths):
    gain_attn, w_query, w_key, w_value, w_out, bias_table, gain_ffn, w_in_ff, w_out_ff, gain_final, w_cross_key, w_cross_value = params
    count = block_lengths.shape[0]
    normed = low(rms_norm(block_in, gain_attn))
    queries = both_ways(matmul(normed, w_query)).reshape(count, PL, HEADS, HEAD)
    key_rows = both_ways(matmul(normed, w_key)).reshape(count, PL, HEADS, HEAD)
    value_rows = both_ways(matmul(normed, w_value)).reshape(count, PL, HEADS, HEAD)
    raw_scores = low_back(0.125 * jnp.einsum('pqhd,pkhd->phqk', queries, key_rows, precision=highest))
    scores = raw_scores + encoder_bias(bias_table)[None]
    valid = jnp.arange(PL)[None, None, None, :] < block_lengths[:, None, None, None]
    scores = jnp.where(valid, scores, -1000000000.0)
    probs = low(jax.nn.softmax(scores, axis=-1))
    attended = both_ways(jnp.einsum('phqk,pkhd->pqhd', probs, value_rows, precision=highest).reshape(count * PL, D))
    middle = block_in + low_back(matmul(attended, w_out))
    normed_ff = low(rms_norm(middle, gain_ffn))
    hidden = low(smooth_unit(low_back(matmul(normed_ff, w_in_ff))))
    result = middle + low_back(matmul(hidden, w_out_ff))
    normed_out = low(rms_norm(result, gain_final))
    return (result, both_ways(matmul(normed_out, w_cross_key)), both_ways(matmul(normed_out, w_cross_value)))

def decode(params, dec_x, cross_keys, cross_values, key_question, key_valid):
    gain_self, w_query, w_key, w_value, w_out, bias_table, gain_cross, w_cross_query, w_cross_out, gain_ffn, w_in_ff, w_out_ff = params
    normed = low(rms_norm(dec_x, gain_self))
    queries = both_ways(matmul(normed, w_query)).reshape(QUESTIONS, ANS, HEADS, HEAD)
    key_rows = both_ways(matmul(normed, w_key)).reshape(QUESTIONS, ANS, HEADS, HEAD)
    value_rows = both_ways(matmul(normed, w_value)).reshape(QUESTIONS, ANS, HEADS, HEAD)
    raw_scores = low_back(0.125 * jnp.einsum('qihd,qjhd->qhij', queries, key_rows, precision=highest))
    scores = raw_scores + decoder_bias(bias_table)[None]
    causal = jnp.arange(ANS)[None, :] <= jnp.arange(ANS)[:, None]
    scores = jnp.where(causal, scores, -1000000000.0)
    probs = low(jax.nn.softmax(scores, axis=-1))
    attended = both_ways(jnp.einsum('qhij,qjhd->qihd', probs, value_rows, precision=highest).reshape(DROWS, D))
    middle = dec_x + low_back(matmul(attended, w_out))
    normed_cross = low(rms_norm(middle, gain_cross))
    cross_q = low(matmul(normed_cross, w_cross_query)).reshape(N_PB, QD * ANS, HEADS, HEAD)
    raw_cross = low_back(0.125 * jnp.einsum('grhd,gkhd->ghrk', cross_q, cross_keys, precision=highest))
    row_question = jnp.arange(QD * ANS) // ANS
    permitted = (key_question[:, None, :] == row_question[None, :, None]) & key_valid[:, None, :]
    cross_scores = jnp.where(permitted[:, None], raw_cross, -1000000000.0)
    cross_probs = low(jax.nn.softmax(cross_scores, axis=-1))
    cross_att = low_back(jnp.einsum('ghrk,gkhd->grhd', cross_probs, cross_values, precision=highest).reshape(DROWS, D))
    after_cross = middle + low_back(matmul(cross_att, w_cross_out))
    normed_ff = low(rms_norm(after_cross, gain_ffn))
    hidden = low(smooth_unit(low_back(matmul(normed_ff, w_in_ff))))
    return after_cross + low_back(matmul(hidden, w_out_ff))

def reference(enc_in, dec_in, question_of, lengths, enc_gain_attn, enc_query, enc_key, enc_value, enc_output, enc_bias, enc_gain_ffn, enc_ff_in, enc_ff_out, enc_gain_final, cross_key, cross_value, dec_gain_self, dec_query, dec_key, dec_value, dec_output, dec_bias, dec_gain_cross, cross_query, cross_output, dec_gain_ffn, dec_ff_in, dec_ff_out, enc_cot, dec_cot):
    params = tuple((weight.astype(jnp.float32) for weight in (enc_gain_attn, enc_query, enc_key, enc_value, enc_output, enc_bias, enc_gain_ffn, enc_ff_in, enc_ff_out, enc_gain_final, cross_key, cross_value, dec_gain_self, dec_query, dec_key, dec_value, dec_output, dec_bias, dec_gain_cross, cross_query, cross_output, dec_gain_ffn, dec_ff_in, dec_ff_out)))
    per_block = math.gcd(PASSAGES, max(1, 4096 // PL))
    key_question = jnp.repeat(question_of.reshape(N_PB, N_PA * P_DEV), PL, axis=1)
    key_valid = (jnp.arange(PL)[None, :] < lengths[:, None]).reshape(N_PB, N_PA * TOK_DEV)

    def forward(enc_x, dec_x, weights):
        enc_params = weights[:12]

        def encode_step(carry, pair):
            return (carry, encode_block(enc_params, pair[0], pair[1]))
        blocks_in = enc_x.reshape(PASSAGES // per_block, per_block * PL, D)
        block_lengths = lengths.reshape(PASSAGES // per_block, per_block)
        unused, stacked = lax.scan(jax.checkpoint(encode_step), None, (blocks_in, block_lengths))
        enc_y = stacked[0].reshape(TOKENS, D)
        group_keys = stacked[1].reshape(N_PB, N_PA * TOK_DEV, HEADS, HEAD)
        group_values = stacked[2].reshape(N_PB, N_PA * TOK_DEV, HEADS, HEAD)
        dec_y = decode(weights[12:], dec_x, group_keys, group_values, key_question, key_valid)
        return (enc_y, dec_y)
    outputs, pullback = jax.vjp(forward, enc_in.astype(jnp.float32), dec_in.astype(jnp.float32), params)
    enc_grad, dec_grad, grads = pullback((enc_cot.astype(jnp.float32), dec_cot.astype(jnp.float32)))
    return (outputs[0].astype(jnp.bfloat16), outputs[1].astype(jnp.bfloat16), enc_grad, dec_grad, grads[0], grads[1], grads[2], grads[3], grads[4], grads[5].reshape(BUCKETS * HEADS), grads[6], grads[7], grads[8], grads[9], grads[10], grads[11], grads[12], grads[13], grads[14], grads[15], grads[16], grads[17].reshape(BUCKETS * HEADS), grads[18], grads[19], grads[20], grads[21], grads[22], grads[23])
```

```python
import functools
import math

import jax
import jax.numpy as jnp
import numpy as np
from jax import lax
from jax.experimental import pallas as pl
from jax.experimental.pallas import tpu as pltpu
from jax.sharding import PartitionSpec as P

D = 768
HEADS = 12
HEAD = 64
BUCKETS = 32
PL = 512
ANS = 24

far_distance = 128
epsilon = 1e-06
highest = lax.Precision.HIGHEST


def smooth_unit(values):
    return jax.nn.gelu(values, approximate=True)


def smooth_back(values, grad):
    return jax.vjp(smooth_unit, values)[1](grad)[0]


def bucket_of(offset, bidirectional):
    if bidirectional:
        halves = BUCKETS // 2
        base_bucket = halves if offset > 0 else 0
        distance = abs(offset)
    else:
        halves = BUCKETS
        base_bucket = 0
        distance = max(-offset, 0)
    exact_count = halves // 2
    if distance < exact_count:
        return base_bucket + distance
    scaled = (
        math.log(distance / exact_count)
        / math.log(far_distance / exact_count)
        * (halves - exact_count)
    )
    return base_bucket + min(exact_count + int(scaled), halves - 1)


def causal_onehot(length):
    table = np.zeros((length * length, BUCKETS), np.float32)
    for query_pos in range(length):
        for key_pos in range(length):
            table[query_pos * length + key_pos, bucket_of(key_pos - query_pos, False)] = 1.0
    return table


def to_low(values):
    return values.astype(jnp.bfloat16)


def product(left, right):
    return jnp.dot(left, right, preferred_element_type=jnp.float32)


def product_tn(left, right):
    return lax.dot_general(
        left, right, (((0,), (0,)), ((), ())), preferred_element_type=jnp.float32
    )


def product_nt(left, right):
    return lax.dot_general(
        left, right, (((1,), (1,)), ((), ())), preferred_element_type=jnp.float32
    )


def exact_product(left, right):
    return jnp.dot(left, right.astype(jnp.float32), precision=highest)


def exact_tn(left, right):
    return lax.dot_general(
        left.astype(jnp.float32),
        right.astype(jnp.float32),
        (((0,), (0,)), ((), ())),
        precision=highest,
    )


def exact_nt(left, right):
    return lax.dot_general(
        left, right.astype(jnp.float32), (((1,), (1,)), ((), ())), precision=highest
    )


def norm_forward(values, gain):
    scale = lax.rsqrt(jnp.mean(values * values, axis=-1, keepdims=True) + epsilon)
    return (values * scale * gain, scale)


def norm_backward(values, scale, gain, grad):
    scaled_grad = grad * gain
    gain_grad = jnp.sum(grad * values * scale, axis=0)
    inner = jnp.mean(scaled_grad * values, axis=-1, keepdims=True)
    return (scaled_grad * scale - values * (scale * scale * scale) * inner, gain_grad)


STRIP = 128
WIDE = 1024


def strip_table():
    table = np.zeros((WIDE, BUCKETS), np.float32)
    for place in range(WIDE):
        if place < PL + STRIP * 3:
            offset = PL - STRIP - place
        else:
            offset = PL - STRIP + WIDE - place
        if abs(offset) < PL:
            table[place, bucket_of(offset, True)] = 1.0
    return table


def nn(left, right):
    return lax.dot_general(left, right, (((1,), (0,)), ((), ())), preferred_element_type=jnp.float32)


def head_lanes(values, head):
    lane = lax.broadcasted_iota(jnp.int32, values.shape, 1)
    keep = lane < HEAD if head == 0 else lane >= HEAD
    return jnp.where(keep, values, jnp.zeros_like(values))


def key_mask(length):
    place = lax.broadcasted_iota(jnp.int32, (PL, 1), 0)
    return jnp.where(place < length, 0.0, -1e9)


def build_strip(base_ref, strip_ref):
    for head in range(2):
        row = base_ref[0, head : head + 1, :]
        spread = jnp.broadcast_to(row, (STRIP, WIDE))
        strip_ref[head] = pltpu.roll(spread, 0, 1, stride=1, stride_axis=0)


def attn_forward_kernel(lengths_ref, q_ref, k_ref, v_ref, base_ref, out_ref, lse_ref, strip_ref, score_ref, outT_ref):
    passage = pl.program_id(1)

    @pl.when(passage == 0)
    def _():
        build_strip(base_ref, strip_ref)

    mask = key_mask(lengths_ref[passage])
    q_t = q_ref[...].T
    v_t = v_ref[...].T
    k = k_ref[...]
    blocks = PL // STRIP
    for head in range(2):
        k_head = head_lanes(k, head)
        top = None
        for b in range(blocks):
            rows = slice(b * STRIP, (b + 1) * STRIP)
            start = PL - STRIP - b * STRIP
            s = nn(k_head[rows], q_t) + strip_ref[head, :, start : start + PL] + mask[rows]
            score_ref[head, rows, :] = s
            here = jnp.max(s, axis=0, keepdims=True)
            top = here if top is None else jnp.maximum(top, here)
        total = None
        acc = None
        for b in range(blocks):
            rows = slice(b * STRIP, (b + 1) * STRIP)
            e = jnp.exp(score_ref[head, rows, :] - top)
            here = jnp.sum(e, axis=0, keepdims=True)
            total = here if total is None else total + here
            part = nn(v_t[head * HEAD : (head + 1) * HEAD, rows], to_low(e))
            acc = part if acc is None else acc + part
        outT_ref[head * HEAD : (head + 1) * HEAD, :] = to_low(acc * (1.0 / total))
        lse_ref[0, 0, head : head + 1, :] = top + jnp.log(total)
    out_ref[...] = outT_ref[...].T


def attn_forward(lengths, q, k, v, base):
    passages = lengths.shape[0]
    pairs = HEADS // 2
    tile = pl.BlockSpec((PL, 128), lambda h, p, *_: (p, h))
    return pl.pallas_call(
        attn_forward_kernel,
        grid_spec=pltpu.PrefetchScalarGridSpec(
            num_scalar_prefetch=1,
            grid=(pairs, passages),
            in_specs=[tile, tile, tile, pl.BlockSpec((1, 2, WIDE), lambda h, p, *_: (h, 0, 0))],
            out_specs=[tile, pl.BlockSpec((1, 1, 2, PL), lambda h, p, *_: (h, p, 0, 0))],
            scratch_shapes=[
                pltpu.VMEM((2, STRIP, WIDE), jnp.float32),
                pltpu.VMEM((2, PL, PL), jnp.float32),
                pltpu.VMEM((128, PL), jnp.bfloat16),
            ],
        ),
        out_shape=[
            jax.ShapeDtypeStruct((passages * PL, D), jnp.bfloat16),
            jax.ShapeDtypeStruct((pairs, passages, 2, PL), jnp.float32),
        ],
        compiler_params=pltpu.CompilerParams(vmem_limit_bytes=32 * 2**20),
        name="enc_attention",
    )(lengths, q, k, v, base)


def attn_backward_kernel(
    lengths_ref, q_ref, k_ref, v_ref, o_ref, do_ref, lse_ref, base_ref,
    dq_ref, dk_ref, dv_ref, fold_ref,
    strip_ref, gather_ref, dqT_ref,
):
    passage = pl.program_id(1)

    @pl.when(passage == 0)
    def _():
        build_strip(base_ref, strip_ref)
        gather_ref[...] = jnp.zeros_like(gather_ref)

    mask = key_mask(lengths_ref[passage])
    q = q_ref[...]
    k = k_ref[...]
    v = v_ref[...]
    do = do_ref[...]
    q_t = q.T
    k_t = k.T
    do_t = do.T
    o_t = o_ref[...].T
    weighed = do_t.astype(jnp.float32) * o_t.astype(jnp.float32)
    blocks = PL // STRIP
    lane = lax.broadcasted_iota(jnp.int32, (STRIP, 128), 1)
    first = lane < HEAD
    dks = []
    dvs = []
    for head in range(2):
        heads = slice(head * HEAD, (head + 1) * HEAD)
        delta = jnp.sum(weighed[heads], axis=0, keepdims=True)
        lse = lse_ref[0, 0, head : head + 1, :]
        k_head = head_lanes(k, head)
        v_head = head_lanes(v, head)
        acc = None
        for b in range(blocks):
            rows = slice(b * STRIP, (b + 1) * STRIP)
            start = PL - STRIP - b * STRIP
            s = nn(k_head[rows], q_t) + strip_ref[head, :, start : start + PL] + mask[rows]
            p = jnp.exp(s - lse)
            dp = nn(v_head[rows], do_t)
            ds = p * (dp - delta)
            gather_ref[head, :, start : start + PL] += ds
            ds_low = to_low(ds)
            dv_part = nn(to_low(p), do)
            dk_part = nn(ds_low, q)
            if head == 0:
                dvs.append(dv_part)
                dks.append(dk_part)
            else:
                dv_ref[rows, :] = to_low(jnp.where(first, dvs[b], dv_part))
                dk_ref[rows, :] = to_low(jnp.where(first, dks[b], dk_part))
            part = nn(k_t[heads, rows], ds_low)
            acc = part if acc is None else acc + part
        dqT_ref[heads, :] = to_low(0.125 * acc)
    dq_ref[...] = dqT_ref[...].T

    @pl.when(passage == pl.num_programs(1) - 1)
    def _():
        row = lax.broadcasted_iota(jnp.int32, (8, WIDE), 0)
        for head in range(2):
            total = gather_ref[head, 0:8, :]
            for group in range(1, STRIP // 8):
                total = total + pltpu.roll(gather_ref[head, group * 8 : group * 8 + 8, :], WIDE - group * 8, 1)
            for bit in (1, 2, 4):
                total = jnp.where((row // bit) % 2 == 1, pltpu.roll(total, WIDE - bit, 1), total)
            fold_ref[0, head : head + 1, :] = jnp.sum(total, axis=0, keepdims=True)


def attn_backward(lengths, q, k, v, o, do, lse, base):
    passages = lengths.shape[0]
    pairs = HEADS // 2
    tile = pl.BlockSpec((PL, 128), lambda h, p, *_: (p, h))
    row = pl.BlockSpec((1, 2, WIDE), lambda h, p, *_: (h, 0, 0))
    big = jax.ShapeDtypeStruct((passages * PL, D), jnp.bfloat16)
    return pl.pallas_call(
        attn_backward_kernel,
        grid_spec=pltpu.PrefetchScalarGridSpec(
            num_scalar_prefetch=1,
            grid=(pairs, passages),
            in_specs=[tile] * 5 + [pl.BlockSpec((1, 1, 2, PL), lambda h, p, *_: (h, p, 0, 0)), row],
            out_specs=[tile, tile, tile, row],
            scratch_shapes=[
                pltpu.VMEM((2, STRIP, WIDE), jnp.float32),
                pltpu.VMEM((2, STRIP, WIDE), jnp.float32),
                pltpu.VMEM((128, PL), jnp.bfloat16),
            ],
        ),
        out_shape=[big, big, big, jax.ShapeDtypeStruct((pairs, 2, WIDE), jnp.float32)],
        compiler_params=pltpu.CompilerParams(vmem_limit_bytes=32 * 2**20),
        name="enc_attention_back",
    )(lengths, q, k, v, o, do, lse, base)


MIB = 2**20


def nt(left, right):
    return lax.dot_general(left, right, (((1,), (1,)), ((), ())), preferred_element_type=jnp.float32)


def rms(values, gain):
    scale = lax.rsqrt(jnp.mean(values * values, axis=-1, keepdims=True) + epsilon)
    return values * scale * gain, scale


def rms_back(values, scale, gain, grad):
    scaled = grad * gain
    gain_grad = jnp.sum(grad * values * scale, axis=0, keepdims=True)
    inner = jnp.mean(scaled * values, axis=-1, keepdims=True)
    return scaled * scale - values * (scale * scale * scale) * inner, gain_grad


def gelu_both(v):
    c = math.sqrt(2.0 / math.pi)
    square = v * v
    t = jnp.tanh(v * (c + (c * 0.044715) * square))
    half = 0.5 + 0.5 * t
    slope = half + (half * (1.0 - t)) * v * (c + (3.0 * 0.044715 * c) * square)
    return v * half, slope


def whole(array):
    return pl.BlockSpec(array.shape, lambda *_: (0,) * array.ndim)


def rows_of(tile, width):
    return pl.BlockSpec((tile, width), lambda i: (i, 0))


def sds(shape, kind):
    return jax.ShapeDtypeStruct(shape, kind)


def params(mib):
    return pltpu.CompilerParams(vmem_limit_bytes=mib * MIB)


def qkv_kernel(x_ref, gain_ref, wq_ref, wk_ref, wv_ref, low_ref, q_ref, k_ref, v_ref):
    normed, _ = rms(x_ref[...].astype(jnp.float32), gain_ref[...])
    low = to_low(normed)
    low_ref[...] = low
    q_ref[...] = to_low(0.125 * to_low(nn(low, wq_ref[...])).astype(jnp.float32))
    k_ref[...] = to_low(nn(low, wk_ref[...]))
    v_ref[...] = to_low(nn(low, wv_ref[...]))


def qkv_forward(x, gain, wq, wk, wv):
    tokens = x.shape[0]
    tile = 256
    big = sds((tokens, D), jnp.bfloat16)
    return pl.pallas_call(
        qkv_kernel,
        grid=(tokens // tile,),
        in_specs=[rows_of(tile, D)] + [whole(a) for a in (gain, wq, wk, wv)],
        out_specs=[rows_of(tile, D)] * 4,
        out_shape=[big] * 4,
        compiler_params=params(40),
        name="enc_qkv",
    )(x, gain, wq, wk, wv)


def post_kernel(
    x_ref, att_ref, gain_ffn_ref, gain_final_ref, wo_ref, win_ref, wout_ref, wck_ref, wcv_ref,
    mid_ref, ffn_low_ref, hidden_ref, slope_ref, y_ref, out_ref, final_low_ref, ck_ref, cv_ref,
):
    mid = x_ref[...].astype(jnp.float32) + nn(att_ref[...], wo_ref[...])
    mid_ref[...] = mid
    normed, _ = rms(mid, gain_ffn_ref[...])
    low = to_low(normed)
    ffn_low_ref[...] = low
    y = mid
    width = 768
    for c in range(win_ref.shape[1] // width):
        cols = slice(c * width, (c + 1) * width)
        hidden, slope = gelu_both(nn(low, win_ref[:, cols]))
        hidden = to_low(hidden)
        hidden_ref[:, cols] = hidden
        slope_ref[:, cols] = to_low(slope)
        y = y + nn(hidden, wout_ref[cols, :])
    y_ref[...] = y
    out_ref[...] = to_low(y)
    final, _ = rms(y, gain_final_ref[...])
    final = to_low(final)
    final_low_ref[...] = final
    ck_ref[...] = to_low(nn(final, wck_ref[...]))
    cv_ref[...] = to_low(nn(final, wcv_ref[...]))


def post_forward(x, att, gain_ffn, gain_final, wo, win, wout, wck, wcv):
    tokens = x.shape[0]
    tile = 256
    ff = win.shape[1]
    low = sds((tokens, D), jnp.bfloat16)
    wide = sds((tokens, ff), jnp.bfloat16)
    full = sds((tokens, D), jnp.float32)
    d = rows_of(tile, D)
    f = rows_of(tile, ff)
    return pl.pallas_call(
        post_kernel,
        grid=(tokens // tile,),
        in_specs=[d, d] + [whole(a) for a in (gain_ffn, gain_final, wo, win, wout, wck, wcv)],
        out_specs=[d, d, f, f, d, d, d, d, d],
        out_shape=[full, low, wide, wide, full, low, low, low, low],
        compiler_params=params(56),
        name="enc_post",
    )(x, att, gain_ffn, gain_final, wo, win, wout, wck, wcv)


def back_kernel(
    gkv_ref, y_ref, mid_ref, slope_ref, cot_ref, gain_ffn_ref, gain_final_ref,
    wck_ref, wcv_ref, wout_ref, win_ref, wo_ref,
    eout_ref, epre_ref, emid_ref, grad_mid_ref, att_grad_ref, gain_final_grad_ref, gain_ffn_grad_ref,
):
    @pl.when(pl.program_id(0) == 0)
    def _():
        gain_final_grad_ref[...] = jnp.zeros_like(gain_final_grad_ref)
        gain_ffn_grad_ref[...] = jnp.zeros_like(gain_ffn_grad_ref)

    y = y_ref[...]
    scale = lax.rsqrt(jnp.mean(y * y, axis=-1, keepdims=True) + epsilon)
    final_back = nt(gkv_ref[0], wck_ref[...]) + nt(gkv_ref[1], wcv_ref[...])
    back, gain_grad = rms_back(y, scale, gain_final_ref[...], final_back)
    gain_final_grad_ref[...] += gain_grad
    grad_y = cot_ref[...].astype(jnp.float32) + back
    eout = to_low(grad_y)
    eout_ref[...] = eout
    width = 768
    acc = None
    for c in range(win_ref.shape[1] // width):
        cols = slice(c * width, (c + 1) * width)
        epre = to_low(slope_ref[:, cols].astype(jnp.float32) * nt(eout, wout_ref[cols, :]))
        epre_ref[:, cols] = epre
        part = nt(epre, win_ref[:, cols])
        acc = part if acc is None else acc + part
    mid = mid_ref[...]
    scale = lax.rsqrt(jnp.mean(mid * mid, axis=-1, keepdims=True) + epsilon)
    back, gain_grad = rms_back(mid, scale, gain_ffn_ref[...], acc)
    gain_ffn_grad_ref[...] += gain_grad
    grad_mid = grad_y + back
    grad_mid_ref[...] = grad_mid
    emid = to_low(grad_mid)
    emid_ref[...] = emid
    att_grad_ref[...] = to_low(nt(emid, wo_ref[...]))


def post_backward(gkv, y, mid, slope, cot, gain_ffn, gain_final, wck, wcv, wout, win, wo):
    tokens = y.shape[0]
    tile = 256
    ff = win.shape[1]
    low = sds((tokens, D), jnp.bfloat16)
    d = rows_of(tile, D)
    f = rows_of(tile, ff)
    gain = pl.BlockSpec((1, D), lambda i: (0, 0))
    return pl.pallas_call(
        back_kernel,
        grid=(tokens // tile,),
        in_specs=[pl.BlockSpec((2, tile, D), lambda i: (0, i, 0)), d, d, f, d]
        + [whole(a) for a in (gain_ffn, gain_final, wck, wcv, wout, win, wo)],
        out_specs=[d, f, d, d, d, gain, gain],
        out_shape=[low, sds((tokens, ff), jnp.bfloat16), low, sds((tokens, D), jnp.float32), low]
        + [sds((1, D), jnp.float32)] * 2,
        compiler_params=params(56),
        name="enc_post_back",
    )(gkv, y, mid, slope, cot, gain_ffn, gain_final, wck, wcv, wout, win, wo)


def qkv_back_kernel(dq_ref, dk_ref, dv_ref, x_ref, grad_mid_ref, gain_ref, wq_ref, wk_ref, wv_ref, out_ref, gain_grad_ref):
    @pl.when(pl.program_id(0) == 0)
    def _():
        gain_grad_ref[...] = jnp.zeros_like(gain_grad_ref)

    x = x_ref[...].astype(jnp.float32)
    scale = lax.rsqrt(jnp.mean(x * x, axis=-1, keepdims=True) + epsilon)
    grad = nt(dq_ref[...], wq_ref[...]) + nt(dk_ref[...], wk_ref[...]) + nt(dv_ref[...], wv_ref[...])
    back, gain_grad = rms_back(x, scale, gain_ref[...], grad)
    gain_grad_ref[...] += gain_grad
    out_ref[...] = grad_mid_ref[...] + back


def qkv_backward(dq, dk, dv, x, grad_mid, gain, wq, wk, wv):
    tokens = x.shape[0]
    tile = 256
    d = rows_of(tile, D)
    return pl.pallas_call(
        qkv_back_kernel,
        grid=(tokens // tile,),
        in_specs=[d] * 5 + [whole(a) for a in (gain, wq, wk, wv)],
        out_specs=[d, pl.BlockSpec((1, D), lambda i: (0, 0))],
        out_shape=[sds((tokens, D), jnp.float32), sds((1, D), jnp.float32)],
        compiler_params=params(40),
        name="enc_qkv_back",
    )(dq, dk, dv, x, grad_mid, gain, wq, wk, wv)


def weight_grad_kernel(rows, pb, pa, tiles, per_chain, table_ref, left_ref, *refs):
    rights = refs[: len(tiles)]
    keep_ref, send_ref, turned_ref = refs[len(tiles) :]
    step = pl.program_id(0)
    depth, height = left_ref.shape

    @pl.when(step == 0)
    def _():
        for c in range(height // 256):
            cols = slice(c * 256, (c + 1) * 256)
            turned_ref[cols, :] = left_ref[:, cols].T

    core = table_ref[0, 0]
    chain = step // per_chain
    half_rows = pa * rows

    def work(right):
        for y in range(pb // 2):
            low_part = nn(turned_ref[2 * y * half_rows : (2 * y + 1) * half_rows, :], right)
            high_part = nn(turned_ref[(2 * y + 1) * half_rows : (2 * y + 2) * half_rows, :], right)
            mine = jnp.where(core == 0, low_part, high_part)
            other = jnp.where(core == 0, high_part, low_part)
            for a in range(pa):
                slot = table_ref[chain + 1, y * pa + a]
                keep_ref[slot] = mine[a * rows : (a + 1) * rows]
                send_ref[slot] = other[a * rows : (a + 1) * rows]

    first = 0
    for right_ref, count in zip(rights, tiles):
        if len(tiles) == 1:
            work(right_ref[...])
        else:
            @pl.when((step >= first) & (step < first + count))
            def _(right_ref=right_ref):
                work(right_ref[...])
        first += count


def weight_grad(table, left, rights, pb, pa, width, per_chain):
    tokens, height = left.shape
    rows = height // (pb * pa)
    tiles = [r.shape[1] // width for r in rights]
    total = sum(tiles)
    firsts = np.cumsum([0] + tiles)[:-1]

    def spec(first, count):
        return pl.BlockSpec((tokens, width), lambda i, *_: (0, jnp.clip(i - int(first), 0, count - 1)))

    half = pb * pa // 2
    out = pl.BlockSpec((half, rows, width), lambda i, *_: (0, 0, i))
    shape = sds((half, rows, total * width), jnp.float32)
    return pl.pallas_call(
        functools.partial(weight_grad_kernel, rows, pb, pa, tiles, per_chain),
        grid_spec=pltpu.PrefetchScalarGridSpec(
            num_scalar_prefetch=1,
            grid=(total,),
            in_specs=[pl.BlockSpec((tokens, height), lambda i, *_: (0, 0))] + [spec(f, c) for f, c in zip(firsts, tiles)],
            out_specs=[out, out],
            scratch_shapes=[pltpu.VMEM((height, tokens), jnp.bfloat16)],
        ),
        out_shape=[shape, shape],
        compiler_params=params(56),
        name="weight_grad",
    )(table, left, *rights)


PACK = 896


def permitted_mask(question_ref, length_ref, answer_rows, passages):
    row = lax.broadcasted_iota(jnp.int32, (answer_rows, PL), 0)
    place = lax.broadcasted_iota(jnp.int32, (answer_rows, PL), 1)
    whose = row // ANS
    return jnp.concatenate(
        [(whose == question_ref[p]) & (place < length_ref[p]) for p in range(passages)], axis=1
    )


def cross_part_kernel(question_ref, length_ref, q_ref, ck_ref, cv_ref, part_ref):
    rows = q_ref.shape[0]
    mask = permitted_mask(question_ref, length_ref, rows, ck_ref.shape[0] // PL)
    lane = lax.broadcasted_iota(jnp.int32, (rows, 128), 1)
    stats = jnp.zeros((rows, 128), jnp.float32)
    for pair in range(HEADS // 2):
        cols = slice(pair * 128, (pair + 1) * 128)
        q = q_ref[:, cols]
        k = ck_ref[:, cols]
        v = cv_ref[:, cols]
        outs = []
        for head in range(2):
            s = jnp.where(mask, 0.125 * nt(head_lanes(q, head), k), -1e9)
            top = jnp.max(s, axis=1, keepdims=True)
            e = jnp.exp(s - top)
            total = jnp.sum(e, axis=1, keepdims=True)
            outs.append(nn(to_low(e), v))
            place = 2 * pair + head
            stats = jnp.where(lane == place, top, jnp.where(lane == HEADS + place, total, stats))
        part_ref[:, cols] = jnp.where(lane < HEAD, outs[0], outs[1])
    part_ref[:, D:] = stats


def cross_part(question_of, lengths, q, ck, cv):
    vmem = pl.BlockSpec(memory_space=pltpu.VMEM)
    smem = pl.BlockSpec(memory_space=pltpu.SMEM)
    return pl.pallas_call(
        cross_part_kernel,
        in_specs=[smem, smem, vmem, vmem, vmem],
        out_specs=vmem,
        out_shape=sds((q.shape[0], PACK), jnp.float32),
        compiler_params=params(40),
        name="cross_part",
    )(question_of, lengths, q, ck, cv)


def over_heads(stats, rows):
    lane = lax.broadcasted_iota(jnp.int32, (rows, 128), 1)
    return jnp.concatenate(
        [jnp.where(lane < HEAD, stats[:, 2 * g : 2 * g + 1], stats[:, 2 * g + 1 : 2 * g + 2]) for g in range(HEADS // 2)],
        axis=1,
    )


def merge_kernel(pa, part_ref, out_ref, recv_ref, mine_ref, send_sem, recv_sem, send2_sem, recv2_sem):
    me = lax.axis_index("pa")
    rows = part_ref.shape[1]
    barrier = pltpu.get_barrier_semaphore()
    for off in range(1, pa):
        pl.semaphore_signal(barrier, inc=1, device_id={"pa": lax.rem(me + off, pa)}, device_id_type=pl.DeviceIdType.MESH)
    pl.semaphore_wait(barrier, pa - 1)

    def first(off):
        peer = lax.rem(me + off, pa)
        return pltpu.make_async_remote_copy(
            src_ref=part_ref.at[peer], dst_ref=recv_ref.at[off], send_sem=send_sem.at[off], recv_sem=recv_sem.at[off],
            device_id={"pa": peer}, device_id_type=pl.DeviceIdType.MESH,
        )

    def second(off):
        peer = lax.rem(me + off, pa)
        return pltpu.make_async_remote_copy(
            src_ref=mine_ref, dst_ref=out_ref.at[me], send_sem=send2_sem.at[off], recv_sem=recv2_sem.at[off],
            device_id={"pa": peer}, device_id_type=pl.DeviceIdType.MESH,
        )

    for off in range(1, pa):
        first(off).start()
    recv_ref[0] = part_ref[me]
    for off in range(1, pa):
        first(off).wait()
    tops = [recv_ref[i, :, D : D + 128][:, :HEADS] for i in range(pa)]
    top = tops[0]
    for t in tops[1:]:
        top = jnp.maximum(top, t)
    total = jnp.zeros((rows, HEADS), jnp.float32)
    acc = jnp.zeros((rows, D), jnp.float32)
    for i in range(pa):
        w = jnp.exp(tops[i] - top)
        total = total + w * recv_ref[i, :, D : D + 128][:, HEADS : 2 * HEADS]
        acc = acc + over_heads(w, rows) * recv_ref[i, :, :D]
    mine_ref[:, :D] = acc / over_heads(total, rows)
    lse = top + jnp.log(total)
    mine_ref[:, D:] = jnp.concatenate([lse, jnp.zeros((rows, 128 - HEADS), jnp.float32)], axis=1)
    for off in range(1, pa):
        second(off).start()
    out_ref[me] = mine_ref[...]
    for off in range(1, pa):
        second(off).wait()


def merge(part, pa):
    answer_rows = part.shape[0]
    rows = answer_rows // pa
    block = (pa, rows, PACK)
    vmem = pl.BlockSpec(memory_space=pltpu.VMEM)
    out = pl.pallas_call(
        functools.partial(merge_kernel, pa),
        in_specs=[vmem],
        out_specs=vmem,
        out_shape=sds(block, jnp.float32),
        scratch_shapes=[
            pltpu.VMEM(block, jnp.float32),
            pltpu.VMEM((rows, PACK), jnp.float32),
            pltpu.SemaphoreType.DMA((pa,)),
            pltpu.SemaphoreType.DMA((pa,)),
            pltpu.SemaphoreType.DMA((pa,)),
            pltpu.SemaphoreType.DMA((pa,)),
        ],
        compiler_params=pltpu.CompilerParams(collective_id=0, has_side_effects=True, vmem_limit_bytes=16 * MIB),
        name="cross_merge",
    )(part.reshape(block))
    return out.reshape(answer_rows, PACK)


def cross_back_kernel(question_ref, length_ref, q_ref, ck_ref, cv_ref, grad_ref, att_ref, lse_ref, gq_ref, gkv_ref):
    rows = q_ref.shape[0]
    mask = permitted_mask(question_ref, length_ref, rows, ck_ref.shape[0] // PL)
    lane = lax.broadcasted_iota(jnp.int32, (rows, 128), 1)
    for pair in range(HEADS // 2):
        cols = slice(pair * 128, (pair + 1) * 128)
        q = q_ref[:, cols]
        k = ck_ref[:, cols]
        v = cv_ref[:, cols]
        g = grad_ref[:, cols]
        weighed = g.astype(jnp.float32) * att_ref[:, cols]
        gqs = []
        scores = []
        probs = []
        for head in range(2):
            place = 2 * pair + head
            s = jnp.where(mask, 0.125 * nt(head_lanes(q, head), k), -1e9)
            p = jnp.exp(s - lse_ref[:, place : place + 1])
            dp = nt(head_lanes(g, head), v)
            delta = jnp.sum(head_lanes(weighed, head), axis=1, keepdims=True)
            ds = to_low(p * (dp - delta))
            gqs.append(nn(ds, k))
            scores.append(ds)
            probs.append(to_low(p))
        gq_ref[:, cols] = 0.125 * jnp.where(lane < HEAD, gqs[0], gqs[1])
        both_q = jnp.concatenate([head_lanes(q, 0), head_lanes(q, 1)], axis=0)
        both_g = jnp.concatenate([head_lanes(g, 0), head_lanes(g, 1)], axis=0)
        gkv_ref[0, :, cols] = to_low(0.125 * product_tn(jnp.concatenate(scores, axis=0), both_q))
        gkv_ref[1, :, cols] = to_low(product_tn(jnp.concatenate(probs, axis=0), both_g))


def cross_back(question_of, lengths, q, ck, cv, grad, att, lse):
    vmem = pl.BlockSpec(memory_space=pltpu.VMEM)
    smem = pl.BlockSpec(memory_space=pltpu.SMEM)
    return pl.pallas_call(
        cross_back_kernel,
        in_specs=[smem, smem] + [vmem] * 6,
        out_specs=[vmem, vmem],
        out_shape=[sds((q.shape[0], D), jnp.float32), sds((2, ck.shape[0], D), jnp.bfloat16)],
        compiler_params=params(40),
        name="cross_back",
    )(question_of, lengths, q, ck, cv, grad, att, lse)


def bits_of(mesh_sizes):
    pb, pa = mesh_sizes
    pb_bits = pb.bit_length() - 1
    pa_bits = pa.bit_length() - 1
    ys = [("pb", b) for b in range(1, pb_bits)]
    xs = [("pa", b) for b in range(pa_bits - 2)]
    zs = [("pa", b) for b in range(pa_bits - 2, pa_bits)]
    return xs, ys, zs


def orders_of(mesh_sizes):
    xs, ys, zs = bits_of(mesh_sizes)
    return (xs + ys + zs, ys + xs + zs, zs[:1] + xs + ys + zs[1:])


def exchange_table(mesh_sizes, orders):
    pb, pa = mesh_sizes
    pb_me = lax.axis_index("pb")
    pa_me = lax.axis_index("pa")
    cells = np.arange(pb * pa // 2)
    pb_of = jnp.asarray(cells // pa * 2)
    pa_of = jnp.asarray(cells % pa)
    rows = [jnp.full((cells.size,), pb_me % 2, jnp.int32)]
    for order in orders:
        slot = jnp.zeros((cells.size,), jnp.int32)
        for axis, bit in order:
            far = ((pb_of if axis == "pb" else pa_of) >> bit) ^ ((pb_me if axis == "pb" else pa_me) >> bit)
            slot = slot * 2 + (far & 1).astype(jnp.int32)
        rows.append(slot)
    return jnp.stack(rows)


def swap(values, axis, bit):
    size = lax.axis_size(axis)
    return lax.ppermute(values, axis, [(i, i ^ (1 << bit)) for i in range(size)])


def summed(parts, first, last):
    total = parts[0][first:last]
    for part in parts[1:]:
        total = total + part[first:last]
    return total


def scatter_chain(parts, order):
    count = parts[0].shape[0]
    for axis, bit in order:
        count //= 2
        received = swap(summed(parts, count, 2 * count), axis, bit)
        parts = [part[:count] for part in parts] + [received]
    return summed(parts, 0, 1)[0]


def scatter(pieces, orders, widths=None):
    keep, send = pieces
    received = swap(send, "pb", 0)
    if widths is None:
        return scatter_chain([keep, received], orders[0])
    first = 0
    done = []
    for order, width in zip(orders, widths):
        cols = slice(first, first + width)
        done.append(scatter_chain([keep[:, :, cols], received[:, :, cols]], order))
        first += width
    return jnp.concatenate(done, axis=1)


def scatter_small(values, orders, mesh_sizes):
    pb, pa = mesh_sizes
    full = [("pb", 0)] + list(orders[0])
    count = pb * pa
    width = -(-values.shape[1] // 128) * 128
    values = jnp.pad(values, ((0, 0), (0, width - values.shape[1])))
    pb_me = lax.axis_index("pb")
    pa_me = lax.axis_index("pa")
    cells = np.arange(count)
    pb_of = jnp.zeros((count,), jnp.int32)
    pa_of = jnp.zeros((count,), jnp.int32)
    for place, (axis, bit) in enumerate(full):
        one = jnp.asarray((cells >> (len(full) - 1 - place) & 1) << bit, jnp.int32)
        if axis == "pb":
            pb_of = pb_of + one
        else:
            pa_of = pa_of + one
    shard = (pb_of ^ pb_me) * pa + (pa_of ^ pa_me)
    ordered = jnp.take(values, shard, axis=0).reshape(count, width // 128, 128)
    return scatter_chain([ordered], full).reshape(width)


def local(
    pb, pa,
    enc_in, dec_in, question_of, lengths, enc_gain_attn, enc_query, enc_key, enc_value, enc_output, enc_bias,
    enc_gain_ffn, enc_ff_in, enc_ff_out, enc_gain_final, cross_key, cross_value, dec_gain_self, dec_query, dec_key,
    dec_value, dec_output, dec_bias, dec_gain_cross, cross_query, cross_output, dec_gain_ffn, dec_ff_in, dec_ff_out,
    enc_cot, dec_cot,
):
    sizes = (pb, pa)
    orders = orders_of(sizes)
    answer_rows = dec_in.shape[0]
    questions = answer_rows // ANS
    gain_attn, gain_ffn, gain_final = (g.astype(jnp.float32)[None] for g in (enc_gain_attn, enc_gain_ffn, enc_gain_final))
    gain_self = dec_gain_self.astype(jnp.float32)
    gain_cross = dec_gain_cross.astype(jnp.float32)
    gain_dffn = dec_gain_ffn.astype(jnp.float32)
    table = exchange_table(sizes, orders)
    enc_table = jnp.asarray(strip_table())
    dec_table = jnp.asarray(causal_onehot(ANS))
    base = jnp.dot(enc_table, enc_bias.astype(jnp.float32), precision=highest).T.reshape(HEADS // 2, 2, WIDE)

    attn_low, enc_queries, enc_keys, enc_values = qkv_forward(enc_in, gain_attn, enc_query, enc_key, enc_value)
    enc_attended, enc_lse = attn_forward(lengths, enc_queries, enc_keys, enc_values, base)
    enc_mid, ffn_low, enc_hidden, enc_slope, enc_y, enc_out, final_low, cross_keys, cross_values = post_forward(
        enc_in, enc_attended, gain_ffn, gain_final, enc_output, enc_ff_in, enc_ff_out, cross_key, cross_value
    )

    dec_x = dec_in.astype(jnp.float32)
    self_normed, self_scale = norm_forward(dec_x, gain_self)
    self_low = to_low(self_normed)
    dec_queries = to_low(product(self_low, dec_query)).reshape(questions, ANS, HEADS, HEAD)
    dec_keys = to_low(product(self_low, dec_key)).reshape(questions, ANS, HEADS, HEAD)
    dec_values = to_low(product(self_low, dec_value)).reshape(questions, ANS, HEADS, HEAD)
    dec_position = jnp.dot(dec_table, dec_bias.astype(jnp.float32), precision=highest).T.reshape(HEADS, ANS, ANS)
    causal = jnp.arange(ANS)[None, :] <= jnp.arange(ANS)[:, None]
    raw_scores = 0.125 * jnp.einsum("qihd,qjhd->qhij", dec_queries, dec_keys, preferred_element_type=jnp.float32)
    self_scores = jnp.where(causal, raw_scores + dec_position[None], -1000000000.0)
    self_top = jnp.max(self_scores, axis=-1, keepdims=True)
    self_exp = jnp.exp(self_scores - self_top)
    dec_probs = self_exp / jnp.sum(self_exp, axis=-1, keepdims=True)
    dec_attended = to_low(
        jnp.einsum("qhij,qjhd->qihd", to_low(dec_probs), dec_values, preferred_element_type=jnp.float32).reshape(answer_rows, D)
    )
    dec_mid = dec_x + product(dec_attended, dec_output)
    cross_normed, cross_scale = norm_forward(dec_mid, gain_cross)
    cross_low = to_low(cross_normed)
    cross_queries = to_low(product(cross_low, cross_query))

    merged = merge(cross_part(question_of, lengths, cross_queries, cross_keys, cross_values), pa)
    cross_attended = merged[:, :D]
    dec_after = dec_mid + exact_product(cross_attended, cross_output)
    dffn_normed, dffn_scale = norm_forward(dec_after, gain_dffn)
    dffn_low = to_low(dffn_normed)
    dec_pre = product(dffn_low, dec_ff_in)
    dec_hidden = to_low(smooth_unit(dec_pre))
    dec_y = dec_after + product(dec_hidden, dec_ff_out)
    grad_dec_y = dec_cot.astype(jnp.float32)
    out_grad_low = dec_cot
    pre_grad_low = to_low(smooth_back(dec_pre, product_nt(out_grad_low, dec_ff_out)))
    back_after, dec_gain_ffn_grad = norm_backward(dec_after, dffn_scale, gain_dffn, product_nt(pre_grad_low, dec_ff_in))
    grad_after = grad_dec_y + back_after
    after_low = to_low(grad_after)
    cross_att_grad = to_low(product_nt(after_low, cross_output))

    query_part, grad_cross = cross_back(
        question_of, lengths, cross_queries, cross_keys, cross_values, cross_att_grad, cross_attended, merged[:, D:]
    )
    grad_cross_q = lax.psum(query_part, "pa")

    eout_low, epre_low, emid_low, grad_enc_mid, enc_att_grad, final_gain_grad, ffn_gain_grad = post_backward(
        grad_cross, enc_y, enc_mid, enc_slope, enc_cot, gain_ffn, gain_final, cross_key, cross_value, enc_ff_out, enc_ff_in, enc_output
    )
    cross_terms = scatter(weight_grad(table, final_low, [grad_cross[0], grad_cross[1]], pb, pa, 256, 99), orders)
    ff_out_term = scatter(weight_grad(table[jnp.array([0, 2])], enc_hidden, [eout_low], pb, pa, 256, 99), orders[1:])
    ff_in_term = scatter(weight_grad(table, ffn_low, [epre_low], pb, pa, 512, 2), orders, (1024, 1024, 1024))
    output_term = scatter(weight_grad(table[jnp.array([0, 3])], enc_attended, [emid_low], pb, pa, 256, 99), orders[2:])
    grad_eq, grad_ek, grad_ev, fold = attn_backward(
        lengths, enc_queries, enc_keys, enc_values, enc_attended, enc_att_grad, enc_lse, base
    )
    attn_terms = scatter(
        weight_grad(table, attn_low, [grad_eq, grad_ek, grad_ev], pb, pa, 256, 3), orders, (768, 768, 768)
    )
    enc_in_grad, attn_gain_grad = qkv_backward(
        grad_eq, grad_ek, grad_ev, enc_in, grad_enc_mid, gain_attn, enc_query, enc_key, enc_value
    )
    enc_bias_grad = jnp.dot(fold.reshape(HEADS, WIDE), enc_table, precision=highest).T.reshape(BUCKETS * HEADS)

    back_mid, dec_gain_cross_grad = norm_backward(dec_mid, cross_scale, gain_cross, exact_nt(grad_cross_q, cross_query))
    grad_mid = grad_after + back_mid
    mid_low = to_low(grad_mid)
    dec_att_grad = to_low(product_nt(mid_low, dec_output)).reshape(questions, ANS, HEADS, HEAD)
    dec_dprob = jnp.einsum("qihd,qjhd->qhij", dec_att_grad, dec_values, preferred_element_type=jnp.float32)
    dec_dscore = dec_probs * (dec_dprob - jnp.sum(dec_probs * dec_dprob, axis=-1, keepdims=True))
    dec_bias_grad = jnp.dot(
        jnp.sum(dec_dscore, axis=0).reshape(HEADS, ANS * ANS), dec_table, precision=highest
    ).T.reshape(BUCKETS * HEADS)
    low_dscore = to_low(dec_dscore)
    grad_dq = to_low(
        0.125 * jnp.einsum("qhij,qjhd->qihd", low_dscore, dec_keys, preferred_element_type=jnp.float32)
    ).reshape(answer_rows, D)
    grad_dk = to_low(
        0.125 * jnp.einsum("qhij,qihd->qjhd", low_dscore, dec_queries, preferred_element_type=jnp.float32)
    ).reshape(answer_rows, D)
    grad_dv = to_low(
        jnp.einsum("qhij,qihd->qjhd", to_low(dec_probs), dec_att_grad, preferred_element_type=jnp.float32)
    ).reshape(answer_rows, D)
    self_back = product_nt(grad_dq, dec_query) + product_nt(grad_dk, dec_key) + product_nt(grad_dv, dec_value)
    back_dec_in, dec_gain_self_grad = norm_backward(dec_x, self_scale, gain_self, self_back)
    dec_in_grad = grad_mid + back_dec_in

    column = lax.axis_index("pa")

    def own_columns(values):
        rows = values.shape[1] // (pb * pa)
        cut = values.reshape(answer_rows, pb, pa, rows)
        return lax.dynamic_slice_in_dim(cut, column, 1, 2).reshape(answer_rows, pb * rows)

    def dec_term(left, right, times=product_tn):
        left = own_columns(left)
        return times(left, right).reshape(pb, left.shape[1] // pb, right.shape[1])

    ff_rows = dec_hidden.shape[1]
    thin = [
        dec_term(self_low, grad_dq),
        dec_term(self_low, grad_dk),
        dec_term(self_low, grad_dv),
        dec_term(dec_attended, mid_low),
        dec_term(cross_low, grad_cross_q, exact_tn),
        dec_term(cross_attended, after_low, exact_tn),
        dec_term(dec_hidden, out_grad_low),
    ]
    wide = dec_term(dffn_low, pre_grad_low)
    thin += [wide[:, :, c * D : (c + 1) * D] for c in range(ff_rows // D)]
    heights = [t.shape[1] for t in thin]
    dec_sum = lax.psum_scatter(jnp.concatenate(thin, axis=1), "pb", scatter_dimension=0, tiled=False)
    cuts = np.cumsum([0] + heights)
    got = [dec_sum[a:b] for a, b in zip(cuts[:-1], cuts[1:])]
    dec_ff_in_grad = jnp.concatenate(got[7:], axis=1)

    shards = pb * pa
    share = 1.0 / pa
    small_list = [
        attn_gain_grad[0], ffn_gain_grad[0], final_gain_grad[0], enc_bias_grad,
        dec_gain_self_grad * share, dec_gain_cross_grad * share, dec_gain_ffn_grad * share, dec_bias_grad * share,
    ]
    small_rows = [s.shape[0] // shards for s in small_list]
    small = scatter_small(jnp.concatenate([s.reshape(shards, -1) for s in small_list], axis=1), orders, sizes)
    cuts = np.cumsum([0] + small_rows)
    smalls = [small[a:b] for a, b in zip(cuts[:-1], cuts[1:])]

    return (
        enc_out, to_low(dec_y), enc_in_grad, dec_in_grad,
        smalls[0], attn_terms[:, :D], attn_terms[:, D : 2 * D], attn_terms[:, 2 * D :], output_term, smalls[3],
        smalls[1], ff_in_term, ff_out_term, smalls[2], cross_terms[:, :D], cross_terms[:, D:],
        smalls[4], got[0], got[1], got[2], got[3], smalls[7], smalls[5], got[4], got[5], smalls[6], dec_ff_in_grad, got[6],
    )


def solution(mesh):
    pb, pa = mesh.shape["pb"], mesh.shape["pa"]
    rows = P(("pb", "pa"), None)
    flat = P(("pb", "pa"))
    dec = P("pb", None)
    return jax.shard_map(
        functools.partial(local, pb, pa),
        mesh=mesh,
        in_specs=(rows, dec, flat, flat) + (P(),) * 24 + (rows, dec),
        out_specs=(rows, dec, rows, dec)
        + (flat, rows, rows, rows, rows, flat, flat, rows, rows, flat, rows, rows)
        + (flat, rows, rows, rows, rows, flat, flat, rows, rows, flat, rows, rows),
        check_vma=False,
    )
```

```python
import functools
import math

import jax
import jax.numpy as jnp
import numpy as np
from jax import lax
from jax.experimental import pallas as pl
from jax.experimental.pallas import tpu as pltpu
from jax.sharding import PartitionSpec as P

D = 768
HEADS = 12
HEAD = 64
BUCKETS = 32
PL = 512
ANS = 24

far_distance = 128
epsilon = 1e-06
highest = lax.Precision.HIGHEST


def bucket_of(offset, bidirectional):
    if bidirectional:
        halves = BUCKETS // 2
        base_bucket = halves if offset > 0 else 0
        distance = abs(offset)
    else:
        halves = BUCKETS
        base_bucket = 0
        distance = max(-offset, 0)
    exact_count = halves // 2
    if distance < exact_count:
        return base_bucket + distance
    scaled = (
        math.log(distance / exact_count)
        / math.log(far_distance / exact_count)
        * (halves - exact_count)
    )
    return base_bucket + min(exact_count + int(scaled), halves - 1)


def to_low(values):
    return values.astype(jnp.bfloat16)


def product_tn(left, right):
    return lax.dot_general(
        left, right, (((0,), (0,)), ((), ())), preferred_element_type=jnp.float32
    )


STRIP = 128
WIDE = 1024


def strip_table():
    table = np.zeros((WIDE, BUCKETS), np.float32)
    for place in range(WIDE):
        if place < PL + STRIP * 3:
            offset = PL - STRIP - place
        else:
            offset = PL - STRIP + WIDE - place
        if abs(offset) < PL:
            table[place, bucket_of(offset, True)] = 1.0
    return table


def nn(left, right):
    return lax.dot_general(left, right, (((1,), (0,)), ((), ())), preferred_element_type=jnp.float32)


def head_lanes(values, head):
    lane = lax.broadcasted_iota(jnp.int32, values.shape, 1)
    keep = lane < HEAD if head == 0 else lane >= HEAD
    return jnp.where(keep, values, jnp.zeros_like(values))


def key_mask(length):
    place = lax.broadcasted_iota(jnp.int32, (PL, 1), 0)
    return jnp.where(place < length, 0.0, -1e9)


def build_strip(base_ref, strip_ref):
    for head in range(2):
        row = base_ref[0, head : head + 1, :]
        spread = jnp.broadcast_to(row, (STRIP, WIDE))
        strip_ref[head] = pltpu.roll(spread, 0, 1, stride=1, stride_axis=0)


def attn_forward_kernel(lengths_ref, q_ref, k_ref, v_ref, base_ref, out_ref, lse_ref, strip_ref, score_ref, outT_ref):
    passage = pl.program_id(1)

    @pl.when(passage == 0)
    def _():
        build_strip(base_ref, strip_ref)

    mask = key_mask(lengths_ref[passage])
    q_t = q_ref[...].T
    v_t = v_ref[...].T
    k = k_ref[...]
    blocks = PL // STRIP
    for head in range(2):
        k_head = head_lanes(k, head)
        top = None
        for b in range(blocks):
            rows = slice(b * STRIP, (b + 1) * STRIP)
            start = PL - STRIP - b * STRIP
            s = nn(k_head[rows], q_t) + strip_ref[head, :, start : start + PL] + mask[rows]
            score_ref[head, rows, :] = s
            here = jnp.max(s, axis=0, keepdims=True)
            top = here if top is None else jnp.maximum(top, here)
        total = None
        acc = None
        for b in range(blocks):
            rows = slice(b * STRIP, (b + 1) * STRIP)
            e = jnp.exp(score_ref[head, rows, :] - top)
            here = jnp.sum(e, axis=0, keepdims=True)
            total = here if total is None else total + here
            part = nn(v_t[head * HEAD : (head + 1) * HEAD, rows], to_low(e))
            acc = part if acc is None else acc + part
        outT_ref[head * HEAD : (head + 1) * HEAD, :] = to_low(acc * (1.0 / total))
        lse_ref[0, 0, head : head + 1, :] = top + jnp.log(total)
    out_ref[...] = outT_ref[...].T


def attn_forward(lengths, q, k, v, base):
    passages = lengths.shape[0]
    pairs = HEADS // 2
    tile = pl.BlockSpec((PL, 128), lambda h, p, *_: (p, h))
    return pl.pallas_call(
        attn_forward_kernel,
        grid_spec=pltpu.PrefetchScalarGridSpec(
            num_scalar_prefetch=1,
            grid=(pairs, passages),
            in_specs=[tile, tile, tile, pl.BlockSpec((1, 2, WIDE), lambda h, p, *_: (h, 0, 0))],
            out_specs=[tile, pl.BlockSpec((1, 1, 2, PL), lambda h, p, *_: (h, p, 0, 0))],
            scratch_shapes=[
                pltpu.VMEM((2, STRIP, WIDE), jnp.float32),
                pltpu.VMEM((2, PL, PL), jnp.float32),
                pltpu.VMEM((128, PL), jnp.bfloat16),
            ],
        ),
        out_shape=[
            jax.ShapeDtypeStruct((passages * PL, D), jnp.bfloat16),
            jax.ShapeDtypeStruct((pairs, passages, 2, PL), jnp.float32),
        ],
        compiler_params=pltpu.CompilerParams(vmem_limit_bytes=32 * 2**20),
        name="enc_attention",
    )(lengths, q, k, v, base)


def attn_backward_kernel(
    beside, passage, passages, lengths_ref, q_ref, k_ref, v_ref, o_ref, do_ref, lse_ref, base_ref,
    dq_ref, dk_ref, dv_ref, fold_ref,
    strip_ref, gather_ref, dqT_ref,
):
    @pl.when(passage == 0)
    def _():
        build_strip(base_ref, strip_ref)
        gather_ref[...] = jnp.zeros_like(gather_ref)

    mask = key_mask(lengths_ref[passage])
    q = q_ref[...]
    k = k_ref[...]
    v = v_ref[...]
    do = do_ref[...]
    q_t = q.T
    k_t = k.T
    do_t = do.T
    o_t = o_ref[...].T
    weighed = do_t.astype(jnp.float32) * o_t.astype(jnp.float32)
    blocks = PL // STRIP
    lane = lax.broadcasted_iota(jnp.int32, (STRIP, 128), 1)
    first = lane < HEAD
    dks = []
    dvs = []
    for head in range(2):
        beside(head)
        heads = slice(head * HEAD, (head + 1) * HEAD)
        delta = jnp.sum(weighed[heads], axis=0, keepdims=True)
        lse = lse_ref[0, 0, head : head + 1, :]
        k_head = head_lanes(k, head)
        v_head = head_lanes(v, head)
        acc = None
        for b in range(blocks):
            rows = slice(b * STRIP, (b + 1) * STRIP)
            start = PL - STRIP - b * STRIP
            s = nn(k_head[rows], q_t) + strip_ref[head, :, start : start + PL] + mask[rows]
            p = jnp.exp(s - lse)
            dp = nn(v_head[rows], do_t)
            ds = p * (dp - delta)
            gather_ref[head, :, start : start + PL] += ds
            ds_low = to_low(ds)
            dv_part = nn(to_low(p), do)
            dk_part = nn(ds_low, q)
            if head == 0:
                dvs.append(dv_part)
                dks.append(dk_part)
            else:
                dv_ref[rows, :] = to_low(jnp.where(first, dvs[b], dv_part))
                dk_ref[rows, :] = to_low(jnp.where(first, dks[b], dk_part))
            part = nn(k_t[heads, rows], ds_low)
            acc = part if acc is None else acc + part
        dqT_ref[heads, :] = to_low(0.125 * acc)
    dq_ref[...] = dqT_ref[...].T

    @pl.when(passage == passages - 1)
    def _():
        row = lax.broadcasted_iota(jnp.int32, (8, WIDE), 0)
        for head in range(2):
            total = gather_ref[head, 0:8, :]
            for group in range(1, STRIP // 8):
                total = total + pltpu.roll(gather_ref[head, group * 8 : group * 8 + 8, :], WIDE - group * 8, 1)
            for bit in (1, 2, 4):
                total = jnp.where((row // bit) % 2 == 1, pltpu.roll(total, WIDE - bit, 1), total)
            fold_ref[0, head : head + 1, :] = jnp.sum(total, axis=0, keepdims=True)


MIB = 2**20


def nt(left, right):
    return lax.dot_general(left, right, (((1,), (1,)), ((), ())), preferred_element_type=jnp.float32)


def rms(values, gain):
    scale = lax.rsqrt(jnp.mean(values * values, axis=-1, keepdims=True) + epsilon)
    return values * scale * gain, scale


def rms_back(values, scale, gain, grad):
    scaled = grad * gain
    gain_grad = jnp.sum(grad * values * scale, axis=0, keepdims=True)
    inner = jnp.mean(scaled * values, axis=-1, keepdims=True)
    return scaled * scale - values * (scale * scale * scale) * inner, gain_grad


def gelu_both(v):
    c = math.sqrt(2.0 / math.pi)
    square = v * v
    t = jnp.tanh(v * (c + (c * 0.044715) * square))
    half = 0.5 + 0.5 * t
    slope = half + (half * (1.0 - t)) * v * (c + (3.0 * 0.044715 * c) * square)
    return v * half, slope


def whole(array):
    return pl.BlockSpec(array.shape, lambda *_: (0,) * array.ndim)


def rows_of(tile, width):
    return pl.BlockSpec((tile, width), lambda i: (i, 0))


def sds(shape, kind):
    return jax.ShapeDtypeStruct(shape, kind)


def params(mib):
    return pltpu.CompilerParams(vmem_limit_bytes=mib * MIB)


def qkv_kernel(x_ref, gain_ref, wq_ref, wk_ref, wv_ref, turned_ref, q_ref, k_ref, v_ref):
    normed, _ = rms(x_ref[...].astype(jnp.float32), gain_ref[...])
    low = to_low(normed)
    turned_ref[...] = low.T
    q_ref[...] = to_low(0.125 * to_low(nn(low, wq_ref[...])).astype(jnp.float32))
    k_ref[...] = to_low(nn(low, wk_ref[...]))
    v_ref[...] = to_low(nn(low, wv_ref[...]))


def qkv_forward(x, gain, wq, wk, wv):
    tokens = x.shape[0]
    tile = 256
    big = sds((tokens, D), jnp.bfloat16)
    return pl.pallas_call(
        qkv_kernel,
        grid=(tokens // tile,),
        in_specs=[rows_of(tile, D)] + [whole(a) for a in (gain, wq, wk, wv)],
        out_specs=[pl.BlockSpec((D, tile), lambda i: (0, i))] + [rows_of(tile, D)] * 3,
        out_shape=[sds((D, tokens), jnp.bfloat16)] + [big] * 3,
        compiler_params=params(40),
        name="enc_qkv",
    )(x, gain, wq, wk, wv)


def post_kernel(
    x_ref, att_ref, gain_ffn_ref, gain_final_ref, wo_ref, win_ref, wout_ref, wck_ref, wcv_ref,
    mid_ref, ffn_low_ref, hidden_ref, slope_ref, y_ref, out_ref, final_low_ref, ck_ref, cv_ref,
):
    mid = x_ref[...].astype(jnp.float32) + nn(att_ref[...], wo_ref[...])
    mid_ref[...] = mid
    normed, _ = rms(mid, gain_ffn_ref[...])
    low = to_low(normed)
    ffn_low_ref[...] = low
    y = mid
    width = 768
    for c in range(win_ref.shape[1] // width):
        cols = slice(c * width, (c + 1) * width)
        hidden, slope = gelu_both(nn(low, win_ref[:, cols]))
        hidden = to_low(hidden)
        hidden_ref[:, cols] = hidden
        slope_ref[:, cols] = to_low(slope)
        y = y + nn(hidden, wout_ref[cols, :])
    y_ref[...] = y
    out_ref[...] = to_low(y)
    final, _ = rms(y, gain_final_ref[...])
    final = to_low(final)
    final_low_ref[...] = final
    ck_ref[...] = to_low(nn(final, wck_ref[...]))
    cv_ref[...] = to_low(nn(final, wcv_ref[...]))


def post_forward(x, att, gain_ffn, gain_final, wo, win, wout, wck, wcv):
    tokens = x.shape[0]
    tile = 256
    ff = win.shape[1]
    low = sds((tokens, D), jnp.bfloat16)
    wide = sds((tokens, ff), jnp.bfloat16)
    full = sds((tokens, D), jnp.float32)
    d = rows_of(tile, D)
    f = rows_of(tile, ff)
    return pl.pallas_call(
        post_kernel,
        grid=(tokens // tile,),
        in_specs=[d, d] + [whole(a) for a in (gain_ffn, gain_final, wo, win, wout, wck, wcv)],
        out_specs=[d, d, f, f, d, d, d, d, d],
        out_shape=[full, low, wide, wide, full, low, low, low, low],
        compiler_params=params(56),
        name="enc_post",
    )(x, att, gain_ffn, gain_final, wo, win, wout, wck, wcv)


def back_kernel(
    gkv_ref, y_ref, mid_ref, slope_ref, cot_ref, gain_ffn_ref, gain_final_ref,
    wck_ref, wcv_ref, wout_ref, win_ref, wo_ref,
    eout_ref, epre_ref, emid_ref, grad_mid_ref, att_grad_ref, gain_final_grad_ref, gain_ffn_grad_ref,
):
    @pl.when(pl.program_id(0) == 0)
    def _():
        gain_final_grad_ref[...] = jnp.zeros_like(gain_final_grad_ref)
        gain_ffn_grad_ref[...] = jnp.zeros_like(gain_ffn_grad_ref)

    y = y_ref[...]
    scale = lax.rsqrt(jnp.mean(y * y, axis=-1, keepdims=True) + epsilon)
    final_back = nt(gkv_ref[0], wck_ref[...]) + nt(gkv_ref[1], wcv_ref[...])
    back, gain_grad = rms_back(y, scale, gain_final_ref[...], final_back)
    gain_final_grad_ref[...] += gain_grad
    grad_y = cot_ref[...].astype(jnp.float32) + back
    eout = to_low(grad_y)
    eout_ref[...] = eout
    width = 768
    acc = None
    for c in range(win_ref.shape[1] // width):
        cols = slice(c * width, (c + 1) * width)
        epre = to_low(slope_ref[:, cols].astype(jnp.float32) * nt(eout, wout_ref[cols, :]))
        epre_ref[:, cols] = epre
        part = nt(epre, win_ref[:, cols])
        acc = part if acc is None else acc + part
    mid = mid_ref[...]
    scale = lax.rsqrt(jnp.mean(mid * mid, axis=-1, keepdims=True) + epsilon)
    back, gain_grad = rms_back(mid, scale, gain_ffn_ref[...], acc)
    gain_ffn_grad_ref[...] += gain_grad
    grad_mid = grad_y + back
    grad_mid_ref[...] = grad_mid
    emid = to_low(grad_mid)
    emid_ref[...] = emid
    att_grad_ref[...] = to_low(nt(emid, wo_ref[...]))


def post_backward(gkv, y, mid, slope, cot, gain_ffn, gain_final, wck, wcv, wout, win, wo):
    tokens = y.shape[0]
    tile = 256
    ff = win.shape[1]
    low = sds((tokens, D), jnp.bfloat16)
    d = rows_of(tile, D)
    f = rows_of(tile, ff)
    gain = pl.BlockSpec((1, D), lambda i: (0, 0))
    return pl.pallas_call(
        back_kernel,
        grid=(tokens // tile,),
        in_specs=[pl.BlockSpec((2, tile, D), lambda i: (0, i, 0)), d, d, f, d]
        + [whole(a) for a in (gain_ffn, gain_final, wck, wcv, wout, win, wo)],
        out_specs=[d, f, d, d, d, gain, gain],
        out_shape=[low, sds((tokens, ff), jnp.bfloat16), low, sds((tokens, D), jnp.float32), low]
        + [sds((1, D), jnp.float32)] * 2,
        compiler_params=params(56),
        name="enc_post_back",
    )(gkv, y, mid, slope, cot, gain_ffn, gain_final, wck, wcv, wout, win, wo)


def qkv_back_kernel(opening, dq_ref, dk_ref, dv_ref, x_ref, grad_mid_ref, gain_ref, wq_ref, wk_ref, wv_ref, out_ref, gain_grad_ref):
    @pl.when(opening)
    def _():
        gain_grad_ref[...] = jnp.zeros_like(gain_grad_ref)

    x = x_ref[...].astype(jnp.float32)
    scale = lax.rsqrt(jnp.mean(x * x, axis=-1, keepdims=True) + epsilon)
    grad = nt(dq_ref[...], wq_ref[...]) + nt(dk_ref[...], wk_ref[...]) + nt(dv_ref[...], wv_ref[...])
    back, gain_grad = rms_back(x, scale, gain_ref[...], grad)
    gain_grad_ref[...] += gain_grad
    out_ref[...] = grad_mid_ref[...] + back


def weight_grad_kernel(rows, pb, pa, tiles, per_chain, table_ref, left_ref, *refs):
    rights = refs[: len(tiles)]
    keep_ref, send_ref, turned_ref = refs[len(tiles) :]
    step = pl.program_id(0)
    depth, height = left_ref.shape

    @pl.when(step == 0)
    def _():
        for c in range(height // 256):
            cols = slice(c * 256, (c + 1) * 256)
            turned_ref[cols, :] = left_ref[:, cols].T

    core = table_ref[0, 0]
    chain = step // per_chain
    half_rows = pa * rows

    def work(right):
        for y in range(pb // 2):
            low_part = nn(turned_ref[2 * y * half_rows : (2 * y + 1) * half_rows, :], right)
            high_part = nn(turned_ref[(2 * y + 1) * half_rows : (2 * y + 2) * half_rows, :], right)
            mine = jnp.where(core == 0, low_part, high_part)
            other = jnp.where(core == 0, high_part, low_part)
            for a in range(pa):
                slot = table_ref[chain + 1, y * pa + a]
                keep_ref[slot] = mine[a * rows : (a + 1) * rows]
                send_ref[slot] = other[a * rows : (a + 1) * rows]

    first = 0
    for right_ref, count in zip(rights, tiles):
        if len(tiles) == 1:
            work(right_ref[...])
        else:
            @pl.when((step >= first) & (step < first + count))
            def _(right_ref=right_ref):
                work(right_ref[...])
        first += count


def weight_grad(table, left, rights, pb, pa, width, per_chain):
    tokens, height = left.shape
    rows = height // (pb * pa)
    tiles = [r.shape[1] // width for r in rights]
    total = sum(tiles)
    firsts = np.cumsum([0] + tiles)[:-1]

    def spec(first, count):
        return pl.BlockSpec((tokens, width), lambda i, *_: (0, jnp.clip(i - int(first), 0, count - 1)))

    half = pb * pa // 2
    out = pl.BlockSpec((half, rows, width), lambda i, *_: (0, 0, i))
    shape = sds((half, rows, total * width), jnp.float32)
    return pl.pallas_call(
        functools.partial(weight_grad_kernel, rows, pb, pa, tiles, per_chain),
        grid_spec=pltpu.PrefetchScalarGridSpec(
            num_scalar_prefetch=1,
            grid=(total,),
            in_specs=[pl.BlockSpec((tokens, height), lambda i, *_: (0, 0))] + [spec(f, c) for f, c in zip(firsts, tiles)],
            out_specs=[out, out],
            scratch_shapes=[pltpu.VMEM((height, tokens), jnp.bfloat16)],
        ),
        out_shape=[shape, shape],
        compiler_params=params(56),
        name="weight_grad",
    )(table, left, *rights)


PACK = 896


def permitted_mask(question_ref, length_ref, answer_rows, passages):
    row = lax.broadcasted_iota(jnp.int32, (answer_rows, PL), 0)
    place = lax.broadcasted_iota(jnp.int32, (answer_rows, PL), 1)
    whose = row // ANS
    return jnp.concatenate(
        [(whose == question_ref[p]) & (place < length_ref[p]) for p in range(passages)], axis=1
    )


def cross_part_kernel(question_ref, length_ref, q_ref, ck_ref, cv_ref, part_ref):
    rows = q_ref.shape[0]
    mask = permitted_mask(question_ref, length_ref, rows, ck_ref.shape[0] // PL)
    lane = lax.broadcasted_iota(jnp.int32, (rows, 128), 1)
    stats = jnp.zeros((rows, 128), jnp.float32)
    for pair in range(HEADS // 2):
        cols = slice(pair * 128, (pair + 1) * 128)
        q = q_ref[:, cols]
        k = ck_ref[:, cols]
        v = cv_ref[:, cols]
        outs = []
        for head in range(2):
            s = jnp.where(mask, 0.125 * nt(head_lanes(q, head), k), -1e9)
            top = jnp.max(s, axis=1, keepdims=True)
            e = jnp.exp(s - top)
            total = jnp.sum(e, axis=1, keepdims=True)
            outs.append(nn(to_low(e), v))
            place = 2 * pair + head
            stats = jnp.where(lane == place, top, jnp.where(lane == HEADS + place, total, stats))
        part_ref[:, cols] = jnp.where(lane < HEAD, outs[0], outs[1])
    part_ref[:, D:] = stats


def cross_part(question_of, lengths, q, ck, cv):
    vmem = pl.BlockSpec(memory_space=pltpu.VMEM)
    smem = pl.BlockSpec(memory_space=pltpu.SMEM)
    return pl.pallas_call(
        cross_part_kernel,
        in_specs=[smem, smem, vmem, vmem, vmem],
        out_specs=vmem,
        out_shape=sds((q.shape[0], PACK), jnp.float32),
        compiler_params=params(40),
        name="cross_part",
    )(question_of, lengths, q, ck, cv)


def over_heads(stats, rows):
    lane = lax.broadcasted_iota(jnp.int32, (rows, 128), 1)
    return jnp.concatenate(
        [jnp.where(lane < HEAD, stats[:, 2 * g : 2 * g + 1], stats[:, 2 * g + 1 : 2 * g + 2]) for g in range(HEADS // 2)],
        axis=1,
    )


def merge_kernel(pa, part_ref, out_ref, recv_ref, mine_ref, send_sem, recv_sem, send2_sem, recv2_sem):
    me = lax.axis_index("pa")
    rows = part_ref.shape[1]
    barrier = pltpu.get_barrier_semaphore()
    for off in range(1, pa):
        pl.semaphore_signal(barrier, inc=1, device_id={"pa": lax.rem(me + off, pa)}, device_id_type=pl.DeviceIdType.MESH)
    pl.semaphore_wait(barrier, pa - 1)

    def first(off):
        peer = lax.rem(me + off, pa)
        return pltpu.make_async_remote_copy(
            src_ref=part_ref.at[peer], dst_ref=recv_ref.at[off], send_sem=send_sem.at[off], recv_sem=recv_sem.at[off],
            device_id={"pa": peer}, device_id_type=pl.DeviceIdType.MESH,
        )

    def second(off):
        peer = lax.rem(me + off, pa)
        return pltpu.make_async_remote_copy(
            src_ref=mine_ref, dst_ref=out_ref.at[me], send_sem=send2_sem.at[off], recv_sem=recv2_sem.at[off],
            device_id={"pa": peer}, device_id_type=pl.DeviceIdType.MESH,
        )

    for off in range(1, pa):
        first(off).start()
    recv_ref[0] = part_ref[me]
    for off in range(1, pa):
        first(off).wait()
    tops = [recv_ref[i, :, D : D + 128][:, :HEADS] for i in range(pa)]
    top = tops[0]
    for t in tops[1:]:
        top = jnp.maximum(top, t)
    total = jnp.zeros((rows, HEADS), jnp.float32)
    acc = jnp.zeros((rows, D), jnp.float32)
    for i in range(pa):
        w = jnp.exp(tops[i] - top)
        total = total + w * recv_ref[i, :, D : D + 128][:, HEADS : 2 * HEADS]
        acc = acc + over_heads(w, rows) * recv_ref[i, :, :D]
    mine_ref[:, :D] = acc / over_heads(total, rows)
    lse = top + jnp.log(total)
    mine_ref[:, D:] = jnp.concatenate([lse, jnp.zeros((rows, 128 - HEADS), jnp.float32)], axis=1)
    for off in range(1, pa):
        second(off).start()
    out_ref[me] = mine_ref[...]
    for off in range(1, pa):
        second(off).wait()


def merge(part, pa):
    answer_rows = part.shape[0]
    rows = answer_rows // pa
    block = (pa, rows, PACK)
    vmem = pl.BlockSpec(memory_space=pltpu.VMEM)
    out = pl.pallas_call(
        functools.partial(merge_kernel, pa),
        in_specs=[vmem],
        out_specs=vmem,
        out_shape=sds(block, jnp.float32),
        scratch_shapes=[
            pltpu.VMEM(block, jnp.float32),
            pltpu.VMEM((rows, PACK), jnp.float32),
            pltpu.SemaphoreType.DMA((pa,)),
            pltpu.SemaphoreType.DMA((pa,)),
            pltpu.SemaphoreType.DMA((pa,)),
            pltpu.SemaphoreType.DMA((pa,)),
        ],
        compiler_params=pltpu.CompilerParams(collective_id=0, has_side_effects=True, vmem_limit_bytes=16 * MIB),
        name="cross_merge",
    )(part.reshape(block))
    return out.reshape(answer_rows, PACK)


def cross_back_kernel(question_ref, length_ref, q_ref, ck_ref, cv_ref, grad_ref, att_ref, lse_ref, gq_ref, gkv_ref):
    rows = q_ref.shape[0]
    mask = permitted_mask(question_ref, length_ref, rows, ck_ref.shape[0] // PL)
    lane = lax.broadcasted_iota(jnp.int32, (rows, 128), 1)
    for pair in range(HEADS // 2):
        cols = slice(pair * 128, (pair + 1) * 128)
        q = q_ref[:, cols]
        k = ck_ref[:, cols]
        v = cv_ref[:, cols]
        g = grad_ref[:, cols]
        weighed = g.astype(jnp.float32) * att_ref[:, cols]
        gqs = []
        scores = []
        probs = []
        for head in range(2):
            place = 2 * pair + head
            s = jnp.where(mask, 0.125 * nt(head_lanes(q, head), k), -1e9)
            p = jnp.exp(s - lse_ref[:, place : place + 1])
            dp = nt(head_lanes(g, head), v)
            delta = jnp.sum(head_lanes(weighed, head), axis=1, keepdims=True)
            ds = to_low(p * (dp - delta))
            gqs.append(nn(ds, k))
            scores.append(ds)
            probs.append(to_low(p))
        gq_ref[:, cols] = 0.125 * jnp.where(lane < HEAD, gqs[0], gqs[1])
        both_q = jnp.concatenate([head_lanes(q, 0), head_lanes(q, 1)], axis=0)
        both_g = jnp.concatenate([head_lanes(g, 0), head_lanes(g, 1)], axis=0)
        gkv_ref[0, :, cols] = to_low(0.125 * product_tn(jnp.concatenate(scores, axis=0), both_q))
        gkv_ref[1, :, cols] = to_low(product_tn(jnp.concatenate(probs, axis=0), both_g))


def cross_back(question_of, lengths, q, ck, cv, grad, att, lse):
    vmem = pl.BlockSpec(memory_space=pltpu.VMEM)
    smem = pl.BlockSpec(memory_space=pltpu.SMEM)
    return pl.pallas_call(
        cross_back_kernel,
        in_specs=[smem, smem] + [vmem] * 6,
        out_specs=[vmem, vmem],
        out_shape=[sds((q.shape[0], D), jnp.float32), sds((2, ck.shape[0], D), jnp.bfloat16)],
        compiler_params=params(40),
        name="cross_back",
    )(question_of, lengths, q, ck, cv, grad, att, lse)


def causal_row(length):
    table = np.zeros((128, BUCKETS), np.float32)
    for back in range(length):
        table[-back % 128, bucket_of(-back, False)] = 1.0
    return table


def in_three(values):
    high = to_low(values)
    rest = values - high.astype(jnp.float32)
    middle = to_low(rest)
    return high, middle, to_low(rest - middle.astype(jnp.float32))


def dec_pre_kernel(
    x_ref, gain_self_ref, gain_cross_ref, base_ref, wq_ref, wk_ref, wv_ref, wo_ref, wcq_ref,
    low_ref, q_ref, k_ref, v_ref, probs_ref, att_ref, mid_ref, cross_low_ref, cross_q_ref,
):
    rows = x_ref.shape[0]
    x = x_ref[...].astype(jnp.float32)
    normed, _ = rms(x, gain_self_ref[...])
    low = to_low(normed)
    low_ref[...] = low
    q = to_low(0.125 * to_low(nn(low, wq_ref[...])).astype(jnp.float32))
    k = to_low(nn(low, wk_ref[...]))
    v = to_low(nn(low, wv_ref[...]))
    q_ref[...] = q
    k_ref[...] = k
    v_ref[...] = v
    i = lax.broadcasted_iota(jnp.int32, (rows, rows), 0)
    j = lax.broadcasted_iota(jnp.int32, (rows, rows), 1)
    mask = (j <= i) & (i // ANS == j // ANS)
    lane = lax.broadcasted_iota(jnp.int32, (rows, 128), 1)
    for pair in range(HEADS // 2):
        cols = slice(pair * 128, (pair + 1) * 128)
        outs = []
        for half in range(2):
            head = 2 * pair + half
            spread = jnp.broadcast_to(base_ref[head : head + 1, :], (rows, 128))
            bias = pltpu.roll(spread, 0, 1, stride=1, stride_axis=0)[:, :rows]
            s = jnp.where(mask, nt(head_lanes(q[:, cols], half), k[:, cols]) + bias, -1e9)
            e = jnp.exp(s - jnp.max(s, axis=1, keepdims=True))
            p = e / jnp.sum(e, axis=1, keepdims=True)
            probs_ref[head] = p
            outs.append(nn(to_low(p), v[:, cols]))
        att_ref[:, cols] = to_low(jnp.where(lane < HEAD, outs[0], outs[1]))
    mid = x + nn(att_ref[...], wo_ref[...])
    mid_ref[...] = mid
    normed, _ = rms(mid, gain_cross_ref[...])
    low = to_low(normed)
    cross_low_ref[...] = low
    cross_q_ref[...] = to_low(nn(low, wcq_ref[...]))


def in_vmem(kernel, outs, name, *args, smem=0):
    vmem = pl.BlockSpec(memory_space=pltpu.VMEM)
    return pl.pallas_call(
        kernel,
        in_specs=[pl.BlockSpec(memory_space=pltpu.SMEM)] * smem + [vmem] * (len(args) - smem),
        out_specs=[vmem] * len(outs),
        out_shape=outs,
        compiler_params=params(56),
        name=name,
    )(*args)


def dec_pre(x, gain_self, gain_cross, base, wq, wk, wv, wo, wcq):
    rows = x.shape[0]
    low = sds((rows, D), jnp.bfloat16)
    full = sds((rows, D), jnp.float32)
    outs = [low, low, low, low, sds((HEADS, rows, rows), jnp.float32), low, full, low, low]
    return in_vmem(dec_pre_kernel, outs, "dec_pre", x, gain_self, gain_cross, base, wq, wk, wv, wo, wcq)


def dec_mid_kernel(
    merged_ref, mid_ref, cot_ref, gain_ref, wco_ref, win_ref, wout_ref,
    out_ref, low_ref, hidden_ref, pre_grad_ref, after_low_ref, grad_after_ref, att_grad_ref, gain_grad_ref, slope_ref,
):
    rows = mid_ref.shape[0]
    three = nn(jnp.concatenate(in_three(merged_ref[:, :D]), axis=0), wco_ref[...])
    after = mid_ref[...] + (three[:rows] + three[rows : 2 * rows] + three[2 * rows :])
    normed, scale = rms(after, gain_ref[...])
    low = to_low(normed)
    low_ref[...] = low
    y = after
    width = 768
    chunks = [slice(c * width, (c + 1) * width) for c in range(win_ref.shape[1] // width)]
    for cols in chunks:
        hidden, slope = gelu_both(nn(low, win_ref[:, cols]))
        hidden = to_low(hidden)
        hidden_ref[:, cols] = hidden
        slope_ref[:, cols] = slope
        y = y + nn(hidden, wout_ref[cols, :])
    out_ref[...] = to_low(y)
    cot = cot_ref[...]
    acc = None
    for cols in chunks:
        pre = to_low(slope_ref[:, cols] * nt(cot, wout_ref[cols, :]))
        pre_grad_ref[:, cols] = pre
        part = nt(pre, win_ref[:, cols])
        acc = part if acc is None else acc + part
    back, gain_grad = rms_back(after, scale, gain_ref[...], acc)
    gain_grad_ref[...] = gain_grad
    grad_after = cot.astype(jnp.float32) + back
    grad_after_ref[...] = grad_after
    after_low = to_low(grad_after)
    after_low_ref[...] = after_low
    att_grad_ref[...] = to_low(nt(after_low, wco_ref[...]))


def dec_mid_call(merged, mid, cot, gain, wco, win, wout):
    rows = mid.shape[0]
    ff = win.shape[1]
    low = sds((rows, D), jnp.bfloat16)
    full = sds((rows, D), jnp.float32)
    wide = sds((rows, ff), jnp.bfloat16)
    outs = [low, low, wide, wide, low, full, low, sds((1, D), jnp.float32)]
    vmem = pl.BlockSpec(memory_space=pltpu.VMEM)
    return pl.pallas_call(
        dec_mid_kernel,
        in_specs=[vmem] * 7,
        out_specs=[vmem] * len(outs),
        out_shape=outs,
        scratch_shapes=[pltpu.VMEM((rows, ff), jnp.float32)],
        compiler_params=params(56),
        name="dec_mid",
    )(merged, mid, cot, gain, wco, win, wout)


def dec_post_kernel(
    gq_ref, grad_after_ref, mid_ref, x_ref, q_ref, k_ref, v_ref, probs_ref, gain_self_ref, gain_cross_ref,
    wq_ref, wk_ref, wv_ref, wo_ref, wcq_ref, after_ref,
    mid_low_ref, dq_ref, dk_ref, dv_ref, out_ref, gain_self_grad_ref, gain_cross_grad_ref, fold_ref,
):
    rows = x_ref.shape[0]
    mid = mid_ref[...]
    scale = lax.rsqrt(jnp.mean(mid * mid, axis=-1, keepdims=True) + epsilon)
    three = nt(jnp.concatenate(in_three(gq_ref[...]), axis=0), wcq_ref[...])
    back, gain_grad = rms_back(mid, scale, gain_cross_ref[...], three[:rows] + three[rows : 2 * rows] + three[2 * rows :])
    gain_cross_grad_ref[...] = gain_grad
    grad_mid = grad_after_ref[...] + back
    mid_low = to_low(grad_mid)
    mid_low_ref[...] = mid_low
    att_grad = to_low(nt(mid_low, wo_ref[...]))
    lane = lax.broadcasted_iota(jnp.int32, (rows, 128), 1)
    row8 = lax.broadcasted_iota(jnp.int32, (8, 128), 0)
    for pair in range(HEADS // 2):
        cols = slice(pair * 128, (pair + 1) * 128)
        q = q_ref[:, cols]
        k = k_ref[:, cols]
        v = v_ref[:, cols]
        g = att_grad[:, cols]
        dqs = []
        scores = []
        probs = []
        for half in range(2):
            head = 2 * pair + half
            p = probs_ref[head]
            dp = nt(head_lanes(g, half), v)
            ds = p * (dp - jnp.sum(p * dp, axis=1, keepdims=True))
            wide = jnp.concatenate([ds, jnp.zeros((rows, 128 - rows), jnp.float32)], axis=1)
            total = wide[0:8]
            for group in range(1, rows // 8):
                total = total + pltpu.roll(wide[group * 8 : group * 8 + 8], 128 - group * 8, 1)
            for bit in (1, 2, 4):
                total = jnp.where((row8 // bit) % 2 == 1, pltpu.roll(total, 128 - bit, 1), total)
            fold_ref[head : head + 1, :] = jnp.sum(total, axis=0, keepdims=True)
            ds = to_low(ds)
            dqs.append(nn(ds, k))
            scores.append(ds)
            probs.append(to_low(p))
        dq_ref[:, cols] = to_low(0.125 * jnp.where(lane < HEAD, dqs[0], dqs[1]))
        both_q = jnp.concatenate([head_lanes(q, 0), head_lanes(q, 1)], axis=0)
        both_g = jnp.concatenate([head_lanes(g, 0), head_lanes(g, 1)], axis=0)
        dk_ref[:, cols] = to_low(product_tn(jnp.concatenate(scores, axis=0), both_q))
        dv_ref[:, cols] = to_low(product_tn(jnp.concatenate(probs, axis=0), both_g))
    x = x_ref[...].astype(jnp.float32)
    scale = lax.rsqrt(jnp.mean(x * x, axis=-1, keepdims=True) + epsilon)
    grad = nt(dq_ref[...], wq_ref[...]) + nt(dk_ref[...], wk_ref[...]) + nt(dv_ref[...], wv_ref[...])
    back, gain_grad = rms_back(x, scale, gain_self_ref[...], grad)
    gain_self_grad_ref[...] = gain_grad
    out_ref[...] = grad_mid + back


def dec_post(gq, grad_after, mid, x, q, k, v, probs, gain_self, gain_cross, wq, wk, wv, wo, wcq, after):
    rows = x.shape[0]
    low = sds((rows, D), jnp.bfloat16)
    gain = sds((1, D), jnp.float32)
    outs = [low, low, low, low, sds((rows, D), jnp.float32), gain, gain, sds((HEADS, 128), jnp.float32)]
    vmem = pl.BlockSpec(memory_space=pltpu.VMEM)
    return pl.pallas_call(
        dec_post_kernel,
        in_specs=[vmem] * 15 + [pl.BlockSpec(memory_space=pl.ANY)],
        out_specs=[vmem] * len(outs),
        out_shape=outs,
        compiler_params=params(60),
        name="dec_post",
    )(gq, grad_after, mid, x, q, k, v, probs, gain_self, gain_cross, wq, wk, wv, wo, wcq, after)


def dec_weight_kernel(
    pb, pa, column_ref, low_ref, dq_ref, dk_ref, dv_ref, att_ref, mid_low_ref, cross_low_ref, gq_ref, merged_ref, after_low_ref,
    hidden_ref, cot_ref, dffn_low_ref, pre_grad_ref, out_ref, turned_ref, wide_ref,
):
    shards = pb * pa
    column = column_ref[0]
    rows = D // shards
    depth = low_ref.shape[0]

    def own(left, scratch):
        height = left.shape[1]
        here = height // shards
        span = left.shape[0]
        scratch[:, :span] = left.astype(jnp.float32).T
        cut = [scratch[pl.ds((b * pa + column) * here, here), :span] for b in range(pb)]
        return to_low(jnp.concatenate(cut, axis=0)), here

    first = 0

    def put(values, here):
        nonlocal first
        for b in range(pb):
            out_ref[b, first : first + here, :] = values[b * here : (b + 1) * here]
        first += here

    left, here = own(low_ref[...], turned_ref)
    for right_ref in (dq_ref, dk_ref, dv_ref):
        put(nn(left, right_ref[...]), here)
    left, here = own(att_ref[...], turned_ref)
    put(nn(left, mid_low_ref[...]), here)
    left, here = own(cross_low_ref[...], turned_ref)
    a, b, c = in_three(gq_ref[...])
    put(nn(left, a) + nn(left, b) + nn(left, c), here)
    right = after_low_ref[...]
    a, b, c = (own(part, turned_ref)[0] for part in in_three(merged_ref[:, :D]))
    put(nn(a, right) + nn(b, right) + nn(c, right), here)
    left, wide = own(hidden_ref[...], wide_ref)
    put(nn(left, cot_ref[...]), wide)
    left, here = own(dffn_low_ref[...], turned_ref)
    for c in range(pre_grad_ref.shape[1] // D):
        put(nn(left, pre_grad_ref[:, c * D : (c + 1) * D]), here)


def dec_weight_grads(pb, pa, column, *args):
    rows, ff = args[-1].shape
    shards = pb * pa
    height = (6 * D + ff + ff) // shards
    vmem = pl.BlockSpec(memory_space=pltpu.VMEM)
    return pl.pallas_call(
        functools.partial(dec_weight_kernel, pb, pa),
        in_specs=[pl.BlockSpec(memory_space=pltpu.SMEM)] + [vmem] * len(args),
        out_specs=vmem,
        out_shape=sds((pb, height, D), jnp.float32),
        scratch_shapes=[pltpu.VMEM((D, rows), jnp.float32), pltpu.VMEM((ff, rows), jnp.float32)],
        compiler_params=params(56),
        name="dec_weight_grads",
    )(column, *args)


def bits_of(mesh_sizes):
    pb, pa = mesh_sizes
    pb_bits = pb.bit_length() - 1
    pa_bits = pa.bit_length() - 1
    ys = [("pb", b) for b in range(1, pb_bits)]
    xs = [("pa", b) for b in range(pa_bits - 2)]
    zs = [("pa", b) for b in range(pa_bits - 2, pa_bits)]
    return xs, ys, zs


def orders_of(mesh_sizes):
    xs, ys, zs = bits_of(mesh_sizes)
    return (xs + ys + zs, ys + xs + zs, zs[:1] + xs + ys + zs[1:])


def exchange_table(mesh_sizes, orders):
    pb, pa = mesh_sizes
    pb_me = lax.axis_index("pb")
    pa_me = lax.axis_index("pa")
    cells = np.arange(pb * pa // 2)
    pb_of = jnp.asarray(cells // pa * 2)
    pa_of = jnp.asarray(cells % pa)
    rows = [jnp.full((cells.size,), pb_me % 2, jnp.int32)]
    for order in orders:
        slot = jnp.zeros((cells.size,), jnp.int32)
        for axis, bit in order:
            far = ((pb_of if axis == "pb" else pa_of) >> bit) ^ ((pb_me if axis == "pb" else pa_me) >> bit)
            slot = slot * 2 + (far & 1).astype(jnp.int32)
        rows.append(slot)
    return jnp.stack(rows)


MESH = pl.DeviceIdType.MESH
LINK = 0.088
PAIR = 0.45
NEAR = ("pb", 0)


def link_of(step, sizes):
    xs, ys, zs = bits_of(sizes)
    if step == NEAR:
        return "core"
    if step in ys:
        return "y"
    return "x" if step in xs else "z"


def link_time(step, megabytes, sizes):
    if step == NEAR:
        return megabytes / PAIR
    return 2 * megabytes * (2 if step == bits_of(sizes)[2][-1] else 1) / LINK


class Piece:
    def __init__(self, array, first, width, order, place=None):
        self.array, self.first, self.width, self.order, self.place = array, first, width, order, place


def plan(pieces, shapes, starts, sizes, depth=2):
    free, held, queues = {}, {}, {}
    pending = [(start, i, -1) for i, start in enumerate(starts)]
    events = []

    def send(now, i, step, sends):
        piece = pieces[i]
        link = link_of(piece.order[step], sizes)
        if held.get(link, 0) >= depth:
            queues.setdefault(link, []).append((i, step))
            return
        held[link] = held.get(link, 0) + 1
        half, rows = shapes[piece.array][:2]
        megabytes = (half >> (step + piece.skip)) * rows * piece.width * 4e-6
        begin = max(now, free.get(link, 0.0))
        free[link] = begin + link_time(piece.order[step], megabytes, sizes)
        pending.append((free[link] + 1.5, i, step))
        sends.append((i, step))

    while pending:
        pending.sort()
        now, i, step = pending.pop(0)
        sends = []
        if step >= 0:
            link = link_of(pieces[i].order[step], sizes)
            held[link] -= 1
            waiting = queues.get(link, [])
            if waiting:
                send(now, *waiting.pop(0), sends)
        if step + 1 < len(pieces[i].order):
            send(now + 0.5, i, step + 1, sends)
        events.append((now, i, step, sends))
    return events


def partner(step):
    axis, bit = step
    me = lax.axis_index(axis)
    size = 1 << bit
    there = me + size - 2 * size * lax.rem(me // size, 2)
    return {"pb": lax.axis_index("pb"), "pa": lax.axis_index("pa"), axis: there}


def all_steps(sizes):
    xs, ys, zs = bits_of(sizes)
    return [NEAR] + xs + ys + zs


def greet(sizes):
    barrier = pltpu.get_barrier_semaphore()
    for step in all_steps(sizes):
        pl.semaphore_signal(barrier, inc=1, device_id=partner(step), device_id_type=MESH)
    pl.semaphore_wait(barrier, len(all_steps(sizes)))


class Exchange:
    def __init__(self, sizes, pieces, shapes, starts):
        self.sizes, self.pieces, self.shapes = sizes, pieces, shapes
        for piece in pieces:
            piece.skip = 1 if piece.place is None else 0
        self.events = plan(pieces, shapes, starts, sizes)
        self.stages = len(all_steps(sizes))
        self.own = [p for p in pieces if p.place is not None]
        self.outside = [p for p in pieces if p.place is None]
        self.staged = sorted({p.array for p in self.outside})

    def scratch(self):
        out = []
        for array in self.staged:
            half, rows = self.shapes[array][:2]
            width = max(p.width for p in self.outside if p.array == array)
            out += [pltpu.VMEM((half, rows, width), jnp.float32), pltpu.SemaphoreType.DMA]
        for piece in self.outside:
            half, rows = self.shapes[piece.array][:2]
            out += [
                pltpu.VMEM((half, rows, piece.width), jnp.float32),
                pltpu.VMEM((half - 1, rows, piece.width), jnp.float32),
                pltpu.SemaphoreType.DMA,
            ]
        if self.own:
            half, rows = self.shapes[self.own[0].array][:2]
            block = (rows, self.own[0].width)
            count = len(self.own)
            out += [
                pltpu.VMEM((count, half) + block, jnp.float32),
                pltpu.VMEM((count, half) + block, jnp.float32),
                pltpu.VMEM((count, 2 * half - 1) + block, jnp.float32),
            ]
        count = len(self.pieces)
        return out + [pltpu.SemaphoreType.DMA((count, self.stages)), pltpu.SemaphoreType.DMA((count, self.stages))]

    def bind(self, keeps, nears, outs, scratch):
        self.keeps, self.nears, self.outs = keeps, nears, outs
        scratch = list(scratch)
        self.stage_of = {array: (scratch.pop(0), scratch.pop(0)) for array in self.staged}
        self.bufs, self.recvs, self.load_sems = {}, {}, {}
        for i, piece in enumerate(self.pieces):
            if piece.place is None:
                self.bufs[i], self.recvs[i], self.load_sems[i] = scratch.pop(0), scratch.pop(0), scratch.pop(0)
        if self.own:
            self.keep_of, self.send_of, recv = scratch.pop(0), scratch.pop(0), scratch.pop(0)
            for i, piece in enumerate(self.pieces):
                if piece.place is not None:
                    self.bufs[i], self.recvs[i] = self.keep_of.at[piece.place], recv.at[piece.place]
        self.send_sems, self.recv_sems = scratch

    def loads(self, i):
        piece = self.pieces[i]
        cols = pl.ds(piece.first, piece.width)
        stage, sem = self.stage_of[piece.array]
        return (
            pltpu.make_async_copy(self.keeps[piece.array].at[:, :, cols], self.bufs[i], self.load_sems[i]),
            pltpu.make_async_copy(self.nears[piece.array].at[:, :, cols], stage, sem),
        )

    def sizes_of(self, i, step):
        piece = self.pieces[i]
        half = self.shapes[piece.array][0]
        count = half >> (step + piece.skip)
        return count, (half >> piece.skip) * 2 - 2 * count

    def copy(self, i, step):
        piece = self.pieces[i]
        count, first = self.sizes_of(i, step)
        if step == 0 and piece.skip == 0:
            source = self.send_of.at[piece.place]
        else:
            source = self.bufs[i].at[pl.ds(count, count)]
        return pltpu.make_async_remote_copy(
            src_ref=source, dst_ref=self.recvs[i].at[pl.ds(first, count)],
            send_sem=self.send_sems.at[i, step], recv_sem=self.recv_sems.at[i, step],
            device_id=partner(piece.order[step]), device_id_type=MESH,
        )

    def first_loads(self):
        for array in self.staged:
            self.start_load(next(i for i, p in enumerate(self.pieces) if p.array == array and p.place is None))

    def start_load(self, i):
        for load in self.loads(i):
            load.start()

    def event(self, i, step, sends):
        piece = self.pieces[i]
        buf, recv = self.bufs[i], self.recvs[i]
        last = step + 1 == len(piece.order)
        if step < 0 and piece.skip == 1:
            for load in self.loads(i):
                load.wait()
            stage = self.stage_of[piece.array][0]
            count = self.shapes[piece.array][0]

            def add(slot, _):
                buf[slot] = buf[slot] + stage[slot]
                return 0

        elif step >= 0:
            count, first = self.sizes_of(i, step)
            self.copy(i, step).wait_recv()

            def add(slot, _):
                buf[slot] = buf[slot] + recv[first + slot]
                return 0

        else:
            count = 0
        if last:
            self.outs[piece.array][:, piece.first : piece.first + piece.width] = buf[0] + recv[first]
        elif count:
            lax.fori_loop(count // 2, count, add, 0)
        for send in sends:
            self.copy(*send).start()
        if not last and count:
            lax.fori_loop(0, count // 2, add, 0)
        if step < 0 and piece.skip == 1:
            rest = [j for j, p in enumerate(self.pieces) if p.array == piece.array and j > i]
            if rest:
                self.start_load(rest[0])

    def finish(self):
        for i, piece in enumerate(self.pieces):
            for step in range(len(piece.order)):
                self.copy(i, step).wait_send()

    def points(self, times, ready):
        out = [[] for _ in times]
        place = 0
        for when, i, step, sends in self.events:
            while place < len(times) - 1 and times[place] < when:
                place += 1
            if step < 0 and self.pieces[i].place is not None:
                place = max(place, ready[self.pieces[i].place])
            out[place].append((i, step, sends))
        return out


class Everywhere:
    def __init__(self, sizes, shape):
        self.steps = all_steps(sizes)
        self.shape = shape

    def scratch(self):
        count = len(self.steps)
        return [
            pltpu.VMEM((count + 1,) + self.shape, jnp.float32),
            pltpu.VMEM((count,) + self.shape, jnp.float32),
            pltpu.SemaphoreType.DMA((count,)),
            pltpu.SemaphoreType.DMA((count,)),
        ]

    def bind(self, scratch):
        self.sums, self.recvs, self.send_sems, self.recv_sems = scratch

    def copy(self, k):
        return pltpu.make_async_remote_copy(
            src_ref=self.sums.at[k], dst_ref=self.recvs.at[k], send_sem=self.send_sems.at[k], recv_sem=self.recv_sems.at[k],
            device_id=partner(self.steps[k]), device_id_type=MESH,
        )

    def arrive(self, k):
        self.copy(k).wait_recv()
        self.sums[k + 1] = self.sums[k] + self.recvs[k]
        if k + 1 < len(self.steps):
            self.copy(k + 1).start()

    def finish(self):
        for k in range(len(self.steps)):
            self.copy(k).wait_send()


SMALL = (32, 1024)
ATTN_STEP = 3.6
GRAD_STEP = 1.5
BACK_STEP = 1.8


def slots_of(sizes, order):
    pb, pa = sizes
    far = {}
    for axis, bit in order:
        me = lax.rem(lax.axis_index(axis) // (1 << bit), 2)
        far[axis, bit] = (me, 1 - me)
    cells = []
    for y in range(pb // 2):
        for a in range(pa):
            slot = 0
            for axis, bit in order:
                slot = slot * 2 + far[axis, bit][(2 * y if axis == "pb" else a) >> bit & 1]
            cells.append(slot)
    return cells


def last_kernel(
    exchange, everywhere, points, orders, passages, share, arrays,
    lengths_ref, q_ref, k_ref, v_ref, o_ref, do_ref, lse_ref, base_ref, turned_ref, x_ref, grad_mid_ref, gain_ref, wq_ref, wk_ref, wv_ref,
    dec_fold_ref, *refs,
):
    gains, refs = refs[:5], refs[5:]
    keeps, nears, refs = refs[:arrays], refs[arrays : 2 * arrays], refs[2 * arrays :]
    after, refs = refs[0], refs[1:]
    out_ref, small_ref = refs[:2]
    moved, refs = refs[2 : 3 + arrays], refs[3 + arrays :]
    strip_ref, gather_ref, dqT_ref, grads_ref, fold_ref, gain_grad_ref = refs[:6]
    everywhere.bind(refs[6:10])
    exchange.bind(keeps, nears, moved, refs[10:])
    step = pl.program_id(0)
    sizes = exchange.sizes
    pb, pa = sizes
    attn_steps = HEADS // 2 * passages
    tiles = len(exchange.own)
    grad_end = attn_steps + tiles

    @pl.when(step == 0)
    def _():
        exchange.first_loads()
        greet(sizes)

    def beside(place):
        for k, events in enumerate(points[:-1]):
            if k < 2 * attn_steps and k % 2 == place and events:

                @pl.when(step == k // 2)
                def _(events=events):
                    for event in events:
                        exchange.event(*event)

    def at_end(number, k):
        if points[k]:

            @pl.when(step == number)
            def _():
                for event in points[k]:
                    exchange.event(*event)

    @pl.when(step < attn_steps)
    def _():
        pair = step // passages
        passage = lax.rem(step, passages)
        place = pl.ds(pl.multiple_of(passage * PL, PL), PL), pl.ds(pl.multiple_of(pair * 128, 128), 128)
        attn_backward_kernel(
            beside, passage, passages, lengths_ref, q_ref, k_ref, v_ref, o_ref, do_ref, lse_ref, base_ref,
            grads_ref.at[(0,) + place], grads_ref.at[(1,) + place], grads_ref.at[(2,) + place], fold_ref.at[pl.ds(pair, 1)],
            strip_ref, gather_ref, dqT_ref,
        )

    @pl.when((step >= attn_steps) & (step < grad_end))
    def _():
        number = step - attn_steps
        width = exchange.own[0].width
        each = D // width
        column = pl.ds(pl.multiple_of(lax.rem(number, each) * width, width), width)
        right = grads_ref[number // each, :, column]
        chain = lax.rem(number, len(orders))
        choices = [slots_of(sizes, order) for order in orders]
        core = lax.rem(lax.axis_index("pb"), 2)
        rows = exchange.shapes[exchange.own[0].array][1]
        half_rows = pa * rows
        for y in range(pb // 2):
            low_part = nn(turned_ref[2 * y * half_rows : (2 * y + 1) * half_rows, :], right)
            high_part = nn(turned_ref[(2 * y + 1) * half_rows : (2 * y + 2) * half_rows, :], right)
            mine = jnp.where(core == 0, low_part, high_part)
            other = jnp.where(core == 0, high_part, low_part)
            for a in range(pa):
                slot = choices[0][y * pa + a]
                for c in range(1, len(orders)):
                    slot = jnp.where(chain == c, choices[c][y * pa + a], slot)
                exchange.keep_of[number, slot] = mine[a * rows : (a + 1) * rows]
                exchange.send_of[number, slot] = other[a * rows : (a + 1) * rows]

    @pl.when(step >= grad_end)
    def _():
        rows = pl.ds(pl.multiple_of((step - grad_end) * x_ref.shape[0], x_ref.shape[0]), x_ref.shape[0])
        qkv_back_kernel(
            step == grad_end, grads_ref.at[0, rows], grads_ref.at[1, rows], grads_ref.at[2, rows],
            x_ref, grad_mid_ref, gain_ref, wq_ref, wk_ref, wv_ref, out_ref, gain_grad_ref,
        )

    for k in range(2 * attn_steps, len(points) - 1):
        at_end(k - attn_steps, k)

    @pl.when(step == pl.num_programs(0) - 1)
    def _():
        first = everywhere.sums
        first[0] = jnp.zeros(SMALL, jnp.float32)
        first[0, 0:1, :D] = gain_grad_ref[...]
        for r, ref in enumerate(gains):
            first[0, r + 1 : r + 2, :D] = ref[...] if r < 2 else ref[...] * share
        for pair in range(HEADS // 2):
            first[0, 8 + 2 * pair : 10 + 2 * pair, :] = fold_ref[pair]
        first[0, 8 + HEADS : 8 + 2 * HEADS, :128] = dec_fold_ref[...] * share
        everywhere.copy(0).start()
        left = points[-1]
        steps = len(everywhere.steps)
        every = max(1, len(left) // (steps + 1))
        done = 0
        for n, event in enumerate(left):
            if n % every == every - 1 and done < steps:
                everywhere.arrive(done)
                done += 1
            exchange.event(*event)
        for k in range(done, steps):
            everywhere.arrive(k)
        small_ref[...] = everywhere.sums[steps]
        exchange.finish()
        everywhere.finish()


def groups_of(orders, groups):
    pieces, starts = [], []
    for number, (_, _, widths) in enumerate(groups):
        first = 0
        for c, piece_width in enumerate(widths):
            starts.append(4.0 + 1.5 * len(pieces))
            pieces.append(Piece(number, first, piece_width, orders[c % len(orders)]))
            first += piece_width
    return pieces, starts


def last_part(
    sizes, orders, groups, after, lengths, q, k, v, o, do, lse, base, turned, x, grad_mid, gain, wq, wk, wv, dec_fold, gains,
):
    pb, pa = sizes
    passages = lengths.shape[0]
    tokens = x.shape[0]
    pairs = HEADS // 2
    tile_rows = 256
    width = 256
    attn_steps = pairs * passages
    own_count = 3 * D // width
    back_steps = tokens // tile_rows
    steps = attn_steps + own_count + back_steps
    half = pb * pa // 2
    shapes = [g[0].shape for g in groups] + [(half, D // (pb * pa), 3 * D)]
    pieces, starts = groups_of(orders, groups)
    times = [ATTN_STEP * s / 2 for s in range(2 * attn_steps)]
    ready = []
    for n in range(own_count):
        ready.append(len(times))
        times.append(ATTN_STEP * attn_steps + GRAD_STEP * (n + 1))
        starts.append(times[-1])
        pieces.append(Piece(len(groups), n * width, width, [NEAR] + orders[n % len(orders)], n))
    for s in range(back_steps - 1):
        times.append(ATTN_STEP * attn_steps + GRAD_STEP * own_count + BACK_STEP * (s + 1))
    exchange = Exchange(sizes, pieces, shapes, starts)
    everywhere = Everywhere(sizes, SMALL)
    points = exchange.points(times + [1e9], ready)

    def attn_place(i):
        at = jnp.minimum(i, attn_steps - 1)
        return at // passages, lax.rem(at, passages)

    def tile_map(i):
        pair, passage = attn_place(i)
        return passage, pair

    def lse_map(i):
        pair, passage = attn_place(i)
        return pair, passage, 0, 0

    def once(array):
        return pl.BlockSpec(array.shape, lambda i: (0,) * array.ndim, pipeline_mode=pl.Buffered(1))

    def row_map(i):
        return jnp.maximum(i - attn_steps - own_count, 0), 0

    tile = pl.BlockSpec((PL, 128), tile_map)
    rows = pl.BlockSpec((tile_rows, D), row_map)
    hbm = pl.BlockSpec(memory_space=pl.ANY)
    keeps, nears = [g[0] for g in groups], [g[1] for g in groups]
    return pl.pallas_call(
        functools.partial(last_kernel, exchange, everywhere, points, orders, passages, 1.0 / pa, len(groups)),
        grid=(steps,),
        in_specs=[pl.BlockSpec(memory_space=pltpu.SMEM)]
        + [tile] * 5
        + [pl.BlockSpec((1, 1, 2, PL), lse_map), pl.BlockSpec((1, 2, WIDE), lambda i: (attn_place(i)[0], 0, 0)), once(turned), rows, rows]
        + [once(a) for a in (gain, wq, wk, wv, dec_fold) + tuple(gains)]
        + [hbm] * (2 * len(groups) + 1),
        out_specs=[rows, pl.BlockSpec(SMALL, lambda i: (0, 0))] + [pl.BlockSpec(s[1:], lambda i: (0, 0)) for s in shapes],
        out_shape=[sds((tokens, D), jnp.float32), sds(SMALL, jnp.float32)] + [sds(s[1:], jnp.float32) for s in shapes],
        scratch_shapes=[
            pltpu.VMEM((2, STRIP, WIDE), jnp.float32),
            pltpu.VMEM((2, STRIP, WIDE), jnp.float32),
            pltpu.VMEM((128, PL), jnp.bfloat16),
            pltpu.VMEM((3, tokens, D), jnp.bfloat16),
            pltpu.VMEM((pairs, 2, WIDE), jnp.float32),
            pltpu.VMEM((1, D), jnp.float32),
        ]
        + everywhere.scratch()
        + exchange.scratch(),
        compiler_params=pltpu.CompilerParams(collective_id=1, has_side_effects=True, vmem_limit_bytes=63 * MIB),
        name="enc_last",
    )(lengths, q, k, v, o, do, lse, base, turned, x, grad_mid, gain, wq, wk, wv, dec_fold, *gains, *keeps, *nears, after)


def exchange_kernel(exchange, arrays, *refs):
    exchange.bind(refs[:arrays], refs[arrays : 2 * arrays], refs[2 * arrays : 3 * arrays], refs[3 * arrays :])
    exchange.first_loads()
    greet(exchange.sizes)
    for _, *event in exchange.events:
        exchange.event(*event)
    exchange.finish()


def exchange_only(sizes, orders, groups):
    shapes = [g[0].shape for g in groups]
    exchange = Exchange(sizes, *groups_of(orders, groups)[:1], shapes, groups_of(orders, groups)[1])
    return pl.pallas_call(
        functools.partial(exchange_kernel, exchange, len(groups)),
        in_specs=[pl.BlockSpec(memory_space=pl.ANY)] * (2 * len(groups)),
        out_specs=[pl.BlockSpec(memory_space=pltpu.VMEM)] * len(groups),
        out_shape=[sds(s[1:], jnp.float32) for s in shapes],
        scratch_shapes=exchange.scratch(),
        compiler_params=pltpu.CompilerParams(collective_id=2, has_side_effects=True, vmem_limit_bytes=63 * MIB),
        name="exchange",
    )(*[g[0] for g in groups], *[g[1] for g in groups])


def local(
    pb, pa,
    enc_in, dec_in, question_of, lengths, enc_gain_attn, enc_query, enc_key, enc_value, enc_output, enc_bias,
    enc_gain_ffn, enc_ff_in, enc_ff_out, enc_gain_final, cross_key, cross_value, dec_gain_self, dec_query, dec_key,
    dec_value, dec_output, dec_bias, dec_gain_cross, cross_query, cross_output, dec_gain_ffn, dec_ff_in, dec_ff_out,
    enc_cot, dec_cot,
):
    sizes = (pb, pa)
    orders = orders_of(sizes)
    answer_rows = dec_in.shape[0]
    gain_attn, gain_ffn, gain_final = (g.astype(jnp.float32)[None] for g in (enc_gain_attn, enc_gain_ffn, enc_gain_final))
    gain_self, gain_cross, gain_dffn = (g.astype(jnp.float32)[None] for g in (dec_gain_self, dec_gain_cross, dec_gain_ffn))
    table = exchange_table(sizes, orders)
    enc_table = jnp.asarray(strip_table())
    dec_table = jnp.asarray(causal_row(ANS))
    base = jnp.dot(enc_table, enc_bias.astype(jnp.float32), precision=highest).T.reshape(HEADS // 2, 2, WIDE)

    attn_turned, enc_queries, enc_keys, enc_values = qkv_forward(enc_in, gain_attn, enc_query, enc_key, enc_value)
    enc_attended, enc_lse = attn_forward(lengths, enc_queries, enc_keys, enc_values, base)
    enc_mid, ffn_low, enc_hidden, enc_slope, enc_y, enc_out, final_low, cross_keys, cross_values = post_forward(
        enc_in, enc_attended, gain_ffn, gain_final, enc_output, enc_ff_in, enc_ff_out, cross_key, cross_value
    )

    dec_base = jnp.dot(dec_table, dec_bias.astype(jnp.float32), precision=highest).T
    self_low, dec_queries, dec_keys, dec_values, dec_probs, dec_attended, dec_mid, cross_low, cross_queries = dec_pre(
        dec_in, gain_self, gain_cross, dec_base, dec_query, dec_key, dec_value, dec_output, cross_query
    )

    merged = merge(cross_part(question_of, lengths, cross_queries, cross_keys, cross_values), pa)
    dec_out, dffn_low, dec_hidden, pre_grad_low, after_low, grad_after, cross_att_grad, dec_gain_ffn_grad = dec_mid_call(
        merged, dec_mid, dec_cot, gain_dffn, cross_output, dec_ff_in, dec_ff_out
    )
    query_part, grad_cross = cross_back(
        question_of, lengths, cross_queries, cross_keys, cross_values, cross_att_grad, merged[:, :D], merged[:, D:]
    )
    grad_cross_q = lax.psum(query_part, "pa")

    def near(terms):
        keep, send = terms
        return keep, lax.ppermute(send, "pb", [(i, i ^ 1) for i in range(pb)])

    cross_terms = near(weight_grad(table, final_low, [grad_cross[0], grad_cross[1]], pb, pa, 256, 2))
    eout_low, epre_low, emid_low, grad_enc_mid, enc_att_grad, final_gain_grad, ffn_gain_grad = post_backward(
        grad_cross, enc_y, enc_mid, enc_slope, enc_cot, gain_ffn, gain_final, cross_key, cross_value, enc_ff_out, enc_ff_in, enc_output,
    )
    out_terms = near(weight_grad(table, enc_hidden, [eout_low], pb, pa, 256, 1))
    in_terms = near(weight_grad(table, ffn_low, [epre_low], pb, pa, 512, 2))
    mix_terms = near(weight_grad(table, enc_attended, [emid_low], pb, pa, 256, 1))

    mid_low, grad_dq, grad_dk, grad_dv, dec_in_grad, dec_gain_self_grad, dec_gain_cross_grad, dec_fold = dec_post(
        grad_cross_q, grad_after, dec_mid, dec_in, dec_queries, dec_keys, dec_values, dec_probs, gain_self, gain_cross,
        dec_query, dec_key, dec_value, dec_output, cross_query, mix_terms[0],
    )
    thin = dec_weight_grads(
        pb, pa, lax.axis_index("pa").reshape(1), self_low, grad_dq, grad_dk, grad_dv, dec_attended, mid_low, cross_low, grad_cross_q,
        merged, after_low, dec_hidden, dec_cot, dffn_low, pre_grad_low,
    )
    dec_sum = lax.psum_scatter(thin, "pb", scatter_dimension=0, tiled=False)
    small_height = D // (pb * pa)
    wide_height = dec_hidden.shape[1] // (pb * pa)
    cuts = np.cumsum([0] + [small_height] * 6 + [wide_height] + [small_height] * (dec_hidden.shape[1] // D))
    got = [dec_sum[a:b] for a, b in zip(cuts[:-1], cuts[1:])]
    dec_ff_in_grad = jnp.concatenate(got[7:], axis=1)

    groups = [
        cross_terms + ((512, 512, 512),), out_terms + ((256, 256, 256),), in_terms + ((1024, 1024, 1024),), mix_terms + ((256, 256, 256),),
    ]
    alone = [] if D // (pb * pa) % 8 == 0 else [groups.pop(2)]
    enc_in_grad, small, *summed = last_part(
        sizes, orders, groups, thin, lengths, enc_queries, enc_keys, enc_values, enc_attended, enc_att_grad, enc_lse, base,
        attn_turned, enc_in, grad_enc_mid, gain_attn, enc_query, enc_key, enc_value, dec_fold,
        (ffn_gain_grad, final_gain_grad, dec_gain_self_grad, dec_gain_cross_grad, dec_gain_ffn_grad),
    )
    summed[2:2] = exchange_only(sizes, orders, alone) if alone else []
    cross_terms, ff_out_term, ff_in_term, output_term, attn_terms = summed
    shards = pb * pa
    shard = lax.axis_index("pb") * pa + lax.axis_index("pa")
    gains = lax.dynamic_slice_in_dim(small[:6, :D], shard * (D // shards), D // shards, 1)
    width = BUCKETS * HEADS // shards

    def bias_grad(folded, to_bucket):
        flat = jnp.dot(folded, to_bucket, precision=highest).T.reshape(BUCKETS * HEADS)
        return lax.dynamic_slice_in_dim(flat, shard * width, width)

    enc_bias_grad = bias_grad(small[8 : 8 + HEADS], enc_table)
    dec_bias_grad = bias_grad(small[8 + HEADS :, :128], dec_table)

    return (
        enc_out, dec_out, enc_in_grad, dec_in_grad,
        gains[0], attn_terms[:, :D], attn_terms[:, D : 2 * D], attn_terms[:, 2 * D :], output_term, enc_bias_grad,
        gains[1], ff_in_term, ff_out_term, gains[2], cross_terms[:, :D], cross_terms[:, D:],
        gains[3], got[0], got[1], got[2], got[3], dec_bias_grad, gains[4], got[4], got[5], gains[5], dec_ff_in_grad, got[6],
    )


def solution(mesh):
    pb, pa = mesh.shape["pb"], mesh.shape["pa"]
    rows = P(("pb", "pa"), None)
    flat = P(("pb", "pa"))
    dec = P("pb", None)
    return jax.shard_map(
        functools.partial(local, pb, pa),
        mesh=mesh,
        in_specs=(rows, dec, flat, flat) + (P(),) * 24 + (rows, dec),
        out_specs=(rows, dec, rows, dec)
        + (flat, rows, rows, rows, rows, flat, flat, rows, rows, flat, rows, rows)
        + (flat, rows, rows, rows, rows, flat, flat, rows, rows, flat, rows, rows),
        check_vma=False,
    )
```

```python
import functools
import math

import jax
import jax.numpy as jnp
import numpy as np
from jax import lax
from jax.experimental import pallas as pl
from jax.experimental.pallas import tpu as pltpu
from jax.sharding import PartitionSpec as P

D = 768
HEADS = 12
HEAD = 64
BUCKETS = 32
PL = 512
ANS = 24

far_distance = 128
epsilon = 1e-06
highest = lax.Precision.HIGHEST


def bucket_of(offset, bidirectional):
    if bidirectional:
        halves = BUCKETS // 2
        base_bucket = halves if offset > 0 else 0
        distance = abs(offset)
    else:
        halves = BUCKETS
        base_bucket = 0
        distance = max(-offset, 0)
    exact_count = halves // 2
    if distance < exact_count:
        return base_bucket + distance
    scaled = (
        math.log(distance / exact_count)
        / math.log(far_distance / exact_count)
        * (halves - exact_count)
    )
    return base_bucket + min(exact_count + int(scaled), halves - 1)


def to_low(values):
    return values.astype(jnp.bfloat16)


def product_tn(left, right):
    return lax.dot_general(
        left, right, (((0,), (0,)), ((), ())), preferred_element_type=jnp.float32
    )


STRIP = 128
WIDE = 1024


def strip_table():
    table = np.zeros((WIDE, BUCKETS), np.float32)
    for place in range(WIDE):
        if place < PL + STRIP * 3:
            offset = PL - STRIP - place
        else:
            offset = PL - STRIP + WIDE - place
        if abs(offset) < PL:
            table[place, bucket_of(offset, True)] = 1.0
    return table


def nn(left, right):
    return lax.dot_general(left, right, (((1,), (0,)), ((), ())), preferred_element_type=jnp.float32)


def head_lanes(values, head):
    lane = lax.broadcasted_iota(jnp.int32, values.shape, 1)
    keep = lane < HEAD if head == 0 else lane >= HEAD
    return jnp.where(keep, values, jnp.zeros_like(values))


def key_mask(length):
    place = lax.broadcasted_iota(jnp.int32, (PL, 1), 0)
    return jnp.where(place < length, 0.0, -1e9)


def build_strip(base_ref, strip_ref):
    for head in range(2):
        row = base_ref[0, head : head + 1, :]
        spread = jnp.broadcast_to(row, (STRIP, WIDE))
        strip_ref[head] = pltpu.roll(spread, 0, 1, stride=1, stride_axis=0)


def attn_forward_kernel(lengths_ref, q_ref, k_ref, v_ref, bias_ref, table_ref, out_ref, turned_ref, lse_ref, base_ref, rows_ref, strip_ref, score_ref):
    passage = pl.program_id(1)

    @pl.when((passage == 0) & (pl.program_id(0) == 0))
    def _():
        every = product_tn(bias_ref[...], table_ref[...])
        for pair in range(HEADS // 2):
            rows_ref[pair] = every[2 * pair : 2 * pair + 2]

    base_ref[...] = rows_ref[pl.ds(pl.program_id(0), 1)]

    @pl.when(passage == 0)
    def _():
        build_strip(base_ref, strip_ref)

    mask = key_mask(lengths_ref[passage])
    q_t = q_ref[...].T
    v_t = v_ref[...].T
    k = k_ref[...]
    blocks = PL // STRIP
    for head in range(2):
        k_head = head_lanes(k, head)
        top = None
        for b in range(blocks):
            rows = slice(b * STRIP, (b + 1) * STRIP)
            start = PL - STRIP - b * STRIP
            s = nn(k_head[rows], q_t) + strip_ref[head, :, start : start + PL] + mask[rows]
            score_ref[head, rows, :] = s
            here = jnp.max(s, axis=0, keepdims=True)
            top = here if top is None else jnp.maximum(top, here)
        total = None
        acc = None
        for b in range(blocks):
            rows = slice(b * STRIP, (b + 1) * STRIP)
            e = jnp.exp(score_ref[head, rows, :] - top)
            here = jnp.sum(e, axis=0, keepdims=True)
            total = here if total is None else total + here
            part = nn(v_t[head * HEAD : (head + 1) * HEAD, rows], to_low(e))
            acc = part if acc is None else acc + part
        turned_ref[head * HEAD : (head + 1) * HEAD, :] = to_low(acc * (1.0 / total))
        lse_ref[0, 0, head : head + 1, :] = top + jnp.log(total)
    out_ref[...] = turned_ref[...].T


def attn_forward(lengths, q, k, v, bias, table):
    passages = lengths.shape[0]
    pairs = HEADS // 2
    tile = pl.BlockSpec((PL, 128), lambda h, p, *_: (p, h))
    return pl.pallas_call(
        attn_forward_kernel,
        grid_spec=pltpu.PrefetchScalarGridSpec(
            num_scalar_prefetch=1,
            grid=(pairs, passages),
            in_specs=[tile, tile, tile, pl.BlockSpec(bias.shape, lambda h, p, *_: (0, 0)), pl.BlockSpec(table.shape, lambda h, p, *_: (0, 0))],
            out_specs=[
                tile,
                pl.BlockSpec((128, PL), lambda h, p, *_: (h, p)),
                pl.BlockSpec((1, 1, 2, PL), lambda h, p, *_: (h, p, 0, 0)),
                pl.BlockSpec((1, 2, WIDE), lambda h, p, *_: (h, 0, 0)),
            ],
            scratch_shapes=[
                pltpu.VMEM((pairs, 2, WIDE), jnp.float32),
                pltpu.VMEM((2, STRIP, WIDE), jnp.float32),
                pltpu.VMEM((2, PL, PL), jnp.float32),
            ],
        ),
        out_shape=[
            jax.ShapeDtypeStruct((passages * PL, D), jnp.bfloat16),
            jax.ShapeDtypeStruct((D, passages * PL), jnp.bfloat16),
            jax.ShapeDtypeStruct((pairs, passages, 2, PL), jnp.float32),
            jax.ShapeDtypeStruct((pairs, 2, WIDE), jnp.float32),
        ],
        compiler_params=pltpu.CompilerParams(vmem_limit_bytes=62 * 2**20),
        name="enc_attention",
    )(lengths, q, k, v, bias, table)


def attn_backward_kernel(
    beside, passage, passages, lengths_ref, q_ref, k_ref, v_ref, o_ref, do_ref, lse_ref, base_ref,
    dq_ref, dk_ref, dv_ref, fold_ref,
    strip_ref, gather_ref, dqT_ref,
):
    @pl.when(passage == 0)
    def _():
        build_strip(base_ref, strip_ref)
        gather_ref[...] = jnp.zeros_like(gather_ref)

    mask = key_mask(lengths_ref[passage])
    q = q_ref[...]
    k = k_ref[...]
    v = v_ref[...]
    do = do_ref[...]
    q_t = q.T
    k_t = k.T
    do_t = do.T
    o_t = o_ref[...].T
    weighed = do_t.astype(jnp.float32) * o_t.astype(jnp.float32)
    blocks = PL // STRIP
    lane = lax.broadcasted_iota(jnp.int32, (STRIP, 128), 1)
    first = lane < HEAD
    dks = []
    dvs = []
    for head in range(2):
        beside(head)
        heads = slice(head * HEAD, (head + 1) * HEAD)
        delta = jnp.sum(weighed[heads], axis=0, keepdims=True)
        lse = lse_ref[0, 0, head : head + 1, :]
        k_head = head_lanes(k, head)
        v_head = head_lanes(v, head)
        acc = None
        for b in range(blocks):
            rows = slice(b * STRIP, (b + 1) * STRIP)
            start = PL - STRIP - b * STRIP
            s = nn(k_head[rows], q_t) + strip_ref[head, :, start : start + PL] + mask[rows]
            p = jnp.exp(s - lse)
            dp = nn(v_head[rows], do_t)
            ds = p * (dp - delta)
            gather_ref[head, :, start : start + PL] += ds
            ds_low = to_low(ds)
            dv_part = nn(to_low(p), do)
            dk_part = nn(ds_low, q)
            if head == 0:
                dvs.append(dv_part)
                dks.append(dk_part)
            else:
                dv_ref[rows, :] = to_low(jnp.where(first, dvs[b], dv_part))
                dk_ref[rows, :] = to_low(jnp.where(first, dks[b], dk_part))
            part = nn(k_t[heads, rows], ds_low)
            acc = part if acc is None else acc + part
        dqT_ref[heads, :] = to_low(0.125 * acc)
    dq_ref[...] = dqT_ref[...].T

    @pl.when(passage == passages - 1)
    def _():
        row = lax.broadcasted_iota(jnp.int32, (8, WIDE), 0)
        for head in range(2):
            total = gather_ref[head, 0:8, :]
            for group in range(1, STRIP // 8):
                total = total + pltpu.roll(gather_ref[head, group * 8 : group * 8 + 8, :], WIDE - group * 8, 1)
            for bit in (1, 2, 4):
                total = jnp.where((row // bit) % 2 == 1, pltpu.roll(total, WIDE - bit, 1), total)
            fold_ref[0, head : head + 1, :] = jnp.sum(total, axis=0, keepdims=True)


MIB = 2**20


def nt(left, right):
    return lax.dot_general(left, right, (((1,), (1,)), ((), ())), preferred_element_type=jnp.float32)


def rms(values, gain):
    scale = lax.rsqrt(jnp.mean(values * values, axis=-1, keepdims=True) + epsilon)
    return values * scale * gain, scale


def rms_back(values, scale, gain, grad):
    scaled = grad * gain
    gain_grad = jnp.sum(grad * values * scale, axis=0, keepdims=True)
    inner = jnp.mean(scaled * values, axis=-1, keepdims=True)
    return scaled * scale - values * (scale * scale * scale) * inner, gain_grad


def gelu_both(v):
    c = math.sqrt(2.0 / math.pi)
    square = v * v
    t = jnp.tanh(v * (c + (c * 0.044715) * square))
    half = 0.5 + 0.5 * t
    slope = half + (half * (1.0 - t)) * v * (c + (3.0 * 0.044715 * c) * square)
    return v * half, slope


GAIN_ATTN, GAIN_FFN, GAIN_FINAL, GAIN_SELF, GAIN_CROSS, GAIN_DFFN = range(6)


def gain_of(gains_ref, which):
    return gains_ref[which : which + 1, :]


def whole(array):
    return pl.BlockSpec(array.shape, lambda *_: (0,) * array.ndim)


def rows_of(tile, width):
    return pl.BlockSpec((tile, width), lambda i: (i, 0))


def sds(shape, kind):
    return jax.ShapeDtypeStruct(shape, kind)


def params(mib):
    return pltpu.CompilerParams(vmem_limit_bytes=mib * MIB)


def qkv_kernel(x_ref, gains_ref, wq_ref, wk_ref, wv_ref, turned_ref, q_ref, k_ref, v_ref):
    normed, _ = rms(x_ref[...].astype(jnp.float32), gain_of(gains_ref, GAIN_ATTN))
    low = to_low(normed)
    turned_ref[...] = low.T
    q_ref[...] = to_low(0.125 * to_low(nn(low, wq_ref[...])).astype(jnp.float32))
    k_ref[...] = to_low(nn(low, wk_ref[...]))
    v_ref[...] = to_low(nn(low, wv_ref[...]))


def qkv_forward(x, gains, wq, wk, wv):
    tokens = x.shape[0]
    tile = 256
    big = sds((tokens, D), jnp.bfloat16)
    return pl.pallas_call(
        qkv_kernel,
        grid=(tokens // tile,),
        in_specs=[rows_of(tile, D)] + [whole(a) for a in (gains, wq, wk, wv)],
        out_specs=[pl.BlockSpec((D, tile), lambda i: (0, i))] + [rows_of(tile, D)] * 3,
        out_shape=[sds((D, tokens), jnp.bfloat16)] + [big] * 3,
        compiler_params=params(62),
        name="enc_qkv",
    )(x, gains, wq, wk, wv)


def post_kernel(
    x_ref, att_ref, gains_ref, wo_ref, win_ref, wout_ref, wck_ref, wcv_ref,
    mid_ref, ffn_turned_ref, hidden_turned_ref, slope_ref, y_ref, out_ref, final_turned_ref, ck_ref, cv_ref,
):
    mid = x_ref[...].astype(jnp.float32) + nn(att_ref[...], wo_ref[...])
    mid_ref[...] = mid
    normed, _ = rms(mid, gain_of(gains_ref, GAIN_FFN))
    low = to_low(normed)
    ffn_turned_ref[...] = low.T
    y = mid
    width = 768
    for c in range(win_ref.shape[1] // width):
        cols = slice(c * width, (c + 1) * width)
        hidden, slope = gelu_both(nn(low, win_ref[:, cols]))
        hidden = to_low(hidden)
        hidden_turned_ref[cols, :] = hidden.T
        slope_ref[:, cols] = to_low(slope)
        y = y + nn(hidden, wout_ref[cols, :])
    y_ref[...] = y
    out_ref[...] = to_low(y)
    final, _ = rms(y, gain_of(gains_ref, GAIN_FINAL))
    final = to_low(final)
    final_turned_ref[...] = final.T
    ck_ref[...] = to_low(nn(final, wck_ref[...]))
    cv_ref[...] = to_low(nn(final, wcv_ref[...]))


def post_forward(x, att, gains, wo, win, wout, wck, wcv):
    tokens = x.shape[0]
    tile = 256
    ff = win.shape[1]
    low = sds((tokens, D), jnp.bfloat16)
    wide = sds((tokens, ff), jnp.bfloat16)
    full = sds((tokens, D), jnp.float32)
    d = rows_of(tile, D)
    f = rows_of(tile, ff)
    turned = pl.BlockSpec((D, tile), lambda i: (0, i))
    flat = sds((D, tokens), jnp.bfloat16)
    return pl.pallas_call(
        post_kernel,
        grid=(tokens // tile,),
        in_specs=[d, d] + [whole(a) for a in (gains, wo, win, wout, wck, wcv)],
        out_specs=[d, turned, pl.BlockSpec((ff, tile), lambda i: (0, i)), f, d, d, turned, d, d],
        out_shape=[full, flat, sds((ff, tokens), jnp.bfloat16), wide, full, low, flat, low, low],
        compiler_params=params(62),
        name="enc_post",
    )(x, att, gains, wo, win, wout, wck, wcv)


def back_kernel(
    gkv_ref, y_ref, mid_ref, slope_ref, cot_ref, gains_ref,
    wck_ref, wcv_ref, wout_ref, win_ref, wo_ref, after_ref,
    eout_ref, epre_ref, emid_ref, grad_mid_ref, att_grad_ref, gain_final_grad_ref, gain_ffn_grad_ref, tick_ref,
):
    tick_ref[...] = jnp.zeros_like(tick_ref)

    @pl.when(pl.program_id(0) == 0)
    def _():
        gain_final_grad_ref[...] = jnp.zeros_like(gain_final_grad_ref)
        gain_ffn_grad_ref[...] = jnp.zeros_like(gain_ffn_grad_ref)

    y = y_ref[...]
    scale = lax.rsqrt(jnp.mean(y * y, axis=-1, keepdims=True) + epsilon)
    final_back = nt(gkv_ref[0], wck_ref[...]) + nt(gkv_ref[1], wcv_ref[...])
    back, gain_grad = rms_back(y, scale, gain_of(gains_ref, GAIN_FINAL), final_back)
    gain_final_grad_ref[...] += gain_grad
    grad_y = cot_ref[...].astype(jnp.float32) + back
    eout = to_low(grad_y)
    eout_ref[...] = eout
    width = 768
    acc = None
    for c in range(win_ref.shape[1] // width):
        cols = slice(c * width, (c + 1) * width)
        epre = to_low(slope_ref[:, cols].astype(jnp.float32) * nt(eout, wout_ref[cols, :]))
        epre_ref[:, cols] = epre
        part = nt(epre, win_ref[:, cols])
        acc = part if acc is None else acc + part
    mid = mid_ref[...]
    scale = lax.rsqrt(jnp.mean(mid * mid, axis=-1, keepdims=True) + epsilon)
    back, gain_grad = rms_back(mid, scale, gain_of(gains_ref, GAIN_FFN), acc)
    gain_ffn_grad_ref[...] += gain_grad
    grad_mid = grad_y + back
    grad_mid_ref[...] = grad_mid
    emid = to_low(grad_mid)
    emid_ref[...] = emid
    att_grad_ref[...] = to_low(nt(emid, wo_ref[...]))


def post_backward(gkv, y, mid, slope, cot, gains, wck, wcv, wout, win, wo, after):
    tokens = y.shape[0]
    tile = 256
    ff = win.shape[1]
    low = sds((tokens, D), jnp.bfloat16)
    d = rows_of(tile, D)
    f = rows_of(tile, ff)
    gain = pl.BlockSpec((1, D), lambda i: (0, 0))
    return pl.pallas_call(
        back_kernel,
        grid=(tokens // tile,),
        in_specs=[pl.BlockSpec((2, tile, D), lambda i: (0, i, 0)), d, d, f, d]
        + [whole(a) for a in (gains, wck, wcv, wout, win, wo)]
        + [pl.BlockSpec(memory_space=pl.ANY)],
        out_specs=[d, f, d, d, d, gain, gain, pl.BlockSpec((1, 128), lambda i: (0, 0))],
        out_shape=[low, sds((tokens, ff), jnp.bfloat16), low, sds((tokens, D), jnp.float32), low]
        + [sds((1, D), jnp.float32)] * 2
        + [sds((1, 128), jnp.float32)],
        compiler_params=params(62),
        name="enc_post_back",
    )(gkv, y, mid, slope, cot, gains, wck, wcv, wout, win, wo, after)


def qkv_back_kernel(opening, dq_ref, dk_ref, dv_ref, x_ref, grad_mid_ref, gains_ref, wq_ref, wk_ref, wv_ref, out_ref, gain_grad_ref):
    @pl.when(opening)
    def _():
        gain_grad_ref[...] = jnp.zeros_like(gain_grad_ref)

    x = x_ref[...].astype(jnp.float32)
    scale = lax.rsqrt(jnp.mean(x * x, axis=-1, keepdims=True) + epsilon)
    grad = nt(dq_ref[...], wq_ref[...]) + nt(dk_ref[...], wk_ref[...]) + nt(dv_ref[...], wv_ref[...])
    back, gain_grad = rms_back(x, scale, gain_of(gains_ref, GAIN_ATTN), grad)
    gain_grad_ref[...] += gain_grad
    out_ref[...] = grad_mid_ref[...] + back


def weight_grad_kernel(rows, pb, pa, tiles, per_chain, table_ref, turned_ref, *refs):
    rights = refs[: len(tiles)]
    keep_ref, send_ref, tick_ref = refs[-3:]
    step = pl.program_id(0)
    core = table_ref[0, 0]
    chain = step // per_chain
    half_rows = pa * rows
    tick_ref[...] = jnp.zeros_like(tick_ref)

    def work(right):
        for y in range(pb // 2):
            low_part = nn(turned_ref[2 * y * half_rows : (2 * y + 1) * half_rows, :], right)
            high_part = nn(turned_ref[(2 * y + 1) * half_rows : (2 * y + 2) * half_rows, :], right)
            mine = jnp.where(core == 0, low_part, high_part)
            other = jnp.where(core == 0, high_part, low_part)
            for a in range(pa):
                slot = table_ref[chain + 1, y * pa + a]
                keep_ref[slot] = mine[a * rows : (a + 1) * rows]
                send_ref[slot] = other[a * rows : (a + 1) * rows]

    first = 0
    for right_ref, count in zip(rights, tiles):
        if len(tiles) == 1:
            work(right_ref[...])
        else:

            @pl.when((step >= first) & (step < first + count))
            def _(right_ref=right_ref):
                work(right_ref[...] if len(right_ref.shape) == 2 else right_ref[0])

        first += count


def weight_grad(table, turned, rights, pb, pa, width, per_chain, after=()):
    height, tokens = turned.shape
    rows = height // (pb * pa)
    arrays = [r[0] if isinstance(r, tuple) else r for r in rights]
    tiles = [a.shape[-1] // width for a in arrays]
    total = sum(tiles)
    firsts = np.cumsum([0] + tiles)[:-1]

    def spec(right, first, count):
        def column(i):
            return jnp.clip(i - int(first), 0, count - 1)

        if isinstance(right, tuple):
            return pl.BlockSpec((1, tokens, width), lambda i, *_: (right[1], 0, column(i)))
        return pl.BlockSpec((tokens, width), lambda i, *_: (0, column(i)))

    half = pb * pa // 2
    out = pl.BlockSpec((half, rows, width), lambda i, *_: (0, 0, i))
    shape = sds((half, rows, total * width), jnp.float32)
    return pl.pallas_call(
        functools.partial(weight_grad_kernel, rows, pb, pa, tiles, per_chain),
        grid_spec=pltpu.PrefetchScalarGridSpec(
            num_scalar_prefetch=1,
            grid=(total,),
            in_specs=[pl.BlockSpec((height, tokens), lambda i, *_: (0, 0))]
            + [spec(r, f, c) for r, f, c in zip(rights, firsts, tiles)]
            + [pl.BlockSpec(memory_space=pl.ANY)] * len(after),
            out_specs=[out, out, pl.BlockSpec((1, 128), lambda i, *_: (0, 0))],
        ),
        out_shape=[shape, shape, sds((1, 128), jnp.float32)],
        compiler_params=params(62),
        name="weight_grad",
    )(table, turned, *arrays, *after)


PACK = 896


def permitted_mask(question_ref, length_ref, answer_rows, passages):
    row = lax.broadcasted_iota(jnp.int32, (answer_rows, PL), 0)
    place = lax.broadcasted_iota(jnp.int32, (answer_rows, PL), 1)
    whose = row // ANS
    return jnp.concatenate(
        [(whose == question_ref[p]) & (place < length_ref[p]) for p in range(passages)], axis=1
    )


def cross_part_kernel(question_ref, length_ref, q_ref, ck_ref, cv_ref, part_ref):
    rows = q_ref.shape[0]
    mask = permitted_mask(question_ref, length_ref, rows, ck_ref.shape[0] // PL)
    lane = lax.broadcasted_iota(jnp.int32, (rows, 128), 1)
    stats = jnp.zeros((rows, 128), jnp.float32)
    for pair in range(HEADS // 2):
        cols = slice(pair * 128, (pair + 1) * 128)
        q = q_ref[:, cols]
        k = ck_ref[:, cols]
        v = cv_ref[:, cols]
        outs = []
        for head in range(2):
            s = jnp.where(mask, 0.125 * nt(head_lanes(q, head), k), -1e9)
            top = jnp.max(s, axis=1, keepdims=True)
            e = jnp.exp(s - top)
            total = jnp.sum(e, axis=1, keepdims=True)
            outs.append(nn(to_low(e), v))
            place = 2 * pair + head
            stats = jnp.where(lane == place, top, jnp.where(lane == HEADS + place, total, stats))
        part_ref[:, cols] = jnp.where(lane < HEAD, outs[0], outs[1])
    part_ref[:, D:] = stats


def cross_part(question_of, lengths, q, ck, cv):
    vmem = pl.BlockSpec(memory_space=pltpu.VMEM)
    smem = pl.BlockSpec(memory_space=pltpu.SMEM)
    return pl.pallas_call(
        cross_part_kernel,
        in_specs=[smem, smem, vmem, vmem, vmem],
        out_specs=vmem,
        out_shape=sds((q.shape[0], PACK), jnp.float32),
        compiler_params=params(40),
        name="cross_part",
    )(question_of, lengths, q, ck, cv)


def over_heads(stats, rows):
    lane = lax.broadcasted_iota(jnp.int32, (rows, 128), 1)
    return jnp.concatenate(
        [jnp.where(lane < HEAD, stats[:, 2 * g : 2 * g + 1], stats[:, 2 * g + 1 : 2 * g + 2]) for g in range(HEADS // 2)],
        axis=1,
    )


def merge_kernel(pa, part_ref, out_ref, recv_ref, mine_ref, send_sem, recv_sem, send2_sem, recv2_sem):
    me = lax.axis_index("pa")
    rows = part_ref.shape[1]
    barrier = pltpu.get_barrier_semaphore()
    for off in range(1, pa):
        pl.semaphore_signal(barrier, inc=1, device_id={"pa": lax.rem(me + off, pa)}, device_id_type=pl.DeviceIdType.MESH)
    pl.semaphore_wait(barrier, pa - 1)

    def first(off):
        peer = lax.rem(me + off, pa)
        return pltpu.make_async_remote_copy(
            src_ref=part_ref.at[peer], dst_ref=recv_ref.at[off], send_sem=send_sem.at[off], recv_sem=recv_sem.at[off],
            device_id={"pa": peer}, device_id_type=pl.DeviceIdType.MESH,
        )

    def second(off):
        peer = lax.rem(me + off, pa)
        return pltpu.make_async_remote_copy(
            src_ref=mine_ref, dst_ref=out_ref.at[me], send_sem=send2_sem.at[off], recv_sem=recv2_sem.at[off],
            device_id={"pa": peer}, device_id_type=pl.DeviceIdType.MESH,
        )

    for off in range(1, pa):
        first(off).start()
    recv_ref[0] = part_ref[me]
    for off in range(1, pa):
        first(off).wait()
    tops = [recv_ref[i, :, D : D + 128][:, :HEADS] for i in range(pa)]
    top = tops[0]
    for t in tops[1:]:
        top = jnp.maximum(top, t)
    total = jnp.zeros((rows, HEADS), jnp.float32)
    acc = jnp.zeros((rows, D), jnp.float32)
    for i in range(pa):
        w = jnp.exp(tops[i] - top)
        total = total + w * recv_ref[i, :, D : D + 128][:, HEADS : 2 * HEADS]
        acc = acc + over_heads(w, rows) * recv_ref[i, :, :D]
    mine_ref[:, :D] = acc / over_heads(total, rows)
    lse = top + jnp.log(total)
    mine_ref[:, D:] = jnp.concatenate([lse, jnp.zeros((rows, 128 - HEADS), jnp.float32)], axis=1)
    for off in range(1, pa):
        second(off).start()
    out_ref[me] = mine_ref[...]
    for off in range(1, pa):
        second(off).wait()


def merge(part, pa):
    answer_rows = part.shape[0]
    rows = answer_rows // pa
    block = (pa, rows, PACK)
    vmem = pl.BlockSpec(memory_space=pltpu.VMEM)
    out = pl.pallas_call(
        functools.partial(merge_kernel, pa),
        in_specs=[vmem],
        out_specs=vmem,
        out_shape=sds(block, jnp.float32),
        scratch_shapes=[
            pltpu.VMEM(block, jnp.float32),
            pltpu.VMEM((rows, PACK), jnp.float32),
            pltpu.SemaphoreType.DMA((pa,)),
            pltpu.SemaphoreType.DMA((pa,)),
            pltpu.SemaphoreType.DMA((pa,)),
            pltpu.SemaphoreType.DMA((pa,)),
        ],
        compiler_params=pltpu.CompilerParams(collective_id=0, has_side_effects=True, vmem_limit_bytes=16 * MIB),
        name="cross_merge",
    )(part.reshape(block))
    return out.reshape(answer_rows, PACK)


def cross_back_kernel(question_ref, length_ref, q_ref, ck_ref, cv_ref, grad_ref, att_ref, lse_ref, gq_ref, gkv_ref):
    rows = q_ref.shape[0]
    mask = permitted_mask(question_ref, length_ref, rows, ck_ref.shape[0] // PL)
    lane = lax.broadcasted_iota(jnp.int32, (rows, 128), 1)
    for pair in range(HEADS // 2):
        cols = slice(pair * 128, (pair + 1) * 128)
        q = q_ref[:, cols]
        k = ck_ref[:, cols]
        v = cv_ref[:, cols]
        g = grad_ref[:, cols]
        weighed = g.astype(jnp.float32) * att_ref[:, cols]
        gqs = []
        scores = []
        probs = []
        for head in range(2):
            place = 2 * pair + head
            s = jnp.where(mask, 0.125 * nt(head_lanes(q, head), k), -1e9)
            p = jnp.exp(s - lse_ref[:, place : place + 1])
            dp = nt(head_lanes(g, head), v)
            delta = jnp.sum(head_lanes(weighed, head), axis=1, keepdims=True)
            ds = to_low(p * (dp - delta))
            gqs.append(nn(ds, k))
            scores.append(ds)
            probs.append(to_low(p))
        gq_ref[:, cols] = 0.125 * jnp.where(lane < HEAD, gqs[0], gqs[1])
        both_q = jnp.concatenate([head_lanes(q, 0), head_lanes(q, 1)], axis=0)
        both_g = jnp.concatenate([head_lanes(g, 0), head_lanes(g, 1)], axis=0)
        gkv_ref[0, :, cols] = to_low(0.125 * product_tn(jnp.concatenate(scores, axis=0), both_q))
        gkv_ref[1, :, cols] = to_low(product_tn(jnp.concatenate(probs, axis=0), both_g))


def cross_back(question_of, lengths, q, ck, cv, grad, att, lse):
    vmem = pl.BlockSpec(memory_space=pltpu.VMEM)
    smem = pl.BlockSpec(memory_space=pltpu.SMEM)
    return pl.pallas_call(
        cross_back_kernel,
        in_specs=[smem, smem] + [vmem] * 6,
        out_specs=[vmem, vmem],
        out_shape=[sds((q.shape[0], D), jnp.float32), sds((2, ck.shape[0], D), jnp.bfloat16)],
        compiler_params=params(40),
        name="cross_back",
    )(question_of, lengths, q, ck, cv, grad, att, lse)


def causal_row(length):
    table = np.zeros((128, BUCKETS), np.float32)
    for back in range(length):
        table[-back % 128, bucket_of(-back, False)] = 1.0
    return table


def in_three(values):
    high = to_low(values)
    rest = values - high.astype(jnp.float32)
    middle = to_low(rest)
    return high, middle, to_low(rest - middle.astype(jnp.float32))


def dec_pre_kernel(
    x_ref, gains_ref, bias_ref, table_ref, wq_ref, wk_ref, wv_ref, wo_ref, wcq_ref,
    low_ref, q_ref, k_ref, v_ref, probs_ref, att_ref, mid_ref, cross_low_ref, cross_q_ref,
):
    rows = x_ref.shape[0]
    base = product_tn(bias_ref[...], table_ref[...])
    x = x_ref[...].astype(jnp.float32)
    normed, _ = rms(x, gain_of(gains_ref, GAIN_SELF))
    low = to_low(normed)
    low_ref[...] = low
    q = to_low(0.125 * to_low(nn(low, wq_ref[...])).astype(jnp.float32))
    k = to_low(nn(low, wk_ref[...]))
    v = to_low(nn(low, wv_ref[...]))
    q_ref[...] = q
    k_ref[...] = k
    v_ref[...] = v
    i = lax.broadcasted_iota(jnp.int32, (rows, rows), 0)
    j = lax.broadcasted_iota(jnp.int32, (rows, rows), 1)
    mask = (j <= i) & (i // ANS == j // ANS)
    lane = lax.broadcasted_iota(jnp.int32, (rows, 128), 1)
    for pair in range(HEADS // 2):
        cols = slice(pair * 128, (pair + 1) * 128)
        outs = []
        for half in range(2):
            head = 2 * pair + half
            spread = jnp.broadcast_to(base[head : head + 1, :], (rows, 128))
            bias = pltpu.roll(spread, 0, 1, stride=1, stride_axis=0)[:, :rows]
            s = jnp.where(mask, nt(head_lanes(q[:, cols], half), k[:, cols]) + bias, -1e9)
            e = jnp.exp(s - jnp.max(s, axis=1, keepdims=True))
            p = e / jnp.sum(e, axis=1, keepdims=True)
            probs_ref[head] = p
            outs.append(nn(to_low(p), v[:, cols]))
        att_ref[:, cols] = to_low(jnp.where(lane < HEAD, outs[0], outs[1]))
    mid = x + nn(att_ref[...], wo_ref[...])
    mid_ref[...] = mid
    normed, _ = rms(mid, gain_of(gains_ref, GAIN_CROSS))
    low = to_low(normed)
    cross_low_ref[...] = low
    cross_q_ref[...] = to_low(nn(low, wcq_ref[...]))


def in_vmem(kernel, outs, name, *args, smem=0):
    vmem = pl.BlockSpec(memory_space=pltpu.VMEM)
    return pl.pallas_call(
        kernel,
        in_specs=[pl.BlockSpec(memory_space=pltpu.SMEM)] * smem + [vmem] * (len(args) - smem),
        out_specs=[vmem] * len(outs),
        out_shape=outs,
        compiler_params=params(62),
        name=name,
    )(*args)


def dec_pre(x, gains, bias, table, wq, wk, wv, wo, wcq):
    rows = x.shape[0]
    low = sds((rows, D), jnp.bfloat16)
    full = sds((rows, D), jnp.float32)
    outs = [low, low, low, low, sds((HEADS, rows, rows), jnp.float32), low, full, low, low]
    return in_vmem(dec_pre_kernel, outs, "dec_pre", x, gains, bias, table, wq, wk, wv, wo, wcq)


def dec_mid_kernel(
    merged_ref, mid_ref, cot_ref, gains_ref, wco_ref, win_ref, wout_ref,
    out_ref, low_ref, hidden_ref, pre_grad_ref, after_low_ref, grad_after_ref, att_grad_ref, gain_grad_ref, slope_ref,
):
    rows = mid_ref.shape[0]
    three = nn(jnp.concatenate(in_three(merged_ref[:, :D]), axis=0), wco_ref[...])
    after = mid_ref[...] + (three[:rows] + three[rows : 2 * rows] + three[2 * rows :])
    normed, scale = rms(after, gain_of(gains_ref, GAIN_DFFN))
    low = to_low(normed)
    low_ref[...] = low
    y = after
    width = 768
    chunks = [slice(c * width, (c + 1) * width) for c in range(win_ref.shape[1] // width)]
    for cols in chunks:
        hidden, slope = gelu_both(nn(low, win_ref[:, cols]))
        hidden = to_low(hidden)
        hidden_ref[:, cols] = hidden
        slope_ref[:, cols] = slope
        y = y + nn(hidden, wout_ref[cols, :])
    out_ref[...] = to_low(y)
    cot = cot_ref[...]
    acc = None
    for cols in chunks:
        pre = to_low(slope_ref[:, cols] * nt(cot, wout_ref[cols, :]))
        pre_grad_ref[:, cols] = pre
        part = nt(pre, win_ref[:, cols])
        acc = part if acc is None else acc + part
    back, gain_grad = rms_back(after, scale, gain_of(gains_ref, GAIN_DFFN), acc)
    gain_grad_ref[...] = gain_grad
    grad_after = cot.astype(jnp.float32) + back
    grad_after_ref[...] = grad_after
    after_low = to_low(grad_after)
    after_low_ref[...] = after_low
    att_grad_ref[...] = to_low(nt(after_low, wco_ref[...]))


def dec_mid_call(merged, mid, cot, gain, wco, win, wout):
    rows = mid.shape[0]
    ff = win.shape[1]
    low = sds((rows, D), jnp.bfloat16)
    full = sds((rows, D), jnp.float32)
    wide = sds((rows, ff), jnp.bfloat16)
    outs = [low, low, wide, wide, low, full, low, sds((1, D), jnp.float32)]
    vmem = pl.BlockSpec(memory_space=pltpu.VMEM)
    return pl.pallas_call(
        dec_mid_kernel,
        in_specs=[vmem] * 7,
        out_specs=[vmem] * len(outs),
        out_shape=outs,
        scratch_shapes=[pltpu.VMEM((rows, ff), jnp.float32)],
        compiler_params=params(62),
        name="dec_mid",
    )(merged, mid, cot, gain, wco, win, wout)


def dec_post_kernel(
    gq_ref, grad_after_ref, mid_ref, x_ref, q_ref, k_ref, v_ref, probs_ref, gains_ref,
    wq_ref, wk_ref, wv_ref, wo_ref, wcq_ref, after_ref,
    mid_low_ref, dq_ref, dk_ref, dv_ref, out_ref, gain_self_grad_ref, gain_cross_grad_ref, fold_ref,
):
    rows = x_ref.shape[0]
    mid = mid_ref[...]
    scale = lax.rsqrt(jnp.mean(mid * mid, axis=-1, keepdims=True) + epsilon)
    three = nt(jnp.concatenate(in_three(gq_ref[...]), axis=0), wcq_ref[...])
    back, gain_grad = rms_back(mid, scale, gain_of(gains_ref, GAIN_CROSS), three[:rows] + three[rows : 2 * rows] + three[2 * rows :])
    gain_cross_grad_ref[...] = gain_grad
    grad_mid = grad_after_ref[...] + back
    mid_low = to_low(grad_mid)
    mid_low_ref[...] = mid_low
    att_grad = to_low(nt(mid_low, wo_ref[...]))
    lane = lax.broadcasted_iota(jnp.int32, (rows, 128), 1)
    row8 = lax.broadcasted_iota(jnp.int32, (8, 128), 0)
    for pair in range(HEADS // 2):
        cols = slice(pair * 128, (pair + 1) * 128)
        q = q_ref[:, cols]
        k = k_ref[:, cols]
        v = v_ref[:, cols]
        g = att_grad[:, cols]
        dqs = []
        scores = []
        probs = []
        for half in range(2):
            head = 2 * pair + half
            p = probs_ref[head]
            dp = nt(head_lanes(g, half), v)
            ds = p * (dp - jnp.sum(p * dp, axis=1, keepdims=True))
            wide = jnp.concatenate([ds, jnp.zeros((rows, 128 - rows), jnp.float32)], axis=1)
            total = wide[0:8]
            for group in range(1, rows // 8):
                total = total + pltpu.roll(wide[group * 8 : group * 8 + 8], 128 - group * 8, 1)
            for bit in (1, 2, 4):
                total = jnp.where((row8 // bit) % 2 == 1, pltpu.roll(total, 128 - bit, 1), total)
            fold_ref[head : head + 1, :] = jnp.sum(total, axis=0, keepdims=True)
            ds = to_low(ds)
            dqs.append(nn(ds, k))
            scores.append(ds)
            probs.append(to_low(p))
        dq_ref[:, cols] = to_low(0.125 * jnp.where(lane < HEAD, dqs[0], dqs[1]))
        both_q = jnp.concatenate([head_lanes(q, 0), head_lanes(q, 1)], axis=0)
        both_g = jnp.concatenate([head_lanes(g, 0), head_lanes(g, 1)], axis=0)
        dk_ref[:, cols] = to_low(product_tn(jnp.concatenate(scores, axis=0), both_q))
        dv_ref[:, cols] = to_low(product_tn(jnp.concatenate(probs, axis=0), both_g))
    x = x_ref[...].astype(jnp.float32)
    scale = lax.rsqrt(jnp.mean(x * x, axis=-1, keepdims=True) + epsilon)
    grad = nt(dq_ref[...], wq_ref[...]) + nt(dk_ref[...], wk_ref[...]) + nt(dv_ref[...], wv_ref[...])
    back, gain_grad = rms_back(x, scale, gain_of(gains_ref, GAIN_SELF), grad)
    gain_self_grad_ref[...] = gain_grad
    out_ref[...] = grad_mid + back


def dec_post(gq, grad_after, mid, x, q, k, v, probs, gains, wq, wk, wv, wo, wcq, after):
    rows = x.shape[0]
    low = sds((rows, D), jnp.bfloat16)
    gain = sds((1, D), jnp.float32)
    outs = [low, low, low, low, sds((rows, D), jnp.float32), gain, gain, sds((HEADS, 128), jnp.float32)]
    vmem = pl.BlockSpec(memory_space=pltpu.VMEM)
    return pl.pallas_call(
        dec_post_kernel,
        in_specs=[vmem] * 14 + [pl.BlockSpec(memory_space=pl.ANY)],
        out_specs=[vmem] * len(outs),
        out_shape=outs,
        compiler_params=params(62),
        name="dec_post",
    )(gq, grad_after, mid, x, q, k, v, probs, gains, wq, wk, wv, wo, wcq, after)


def dec_weight_kernel(
    pb, pa, place_ref, low_ref, dq_ref, dk_ref, dv_ref, att_ref, mid_low_ref, cross_low_ref, gq_ref, merged_ref, after_low_ref,
    hidden_ref, cot_ref, dffn_low_ref, pre_grad_ref, keep_ref, send_ref, turned_ref, wide_ref,
):
    shards = pb * pa
    column = place_ref[0]
    core = place_ref[1]
    rows = D // shards
    depth = low_ref.shape[0]

    def own(left, scratch):
        height = left.shape[1]
        here = height // shards
        span = left.shape[0]
        scratch[:, :span] = left.astype(jnp.float32).T
        cut = [scratch[pl.ds((b * pa + column) * here, here), :span] for b in range(pb)]
        return to_low(jnp.concatenate(cut, axis=0)), here

    first = 0

    def put(values, here):
        nonlocal first
        for y in range(pb // 2):
            low_part = values[2 * y * here : (2 * y + 1) * here]
            high_part = values[(2 * y + 1) * here : (2 * y + 2) * here]
            slot = place_ref[2 + y]
            keep_ref[slot, first : first + here, :] = jnp.where(core == 0, low_part, high_part)
            send_ref[slot, first : first + here, :] = jnp.where(core == 0, high_part, low_part)
        first += here

    left, here = own(low_ref[...], turned_ref)
    for right_ref in (dq_ref, dk_ref, dv_ref):
        put(nn(left, right_ref[...]), here)
    left, here = own(att_ref[...], turned_ref)
    put(nn(left, mid_low_ref[...]), here)
    left, here = own(cross_low_ref[...], turned_ref)
    a, b, c = in_three(gq_ref[...])
    put(nn(left, a) + nn(left, b) + nn(left, c), here)
    right = after_low_ref[...]
    a, b, c = (own(part, turned_ref)[0] for part in in_three(merged_ref[:, :D]))
    put(nn(a, right) + nn(b, right) + nn(c, right), here)
    left, wide = own(hidden_ref[...], wide_ref)
    put(nn(left, cot_ref[...]), wide)
    left, here = own(dffn_low_ref[...], turned_ref)
    for c in range(pre_grad_ref.shape[1] // D):
        put(nn(left, pre_grad_ref[:, c * D : (c + 1) * D]), here)


def dec_weight_grads(pb, pa, place, *args):
    rows, ff = args[-1].shape
    shards = pb * pa
    height = (6 * D + ff + ff) // shards
    vmem = pl.BlockSpec(memory_space=pltpu.VMEM)
    return pl.pallas_call(
        functools.partial(dec_weight_kernel, pb, pa),
        in_specs=[pl.BlockSpec(memory_space=pltpu.SMEM)] + [vmem] * len(args),
        out_specs=[vmem, vmem],
        out_shape=[sds((pb // 2, height, D), jnp.float32)] * 2,
        scratch_shapes=[pltpu.VMEM((D, rows), jnp.float32), pltpu.VMEM((ff, rows), jnp.float32)],
        compiler_params=params(62),
        name="dec_weight_grads",
    )(place, *args)


def finish_kernel(pb, pa, heights, small_ref, dec_ref, enc_table_ref, dec_table_ref, *outs):
    shards = pb * pa
    shard = lax.axis_index("pb") * pa + lax.axis_index("pa")
    width = D // shards
    rolled = pltpu.roll(small_ref[0:8, :D], lax.rem(D - shard * width, D), 1)
    for r in range(6):
        outs[r][...] = rolled[r, :width]
    share = BUCKETS * HEADS // shards
    bucket = shard * share // HEADS
    head = lax.rem(shard * share, HEADS)

    def bias_grad(folded, table_ref, out_ref):
        table = table_ref[...]
        by_bucket = sum(nt(table, part) for part in in_three(folded))
        row = lax.broadcasted_iota(jnp.int32, by_bucket.shape, 0)
        mine = jnp.sum(jnp.where(row == bucket, by_bucket, 0.0), axis=0, keepdims=True)
        mine = jnp.concatenate([mine, jnp.zeros((1, 128 - HEADS), jnp.float32)], axis=1)
        mine = jnp.broadcast_to(mine, (8, 128))
        out_ref[...] = pltpu.roll(mine, lax.rem(128 - head, 128), 1)[0, :share]

    bias_grad(small_ref[8 : 8 + HEADS, :], enc_table_ref, outs[6])
    dec_fold = jnp.concatenate([small_ref[0:6, D : D + 128], small_ref[0:6, D + 128 : D + 256]], axis=0)
    bias_grad(dec_fold, dec_table_ref, outs[7])
    first = 0
    for number, height in enumerate(heights):
        outs[8 + number][...] = dec_ref[first : first + height]
        first += height
    wide_ref = outs[8 + len(heights)]
    for c in range(wide_ref.shape[1] // D):
        wide_ref[:, c * D : (c + 1) * D] = dec_ref[first : first + width]
        first += width


def finish(pb, pa, small, dec_sum, enc_table, dec_table, ff):
    shards = pb * pa
    width = D // shards
    share = BUCKETS * HEADS // shards
    heights = [width] * 6 + [ff // shards]
    outs = [sds((width,), jnp.float32)] * 6 + [sds((share,), jnp.float32)] * 2
    outs += [sds((h, D), jnp.float32) for h in heights] + [sds((width, ff), jnp.float32)]
    return in_vmem(functools.partial(finish_kernel, pb, pa, heights), outs, "finish", small, dec_sum, enc_table, dec_table)


def bits_of(mesh_sizes):
    pb, pa = mesh_sizes
    pb_bits = pb.bit_length() - 1
    pa_bits = pa.bit_length() - 1
    ys = [("pb", b) for b in range(1, pb_bits)]
    xs = [("pa", b) for b in range(pa_bits - 2)]
    zs = [("pa", b) for b in range(pa_bits - 2, pa_bits)]
    return xs, ys, zs


def orders_of(mesh_sizes):
    xs, ys, zs = bits_of(mesh_sizes)
    return (xs + ys + zs, ys + xs + zs, zs[:1] + xs + ys + zs[1:], zs[:1] + ys + xs + zs[1:])


def exchange_table(mesh_sizes, orders):
    pb, pa = mesh_sizes
    pb_me = lax.axis_index("pb")
    pa_me = lax.axis_index("pa")
    cells = np.arange(pb * pa // 2)
    pb_of = jnp.asarray(cells // pa * 2)
    pa_of = jnp.asarray(cells % pa)
    rows = [jnp.full((cells.size,), pb_me % 2, jnp.int32)]
    for order in orders:
        slot = jnp.zeros((cells.size,), jnp.int32)
        for axis, bit in order:
            far = ((pb_of if axis == "pb" else pa_of) >> bit) ^ ((pb_me if axis == "pb" else pa_me) >> bit)
            slot = slot * 2 + (far & 1).astype(jnp.int32)
        rows.append(slot)
    return jnp.stack(rows)


MESH = pl.DeviceIdType.MESH
LINK = 0.11
PAIR = 0.45
NEAR = ("pb", 0)


def link_of(step, sizes):
    xs, ys, zs = bits_of(sizes)
    if step == NEAR:
        return "core"
    if step in ys:
        return "y"
    if step in xs:
        return "x"
    return "z far" if step == zs[-1] else "z"


def link_time(step, megabytes, sizes):
    if step == NEAR:
        return megabytes / PAIR
    return 2 * megabytes * (2 if step == bits_of(sizes)[2][-1] else 1) / LINK


class Piece:
    def __init__(self, array, first, width, order, place=None, start=0.0, met=False):
        self.array, self.first, self.width, self.order = array, first, width, [NEAR] + list(order)
        self.place, self.start, self.met = place, start, met


DEPTH = 3


def block_of(piece, shapes):
    return tuple(shapes[piece.array][:2]) + (piece.width,)


def plan(pieces, shapes, sizes):
    free, held, queues = {}, {}, {}
    pending = [(piece.start, i, "ready", 0) for i, piece in enumerate(pieces)]
    events = []

    def key_of(what, i, step):
        return ("load", block_of(pieces[i], shapes)) if what == "load" else link_of(pieces[i].order[step], sizes)

    def start(now, what, i, step, starts):
        key = key_of(what, i, step)
        if key != "core" and held.get(key, 0) >= (1 if what == "load" else DEPTH):
            queues.setdefault(key, []).append((what, i, step))
            return
        held[key] = held.get(key, 0) + 1
        half, rows = shapes[pieces[i].array][:2]
        megabytes = (half >> step) * rows * pieces[i].width * 4e-6
        begin = max(now, free.get(key, 0.0))
        if what == "load":
            free[key] = begin + 1.0 + megabytes * 0.8
            pending.append((free[key], i, "loaded", 0))
        else:
            free[key] = begin + link_time(pieces[i].order[step], megabytes, sizes)
            pending.append((free[key] + 1.5, i, "arrived", step))
        starts.append((what, i, step))

    while pending:
        pending.sort()
        now, i, what, step = pending.pop(0)
        starts = []
        if what != "ready":
            key = key_of("load" if what == "loaded" else "send", i, step)
            held[key] -= 1
            if queues.get(key):
                start(now, *queues[key].pop(0), starts)
        if what == "ready":
            start(now, "load" if pieces[i].met else "send", i, 0, starts)
        elif what == "arrived" and step == 0:
            start(now, "load", i, 0, starts)
        elif what == "loaded":
            start(now + 0.5, "send", i, 1, starts)
        elif step + 1 < len(pieces[i].order):
            start(now + 0.5, "send", i, step + 1, starts)
        events.append((now, what, i, step, starts))
    return events


def partner(step):
    axis, bit = step
    me = lax.axis_index(axis)
    size = 1 << bit
    there = me + size - 2 * size * lax.rem(me // size, 2)
    return {"pb": lax.axis_index("pb"), "pa": lax.axis_index("pa"), axis: there}


def all_steps(sizes):
    xs, ys, zs = bits_of(sizes)
    return [NEAR] + xs + ys + zs


def greet(sizes):
    barrier = pltpu.get_barrier_semaphore()
    for step in all_steps(sizes):
        pl.semaphore_signal(barrier, inc=1, device_id=partner(step), device_id_type=MESH)
    pl.semaphore_wait(barrier, len(all_steps(sizes)))


class Exchange:
    def __init__(self, sizes, pieces, shapes):
        self.sizes, self.pieces, self.shapes = sizes, pieces, shapes
        self.events = plan(pieces, shapes, sizes)
        self.stages = len(all_steps(sizes))
        self.arrays = range(len(shapes))
        self.own = [a for a in self.arrays if any(p.array == a and p.place is not None for p in pieces)]
        self.block = [block_of(pieces[self.of(a)[0]], shapes) for a in self.arrays]
        self.blocks = sorted(set(self.block))
        self.before = {}
        for n, a in enumerate(self.own):
            earlier = [b for b in self.own[:n] if self.block[b] == self.block[a]]
            if earlier:
                self.before[a] = earlier[-1]

    def of(self, array):
        return [i for i, p in enumerate(self.pieces) if p.array == array]

    def scratch(self):
        out = [pltpu.VMEM(block, jnp.float32) for block in self.blocks]
        for array in self.arrays:
            half, *block = self.block[array]
            count = len(self.of(array))
            out += [
                pltpu.VMEM((count, half, *block), jnp.float32),
                pltpu.VMEM((count, half - 1, *block), jnp.float32),
            ]
        count = len(self.pieces)
        return out + [
            pltpu.SemaphoreType.DMA((count,)),
            pltpu.SemaphoreType.DMA((count,)),
            pltpu.SemaphoreType.DMA((count, self.stages)),
            pltpu.SemaphoreType.DMA((count, self.stages)),
        ]

    def bind(self, keeps, sends, nears, outs, staging, scratch):
        self.keeps, self.sends, self.nears, self.outs, self.staging = keeps, sends, nears, outs, staging
        places = dict(zip(self.blocks, scratch))
        self.loaded = [places[block] for block in self.block]
        scratch = scratch[len(self.blocks) :]
        self.kept = [scratch[2 * a] for a in self.arrays]
        recvs = [scratch[2 * a + 1] for a in self.arrays]
        self.near_sems, self.keep_sems, self.send_sems, self.recv_sems = scratch[2 * len(self.shapes) :]
        self.bufs, self.recvs = {}, {}
        for array in self.arrays:
            for number, i in enumerate(self.of(array)):
                self.bufs[i], self.recvs[i] = self.kept[array].at[number], recvs[array].at[number]

    def loads(self, i):
        piece = self.pieces[i]
        cols = pl.ds(piece.first, piece.width)
        out = [pltpu.make_async_copy(self.nears[piece.array].at[:, :, cols], self.loaded[piece.array], self.near_sems.at[i])]
        if piece.place is None:
            out.append(pltpu.make_async_copy(self.keeps[piece.array].at[:, :, cols], self.bufs[i], self.keep_sems.at[i]))
        return out

    def sizes_of(self, i, step):
        half = self.shapes[self.pieces[i].array][0]
        count = half >> step
        return count, half - 2 * count

    def copy(self, i, step):
        piece = self.pieces[i]
        count, first = self.sizes_of(i, step)
        if step == 0:
            if piece.place is None:
                source = self.sends[piece.array].at[:, :, pl.ds(piece.first, piece.width)]
            else:
                source = self.staging[piece.array].at[piece.place % 2]
            target = self.nears[piece.array].at[:, :, pl.ds(piece.first, piece.width)]
        else:
            source = self.bufs[i].at[pl.ds(count, count)]
            target = self.recvs[i].at[pl.ds(first, count)]
        return pltpu.make_async_remote_copy(
            src_ref=source, dst_ref=target, send_sem=self.send_sems.at[i, step], recv_sem=self.recv_sems.at[i, step],
            device_id=partner(piece.order[step]), device_id_type=MESH,
        )

    def free_staging(self, array, place):
        if place >= 2:
            self.copy(self.of(array)[place - 2], 0).wait_send()
        elif array in self.before:
            self.copy([i for i in self.of(self.before[array]) if self.pieces[i].place % 2 == place][-1], 0).wait_send()

    def event(self, what, i, step, starts):
        piece = self.pieces[i]
        buf = self.bufs[i]
        last = what == "arrived" and step + 1 == len(piece.order)
        count = 0
        if what == "loaded":
            for load in self.loads(i):
                load.wait()
            source, first, count = self.loaded[piece.array], 0, self.shapes[piece.array][0]
        elif what == "arrived":
            self.copy(i, step).wait_recv()
            if step > 0:
                source = self.recvs[i]
                count, first = self.sizes_of(i, step)

        def add(slot, _):
            buf[slot] = buf[slot] + source[first + slot]
            return 0

        if last:
            self.outs[piece.array][:, piece.first : piece.first + piece.width] = buf[0] + source[first]
        elif count:
            lax.fori_loop(count // 2, count, add, 0, unroll=min(4, count // 2))
        mine = [s for s in starts if s[0] == "send"]
        for _, j, k in mine:
            self.copy(j, k).start()
        if not last and count:
            lax.fori_loop(0, count // 2, add, 0, unroll=min(4, count // 2))
        for kind, j, _ in starts:
            if kind == "load":
                for load in self.loads(j):
                    load.start()

    def finish(self):
        for i, piece in enumerate(self.pieces):
            waited = piece.place is not None and (
                piece.place + 2 < len(self.of(piece.array)) or piece.array in self.before.values()
            )
            first = 1 if waited or piece.met else 0
            for step in range(first, len(piece.order)):
                self.copy(i, step).wait_send()

    def points(self, times, ready):
        out = [[] for _ in times]
        place = 0
        for when, what, i, step, starts in self.events:
            while place < len(times) - 1 and times[place] < when:
                place += 1
            if what == "ready" and i in ready:
                place = max(place, ready[i])
            out[place].append((what, i, step, starts))
        return out
class Everywhere:
    def __init__(self, sizes, shape):
        self.steps = all_steps(sizes)
        self.shape = shape

    def scratch(self):
        count = len(self.steps)
        return [
            pltpu.VMEM((count + 1,) + self.shape, jnp.float32),
            pltpu.VMEM((count,) + self.shape, jnp.float32),
            pltpu.SemaphoreType.DMA((count,)),
            pltpu.SemaphoreType.DMA((count,)),
        ]

    def bind(self, scratch):
        self.sums, self.recvs, self.send_sems, self.recv_sems = scratch

    def copy(self, k):
        return pltpu.make_async_remote_copy(
            src_ref=self.sums.at[k], dst_ref=self.recvs.at[k], send_sem=self.send_sems.at[k], recv_sem=self.recv_sems.at[k],
            device_id=partner(self.steps[k]), device_id_type=MESH,
        )

    def arrive(self, k):
        self.copy(k).wait_recv()
        self.sums[k + 1] = self.sums[k] + self.recvs[k]
        if k + 1 < len(self.steps):
            self.copy(k + 1).start()

    def finish(self):
        for k in range(len(self.steps)):
            self.copy(k).wait_send()


SMALL = (24, 1024)
ATTN_STEP = 3.6
OPENING = 7.0
TILE_US = 0.0052
BACK_STEP = 1.2


def slots_of(sizes, order):
    pb, pa = sizes
    far = {}
    for axis, bit in order:
        me = lax.rem(lax.axis_index(axis) // (1 << bit), 2)
        far[axis, bit] = (me, 1 - me)
    cells = []
    for y in range(pb // 2):
        for a in range(pa):
            slot = 0
            for axis, bit in order:
                slot = slot * 2 + far[axis, bit][(2 * y if axis == "pb" else a) >> bit & 1]
            cells.append(slot)
    return cells


class Phase:
    def __init__(self, name, first, count, us):
        self.name, self.first, self.count, self.us = name, first, count, us


def last_kernel(
    exchange, everywhere, points, orders, phases, passages, share, outside, gradients,
    lengths_ref, q_ref, k_ref, v_ref, o_ref, do_ref, lse_ref, base_ref, x_ref, grad_mid_ref, gains_ref, wq_ref, wk_ref, wv_ref,
    dec_fold_ref, *refs,
):
    refs = list(refs)

    def take(count):
        out = refs[:count]
        del refs[:count]
        return out

    gains = take(5)
    lefts = take(len(gradients))
    rights = take(len(gradients) - 1)
    keeps, others = take(len(outside)), take(len(outside))
    out_ref, small_ref = take(2)
    moved = take(len(exchange.shapes))
    nears = [other if met else take(1)[0] for other, met in zip(others, outside)] + take(len(gradients))
    strip_ref, gather_ref, dqT_ref, grads_ref, fold_ref, gain_grad_ref = take(6)
    staging = {}
    for array in exchange.own:
        staging[array] = staging[exchange.before[array]] if array in exchange.before else take(1)[0]
    everywhere.bind(take(4))
    exchange.bind(keeps, others, nears, moved, staging, refs)
    step = pl.program_id(0)
    sizes = exchange.sizes
    pb, pa = sizes

    @pl.when(step == 0)
    def _():
        greet(sizes)
        for event in points["start"][0]:
            exchange.event(*event)

    def run(place):
        for at, events in points.get(place, {}).items():
            if events:

                @pl.when(step == at)
                def _(events=events):
                    for event in events:
                        exchange.event(*event)

    def attention(phase):
        number = step - phase.first
        pair = number // passages
        passage = lax.rem(number, passages)
        place = pl.ds(pl.multiple_of(passage * PL, PL), PL), pl.ds(pl.multiple_of(pair * 128, 128), 128)
        attn_backward_kernel(
            lambda head: run(("attention", head)), passage, passages, lengths_ref, q_ref, k_ref, v_ref, o_ref, do_ref, lse_ref, base_ref,
            grads_ref.at[(0,) + place], grads_ref.at[(1,) + place], grads_ref.at[(2,) + place], fold_ref.at[pl.ds(pair, 1)],
            strip_ref, gather_ref, dqT_ref,
        )

    def gradient(phase, array, left_ref, right_ref):
        number = step - phase.first
        width = exchange.pieces[exchange.of(array)[0]].width
        if right_ref is None:
            each = D // width
            column = pl.ds(pl.multiple_of(lax.rem(number, each) * width, width), width)
            right = grads_ref[number // each, :, column]
        else:
            right = right_ref[...]
        for place in range(0 if array in exchange.before else 2, phase.count):

            @pl.when(number == place)
            def _(place=place):
                exchange.free_staging(array, place)

        chain = 0
        for place, c in enumerate(gradients[array - len(outside)][3]):
            chain = jnp.where(number == place, c, chain)
        choices = [slots_of(sizes, order) for order in orders]
        core = lax.rem(lax.axis_index("pb"), 2)
        rows = exchange.shapes[array][1]
        half_rows = pa * rows
        kept, staged = exchange.kept[array], exchange.staging[array]
        for y in range(pb // 2):
            low_part = nn(left_ref[2 * y * half_rows : (2 * y + 1) * half_rows, :], right)
            high_part = nn(left_ref[(2 * y + 1) * half_rows : (2 * y + 2) * half_rows, :], right)
            mine = jnp.where(core == 0, low_part, high_part)
            other = jnp.where(core == 0, high_part, low_part)
            for a in range(pa):
                slot = choices[0][y * pa + a]
                for c in range(1, len(orders)):
                    slot = jnp.where(chain == c, choices[c][y * pa + a], slot)
                kept[number, slot] = mine[a * rows : (a + 1) * rows]
                staged[lax.rem(number, 2), slot] = other[a * rows : (a + 1) * rows]

    def back(phase):
        height = x_ref.shape[0]
        rows = pl.ds(pl.multiple_of((step - phase.first) * height, height), height)
        qkv_back_kernel(
            step == phase.first, grads_ref.at[0, rows], grads_ref.at[1, rows], grads_ref.at[2, rows],
            x_ref, grad_mid_ref, gains_ref, wq_ref, wk_ref, wv_ref, out_ref, gain_grad_ref,
        )

    for phase in phases:

        @pl.when((step >= phase.first) & (step < phase.first + phase.count))
        def _(phase=phase):
            if phase.name == "attention":
                attention(phase)
            elif phase.name == "back":
                back(phase)
            else:
                k = phase.name
                gradient(phase, exchange.own[k], lefts[k], rights[k] if k < len(rights) else None)

    run("end")

    @pl.when(step == pl.num_programs(0) - 1)
    def _():
        first = everywhere.sums
        first[0] = jnp.zeros(SMALL, jnp.float32)
        first[0, 0:1, :D] = gain_grad_ref[...]
        for r, ref in enumerate(gains):
            first[0, r + 1 : r + 2, :D] = ref[...] if r < 2 else ref[...] * share
        for pair in range(HEADS // 2):
            first[0, 8 + 2 * pair : 10 + 2 * pair, :] = fold_ref[pair]
        for part in range(2):
            lanes = slice(D + part * 128, D + (part + 1) * 128)
            first[0, 0:6, lanes] = dec_fold_ref[6 * part : 6 * part + 6] * share
        everywhere.copy(0).start()
        left = points["rest"]
        steps = len(everywhere.steps)
        every = max(1, len(left) // (steps + 1))
        done = 0
        for n, event in enumerate(left):
            if n % every == every - 1 and done < steps:
                everywhere.arrive(done)
                done += 1
            exchange.event(*event)
        for k in range(done, steps):
            everywhere.arrive(k)
        small_ref[...] = everywhere.sums[steps]
        exchange.finish()
        everywhere.finish()


def outside_pieces(orders, groups):
    pieces = []
    for number, (_, _, met, chains, width) in enumerate(groups):
        for c, chain in enumerate(chains):
            order = chain if isinstance(chain, list) else orders[chain]
            pieces.append(Piece(number, c * width, width, order, start=0.1 * number + 0.01 * c, met=met))
    return pieces


def last_part(
    sizes, orders, groups, gradients, lengths, q, k, v, o, do, lse, base, x, grad_mid, gains, wq, wk, wv, dec_fold, grads_of_gains,
):
    pb, pa = sizes
    passages = lengths.shape[0]
    tokens = x.shape[0]
    pairs = HEADS // 2
    tile_rows = 128
    half = pb * pa // 2
    shapes = [g[0].shape for g in groups]
    widths = [right.shape[1] if right is not None else 3 * D for _, right, *_ in gradients]
    shapes += [(half, left.shape[0] // (pb * pa), w) for (left, *_), w in zip(gradients, widths)]

    phases = []
    names = list(range(len(gradients) - 1)) + ["attention", len(gradients) - 1, "back"]
    step = 0
    for name in names:
        if name == "attention":
            count, us = pairs * passages, ATTN_STEP
        elif name == "back":
            count, us = tokens // tile_rows, BACK_STEP
        else:
            count, us = widths[name] // gradients[name][2], TILE_US * gradients[name][2]
        phases.append(Phase(name, step, count, us))
        step += count
    steps = step
    pieces = outside_pieces(orders, groups)
    times, labels, ready = [OPENING], [("start", 0)], {}
    now = OPENING
    for phase in phases:
        for n in range(phase.count):
            number = phase.first + n
            if phase.name == "attention":
                times += [now, now + phase.us / 2]
                labels += [(("attention", 0), number), (("attention", 1), number)]
            now += phase.us
            if phase.name != "attention" and number < steps - 1:
                times.append(now)
                labels.append(("end", number))
            if isinstance(phase.name, int):
                ready[len(pieces)] = len(times) - 1
                width = gradients[phase.name][2]
                pieces.append(Piece(len(groups) + phase.name, n * width, width, orders[gradients[phase.name][3][n]], n, now))
    exchange = Exchange(sizes, pieces, shapes)
    everywhere = Everywhere(sizes, SMALL)
    points = {}
    found = exchange.points(times + [1e9], ready)
    for (place, number), events in zip(labels, found):
        points.setdefault(place, {})[number] = events
    points["rest"] = found[-1]
    by_name = {phase.name: phase for phase in phases}

    def at(name, i):
        phase = by_name[name]
        return jnp.clip(i - phase.first, 0, phase.count - 1)

    def pair_of(i):
        return at("attention", i) // passages

    def passage_of(i):
        return lax.rem(at("attention", i), passages)

    def once(array):
        return pl.BlockSpec(array.shape, lambda i: (0,) * array.ndim, pipeline_mode=pl.Buffered(1))

    tile = pl.BlockSpec((PL, 128), lambda i: (passage_of(i), pair_of(i)))
    rows = pl.BlockSpec((tile_rows, D), lambda i: (at("back", i), 0))
    hbm = pl.BlockSpec(memory_space=pl.ANY)
    keeps, others = [g[0] for g in groups], [g[1] for g in groups]
    outside = [g[2] for g in groups]
    lefts = [left for left, *_ in gradients]
    rights = [right for _, right, *_ in gradients[:-1]]
    right_specs = [
        pl.BlockSpec((tokens, width), lambda i, name=name: (0, at(name, i)), pipeline_mode=pl.Buffered(1)) for name, (_, _, width, _) in enumerate(gradients[:-1])
    ]
    own_shapes = shapes[len(groups) :]
    near_shapes = [s for s, met in zip(shapes, outside) if not met] + own_shapes
    return pl.pallas_call(
        functools.partial(
            last_kernel, exchange, everywhere, points, orders, phases, passages, 1.0 / pa, outside, gradients
        ),
        grid=(steps,),
        in_specs=[pl.BlockSpec(memory_space=pltpu.SMEM)]
        + [tile] * 5
        + [pl.BlockSpec((1, 1, 2, PL), lambda i: (pair_of(i), passage_of(i), 0, 0)), pl.BlockSpec((1, 2, WIDE), lambda i: (pair_of(i), 0, 0))]
        + [rows, rows]
        + [once(a) for a in (gains, wq, wk, wv, dec_fold) + tuple(grads_of_gains)]
        + [once(left) for left in lefts]
        + right_specs
        + [hbm] * (2 * len(groups)),
        out_specs=[rows, pl.BlockSpec(SMALL, lambda i: (0, 0), pipeline_mode=pl.Buffered(1))]
        + [pl.BlockSpec(s[1:], lambda i: (0, 0), pipeline_mode=pl.Buffered(1)) for s in shapes]
        + [hbm] * len(near_shapes),
        out_shape=[sds((tokens, D), jnp.float32), sds(SMALL, jnp.float32)]
        + [sds(s[1:], jnp.float32) for s in shapes]
        + [sds(s, jnp.float32) for s in near_shapes],
        scratch_shapes=[
            pltpu.VMEM((2, STRIP, WIDE), jnp.float32),
            pltpu.VMEM((2, STRIP, WIDE), jnp.float32),
            pltpu.VMEM((128, PL), jnp.bfloat16),
            pltpu.VMEM((3, tokens, D), jnp.bfloat16),
            pltpu.VMEM((pairs, 2, WIDE), jnp.float32),
            pltpu.VMEM((1, D), jnp.float32),
        ]
        + [pltpu.VMEM((2,) + exchange.block[a], jnp.float32) for a in exchange.own if a not in exchange.before]
        + everywhere.scratch()
        + exchange.scratch(),
        compiler_params=pltpu.CompilerParams(collective_id=1, has_side_effects=True, vmem_limit_bytes=63 * MIB + MIB // 2),
        name="enc_last",
    )(
        lengths, q, k, v, o, do, lse, base, x, grad_mid, gains, wq, wk, wv, dec_fold, *grads_of_gains, *lefts, *rights, *keeps, *others
    )[: 2 + len(shapes)]


def exchange_kernel(exchange, arrays, *refs):
    exchange.bind(refs[:arrays], {}, refs[arrays : 2 * arrays], refs[2 * arrays : 3 * arrays], {}, refs[3 * arrays :])
    greet(exchange.sizes)
    for _, *event in exchange.events:
        exchange.event(*event)
    exchange.finish()


def exchange_only(sizes, orders, groups):
    shapes = [g[0].shape for g in groups]
    exchange = Exchange(sizes, outside_pieces(orders, groups), shapes)
    return pl.pallas_call(
        functools.partial(exchange_kernel, exchange, len(groups)),
        in_specs=[pl.BlockSpec(memory_space=pl.ANY)] * (2 * len(groups)),
        out_specs=[pl.BlockSpec(memory_space=pltpu.VMEM)] * len(groups),
        out_shape=[sds(s[1:], jnp.float32) for s in shapes],
        scratch_shapes=exchange.scratch(),
        compiler_params=pltpu.CompilerParams(collective_id=2, has_side_effects=True, vmem_limit_bytes=63 * MIB),
        name="exchange",
    )(*[g[0] for g in groups], *[g[1] for g in groups])


def local(
    pb, pa,
    enc_in, dec_in, question_of, lengths, enc_gain_attn, enc_query, enc_key, enc_value, enc_output, enc_bias,
    enc_gain_ffn, enc_ff_in, enc_ff_out, enc_gain_final, cross_key, cross_value, dec_gain_self, dec_query, dec_key,
    dec_value, dec_output, dec_bias, dec_gain_cross, cross_query, cross_output, dec_gain_ffn, dec_ff_in, dec_ff_out,
    enc_cot, dec_cot,
):
    sizes = (pb, pa)
    orders = orders_of(sizes)
    answer_rows = dec_in.shape[0]
    gains = jnp.concatenate([enc_gain_attn, enc_gain_ffn, enc_gain_final, dec_gain_self, dec_gain_cross, dec_gain_ffn])
    gains = gains.astype(jnp.float32).reshape(6, D)
    table = exchange_table(sizes, orders)
    enc_table = jnp.asarray(strip_table().T, jnp.bfloat16)
    dec_table = jnp.asarray(causal_row(ANS).T, jnp.bfloat16)

    attn_turned, enc_queries, enc_keys, enc_values = qkv_forward(enc_in, gains, enc_query, enc_key, enc_value)
    enc_attended, attended_turned, enc_lse, base = attn_forward(lengths, enc_queries, enc_keys, enc_values, enc_bias, enc_table)
    enc_mid, ffn_turned, hidden_turned, enc_slope, enc_y, enc_out, final_turned, cross_keys, cross_values = post_forward(
        enc_in, enc_attended, gains, enc_output, enc_ff_in, enc_ff_out, cross_key, cross_value
    )

    self_low, dec_queries, dec_keys, dec_values, dec_probs, dec_attended, dec_mid, cross_low, cross_queries = dec_pre(
        dec_in, gains, dec_bias, dec_table, dec_query, dec_key, dec_value, dec_output, cross_query
    )

    merged = merge(cross_part(question_of, lengths, cross_queries, cross_keys, cross_values), pa)
    dec_out, dffn_low, dec_hidden, pre_grad_low, after_low, grad_after, cross_att_grad, dec_gain_ffn_grad = dec_mid_call(
        merged, dec_mid, dec_cot, gains, cross_output, dec_ff_in, dec_ff_out
    )
    query_part, grad_cross = cross_back(
        question_of, lengths, cross_queries, cross_keys, cross_values, cross_att_grad, merged[:, :D], merged[:, D:]
    )
    def near(terms):
        keep, send, _ = terms
        return keep, lax.ppermute(send, "pb", [(i, i ^ 1) for i in range(pb)])

    def doubled(values, bits, tick):
        for bit in bits:
            values = values + lax.ppermute(values, "pa", [(i, i ^ (1 << bit)) for i in range(pa)])
        return values + tick[0, 0]

    pa_bits = range(pa.bit_length() - 1)
    terms = weight_grad(table, final_turned, [(grad_cross, 0), (grad_cross, 1)], pb, pa, 256, 2)
    cross_terms = near(terms)
    grad_cross_q = doubled(query_part, pa_bits[:-2], terms[2])
    eout_low, epre_low, emid_low, grad_enc_mid, enc_att_grad, final_gain_grad, ffn_gain_grad, tick = post_backward(
        grad_cross, enc_y, enc_mid, enc_slope, enc_cot, gains, cross_key, cross_value, enc_ff_out, enc_ff_in, enc_output, grad_cross_q
    )
    grad_cross_q = doubled(grad_cross_q, pa_bits[-2:-1], tick)
    terms = weight_grad(table, hidden_turned, [eout_low], pb, pa, 256, 1, (grad_cross_q,))
    out_terms = terms[:2]
    grad_cross_q = doubled(grad_cross_q, pa_bits[-1:], terms[2])

    mid_low, grad_dq, grad_dk, grad_dv, dec_in_grad, dec_gain_self_grad, dec_gain_cross_grad, dec_fold = dec_post(
        grad_cross_q, grad_after, dec_mid, dec_in, dec_queries, dec_keys, dec_values, dec_probs, gains,
        dec_query, dec_key, dec_value, dec_output, cross_query, out_terms[0],
    )
    far = lax.axis_index("pb") // 2
    places = [lax.axis_index("pa"), lax.axis_index("pb") % 2]
    for y in range(pb // 2):
        slot = 0
        for _, bit in bits_of(sizes)[1]:
            slot = slot * 2 + ((far >> (bit - 1)) + (y >> (bit - 1))) % 2
        places.append(slot)
    dec_terms = dec_weight_grads(
        pb, pa, jnp.stack(places).astype(jnp.int32), self_low, grad_dq, grad_dk, grad_dv, dec_attended, mid_low, cross_low, grad_cross_q,
        merged, after_low, dec_hidden, dec_cot, dffn_low, pre_grad_low,
    )
    ys = bits_of(sizes)[1]
    groups = [
        tuple(cross_terms) + (True, (0, 1, 2), 512),
        tuple(out_terms) + (False, (0, 1, 2), 256),
        tuple(dec_terms) + (False, (ys, ys, ys), 256),
    ]
    gradients = [
        (ffn_turned, epre_low, 512, (0, 1, 2, 0, 2, 3)),
        (attended_turned, emid_low, 256, (0, 1, 2)),
        (attn_turned, None, 256, (0, 1, 2, 0, 1, 3, 0, 1, 2)),
    ]
    roomy = D // (pb * pa) % 8 == 0
    if not roomy:
        del gradients[0]
        in_terms = near(weight_grad(table, ffn_turned, [epre_low], pb, pa, 512, 2))
    enc_in_grad, small, *summed = last_part(
        sizes, orders, groups, gradients, lengths, enc_queries, enc_keys, enc_values, enc_attended, enc_att_grad, enc_lse, base,
        enc_in, grad_enc_mid, gains, enc_query, enc_key, enc_value, dec_fold,
        (ffn_gain_grad, final_gain_grad, dec_gain_self_grad, dec_gain_cross_grad, dec_gain_ffn_grad),
    )
    if not roomy:
        summed[3:3] = exchange_only(sizes, orders, [tuple(in_terms) + (True, (0, 1, 2), 1024)])
    cross_terms, ff_out_term, dec_sum, ff_in_term, output_term, attn_terms = summed
    ends = finish(pb, pa, small, dec_sum, enc_table, dec_table, dec_hidden.shape[1])
    gain_grads, (enc_bias_grad, dec_bias_grad), got = ends[:6], ends[6:8], ends[8:]

    return (
        enc_out, dec_out, enc_in_grad, dec_in_grad,
        gain_grads[0], attn_terms[:, :D], attn_terms[:, D : 2 * D], attn_terms[:, 2 * D :], output_term, enc_bias_grad,
        gain_grads[1], ff_in_term, ff_out_term, gain_grads[2], cross_terms[:, :D], cross_terms[:, D:],
        gain_grads[3], got[0], got[1], got[2], got[3], dec_bias_grad, gain_grads[4], got[4], got[5], gain_grads[5], got[7], got[6],
    )


def solution(mesh):
    pb, pa = mesh.shape["pb"], mesh.shape["pa"]
    rows = P(("pb", "pa"), None)
    flat = P(("pb", "pa"))
    dec = P("pb", None)
    return jax.shard_map(
        functools.partial(local, pb, pa),
        mesh=mesh,
        in_specs=(rows, dec, flat, flat) + (P(),) * 24 + (rows, dec),
        out_specs=(rows, dec, rows, dec)
        + (flat, rows, rows, rows, rows, flat, flat, rows, rows, flat, rows, rows)
        + (flat, rows, rows, rows, rows, flat, flat, rows, rows, flat, rows, rows),
        check_vma=False,
    )
```

```python
import functools
import math

import jax
import jax.numpy as jnp
import numpy as np
from jax import lax
from jax.experimental import pallas as pl
from jax.experimental.pallas import tpu as pltpu
from jax.sharding import PartitionSpec as P

D = 768
HEADS = 12
HEAD = 64
BUCKETS = 32
PL = 512
ANS = 24

far_distance = 128
epsilon = 1e-06
highest = lax.Precision.HIGHEST


def bucket_of(offset, bidirectional):
    if bidirectional:
        halves = BUCKETS // 2
        base_bucket = halves if offset > 0 else 0
        distance = abs(offset)
    else:
        halves = BUCKETS
        base_bucket = 0
        distance = max(-offset, 0)
    exact_count = halves // 2
    if distance < exact_count:
        return base_bucket + distance
    scaled = (
        math.log(distance / exact_count)
        / math.log(far_distance / exact_count)
        * (halves - exact_count)
    )
    return base_bucket + min(exact_count + int(scaled), halves - 1)


def to_low(values):
    return values.astype(jnp.bfloat16)


def product_tn(left, right):
    return lax.dot_general(
        left, right, (((0,), (0,)), ((), ())), preferred_element_type=jnp.float32
    )


STRIP = 128
WIDE = 1024


def strip_table():
    table = np.zeros((WIDE, BUCKETS), np.float32)
    for place in range(WIDE):
        if place < PL + STRIP * 3:
            offset = PL - STRIP - place
        else:
            offset = PL - STRIP + WIDE - place
        if abs(offset) < PL:
            table[place, bucket_of(offset, True)] = 1.0
    return table


def nn(left, right):
    return lax.dot_general(left, right, (((1,), (0,)), ((), ())), preferred_element_type=jnp.float32)


def head_lanes(values, head):
    lane = lax.broadcasted_iota(jnp.int32, values.shape, 1)
    keep = lane < HEAD if head == 0 else lane >= HEAD
    return jnp.where(keep, values, jnp.zeros_like(values))


def key_mask(length):
    place = lax.broadcasted_iota(jnp.int32, (PL, 1), 0)
    return jnp.where(place < length, 0.0, -1e9)


def build_strip(base_ref, strip_ref):
    for head in range(2):
        row = base_ref[0, head : head + 1, :]
        spread = jnp.broadcast_to(row, (STRIP, WIDE))
        strip_ref[head] = pltpu.roll(spread, 0, 1, stride=1, stride_axis=0)


def attn_forward_kernel(lengths_ref, q_ref, k_ref, v_ref, bias_ref, table_ref, out_ref, turned_ref, lse_ref, base_ref, rows_ref, strip_ref, score_ref):
    passage = pl.program_id(1)

    @pl.when((passage == 0) & (pl.program_id(0) == 0))
    def _():
        every = nn(bias_ref[...], table_ref[...])
        for pair in range(HEADS // 2):
            rows_ref[pair] = every[2 * pair : 2 * pair + 2]

    base_ref[...] = rows_ref[pl.ds(pl.program_id(0), 1)]

    @pl.when(passage == 0)
    def _():
        build_strip(base_ref, strip_ref)

    mask = key_mask(lengths_ref[passage])
    q_t = q_ref[...].T
    v_t = v_ref[...].T
    k = k_ref[...]
    blocks = PL // STRIP
    for head in range(2):
        k_head = head_lanes(k, head)
        top = None
        for b in range(blocks):
            rows = slice(b * STRIP, (b + 1) * STRIP)
            start = PL - STRIP - b * STRIP
            s = nn(k_head[rows], q_t) + strip_ref[head, :, start : start + PL] + mask[rows]
            score_ref[head, rows, :] = s
            here = jnp.max(s, axis=0, keepdims=True)
            top = here if top is None else jnp.maximum(top, here)
        total = None
        acc = None
        for b in range(blocks):
            rows = slice(b * STRIP, (b + 1) * STRIP)
            e = jnp.exp(score_ref[head, rows, :] - top)
            here = jnp.sum(e, axis=0, keepdims=True)
            total = here if total is None else total + here
            part = nn(v_t[head * HEAD : (head + 1) * HEAD, rows], to_low(e))
            acc = part if acc is None else acc + part
        turned_ref[head * HEAD : (head + 1) * HEAD, :] = to_low(acc * (1.0 / total))
        lse_ref[0, 0, head : head + 1, :] = top + jnp.log(total)
    out_ref[...] = turned_ref[...].T


def attn_forward(lengths, q, k, v, bias, table):
    passages = lengths.shape[0]
    pairs = HEADS // 2
    tile = pl.BlockSpec((PL, 128), lambda h, p, *_: (p, h))
    return pl.pallas_call(
        attn_forward_kernel,
        grid_spec=pltpu.PrefetchScalarGridSpec(
            num_scalar_prefetch=1,
            grid=(pairs, passages),
            in_specs=[tile, tile, tile, pl.BlockSpec(bias.shape, lambda h, p, *_: (0, 0)), pl.BlockSpec(table.shape, lambda h, p, *_: (0, 0))],
            out_specs=[
                tile,
                pl.BlockSpec((128, PL), lambda h, p, *_: (h, p)),
                pl.BlockSpec((1, 1, 2, PL), lambda h, p, *_: (h, p, 0, 0)),
                pl.BlockSpec((1, 2, WIDE), lambda h, p, *_: (h, 0, 0)),
            ],
            scratch_shapes=[
                pltpu.VMEM((pairs, 2, WIDE), jnp.float32),
                pltpu.VMEM((2, STRIP, WIDE), jnp.float32),
                pltpu.VMEM((2, PL, PL), jnp.float32),
            ],
        ),
        out_shape=[
            jax.ShapeDtypeStruct((passages * PL, D), jnp.bfloat16),
            jax.ShapeDtypeStruct((D, passages * PL), jnp.bfloat16),
            jax.ShapeDtypeStruct((pairs, passages, 2, PL), jnp.float32),
            jax.ShapeDtypeStruct((pairs, 2, WIDE), jnp.float32),
        ],
        compiler_params=pltpu.CompilerParams(vmem_limit_bytes=62 * 2**20),
        name="enc_attention",
    )(lengths, q, k, v, bias, table)


def attn_backward_kernel(
    beside, passage, passages, lengths_ref, q_ref, k_ref, v_ref, o_ref, do_ref, lse_ref, base_ref,
    dq_ref, dk_ref, dv_ref, fold_ref,
    strip_ref, gather_ref, dqT_ref,
):
    @pl.when(passage == 0)
    def _():
        build_strip(base_ref, strip_ref)
        gather_ref[...] = jnp.zeros_like(gather_ref)

    mask = key_mask(lengths_ref[passage])
    q = q_ref[...]
    k = k_ref[...]
    v = v_ref[...]
    do = do_ref[...]
    q_t = q.T
    k_t = k.T
    do_t = do.T
    o_t = o_ref[...].T
    weighed = do_t.astype(jnp.float32) * o_t.astype(jnp.float32)
    blocks = PL // STRIP
    lane = lax.broadcasted_iota(jnp.int32, (STRIP, 128), 1)
    first = lane < HEAD
    dks = []
    dvs = []
    for head in range(2):
        beside(head)
        heads = slice(head * HEAD, (head + 1) * HEAD)
        delta = jnp.sum(weighed[heads], axis=0, keepdims=True)
        lse = lse_ref[0, 0, head : head + 1, :]
        k_head = head_lanes(k, head)
        v_head = head_lanes(v, head)
        acc = None
        for b in range(blocks):
            rows = slice(b * STRIP, (b + 1) * STRIP)
            start = PL - STRIP - b * STRIP
            s = nn(k_head[rows], q_t) + strip_ref[head, :, start : start + PL] + mask[rows]
            p = jnp.exp(s - lse)
            dp = nn(v_head[rows], do_t)
            ds = p * (dp - delta)
            gather_ref[head, :, start : start + PL] += ds
            ds_low = to_low(ds)
            dv_part = nn(to_low(p), do)
            dk_part = nn(ds_low, q)
            if head == 0:
                dvs.append(dv_part)
                dks.append(dk_part)
            else:
                dv_ref[rows, :] = to_low(jnp.where(first, dvs[b], dv_part))
                dk_ref[rows, :] = to_low(jnp.where(first, dks[b], dk_part))
            part = nn(k_t[heads, rows], ds_low)
            acc = part if acc is None else acc + part
        dqT_ref[heads, :] = to_low(0.125 * acc)
    dq_ref[...] = dqT_ref[...].T

    @pl.when(passage == passages - 1)
    def _():
        row = lax.broadcasted_iota(jnp.int32, (8, WIDE), 0)
        for head in range(2):
            total = gather_ref[head, 0:8, :]
            for group in range(1, STRIP // 8):
                total = total + pltpu.roll(gather_ref[head, group * 8 : group * 8 + 8, :], WIDE - group * 8, 1)
            for bit in (1, 2, 4):
                total = jnp.where((row // bit) % 2 == 1, pltpu.roll(total, WIDE - bit, 1), total)
            fold_ref[0, head : head + 1, :] = jnp.sum(total, axis=0, keepdims=True)


MIB = 2**20


def nt(left, right):
    return lax.dot_general(left, right, (((1,), (1,)), ((), ())), preferred_element_type=jnp.float32)


def rms(values, gain):
    scale = lax.rsqrt(jnp.mean(values * values, axis=-1, keepdims=True) + epsilon)
    return values * scale * gain, scale


def rms_back(values, scale, gain, grad):
    scaled = grad * gain
    gain_grad = jnp.sum(grad * values * scale, axis=0, keepdims=True)
    inner = jnp.mean(scaled * values, axis=-1, keepdims=True)
    return scaled * scale - values * (scale * scale * scale) * inner, gain_grad


def gelu_both(v):
    c = math.sqrt(2.0 / math.pi)
    square = v * v
    t = jnp.tanh(v * (c + (c * 0.044715) * square))
    half = 0.5 + 0.5 * t
    slope = half + (half * (1.0 - t)) * v * (c + (3.0 * 0.044715 * c) * square)
    return v * half, slope


GAIN_ATTN, GAIN_FFN, GAIN_FINAL, GAIN_SELF, GAIN_CROSS, GAIN_DFFN = range(6)


def gain_of(gains_ref, which):
    return gains_ref[which : which + 1, :]


def whole(array):
    return pl.BlockSpec(array.shape, lambda *_: (0,) * array.ndim)


def rows_of(tile, width):
    return pl.BlockSpec((tile, width), lambda i: (i, 0))


def sds(shape, kind):
    return jax.ShapeDtypeStruct(shape, kind)


def params(mib):
    return pltpu.CompilerParams(vmem_limit_bytes=mib * MIB)


def qkv_kernel(x_ref, gains_ref, wq_ref, wk_ref, wv_ref, turned_ref, q_ref, k_ref, v_ref):
    normed, _ = rms(x_ref[...].astype(jnp.float32), gain_of(gains_ref, GAIN_ATTN))
    low = to_low(normed)
    turned_ref[...] = low.T
    q_ref[...] = to_low(0.125 * to_low(nn(low, wq_ref[...])).astype(jnp.float32))
    k_ref[...] = to_low(nn(low, wk_ref[...]))
    v_ref[...] = to_low(nn(low, wv_ref[...]))


def qkv_forward(x, gains, wq, wk, wv):
    tokens = x.shape[0]
    tile = 256
    big = sds((tokens, D), jnp.bfloat16)
    return pl.pallas_call(
        qkv_kernel,
        grid=(tokens // tile,),
        in_specs=[rows_of(tile, D)] + [whole(a) for a in (gains, wq, wk, wv)],
        out_specs=[pl.BlockSpec((D, tile), lambda i: (0, i))] + [rows_of(tile, D)] * 3,
        out_shape=[sds((D, tokens), jnp.bfloat16)] + [big] * 3,
        compiler_params=params(62),
        name="enc_qkv",
    )(x, gains, wq, wk, wv)


def post_kernel(
    x_ref, att_ref, gains_ref, wo_ref, win_ref, wout_ref, wck_ref, wcv_ref,
    mid_ref, ffn_turned_ref, hidden_turned_ref, slope_ref, y_ref, out_ref, final_turned_ref, ck_ref, cv_ref,
):
    mid = x_ref[...].astype(jnp.float32) + nn(att_ref[...], wo_ref[...])
    mid_ref[...] = mid
    normed, _ = rms(mid, gain_of(gains_ref, GAIN_FFN))
    low = to_low(normed)
    ffn_turned_ref[...] = low.T
    y = mid
    width = 768
    for c in range(win_ref.shape[1] // width):
        cols = slice(c * width, (c + 1) * width)
        hidden, slope = gelu_both(nn(low, win_ref[:, cols]))
        hidden = to_low(hidden)
        hidden_turned_ref[cols, :] = hidden.T
        slope_ref[:, cols] = to_low(slope)
        y = y + nn(hidden, wout_ref[cols, :])
    y_ref[...] = y
    out_ref[...] = to_low(y)
    final, _ = rms(y, gain_of(gains_ref, GAIN_FINAL))
    final = to_low(final)
    final_turned_ref[...] = final.T
    ck_ref[...] = to_low(nn(final, wck_ref[...]))
    cv_ref[...] = to_low(nn(final, wcv_ref[...]))


def post_forward(x, att, gains, wo, win, wout, wck, wcv):
    tokens = x.shape[0]
    tile = 256
    ff = win.shape[1]
    low = sds((tokens, D), jnp.bfloat16)
    wide = sds((tokens, ff), jnp.bfloat16)
    full = sds((tokens, D), jnp.float32)
    d = rows_of(tile, D)
    f = rows_of(tile, ff)
    turned = pl.BlockSpec((D, tile), lambda i: (0, i))
    flat = sds((D, tokens), jnp.bfloat16)
    return pl.pallas_call(
        post_kernel,
        grid=(tokens // tile,),
        in_specs=[d, d] + [whole(a) for a in (gains, wo, win, wout, wck, wcv)],
        out_specs=[d, turned, pl.BlockSpec((ff, tile), lambda i: (0, i)), f, d, d, turned, d, d],
        out_shape=[full, flat, sds((ff, tokens), jnp.bfloat16), wide, full, low, flat, low, low],
        compiler_params=params(62),
        name="enc_post",
    )(x, att, gains, wo, win, wout, wck, wcv)


def back_kernel(
    gkv_ref, y_ref, mid_ref, slope_ref, cot_ref, gains_ref,
    wck_ref, wcv_ref, wout_ref, win_ref, wo_ref,
    eout_ref, epre_ref, emid_ref, grad_mid_ref, att_grad_ref, gain_final_grad_ref, gain_ffn_grad_ref,
):

    @pl.when(pl.program_id(0) == 0)
    def _():
        gain_final_grad_ref[...] = jnp.zeros_like(gain_final_grad_ref)
        gain_ffn_grad_ref[...] = jnp.zeros_like(gain_ffn_grad_ref)

    y = y_ref[...]
    scale = lax.rsqrt(jnp.mean(y * y, axis=-1, keepdims=True) + epsilon)
    final_back = nt(gkv_ref[0], wck_ref[...]) + nt(gkv_ref[1], wcv_ref[...])
    back, gain_grad = rms_back(y, scale, gain_of(gains_ref, GAIN_FINAL), final_back)
    gain_final_grad_ref[...] += gain_grad
    grad_y = cot_ref[...].astype(jnp.float32) + back
    eout = to_low(grad_y)
    eout_ref[...] = eout
    width = 768
    acc = None
    for c in range(win_ref.shape[1] // width):
        cols = slice(c * width, (c + 1) * width)
        epre = to_low(slope_ref[:, cols].astype(jnp.float32) * nt(eout, wout_ref[cols, :]))
        epre_ref[:, cols] = epre
        part = nt(epre, win_ref[:, cols])
        acc = part if acc is None else acc + part
    mid = mid_ref[...]
    scale = lax.rsqrt(jnp.mean(mid * mid, axis=-1, keepdims=True) + epsilon)
    back, gain_grad = rms_back(mid, scale, gain_of(gains_ref, GAIN_FFN), acc)
    gain_ffn_grad_ref[...] += gain_grad
    grad_mid = grad_y + back
    grad_mid_ref[...] = grad_mid
    emid = to_low(grad_mid)
    emid_ref[...] = emid
    att_grad_ref[...] = to_low(nt(emid, wo_ref[...]))


def qkv_back_kernel(opening, dq_ref, dk_ref, dv_ref, x_ref, grad_mid_ref, gains_ref, wq_ref, wk_ref, wv_ref, out_ref, gain_grad_ref):
    @pl.when(opening)
    def _():
        gain_grad_ref[...] = jnp.zeros_like(gain_grad_ref)

    x = x_ref[...].astype(jnp.float32)
    scale = lax.rsqrt(jnp.mean(x * x, axis=-1, keepdims=True) + epsilon)
    grad = nt(dq_ref[...], wq_ref[...]) + nt(dk_ref[...], wk_ref[...]) + nt(dv_ref[...], wv_ref[...])
    back, gain_grad = rms_back(x, scale, gain_of(gains_ref, GAIN_ATTN), grad)
    gain_grad_ref[...] += gain_grad
    out_ref[...] = grad_mid_ref[...] + back


def weight_grad_kernel(rows, pb, pa, tiles, chains, table_ref, turned_ref, *refs):
    rights = refs[: len(tiles)]
    keep_ref, send_ref = refs[-2:]
    step = pl.program_id(0)
    core = table_ref[0, 0]
    chain = chains[0]
    for place, c in enumerate(chains):
        chain = jnp.where(step == place, c, chain)
    half_rows = pa * rows

    def work(right):
        for y in range(pb // 2):
            low_part = nn(turned_ref[2 * y * half_rows : (2 * y + 1) * half_rows, :], right)
            high_part = nn(turned_ref[(2 * y + 1) * half_rows : (2 * y + 2) * half_rows, :], right)
            mine = jnp.where(core == 0, low_part, high_part)
            other = jnp.where(core == 0, high_part, low_part)
            for a in range(pa):
                slot = table_ref[chain + 1, y * pa + a]
                keep_ref[slot] = mine[a * rows : (a + 1) * rows]
                send_ref[slot] = other[a * rows : (a + 1) * rows]

    first = 0
    for right_ref, count in zip(rights, tiles):
        if len(tiles) == 1:
            work(right_ref[...])
        else:

            @pl.when((step >= first) & (step < first + count))
            def _(right_ref=right_ref):
                work(right_ref[...] if len(right_ref.shape) == 2 else right_ref[0])

        first += count


def weight_grad(table, turned, rights, pb, pa, width, chains):
    height, tokens = turned.shape
    rows = height // (pb * pa)
    arrays = [r[0] if isinstance(r, tuple) else r for r in rights]
    tiles = [a.shape[-1] // width for a in arrays]
    total = sum(tiles)
    firsts = np.cumsum([0] + tiles)[:-1]

    def spec(right, first, count):
        def column(i):
            return jnp.clip(i - int(first), 0, count - 1)

        if isinstance(right, tuple):
            return pl.BlockSpec((1, tokens, width), lambda i, *_: (right[1], 0, column(i)))
        return pl.BlockSpec((tokens, width), lambda i, *_: (0, column(i)))

    half = pb * pa // 2
    out = pl.BlockSpec((half, rows, width), lambda i, *_: (0, 0, i))
    shape = sds((half, rows, total * width), jnp.float32)
    return pl.pallas_call(
        functools.partial(weight_grad_kernel, rows, pb, pa, tiles, chains),
        grid_spec=pltpu.PrefetchScalarGridSpec(
            num_scalar_prefetch=1,
            grid=(total,),
            in_specs=[pl.BlockSpec((height, tokens), lambda i, *_: (0, 0))]
            + [spec(r, f, c) for r, f, c in zip(rights, firsts, tiles)],
            out_specs=[out, out],
        ),
        out_shape=[shape, shape],
        compiler_params=params(62),
        name="weight_grad",
    )(table, turned, *arrays)


def gains_kernel(*refs):
    for row, ref in enumerate(refs[:-1]):
        refs[-1][row] = ref[...].astype(jnp.float32)


def gains_together(*gains):
    vmem = pl.BlockSpec(memory_space=pltpu.VMEM)
    return pl.pallas_call(
        gains_kernel,
        in_specs=[vmem] * len(gains),
        out_specs=vmem,
        out_shape=sds((len(gains), D), jnp.float32),
        name="gains",
    )(*gains)


PACK = 896


def permitted_mask(question_ref, length_ref, answer_rows, passages):
    row = lax.broadcasted_iota(jnp.int32, (answer_rows, PL), 0)
    place = lax.broadcasted_iota(jnp.int32, (answer_rows, PL), 1)
    whose = row // ANS
    return jnp.concatenate(
        [(whose == question_ref[p]) & (place < length_ref[p]) for p in range(passages)], axis=1
    )


def cross_part_kernel(question_ref, length_ref, q_ref, ck_ref, cv_ref, part_ref):
    rows = q_ref.shape[0]
    mask = permitted_mask(question_ref, length_ref, rows, ck_ref.shape[0] // PL)
    lane = lax.broadcasted_iota(jnp.int32, (rows, 128), 1)
    stats = jnp.zeros((rows, 128), jnp.float32)
    for pair in range(HEADS // 2):
        cols = slice(pair * 128, (pair + 1) * 128)
        q = q_ref[:, cols]
        k = ck_ref[:, cols]
        v = cv_ref[:, cols]
        outs = []
        for head in range(2):
            s = jnp.where(mask, 0.125 * nt(head_lanes(q, head), k), -1e9)
            top = jnp.max(s, axis=1, keepdims=True)
            e = jnp.exp(s - top)
            total = jnp.sum(e, axis=1, keepdims=True)
            outs.append(nn(to_low(e), v))
            place = 2 * pair + head
            stats = jnp.where(lane == place, top, jnp.where(lane == HEADS + place, total, stats))
        part_ref[:, cols] = jnp.where(lane < HEAD, outs[0], outs[1])
    part_ref[:, D:] = stats


def cross_part(question_of, lengths, q, ck, cv):
    vmem = pl.BlockSpec(memory_space=pltpu.VMEM)
    smem = pl.BlockSpec(memory_space=pltpu.SMEM)
    return pl.pallas_call(
        cross_part_kernel,
        in_specs=[smem, smem, vmem, vmem, vmem],
        out_specs=vmem,
        out_shape=sds((q.shape[0], PACK), jnp.float32),
        compiler_params=params(40),
        name="cross_part",
    )(question_of, lengths, q, ck, cv)


def over_heads(stats, rows):
    lane = lax.broadcasted_iota(jnp.int32, (rows, 128), 1)
    return jnp.concatenate(
        [jnp.where(lane < HEAD, stats[:, 2 * g : 2 * g + 1], stats[:, 2 * g + 1 : 2 * g + 2]) for g in range(HEADS // 2)],
        axis=1,
    )


def merge_kernel(pa, part_ref, out_ref, recv_ref, mine_ref, send_sem, recv_sem, send2_sem, recv2_sem):
    me = lax.axis_index("pa")
    rows = part_ref.shape[1]
    barrier = pltpu.get_barrier_semaphore()
    for off in range(1, pa):
        pl.semaphore_signal(barrier, inc=1, device_id={"pa": lax.rem(me + off, pa)}, device_id_type=pl.DeviceIdType.MESH)
    pl.semaphore_wait(barrier, pa - 1)

    def first(off):
        peer = lax.rem(me + off, pa)
        return pltpu.make_async_remote_copy(
            src_ref=part_ref.at[peer], dst_ref=recv_ref.at[off], send_sem=send_sem.at[off], recv_sem=recv_sem.at[off],
            device_id={"pa": peer}, device_id_type=pl.DeviceIdType.MESH,
        )

    def second(off):
        peer = lax.rem(me + off, pa)
        return pltpu.make_async_remote_copy(
            src_ref=mine_ref, dst_ref=out_ref.at[me], send_sem=send2_sem.at[off], recv_sem=recv2_sem.at[off],
            device_id={"pa": peer}, device_id_type=pl.DeviceIdType.MESH,
        )

    for off in range(1, pa):
        first(off).start()
    recv_ref[0] = part_ref[me]
    for off in range(1, pa):
        first(off).wait()
    tops = [recv_ref[i, :, D : D + 128][:, :HEADS] for i in range(pa)]
    top = tops[0]
    for t in tops[1:]:
        top = jnp.maximum(top, t)
    total = jnp.zeros((rows, HEADS), jnp.float32)
    acc = jnp.zeros((rows, D), jnp.float32)
    for i in range(pa):
        w = jnp.exp(tops[i] - top)
        total = total + w * recv_ref[i, :, D : D + 128][:, HEADS : 2 * HEADS]
        acc = acc + over_heads(w, rows) * recv_ref[i, :, :D]
    mine_ref[:, :D] = acc / over_heads(total, rows)
    lse = top + jnp.log(total)
    mine_ref[:, D:] = jnp.concatenate([lse, jnp.zeros((rows, 128 - HEADS), jnp.float32)], axis=1)
    for off in range(1, pa):
        second(off).start()
    out_ref[me] = mine_ref[...]
    for off in range(1, pa):
        second(off).wait()


def merge(part, pa):
    answer_rows = part.shape[0]
    rows = answer_rows // pa
    block = (pa, rows, PACK)
    vmem = pl.BlockSpec(memory_space=pltpu.VMEM)
    out = pl.pallas_call(
        functools.partial(merge_kernel, pa),
        in_specs=[vmem],
        out_specs=vmem,
        out_shape=sds(block, jnp.float32),
        scratch_shapes=[
            pltpu.VMEM(block, jnp.float32),
            pltpu.VMEM((rows, PACK), jnp.float32),
            pltpu.SemaphoreType.DMA((pa,)),
            pltpu.SemaphoreType.DMA((pa,)),
            pltpu.SemaphoreType.DMA((pa,)),
            pltpu.SemaphoreType.DMA((pa,)),
        ],
        compiler_params=pltpu.CompilerParams(collective_id=0, has_side_effects=True, vmem_limit_bytes=16 * MIB),
        name="cross_merge",
    )(part.reshape(block))
    return out.reshape(answer_rows, PACK)


def cross_back_kernel(question_ref, length_ref, q_ref, ck_ref, cv_ref, grad_ref, att_ref, lse_ref, gq_ref, gkv_ref):
    rows = q_ref.shape[0]
    mask = permitted_mask(question_ref, length_ref, rows, ck_ref.shape[0] // PL)
    lane = lax.broadcasted_iota(jnp.int32, (rows, 128), 1)
    for pair in range(HEADS // 2):
        cols = slice(pair * 128, (pair + 1) * 128)
        q = q_ref[:, cols]
        k = ck_ref[:, cols]
        v = cv_ref[:, cols]
        g = grad_ref[:, cols]
        weighed = g.astype(jnp.float32) * att_ref[:, cols]
        gqs = []
        scores = []
        probs = []
        for head in range(2):
            place = 2 * pair + head
            s = jnp.where(mask, 0.125 * nt(head_lanes(q, head), k), -1e9)
            p = jnp.exp(s - lse_ref[:, place : place + 1])
            dp = nt(head_lanes(g, head), v)
            delta = jnp.sum(head_lanes(weighed, head), axis=1, keepdims=True)
            ds = to_low(p * (dp - delta))
            gqs.append(nn(ds, k))
            scores.append(ds)
            probs.append(to_low(p))
        gq_ref[:, cols] = 0.125 * jnp.where(lane < HEAD, gqs[0], gqs[1])
        both_q = jnp.concatenate([head_lanes(q, 0), head_lanes(q, 1)], axis=0)
        both_g = jnp.concatenate([head_lanes(g, 0), head_lanes(g, 1)], axis=0)
        gkv_ref[0, :, cols] = to_low(0.125 * product_tn(jnp.concatenate(scores, axis=0), both_q))
        gkv_ref[1, :, cols] = to_low(product_tn(jnp.concatenate(probs, axis=0), both_g))


def cross_back(question_of, lengths, q, ck, cv, grad, att, lse):
    vmem = pl.BlockSpec(memory_space=pltpu.VMEM)
    smem = pl.BlockSpec(memory_space=pltpu.SMEM)
    return pl.pallas_call(
        cross_back_kernel,
        in_specs=[smem, smem] + [vmem] * 6,
        out_specs=[vmem, vmem],
        out_shape=[sds((q.shape[0], D), jnp.float32), sds((2, ck.shape[0], D), jnp.bfloat16)],
        compiler_params=params(40),
        name="cross_back",
    )(question_of, lengths, q, ck, cv, grad, att, lse)


def causal_row(length):
    table = np.zeros((128, BUCKETS), np.float32)
    for back in range(length):
        table[-back % 128, bucket_of(-back, False)] = 1.0
    return table


def in_three(values):
    high = to_low(values)
    rest = values - high.astype(jnp.float32)
    middle = to_low(rest)
    return high, middle, to_low(rest - middle.astype(jnp.float32))


def dec_pre_kernel(
    x_ref, gains_ref, bias_ref, table_ref, wq_ref, wk_ref, wv_ref, wo_ref, wcq_ref,
    low_ref, q_ref, k_ref, v_ref, probs_ref, att_ref, mid_ref, cross_low_ref, cross_q_ref,
):
    rows = x_ref.shape[0]
    base = nn(bias_ref[...], table_ref[...])
    x = x_ref[...].astype(jnp.float32)
    normed, _ = rms(x, gain_of(gains_ref, GAIN_SELF))
    low = to_low(normed)
    low_ref[...] = low
    q = to_low(0.125 * to_low(nn(low, wq_ref[...])).astype(jnp.float32))
    k = to_low(nn(low, wk_ref[...]))
    v = to_low(nn(low, wv_ref[...]))
    q_ref[...] = q
    k_ref[...] = k
    v_ref[...] = v
    i = lax.broadcasted_iota(jnp.int32, (rows, rows), 0)
    j = lax.broadcasted_iota(jnp.int32, (rows, rows), 1)
    mask = (j <= i) & (i // ANS == j // ANS)
    lane = lax.broadcasted_iota(jnp.int32, (rows, 128), 1)
    for pair in range(HEADS // 2):
        cols = slice(pair * 128, (pair + 1) * 128)
        outs = []
        for half in range(2):
            head = 2 * pair + half
            spread = jnp.broadcast_to(base[head : head + 1, :], (rows, 128))
            bias = pltpu.roll(spread, 0, 1, stride=1, stride_axis=0)[:, :rows]
            s = jnp.where(mask, nt(head_lanes(q[:, cols], half), k[:, cols]) + bias, -1e9)
            e = jnp.exp(s - jnp.max(s, axis=1, keepdims=True))
            p = e / jnp.sum(e, axis=1, keepdims=True)
            probs_ref[head] = p
            outs.append(nn(to_low(p), v[:, cols]))
        att_ref[:, cols] = to_low(jnp.where(lane < HEAD, outs[0], outs[1]))
    mid = x + nn(att_ref[...], wo_ref[...])
    mid_ref[...] = mid
    normed, _ = rms(mid, gain_of(gains_ref, GAIN_CROSS))
    low = to_low(normed)
    cross_low_ref[...] = low
    cross_q_ref[...] = to_low(nn(low, wcq_ref[...]))


def in_vmem(kernel, outs, name, *args, smem=0):
    vmem = pl.BlockSpec(memory_space=pltpu.VMEM)
    return pl.pallas_call(
        kernel,
        in_specs=[pl.BlockSpec(memory_space=pltpu.SMEM)] * smem + [vmem] * (len(args) - smem),
        out_specs=[vmem] * len(outs),
        out_shape=outs,
        compiler_params=params(62),
        name=name,
    )(*args)


def dec_pre(x, gains, bias, table, wq, wk, wv, wo, wcq):
    rows = x.shape[0]
    low = sds((rows, D), jnp.bfloat16)
    full = sds((rows, D), jnp.float32)
    outs = [low, low, low, low, sds((HEADS, rows, rows), jnp.float32), low, full, low, low]
    return in_vmem(dec_pre_kernel, outs, "dec_pre", x, gains, bias, table, wq, wk, wv, wo, wcq)


def dec_mid_kernel(
    merged_ref, mid_ref, cot_ref, gains_ref, wco_ref, win_ref, wout_ref,
    out_ref, low_ref, hidden_ref, pre_grad_ref, after_low_ref, grad_after_ref, att_grad_ref, gain_grad_ref, slope_ref,
):
    rows = mid_ref.shape[0]
    three = nn(jnp.concatenate(in_three(merged_ref[:, :D]), axis=0), wco_ref[...])
    after = mid_ref[...] + (three[:rows] + three[rows : 2 * rows] + three[2 * rows :])
    normed, scale = rms(after, gain_of(gains_ref, GAIN_DFFN))
    low = to_low(normed)
    low_ref[...] = low
    y = after
    width = 768
    chunks = [slice(c * width, (c + 1) * width) for c in range(win_ref.shape[1] // width)]
    for cols in chunks:
        hidden, slope = gelu_both(nn(low, win_ref[:, cols]))
        hidden = to_low(hidden)
        hidden_ref[:, cols] = hidden
        slope_ref[:, cols] = slope
        y = y + nn(hidden, wout_ref[cols, :])
    out_ref[...] = to_low(y)
    cot = cot_ref[...]
    acc = None
    for cols in chunks:
        pre = to_low(slope_ref[:, cols] * nt(cot, wout_ref[cols, :]))
        pre_grad_ref[:, cols] = pre
        part = nt(pre, win_ref[:, cols])
        acc = part if acc is None else acc + part
    back, gain_grad = rms_back(after, scale, gain_of(gains_ref, GAIN_DFFN), acc)
    gain_grad_ref[...] = gain_grad
    grad_after = cot.astype(jnp.float32) + back
    grad_after_ref[...] = grad_after
    after_low = to_low(grad_after)
    after_low_ref[...] = after_low
    att_grad_ref[...] = to_low(nt(after_low, wco_ref[...]))


def dec_mid_call(merged, mid, cot, gain, wco, win, wout):
    rows = mid.shape[0]
    ff = win.shape[1]
    low = sds((rows, D), jnp.bfloat16)
    full = sds((rows, D), jnp.float32)
    wide = sds((rows, ff), jnp.bfloat16)
    outs = [low, low, wide, wide, low, full, low, sds((1, D), jnp.float32)]
    vmem = pl.BlockSpec(memory_space=pltpu.VMEM)
    return pl.pallas_call(
        dec_mid_kernel,
        in_specs=[vmem] * 7,
        out_specs=[vmem] * len(outs),
        out_shape=outs,
        scratch_shapes=[pltpu.VMEM((rows, ff), jnp.float32)],
        compiler_params=params(62),
        name="dec_mid",
    )(merged, mid, cot, gain, wco, win, wout)


def dec_post_kernel(
    gq_ref, grad_after_ref, mid_ref, x_ref, q_ref, k_ref, v_ref, probs_ref, gains_ref,
    wq_ref, wk_ref, wv_ref, wo_ref, wcq_ref, after_ref,
    mid_low_ref, dq_ref, dk_ref, dv_ref, out_ref, gain_self_grad_ref, gain_cross_grad_ref, fold_ref,
):
    rows = x_ref.shape[0]
    mid = mid_ref[...]
    scale = lax.rsqrt(jnp.mean(mid * mid, axis=-1, keepdims=True) + epsilon)
    three = nt(jnp.concatenate(in_three(gq_ref[...]), axis=0), wcq_ref[...])
    back, gain_grad = rms_back(mid, scale, gain_of(gains_ref, GAIN_CROSS), three[:rows] + three[rows : 2 * rows] + three[2 * rows :])
    gain_cross_grad_ref[...] = gain_grad
    grad_mid = grad_after_ref[...] + back
    mid_low = to_low(grad_mid)
    mid_low_ref[...] = mid_low
    att_grad = to_low(nt(mid_low, wo_ref[...]))
    lane = lax.broadcasted_iota(jnp.int32, (rows, 128), 1)
    row8 = lax.broadcasted_iota(jnp.int32, (8, 128), 0)
    for pair in range(HEADS // 2):
        cols = slice(pair * 128, (pair + 1) * 128)
        q = q_ref[:, cols]
        k = k_ref[:, cols]
        v = v_ref[:, cols]
        g = att_grad[:, cols]
        dqs = []
        scores = []
        probs = []
        for half in range(2):
            head = 2 * pair + half
            p = probs_ref[head]
            dp = nt(head_lanes(g, half), v)
            ds = p * (dp - jnp.sum(p * dp, axis=1, keepdims=True))
            wide = jnp.concatenate([ds, jnp.zeros((rows, 128 - rows), jnp.float32)], axis=1)
            total = wide[0:8]
            for group in range(1, rows // 8):
                total = total + pltpu.roll(wide[group * 8 : group * 8 + 8], 128 - group * 8, 1)
            for bit in (1, 2, 4):
                total = jnp.where((row8 // bit) % 2 == 1, pltpu.roll(total, 128 - bit, 1), total)
            fold_ref[head : head + 1, :] = jnp.sum(total, axis=0, keepdims=True)
            ds = to_low(ds)
            dqs.append(nn(ds, k))
            scores.append(ds)
            probs.append(to_low(p))
        dq_ref[:, cols] = to_low(0.125 * jnp.where(lane < HEAD, dqs[0], dqs[1]))
        both_q = jnp.concatenate([head_lanes(q, 0), head_lanes(q, 1)], axis=0)
        both_g = jnp.concatenate([head_lanes(g, 0), head_lanes(g, 1)], axis=0)
        dk_ref[:, cols] = to_low(product_tn(jnp.concatenate(scores, axis=0), both_q))
        dv_ref[:, cols] = to_low(product_tn(jnp.concatenate(probs, axis=0), both_g))
    x = x_ref[...].astype(jnp.float32)
    scale = lax.rsqrt(jnp.mean(x * x, axis=-1, keepdims=True) + epsilon)
    grad = nt(dq_ref[...], wq_ref[...]) + nt(dk_ref[...], wk_ref[...]) + nt(dv_ref[...], wv_ref[...])
    back, gain_grad = rms_back(x, scale, gain_of(gains_ref, GAIN_SELF), grad)
    gain_self_grad_ref[...] = gain_grad
    out_ref[...] = grad_mid + back


def dec_post(gq, grad_after, mid, x, q, k, v, probs, gains, wq, wk, wv, wo, wcq, after):
    rows = x.shape[0]
    low = sds((rows, D), jnp.bfloat16)
    gain = sds((1, D), jnp.float32)
    outs = [low, low, low, low, sds((rows, D), jnp.float32), gain, gain, sds((HEADS, 128), jnp.float32)]
    vmem = pl.BlockSpec(memory_space=pltpu.VMEM)
    return pl.pallas_call(
        dec_post_kernel,
        in_specs=[vmem] * 14 + [pl.BlockSpec(memory_space=pl.ANY)],
        out_specs=[vmem] * len(outs),
        out_shape=outs,
        compiler_params=params(62),
        name="dec_post",
    )(gq, grad_after, mid, x, q, k, v, probs, gains, wq, wk, wv, wo, wcq, after)


def dec_weight_kernel(
    pb, pa, place_ref, low_ref, dq_ref, dk_ref, dv_ref, att_ref, mid_low_ref, cross_low_ref, gq_ref, merged_ref, after_low_ref,
    hidden_ref, cot_ref, dffn_low_ref, pre_grad_ref, keep_ref, send_ref, turned_ref, wide_ref,
):
    shards = pb * pa
    column = place_ref[0]
    core = place_ref[1]
    rows = D // shards
    depth = low_ref.shape[0]

    def own(left, scratch):
        height = left.shape[1]
        here = height // shards
        span = left.shape[0]
        scratch[:, :span] = left.astype(jnp.float32).T
        cut = [scratch[pl.ds((b * pa + column) * here, here), :span] for b in range(pb)]
        return to_low(jnp.concatenate(cut, axis=0)), here

    first = 0

    def put(values, here):
        nonlocal first
        for y in range(pb // 2):
            low_part = values[2 * y * here : (2 * y + 1) * here]
            high_part = values[(2 * y + 1) * here : (2 * y + 2) * here]
            slot = place_ref[2 + y]
            keep_ref[slot, first : first + here, :] = jnp.where(core == 0, low_part, high_part)
            send_ref[slot, first : first + here, :] = jnp.where(core == 0, high_part, low_part)
        first += here

    left, here = own(low_ref[...], turned_ref)
    for right_ref in (dq_ref, dk_ref, dv_ref):
        put(nn(left, right_ref[...]), here)
    left, here = own(att_ref[...], turned_ref)
    put(nn(left, mid_low_ref[...]), here)
    left, here = own(cross_low_ref[...], turned_ref)
    a, b, c = in_three(gq_ref[...])
    put(nn(left, a) + nn(left, b) + nn(left, c), here)
    right = after_low_ref[...]
    a, b, c = (own(part, turned_ref)[0] for part in in_three(merged_ref[:, :D]))
    put(nn(a, right) + nn(b, right) + nn(c, right), here)
    left, wide = own(hidden_ref[...], wide_ref)
    put(nn(left, cot_ref[...]), wide)
    left, here = own(dffn_low_ref[...], turned_ref)
    for c in range(pre_grad_ref.shape[1] // D):
        put(nn(left, pre_grad_ref[:, c * D : (c + 1) * D]), here)


def dec_weight_grads(pb, pa, place, *args):
    rows, ff = args[-1].shape
    shards = pb * pa
    height = (6 * D + ff + ff) // shards
    vmem = pl.BlockSpec(memory_space=pltpu.VMEM)
    return pl.pallas_call(
        functools.partial(dec_weight_kernel, pb, pa),
        in_specs=[pl.BlockSpec(memory_space=pltpu.SMEM)] + [vmem] * len(args),
        out_specs=[vmem, vmem],
        out_shape=[sds((pb // 2, height, D), jnp.float32)] * 2,
        scratch_shapes=[pltpu.VMEM((D, rows), jnp.float32), pltpu.VMEM((ff, rows), jnp.float32)],
        compiler_params=params(62),
        name="dec_weight_grads",
    )(place, *args)


def finish_kernel(pb, pa, heights, cuts, small_ref, dec_ref, enc_table_ref, dec_table_ref, *refs):
    pieces, outs = refs[: len(cuts)], refs[len(cuts) :]
    shards = pb * pa
    shard = lax.axis_index("pb") * pa + lax.axis_index("pa")
    width = D // shards
    rolled = pltpu.roll(small_ref[0:8, :D], lax.rem(D - shard * width, D), 1)
    for r in range(6):
        outs[r][...] = rolled[r, :width]
    share = BUCKETS * HEADS // shards
    bucket = shard * share // HEADS
    head = lax.rem(shard * share, HEADS)

    def bias_grad(folded, table_ref, out_ref):
        table = table_ref[...]
        by_bucket = sum(nt(table, part) for part in in_three(folded))
        row = lax.broadcasted_iota(jnp.int32, by_bucket.shape, 0)
        mine = jnp.sum(jnp.where(row == bucket, by_bucket, 0.0), axis=0, keepdims=True)
        mine = jnp.concatenate([mine, jnp.zeros((1, 128 - HEADS), jnp.float32)], axis=1)
        mine = jnp.broadcast_to(mine, (8, 128))
        out_ref[...] = pltpu.roll(mine, lax.rem(128 - head, 128), 1)[0, :share]

    bias_grad(small_ref[8 : 8 + HEADS, :], enc_table_ref, outs[6])
    dec_fold = jnp.concatenate([small_ref[0:6, D : D + 128], small_ref[0:6, D + 128 : D + 256]], axis=0)
    bias_grad(dec_fold, dec_table_ref, outs[7])
    first = 0
    for number, height in enumerate(heights):
        outs[8 + number][...] = dec_ref[first : first + height]
        first += height
    at = 8 + len(heights)
    wide_ref = outs[at]
    for c in range(wide_ref.shape[1] // D):
        wide_ref[:, c * D : (c + 1) * D] = dec_ref[first : first + width]
        first += width
    for piece_ref, count in zip(pieces, cuts):
        columns = piece_ref.shape[1] // count
        for c in range(count):
            at += 1
            outs[at][...] = piece_ref[:, c * columns : (c + 1) * columns]


def finish(pb, pa, small, dec_sum, enc_table, dec_table, ff, pieces, cuts):
    shards = pb * pa
    width = D // shards
    share = BUCKETS * HEADS // shards
    heights = [width] * 6 + [ff // shards]
    outs = [sds((width,), jnp.float32)] * 6 + [sds((share,), jnp.float32)] * 2
    outs += [sds((h, D), jnp.float32) for h in heights] + [sds((width, ff), jnp.float32)]
    for piece, count in zip(pieces, cuts):
        outs += [sds((piece.shape[0], piece.shape[1] // count), jnp.float32)] * count
    vmem = pl.BlockSpec(memory_space=pltpu.VMEM)
    return pl.pallas_call(
        functools.partial(finish_kernel, pb, pa, heights, cuts),
        in_specs=[vmem] * (4 + len(pieces)),
        out_specs=[vmem] * len(outs),
        out_shape=outs,
        compiler_params=params(62),
        name="finish",
    )(small, dec_sum, enc_table, dec_table, *pieces)


def bits_of(mesh_sizes):
    pb, pa = mesh_sizes
    pb_bits = pb.bit_length() - 1
    pa_bits = pa.bit_length() - 1
    ys = [("pb", b) for b in range(1, pb_bits)]
    xs = [("pa", b) for b in range(pa_bits - 2)]
    zs = [("pa", b) for b in range(pa_bits - 2, pa_bits)]
    return xs, ys, zs


def orders_of(mesh_sizes):
    xs, ys, zs = bits_of(mesh_sizes)
    return (xs + ys + zs, ys + xs + zs, zs[:1] + xs + ys + zs[1:], zs[:1] + ys + xs + zs[1:])


def exchange_table(mesh_sizes, orders):
    pb, pa = mesh_sizes
    pb_me = lax.axis_index("pb")
    pa_me = lax.axis_index("pa")
    cells = np.arange(pb * pa // 2)
    pb_of = jnp.asarray(cells // pa * 2)
    pa_of = jnp.asarray(cells % pa)
    rows = [jnp.full((cells.size,), pb_me % 2, jnp.int32)]
    for order in orders:
        slot = jnp.zeros((cells.size,), jnp.int32)
        for axis, bit in order:
            far = ((pb_of if axis == "pb" else pa_of) >> bit) ^ ((pb_me if axis == "pb" else pa_me) >> bit)
            slot = slot * 2 + (far & 1).astype(jnp.int32)
        rows.append(slot)
    return jnp.stack(rows)


MESH = pl.DeviceIdType.MESH
LINK = 0.11
PAIR = 0.45
NEAR = ("pb", 0)


def link_of(step, sizes):
    xs, ys, zs = bits_of(sizes)
    if step == NEAR:
        return "core"
    if step in ys:
        return "y"
    if step in xs:
        return "x"
    return "z far" if step == zs[-1] else "z"


def link_time(step, megabytes, sizes, rate=None):
    if step == NEAR:
        return megabytes / PAIR
    return 2 * megabytes * (2 if step == bits_of(sizes)[2][-1] else 1) / (rate or LINK)


class Piece:
    def __init__(self, array, first, width, order, place=None, start=0.0, met=False):
        self.array, self.first, self.width, self.order = array, first, width, [NEAR] + list(order)
        self.place, self.start, self.met = place, start, met


DEPTH = 3


def block_of(piece, shapes):
    return tuple(shapes[piece.array][:2]) + (piece.width,)


def plan(pieces, shapes, sizes, rate=None):
    free, held, queues = {}, {}, {}
    pending = [(piece.start, i, "ready", 0) for i, piece in enumerate(pieces)]
    events = []

    def key_of(what, i, step):
        return ("load", block_of(pieces[i], shapes)) if what == "load" else link_of(pieces[i].order[step], sizes)

    def start(now, what, i, step, starts):
        key = key_of(what, i, step)
        if key != "core" and held.get(key, 0) >= (1 if what == "load" else DEPTH):
            queues.setdefault(key, []).append((what, i, step))
            return
        held[key] = held.get(key, 0) + 1
        half, rows = shapes[pieces[i].array][:2]
        megabytes = (half >> step) * rows * pieces[i].width * 4e-6
        begin = max(now, free.get(key, 0.0))
        if what == "load":
            free[key] = begin + 1.0 + megabytes * 0.8
            pending.append((free[key], i, "loaded", 0))
        else:
            free[key] = begin + link_time(pieces[i].order[step], megabytes, sizes, rate)
            pending.append((free[key] + 1.5, i, "arrived", step))
        starts.append((what, i, step))

    while pending:
        pending.sort()
        now, i, what, step = pending.pop(0)
        starts = []
        if what != "ready":
            key = key_of("load" if what == "loaded" else "send", i, step)
            held[key] -= 1
            if queues.get(key):
                start(now, *queues[key].pop(0), starts)
        if what == "ready":
            start(now, "load" if pieces[i].met else "send", i, 0, starts)
        elif what == "arrived" and step == 0:
            start(now, "load", i, 0, starts)
        elif what == "loaded":
            start(now + 0.5, "send", i, 1, starts)
        elif step + 1 < len(pieces[i].order):
            start(now + 0.5, "send", i, step + 1, starts)
        events.append((now, what, i, step, starts))
    return events


def partner(step):
    axis, bit = step
    me = lax.axis_index(axis)
    size = 1 << bit
    there = me + size - 2 * size * lax.rem(me // size, 2)
    return {"pb": lax.axis_index("pb"), "pa": lax.axis_index("pa"), axis: there}


def all_steps(sizes):
    xs, ys, zs = bits_of(sizes)
    return [NEAR] + xs + ys + zs


def greet(sizes):
    barrier = pltpu.get_barrier_semaphore()
    for step in all_steps(sizes):
        pl.semaphore_signal(barrier, inc=1, device_id=partner(step), device_id_type=MESH)
    pl.semaphore_wait(barrier, len(all_steps(sizes)))


class Exchange:
    def __init__(self, sizes, pieces, shapes, rate=None):
        self.sizes, self.pieces, self.shapes = sizes, pieces, shapes
        self.events = plan(pieces, shapes, sizes, rate)
        self.stages = len(all_steps(sizes))
        self.arrays = range(len(shapes))
        self.own = [a for a in self.arrays if any(p.array == a and p.place is not None for p in pieces)]
        self.block = [block_of(pieces[self.of(a)[0]], shapes) for a in self.arrays]
        self.blocks = sorted(set(self.block))
        self.before = {}
        for n, a in enumerate(self.own):
            earlier = [b for b in self.own[:n] if self.block[b] == self.block[a]]
            if earlier:
                self.before[a] = earlier[-1]

    def of(self, array):
        return [i for i, p in enumerate(self.pieces) if p.array == array]

    def scratch(self):
        out = [pltpu.VMEM(block, jnp.float32) for block in self.blocks]
        for array in self.arrays:
            half, *block = self.block[array]
            count = len(self.of(array))
            out += [
                pltpu.VMEM((count, half, *block), jnp.float32),
                pltpu.VMEM((count, half - 1, *block), jnp.float32),
            ]
        count = len(self.pieces)
        return out + [
            pltpu.SemaphoreType.DMA((count,)),
            pltpu.SemaphoreType.DMA((count,)),
            pltpu.SemaphoreType.DMA((count, self.stages)),
            pltpu.SemaphoreType.DMA((count, self.stages)),
        ]

    def bind(self, keeps, sends, nears, outs, staging, scratch):
        self.keeps, self.sends, self.nears, self.outs, self.staging = keeps, sends, nears, outs, staging
        places = dict(zip(self.blocks, scratch))
        self.loaded = [places[block] for block in self.block]
        scratch = scratch[len(self.blocks) :]
        self.kept = [scratch[2 * a] for a in self.arrays]
        recvs = [scratch[2 * a + 1] for a in self.arrays]
        self.near_sems, self.keep_sems, self.send_sems, self.recv_sems = scratch[2 * len(self.shapes) :]
        self.bufs, self.recvs = {}, {}
        for array in self.arrays:
            for number, i in enumerate(self.of(array)):
                self.bufs[i], self.recvs[i] = self.kept[array].at[number], recvs[array].at[number]

    def loads(self, i):
        piece = self.pieces[i]
        cols = pl.ds(piece.first, piece.width)
        out = [pltpu.make_async_copy(self.nears[piece.array].at[:, :, cols], self.loaded[piece.array], self.near_sems.at[i])]
        if piece.place is None:
            out.append(pltpu.make_async_copy(self.keeps[piece.array].at[:, :, cols], self.bufs[i], self.keep_sems.at[i]))
        return out

    def sizes_of(self, i, step):
        half = self.shapes[self.pieces[i].array][0]
        count = half >> step
        return count, half - 2 * count

    def copy(self, i, step):
        piece = self.pieces[i]
        count, first = self.sizes_of(i, step)
        if step == 0:
            if piece.place is None:
                source = self.sends[piece.array].at[:, :, pl.ds(piece.first, piece.width)]
            else:
                source = self.staging[piece.array].at[piece.place % 2]
            target = self.nears[piece.array].at[:, :, pl.ds(piece.first, piece.width)]
        else:
            source = self.bufs[i].at[pl.ds(count, count)]
            target = self.recvs[i].at[pl.ds(first, count)]
        return pltpu.make_async_remote_copy(
            src_ref=source, dst_ref=target, send_sem=self.send_sems.at[i, step], recv_sem=self.recv_sems.at[i, step],
            device_id=partner(piece.order[step]), device_id_type=MESH,
        )

    def free_staging(self, array, place):
        if place >= 2:
            self.copy(self.of(array)[place - 2], 0).wait_send()
        elif array in self.before:
            self.copy([i for i in self.of(self.before[array]) if self.pieces[i].place % 2 == place][-1], 0).wait_send()

    def event(self, what, i, step, starts):
        piece = self.pieces[i]
        buf = self.bufs[i]
        last = what == "arrived" and step + 1 == len(piece.order)
        count = 0
        if what == "loaded":
            for load in self.loads(i):
                load.wait()
            source, first, count = self.loaded[piece.array], 0, self.shapes[piece.array][0]
        elif what == "arrived":
            self.copy(i, step).wait_recv()
            if step > 0:
                source = self.recvs[i]
                count, first = self.sizes_of(i, step)

        def add(slot, _):
            buf[slot] = buf[slot] + source[first + slot]
            return 0

        if last:
            self.outs[piece.array][:, piece.first : piece.first + piece.width] = buf[0] + source[first]
        elif count:
            lax.fori_loop(count // 2, count, add, 0, unroll=min(4, count // 2))
        mine = [s for s in starts if s[0] == "send"]
        for _, j, k in mine:
            self.copy(j, k).start()
        if not last and count:
            lax.fori_loop(0, count // 2, add, 0, unroll=min(4, count // 2))
        for kind, j, _ in starts:
            if kind == "load":
                for load in self.loads(j):
                    load.start()

    def finish(self):
        for i, piece in enumerate(self.pieces):
            waited = piece.place is not None and (
                piece.place + 2 < len(self.of(piece.array)) or piece.array in self.before.values()
            )
            first = 1 if waited or piece.met else 0
            for step in range(first, len(piece.order)):
                self.copy(i, step).wait_send()

    def points(self, times, ready):
        out = [[] for _ in times]
        place = 0
        for when, what, i, step, starts in self.events:
            while place < len(times) - 1 and times[place] < when:
                place += 1
            if what == "ready" and i in ready:
                place = max(place, ready[i])
            out[place].append((what, i, step, starts))
        return out
class Everywhere:
    def __init__(self, steps, shape):
        self.steps = steps
        self.shape = shape

    def scratch(self):
        count = len(self.steps)
        return [
            pltpu.VMEM((count + 1,) + self.shape, jnp.float32),
            pltpu.VMEM((count,) + self.shape, jnp.float32),
            pltpu.SemaphoreType.DMA((count,)),
            pltpu.SemaphoreType.DMA((count,)),
        ]

    def bind(self, scratch):
        self.sums, self.recvs, self.send_sems, self.recv_sems = scratch

    def copy(self, k):
        return pltpu.make_async_remote_copy(
            src_ref=self.sums.at[k], dst_ref=self.recvs.at[k], send_sem=self.send_sems.at[k], recv_sem=self.recv_sems.at[k],
            device_id=partner(self.steps[k]), device_id_type=MESH,
        )

    def arrive(self, k):
        self.copy(k).wait_recv()
        self.sums[k + 1] = self.sums[k] + self.recvs[k]
        if k + 1 < len(self.steps):
            self.copy(k + 1).start()

    def finish(self):
        for k in range(len(self.steps)):
            self.copy(k).wait_send()


SMALL = (24, 1024)
ATTN_STEP = 3.6
OPENING = 7.0
TILE_US = 0.0052
BACK_STEP = 1.2


def slots_of(sizes, order):
    pb, pa = sizes
    far = {}
    for axis, bit in order:
        me = lax.rem(lax.axis_index(axis) // (1 << bit), 2)
        far[axis, bit] = (me, 1 - me)
    cells = []
    for y in range(pb // 2):
        for a in range(pa):
            slot = 0
            for axis, bit in order:
                slot = slot * 2 + far[axis, bit][(2 * y if axis == "pb" else a) >> bit & 1]
            cells.append(slot)
    return cells


def outside_pieces(orders, groups):
    pieces = []
    for number, (_, _, met, chains, width) in enumerate(groups):
        for c, chain in enumerate(chains):
            order = chain if isinstance(chain, list) else orders[chain]
            pieces.append(Piece(number, c * width, width, order, start=0.1 * number + 0.01 * c, met=met))
    return pieces


def back_host_kernel(adding, sizes, *refs):
    own, part_ref, outs, total_ref, scratch = refs[:11], refs[11], refs[12:19], refs[19], refs[20:]
    adding.bind(scratch)
    step = pl.program_id(0)
    last = pl.num_programs(0) - 1
    steps = len(adding.steps)

    @pl.when(step == 0)
    def _():
        adding.sums[0] = part_ref[...]
        greet(sizes)
        adding.copy(0).start()

    for k in range(steps):

        @pl.when(step == jnp.minimum(k + 1, last))
        def _(k=k):
            adding.arrive(k)

    back_kernel(*own, *outs)

    @pl.when(step == last)
    def _():
        total_ref[...] = adding.sums[steps]
        adding.finish()


def post_backward(sizes, part, gkv, y, mid, slope, cot, gains, wck, wcv, wout, win, wo):
    tokens = y.shape[0]
    tile = 256
    ff = win.shape[1]
    low = sds((tokens, D), jnp.bfloat16)
    d = rows_of(tile, D)
    f = rows_of(tile, ff)
    gain = pl.BlockSpec((1, D), lambda i: (0, 0))
    xs, _, zs = bits_of(sizes)
    adding = Everywhere(xs + zs, part.shape)

    def once(array):
        return pl.BlockSpec(array.shape, lambda i: (0,) * array.ndim, pipeline_mode=pl.Buffered(1))

    return pl.pallas_call(
        functools.partial(back_host_kernel, adding, sizes),
        grid=(tokens // tile,),
        in_specs=[pl.BlockSpec((2, tile, D), lambda i: (0, i, 0)), d, d, f, d] + [once(a) for a in (gains, wck, wcv, wout, win, wo, part)],
        out_specs=[d, f, d, d, d, gain, gain, pl.BlockSpec(part.shape, lambda i: (0, 0))],
        out_shape=[low, sds((tokens, ff), jnp.bfloat16), low, sds((tokens, D), jnp.float32), low]
        + [sds((1, D), jnp.float32)] * 2
        + [sds(part.shape, jnp.float32)],
        scratch_shapes=adding.scratch(),
        compiler_params=pltpu.CompilerParams(collective_id=3, has_side_effects=True, vmem_limit_bytes=62 * MIB),
        name="enc_post_back",
    )(gkv, y, mid, slope, cot, gains, wck, wcv, wout, win, wo, part)


class Phase:
    def __init__(self, name, first, count, us):
        self.name, self.first, self.count, self.us = name, first, count, us


def last_kernel(
    exchange, everywhere, points, orders, phases, passages, share, outside, gradients,
    lengths_ref, q_ref, k_ref, v_ref, o_ref, do_ref, lse_ref, base_ref, x_ref, grad_mid_ref, gains_ref, wq_ref, wk_ref, wv_ref,
    dec_fold_ref, *refs,
):
    refs = list(refs)

    def take(count):
        out = refs[:count]
        del refs[:count]
        return out

    gains = take(5)
    lefts = take(len(gradients))
    rights = take(len(gradients) - 1)
    keeps, others = take(len(outside)), take(len(outside))
    out_ref, small_ref = take(2)
    moved = take(len(exchange.shapes))
    nears = [other if met else take(1)[0] for other, met in zip(others, outside)] + take(len(gradients))
    strip_ref, gather_ref, dqT_ref, grads_ref, fold_ref, gain_grad_ref = take(6)
    staging = {}
    for array in exchange.own:
        staging[array] = staging[exchange.before[array]] if array in exchange.before else take(1)[0]
    everywhere.bind(take(4))
    exchange.bind(keeps, others, nears, moved, staging, refs)
    step = pl.program_id(0)
    sizes = exchange.sizes
    pb, pa = sizes

    @pl.when(step == 0)
    def _():
        greet(sizes)
        for event in points["start"][0]:
            exchange.event(*event)

    def run(place):
        for at, events in points.get(place, {}).items():
            if events:

                @pl.when(step == at)
                def _(events=events):
                    for event in events:
                        exchange.event(*event)

    def attention(phase):
        number = step - phase.first
        pair = number // passages
        passage = lax.rem(number, passages)
        place = pl.ds(pl.multiple_of(passage * PL, PL), PL), pl.ds(pl.multiple_of(pair * 128, 128), 128)
        attn_backward_kernel(
            lambda head: run(("attention", head)), passage, passages, lengths_ref, q_ref, k_ref, v_ref, o_ref, do_ref, lse_ref, base_ref,
            grads_ref.at[(0,) + place], grads_ref.at[(1,) + place], grads_ref.at[(2,) + place], fold_ref.at[pl.ds(pair, 1)],
            strip_ref, gather_ref, dqT_ref,
        )

    def gradient(phase, array, left_ref, right_ref):
        number = step - phase.first
        width = exchange.pieces[exchange.of(array)[0]].width
        if right_ref is None:
            each = D // width
            column = pl.ds(pl.multiple_of(lax.rem(number, each) * width, width), width)
            right = grads_ref[number // each, :, column]
        else:
            right = right_ref[...]
        for place in range(0 if array in exchange.before else 2, phase.count):

            @pl.when(number == place)
            def _(place=place):
                exchange.free_staging(array, place)

        chain = 0
        for place, c in enumerate(gradients[array - len(outside)][3]):
            chain = jnp.where(number == place, c, chain)
        choices = [slots_of(sizes, order) for order in orders]
        core = lax.rem(lax.axis_index("pb"), 2)
        rows = exchange.shapes[array][1]
        half_rows = pa * rows
        kept, staged = exchange.kept[array], exchange.staging[array]
        for y in range(pb // 2):
            low_part = nn(left_ref[2 * y * half_rows : (2 * y + 1) * half_rows, :], right)
            high_part = nn(left_ref[(2 * y + 1) * half_rows : (2 * y + 2) * half_rows, :], right)
            mine = jnp.where(core == 0, low_part, high_part)
            other = jnp.where(core == 0, high_part, low_part)
            for a in range(pa):
                slot = choices[0][y * pa + a]
                for c in range(1, len(orders)):
                    slot = jnp.where(chain == c, choices[c][y * pa + a], slot)
                kept[number, slot] = mine[a * rows : (a + 1) * rows]
                staged[lax.rem(number, 2), slot] = other[a * rows : (a + 1) * rows]

    def back(phase):
        height = x_ref.shape[0]
        rows = pl.ds(pl.multiple_of((step - phase.first) * height, height), height)
        qkv_back_kernel(
            step == phase.first, grads_ref.at[0, rows], grads_ref.at[1, rows], grads_ref.at[2, rows],
            x_ref, grad_mid_ref, gains_ref, wq_ref, wk_ref, wv_ref, out_ref, gain_grad_ref,
        )

    for phase in phases:

        @pl.when((step >= phase.first) & (step < phase.first + phase.count))
        def _(phase=phase):
            if phase.name == "attention":
                attention(phase)
            elif phase.name == "back":
                back(phase)
            else:
                k = phase.name
                gradient(phase, exchange.own[k], lefts[k], rights[k] if k < len(rights) else None)

    run("end")

    @pl.when(step == pl.num_programs(0) - 1)
    def _():
        first = everywhere.sums
        first[0] = jnp.zeros(SMALL, jnp.float32)
        first[0, 0:1, :D] = gain_grad_ref[...]
        for r, ref in enumerate(gains):
            first[0, r + 1 : r + 2, :D] = ref[...] if r < 2 else ref[...] * share
        for pair in range(HEADS // 2):
            first[0, 8 + 2 * pair : 10 + 2 * pair, :] = fold_ref[pair]
        for part in range(2):
            lanes = slice(D + part * 128, D + (part + 1) * 128)
            first[0, 0:6, lanes] = dec_fold_ref[6 * part : 6 * part + 6] * share
        everywhere.copy(0).start()
        left = points["rest"]
        steps = len(everywhere.steps)
        every = max(1, len(left) // (steps + 1))
        done = 0
        for n, event in enumerate(left):
            if n % every == every - 1 and done < steps:
                everywhere.arrive(done)
                done += 1
            exchange.event(*event)
        for k in range(done, steps):
            everywhere.arrive(k)
        small_ref[...] = everywhere.sums[steps]
        exchange.finish()
        everywhere.finish()


def last_part(
    sizes, orders, groups, gradients, lengths, q, k, v, o, do, lse, base, x, grad_mid, gains, wq, wk, wv, dec_fold, grads_of_gains,
):
    pb, pa = sizes
    passages = lengths.shape[0]
    tokens = x.shape[0]
    pairs = HEADS // 2
    tile_rows = 128
    half = pb * pa // 2
    shapes = [g[0].shape for g in groups]
    widths = [right.shape[1] if right is not None else 3 * D for _, right, *_ in gradients]
    shapes += [(half, left.shape[0] // (pb * pa), w) for (left, *_), w in zip(gradients, widths)]

    phases = []
    names = list(range(len(gradients) - 1)) + ["attention", len(gradients) - 1, "back"]
    step = 0
    for name in names:
        if name == "attention":
            count, us = pairs * passages, ATTN_STEP
        elif name == "back":
            count, us = tokens // tile_rows, BACK_STEP
        else:
            count, us = widths[name] // gradients[name][2], TILE_US * gradients[name][2]
        phases.append(Phase(name, step, count, us))
        step += count
    steps = step
    pieces = outside_pieces(orders, groups)
    times, labels, ready = [OPENING], [("start", 0)], {}
    now = OPENING
    for phase in phases:
        for n in range(phase.count):
            number = phase.first + n
            if phase.name == "attention":
                times += [now, now + phase.us / 2]
                labels += [(("attention", 0), number), (("attention", 1), number)]
            now += phase.us
            if phase.name != "attention" and number < steps - 1:
                times.append(now)
                labels.append(("end", number))
            if isinstance(phase.name, int):
                ready[len(pieces)] = len(times) - 1
                width = gradients[phase.name][2]
                pieces.append(Piece(len(groups) + phase.name, n * width, width, orders[gradients[phase.name][3][n]], n, now))
    exchange = Exchange(sizes, pieces, shapes)
    everywhere = Everywhere(all_steps(sizes), SMALL)
    points = {}
    found = exchange.points(times + [1e9], ready)
    for (place, number), events in zip(labels, found):
        points.setdefault(place, {})[number] = events
    points["rest"] = found[-1]
    by_name = {phase.name: phase for phase in phases}

    def at(name, i):
        phase = by_name[name]
        return jnp.clip(i - phase.first, 0, phase.count - 1)

    def pair_of(i):
        return at("attention", i) // passages

    def passage_of(i):
        return lax.rem(at("attention", i), passages)

    def once(array):
        return pl.BlockSpec(array.shape, lambda i: (0,) * array.ndim, pipeline_mode=pl.Buffered(1))

    tile = pl.BlockSpec((PL, 128), lambda i: (passage_of(i), pair_of(i)))
    rows = pl.BlockSpec((tile_rows, D), lambda i: (at("back", i), 0))
    hbm = pl.BlockSpec(memory_space=pl.ANY)
    keeps, others = [g[0] for g in groups], [g[1] for g in groups]
    outside = [g[2] for g in groups]
    lefts = [left for left, *_ in gradients]
    rights = [right for _, right, *_ in gradients[:-1]]
    right_specs = [
        pl.BlockSpec((tokens, width), lambda i, name=name: (0, at(name, i)), pipeline_mode=pl.Buffered(1)) for name, (_, _, width, _) in enumerate(gradients[:-1])
    ]
    own_shapes = shapes[len(groups) :]
    near_shapes = [s for s, met in zip(shapes, outside) if not met] + own_shapes
    return pl.pallas_call(
        functools.partial(
            last_kernel, exchange, everywhere, points, orders, phases, passages, 1.0 / pa, outside, gradients
        ),
        grid=(steps,),
        in_specs=[pl.BlockSpec(memory_space=pltpu.SMEM)]
        + [tile] * 5
        + [pl.BlockSpec((1, 1, 2, PL), lambda i: (pair_of(i), passage_of(i), 0, 0)), pl.BlockSpec((1, 2, WIDE), lambda i: (pair_of(i), 0, 0))]
        + [rows, rows]
        + [once(a) for a in (gains, wq, wk, wv, dec_fold) + tuple(grads_of_gains)]
        + [once(left) for left in lefts]
        + right_specs
        + [hbm] * (2 * len(groups)),
        out_specs=[rows, pl.BlockSpec(SMALL, lambda i: (0, 0), pipeline_mode=pl.Buffered(1))]
        + [pl.BlockSpec(s[1:], lambda i: (0, 0), pipeline_mode=pl.Buffered(1)) for s in shapes]
        + [hbm] * len(near_shapes),
        out_shape=[sds((tokens, D), jnp.float32), sds(SMALL, jnp.float32)]
        + [sds(s[1:], jnp.float32) for s in shapes]
        + [sds(s, jnp.float32) for s in near_shapes],
        scratch_shapes=[
            pltpu.VMEM((2, STRIP, WIDE), jnp.float32),
            pltpu.VMEM((2, STRIP, WIDE), jnp.float32),
            pltpu.VMEM((128, PL), jnp.bfloat16),
            pltpu.VMEM((3, tokens, D), jnp.bfloat16),
            pltpu.VMEM((pairs, 2, WIDE), jnp.float32),
            pltpu.VMEM((1, D), jnp.float32),
        ]
        + [pltpu.VMEM((2,) + exchange.block[a], jnp.float32) for a in exchange.own if a not in exchange.before]
        + everywhere.scratch()
        + exchange.scratch(),
        compiler_params=pltpu.CompilerParams(collective_id=1, has_side_effects=True, vmem_limit_bytes=63 * MIB + MIB // 2),
        name="enc_last",
    )(
        lengths, q, k, v, o, do, lse, base, x, grad_mid, gains, wq, wk, wv, dec_fold, *grads_of_gains, *lefts, *rights, *keeps, *others
    )[: 2 + len(shapes)]


def exchange_kernel(exchange, arrays, *refs):
    exchange.bind(refs[:arrays], {}, refs[arrays : 2 * arrays], refs[2 * arrays : 3 * arrays], {}, refs[3 * arrays :])
    greet(exchange.sizes)
    for _, *event in exchange.events:
        exchange.event(*event)
    exchange.finish()


def exchange_only(sizes, orders, groups):
    shapes = [g[0].shape for g in groups]
    exchange = Exchange(sizes, outside_pieces(orders, groups), shapes)
    return pl.pallas_call(
        functools.partial(exchange_kernel, exchange, len(groups)),
        in_specs=[pl.BlockSpec(memory_space=pl.ANY)] * (2 * len(groups)),
        out_specs=[pl.BlockSpec(memory_space=pltpu.VMEM)] * len(groups),
        out_shape=[sds(s[1:], jnp.float32) for s in shapes],
        scratch_shapes=exchange.scratch(),
        compiler_params=pltpu.CompilerParams(collective_id=2, has_side_effects=True, vmem_limit_bytes=63 * MIB),
        name="exchange",
    )(*[g[0] for g in groups], *[g[1] for g in groups])


def local(
    pb, pa,
    enc_in, dec_in, question_of, lengths, enc_gain_attn, enc_query, enc_key, enc_value, enc_output, enc_bias,
    enc_gain_ffn, enc_ff_in, enc_ff_out, enc_gain_final, cross_key, cross_value, dec_gain_self, dec_query, dec_key,
    dec_value, dec_output, dec_bias, dec_gain_cross, cross_query, cross_output, dec_gain_ffn, dec_ff_in, dec_ff_out,
    enc_cot, dec_cot,
):
    sizes = (pb, pa)
    orders = orders_of(sizes)
    answer_rows = dec_in.shape[0]
    gains = gains_together(enc_gain_attn, enc_gain_ffn, enc_gain_final, dec_gain_self, dec_gain_cross, dec_gain_ffn)
    table = exchange_table(sizes, orders)
    enc_table = jnp.asarray(strip_table().T, jnp.bfloat16)
    dec_table = jnp.asarray(causal_row(ANS).T, jnp.bfloat16)

    attn_turned, enc_queries, enc_keys, enc_values = qkv_forward(enc_in, gains, enc_query, enc_key, enc_value)
    enc_attended, attended_turned, enc_lse, base = attn_forward(lengths, enc_queries, enc_keys, enc_values, enc_bias.T, enc_table)
    enc_mid, ffn_turned, hidden_turned, enc_slope, enc_y, enc_out, final_turned, cross_keys, cross_values = post_forward(
        enc_in, enc_attended, gains, enc_output, enc_ff_in, enc_ff_out, cross_key, cross_value
    )

    self_low, dec_queries, dec_keys, dec_values, dec_probs, dec_attended, dec_mid, cross_low, cross_queries = dec_pre(
        dec_in, gains, dec_bias.T, dec_table, dec_query, dec_key, dec_value, dec_output, cross_query
    )

    merged = merge(cross_part(question_of, lengths, cross_queries, cross_keys, cross_values), pa)
    dec_out, dffn_low, dec_hidden, pre_grad_low, after_low, grad_after, cross_att_grad, dec_gain_ffn_grad = dec_mid_call(
        merged, dec_mid, dec_cot, gains, cross_output, dec_ff_in, dec_ff_out
    )
    query_part, grad_cross = cross_back(
        question_of, lengths, cross_queries, cross_keys, cross_values, cross_att_grad, merged[:, :D], merged[:, D:]
    )
    def near(terms):
        keep, send = terms
        return keep, lax.ppermute(send, "pb", [(i, i ^ 1) for i in range(pb)])

    cross_terms = near(weight_grad(table, final_turned, [(grad_cross, 0), (grad_cross, 1)], pb, pa, 256, (0, 0, 1, 1, 2, 2)))
    eout_low, epre_low, emid_low, grad_enc_mid, enc_att_grad, final_gain_grad, ffn_gain_grad, grad_cross_q = post_backward(
        sizes, query_part,
        grad_cross, enc_y, enc_mid, enc_slope, enc_cot, gains, cross_key, cross_value, enc_ff_out, enc_ff_in, enc_output,
    )
    out_terms = near(weight_grad(table, hidden_turned, [eout_low], pb, pa, 256, (0, 1, 3)))

    mid_low, grad_dq, grad_dk, grad_dv, dec_in_grad, dec_gain_self_grad, dec_gain_cross_grad, dec_fold = dec_post(
        grad_cross_q, grad_after, dec_mid, dec_in, dec_queries, dec_keys, dec_values, dec_probs, gains,
        dec_query, dec_key, dec_value, dec_output, cross_query, out_terms[0],
    )
    far = lax.axis_index("pb") // 2
    places = [lax.axis_index("pa"), lax.axis_index("pb") % 2]
    for y in range(pb // 2):
        slot = 0
        for _, bit in bits_of(sizes)[1]:
            slot = slot * 2 + ((far >> (bit - 1)) + (y >> (bit - 1))) % 2
        places.append(slot)
    dec_terms = dec_weight_grads(
        pb, pa, jnp.stack(places).astype(jnp.int32), self_low, grad_dq, grad_dk, grad_dv, dec_attended, mid_low, cross_low, grad_cross_q,
        merged, after_low, dec_hidden, dec_cot, dffn_low, pre_grad_low,
    )
    ys = bits_of(sizes)[1]
    groups = [
        cross_terms + (True, (0, 1, 2), 512),
        out_terms + (True, (0, 1, 3), 256),
        tuple(dec_terms) + (False, (ys, ys, ys), 256),
    ]
    gradients = [
        (ffn_turned, epre_low, 512, (0, 1, 2, 0, 1, 3)),
        (attended_turned, emid_low, 256, (0, 1, 2)),
        (attn_turned, None, 256, (0, 1, 2, 0, 1, 3, 0, 1, 2)),
    ]
    roomy = D // (pb * pa) % 8 == 0
    if not roomy:
        del gradients[0]
        keep, send = weight_grad(table, ffn_turned, [epre_low], pb, pa, 512, (0, 0, 1, 1, 2, 2))
        in_terms = keep, lax.ppermute(send, "pb", [(i, i ^ 1) for i in range(pb)])
    enc_in_grad, small, *summed = last_part(
        sizes, orders, groups, gradients, lengths, enc_queries, enc_keys, enc_values, enc_attended, enc_att_grad, enc_lse, base,
        enc_in, grad_enc_mid, gains, enc_query, enc_key, enc_value, dec_fold,
        (ffn_gain_grad, final_gain_grad, dec_gain_self_grad, dec_gain_cross_grad, dec_gain_ffn_grad),
    )
    if not roomy:
        summed[3:3] = exchange_only(sizes, orders, [tuple(in_terms) + (True, (0, 1, 2), 1024)])
    cross_sum, ff_out_sum, dec_sum, *summed = summed
    ends = finish(
        pb, pa, small, dec_sum, enc_table, dec_table, dec_hidden.shape[1], [cross_sum, ff_out_sum] + summed, [2, 1, 1, 1, 3]
    )
    gain_grads, (enc_bias_grad, dec_bias_grad), got = ends[:6], ends[6:8], ends[8:16]
    cross_key_grad, cross_value_grad, ff_out_grad, ff_in_grad, output_grad, query_grad, key_grad, value_grad = ends[16:]

    return (
        enc_out, dec_out, enc_in_grad, dec_in_grad,
        gain_grads[0], query_grad, key_grad, value_grad, output_grad, enc_bias_grad,
        gain_grads[1], ff_in_grad, ff_out_grad, gain_grads[2], cross_key_grad, cross_value_grad,
        gain_grads[3], got[0], got[1], got[2], got[3], dec_bias_grad, gain_grads[4], got[4], got[5], gain_grads[5], got[7], got[6],
    )


def solution(mesh):
    pb, pa = mesh.shape["pb"], mesh.shape["pa"]
    rows = P(("pb", "pa"), None)
    flat = P(("pb", "pa"))
    dec = P("pb", None)
    return jax.shard_map(
        functools.partial(local, pb, pa),
        mesh=mesh,
        in_specs=(rows, dec, flat, flat) + (P(),) * 24 + (rows, dec),
        out_specs=(rows, dec, rows, dec)
        + (flat, rows, rows, rows, rows, flat, flat, rows, rows, flat, rows, rows)
        + (flat, rows, rows, rows, rows, flat, flat, rows, rows, flat, rows, rows),
        check_vma=False,
    )
```

```python
import functools
import math

import jax
import jax.numpy as jnp
import numpy as np
from jax import lax
from jax.experimental import pallas as pl
from jax.experimental.pallas import tpu as pltpu
from jax.sharding import PartitionSpec as P

D = 768
HEADS = 12
HEAD = 64
BUCKETS = 32
PL = 512
ANS = 24

far_distance = 128
epsilon = 1e-06
highest = lax.Precision.HIGHEST


def bucket_of(offset, bidirectional):
    if bidirectional:
        halves = BUCKETS // 2
        base_bucket = halves if offset > 0 else 0
        distance = abs(offset)
    else:
        halves = BUCKETS
        base_bucket = 0
        distance = max(-offset, 0)
    exact_count = halves // 2
    if distance < exact_count:
        return base_bucket + distance
    scaled = (
        math.log(distance / exact_count)
        / math.log(far_distance / exact_count)
        * (halves - exact_count)
    )
    return base_bucket + min(exact_count + int(scaled), halves - 1)


def to_low(values):
    return values.astype(jnp.bfloat16)


def product_tn(left, right):
    return lax.dot_general(
        left, right, (((0,), (0,)), ((), ())), preferred_element_type=jnp.float32
    )


STRIP = 128
WIDE = 1024


def strip_table():
    table = np.zeros((WIDE, BUCKETS), np.float32)
    for place in range(WIDE):
        if place < PL + STRIP * 3:
            offset = PL - STRIP - place
        else:
            offset = PL - STRIP + WIDE - place
        if abs(offset) < PL:
            table[place, bucket_of(offset, True)] = 1.0
    return table


def nn(left, right):
    return lax.dot_general(left, right, (((1,), (0,)), ((), ())), preferred_element_type=jnp.float32)


def head_lanes(values, head):
    lane = lax.broadcasted_iota(jnp.int32, values.shape, 1)
    keep = lane < HEAD if head == 0 else lane >= HEAD
    return jnp.where(keep, values, jnp.zeros_like(values))


def key_mask(length):
    place = lax.broadcasted_iota(jnp.int32, (PL, 1), 0)
    return jnp.where(place < length, 0.0, -1e9)


def build_strip(base_ref, strip_ref):
    for head in range(2):
        row = base_ref[0, head : head + 1, :]
        spread = jnp.broadcast_to(row, (STRIP, WIDE))
        strip_ref[head] = pltpu.roll(spread, 0, 1, stride=1, stride_axis=0)


def attn_forward_kernel(lengths_ref, q_ref, k_ref, v_ref, bias_ref, table_ref, out_ref, turned_ref, lse_ref, base_ref, rows_ref, strip_ref, score_ref):
    passage = pl.program_id(1)

    @pl.when((passage == 0) & (pl.program_id(0) == 0))
    def _():
        every = nn(bias_ref[...], table_ref[...])
        for pair in range(HEADS // 2):
            rows_ref[pair] = every[2 * pair : 2 * pair + 2]

    base_ref[...] = rows_ref[pl.ds(pl.program_id(0), 1)]

    @pl.when(passage == 0)
    def _():
        build_strip(base_ref, strip_ref)

    mask = key_mask(lengths_ref[passage])
    q_t = q_ref[...].T
    v_t = v_ref[...].T
    k = k_ref[...]
    blocks = PL // STRIP
    for head in range(2):
        k_head = head_lanes(k, head)
        top = None
        for b in range(blocks):
            rows = slice(b * STRIP, (b + 1) * STRIP)
            start = PL - STRIP - b * STRIP
            s = nn(k_head[rows], q_t) + strip_ref[head, :, start : start + PL] + mask[rows]
            score_ref[head, rows, :] = s
            here = jnp.max(s, axis=0, keepdims=True)
            top = here if top is None else jnp.maximum(top, here)
        total = None
        acc = None
        for b in range(blocks):
            rows = slice(b * STRIP, (b + 1) * STRIP)
            e = jnp.exp(score_ref[head, rows, :] - top)
            here = jnp.sum(e, axis=0, keepdims=True)
            total = here if total is None else total + here
            part = nn(v_t[head * HEAD : (head + 1) * HEAD, rows], to_low(e))
            acc = part if acc is None else acc + part
        turned_ref[head * HEAD : (head + 1) * HEAD, :] = to_low(acc * (1.0 / total))
        lse_ref[0, 0, head : head + 1, :] = top + jnp.log(total)
    out_ref[...] = turned_ref[...].T


def attn_forward(lengths, q, k, v, bias, table):
    passages = lengths.shape[0]
    pairs = HEADS // 2
    tile = pl.BlockSpec((PL, 128), lambda h, p, *_: (p, h))
    return pl.pallas_call(
        attn_forward_kernel,
        grid_spec=pltpu.PrefetchScalarGridSpec(
            num_scalar_prefetch=1,
            grid=(pairs, passages),
            in_specs=[tile, tile, tile, pl.BlockSpec(bias.shape, lambda h, p, *_: (0, 0)), pl.BlockSpec(table.shape, lambda h, p, *_: (0, 0))],
            out_specs=[
                tile,
                pl.BlockSpec((128, PL), lambda h, p, *_: (h, p)),
                pl.BlockSpec((1, 1, 2, PL), lambda h, p, *_: (h, p, 0, 0)),
                pl.BlockSpec((1, 2, WIDE), lambda h, p, *_: (h, 0, 0)),
            ],
            scratch_shapes=[
                pltpu.VMEM((pairs, 2, WIDE), jnp.float32),
                pltpu.VMEM((2, STRIP, WIDE), jnp.float32),
                pltpu.VMEM((2, PL, PL), jnp.float32),
            ],
        ),
        out_shape=[
            jax.ShapeDtypeStruct((passages * PL, D), jnp.bfloat16),
            jax.ShapeDtypeStruct((D, passages * PL), jnp.bfloat16),
            jax.ShapeDtypeStruct((pairs, passages, 2, PL), jnp.float32),
            jax.ShapeDtypeStruct((pairs, 2, WIDE), jnp.float32),
        ],
        compiler_params=pltpu.CompilerParams(vmem_limit_bytes=62 * 2**20),
        name="enc_attention",
    )(lengths, q, k, v, bias, table)


def attn_backward_kernel(
    beside, passage, passages, lengths_ref, q_ref, k_ref, v_ref, o_ref, do_ref, lse_ref, base_ref,
    dq_ref, dk_ref, dv_ref, fold_ref,
    strip_ref, gather_ref, dqT_ref,
):
    @pl.when(passage == 0)
    def _():
        build_strip(base_ref, strip_ref)
        gather_ref[...] = jnp.zeros_like(gather_ref)

    mask = key_mask(lengths_ref[passage])
    q = q_ref[...]
    k = k_ref[...]
    v = v_ref[...]
    do = do_ref[...]
    q_t = q.T
    k_t = k.T
    do_t = do.T
    o_t = o_ref[...].T
    weighed = do_t.astype(jnp.float32) * o_t.astype(jnp.float32)
    blocks = PL // STRIP
    lane = lax.broadcasted_iota(jnp.int32, (STRIP, 128), 1)
    first = lane < HEAD
    dks = []
    dvs = []
    for head in range(2):
        beside(head)
        heads = slice(head * HEAD, (head + 1) * HEAD)
        delta = jnp.sum(weighed[heads], axis=0, keepdims=True)
        lse = lse_ref[0, 0, head : head + 1, :]
        k_head = head_lanes(k, head)
        v_head = head_lanes(v, head)
        acc = None
        for b in range(blocks):
            rows = slice(b * STRIP, (b + 1) * STRIP)
            start = PL - STRIP - b * STRIP
            s = nn(k_head[rows], q_t) + strip_ref[head, :, start : start + PL] + mask[rows]
            p = jnp.exp(s - lse)
            dp = nn(v_head[rows], do_t)
            ds = p * (dp - delta)
            gather_ref[head, :, start : start + PL] += ds
            ds_low = to_low(ds)
            dv_part = nn(to_low(p), do)
            dk_part = nn(ds_low, q)
            if head == 0:
                dvs.append(dv_part)
                dks.append(dk_part)
            else:
                dv_ref[rows, :] = to_low(jnp.where(first, dvs[b], dv_part))
                dk_ref[rows, :] = to_low(jnp.where(first, dks[b], dk_part))
            part = nn(k_t[heads, rows], ds_low)
            acc = part if acc is None else acc + part
        dqT_ref[heads, :] = to_low(0.125 * acc)
    dq_ref[...] = dqT_ref[...].T

    @pl.when(passage == passages - 1)
    def _():
        row = lax.broadcasted_iota(jnp.int32, (8, WIDE), 0)
        for head in range(2):
            total = gather_ref[head, 0:8, :]
            for group in range(1, STRIP // 8):
                total = total + pltpu.roll(gather_ref[head, group * 8 : group * 8 + 8, :], WIDE - group * 8, 1)
            for bit in (1, 2, 4):
                total = jnp.where((row // bit) % 2 == 1, pltpu.roll(total, WIDE - bit, 1), total)
            fold_ref[0, head : head + 1, :] = jnp.sum(total, axis=0, keepdims=True)


MIB = 2**20


def nt(left, right):
    return lax.dot_general(left, right, (((1,), (1,)), ((), ())), preferred_element_type=jnp.float32)


def rms(values, gain):
    scale = lax.rsqrt(jnp.mean(values * values, axis=-1, keepdims=True) + epsilon)
    return values * scale * gain, scale


def rms_back(values, scale, gain, grad):
    scaled = grad * gain
    gain_grad = jnp.sum(grad * values * scale, axis=0, keepdims=True)
    inner = jnp.mean(scaled * values, axis=-1, keepdims=True)
    return scaled * scale - values * (scale * scale * scale) * inner, gain_grad


def gelu_both(v):
    c = math.sqrt(2.0 / math.pi)
    square = v * v
    t = jnp.tanh(v * (c + (c * 0.044715) * square))
    half = 0.5 + 0.5 * t
    slope = half + (half * (1.0 - t)) * v * (c + (3.0 * 0.044715 * c) * square)
    return v * half, slope


GAIN_ATTN, GAIN_FFN, GAIN_FINAL, GAIN_SELF, GAIN_CROSS, GAIN_DFFN = range(6)


def gain_of(gains_ref, which):
    return gains_ref[which : which + 1, :]


def whole(array):
    return pl.BlockSpec(array.shape, lambda *_: (0,) * array.ndim)


def rows_of(tile, width):
    return pl.BlockSpec((tile, width), lambda i: (i, 0))


def sds(shape, kind):
    return jax.ShapeDtypeStruct(shape, kind)


def params(mib):
    return pltpu.CompilerParams(vmem_limit_bytes=mib * MIB)


def qkv_kernel(x_ref, gains_ref, wq_ref, wk_ref, wv_ref, turned_ref, q_ref, k_ref, v_ref):
    normed, _ = rms(x_ref[...].astype(jnp.float32), gain_of(gains_ref, GAIN_ATTN))
    low = to_low(normed)
    turned_ref[...] = low.T
    q_ref[...] = to_low(0.125 * to_low(nn(low, wq_ref[...])).astype(jnp.float32))
    k_ref[...] = to_low(nn(low, wk_ref[...]))
    v_ref[...] = to_low(nn(low, wv_ref[...]))


def qkv_forward(x, gains, wq, wk, wv):
    tokens = x.shape[0]
    tile = 256
    big = sds((tokens, D), jnp.bfloat16)
    return pl.pallas_call(
        qkv_kernel,
        grid=(tokens // tile,),
        in_specs=[rows_of(tile, D)] + [whole(a) for a in (gains, wq, wk, wv)],
        out_specs=[pl.BlockSpec((D, tile), lambda i: (0, i))] + [rows_of(tile, D)] * 3,
        out_shape=[sds((D, tokens), jnp.bfloat16)] + [big] * 3,
        compiler_params=params(62),
        name="enc_qkv",
    )(x, gains, wq, wk, wv)


def post_kernel(
    x_ref, att_ref, gains_ref, wo_ref, win_ref, wout_ref, wck_ref, wcv_ref,
    mid_ref, ffn_turned_ref, hidden_turned_ref, slope_ref, y_ref, out_ref, final_turned_ref, ck_ref, cv_ref,
):
    mid = x_ref[...].astype(jnp.float32) + nn(att_ref[...], wo_ref[...])
    mid_ref[...] = mid
    normed, _ = rms(mid, gain_of(gains_ref, GAIN_FFN))
    low = to_low(normed)
    ffn_turned_ref[...] = low.T
    y = mid
    width = 768
    for c in range(win_ref.shape[1] // width):
        cols = slice(c * width, (c + 1) * width)
        hidden, slope = gelu_both(nn(low, win_ref[:, cols]))
        hidden = to_low(hidden)
        hidden_turned_ref[cols, :] = hidden.T
        slope_ref[:, cols] = to_low(slope)
        y = y + nn(hidden, wout_ref[cols, :])
    y_ref[...] = y
    out_ref[...] = to_low(y)
    final, _ = rms(y, gain_of(gains_ref, GAIN_FINAL))
    final = to_low(final)
    final_turned_ref[...] = final.T
    ck_ref[...] = to_low(nn(final, wck_ref[...]))
    cv_ref[...] = to_low(nn(final, wcv_ref[...]))


def post_forward(x, att, gains, wo, win, wout, wck, wcv):
    tokens = x.shape[0]
    tile = 256
    ff = win.shape[1]
    low = sds((tokens, D), jnp.bfloat16)
    wide = sds((tokens, ff), jnp.bfloat16)
    full = sds((tokens, D), jnp.float32)
    d = rows_of(tile, D)
    f = rows_of(tile, ff)
    turned = pl.BlockSpec((D, tile), lambda i: (0, i))
    flat = sds((D, tokens), jnp.bfloat16)
    return pl.pallas_call(
        post_kernel,
        grid=(tokens // tile,),
        in_specs=[d, d] + [whole(a) for a in (gains, wo, win, wout, wck, wcv)],
        out_specs=[d, turned, pl.BlockSpec((ff, tile), lambda i: (0, i)), f, d, d, turned, d, d],
        out_shape=[full, flat, sds((ff, tokens), jnp.bfloat16), wide, full, low, flat, low, low],
        compiler_params=params(62),
        name="enc_post",
    )(x, att, gains, wo, win, wout, wck, wcv)


def back_kernel(
    gkv_ref, y_ref, mid_ref, slope_ref, cot_ref, gains_ref,
    wck_ref, wcv_ref, wout_ref, win_ref, wo_ref,
    eout_ref, epre_ref, emid_ref, grad_mid_ref, att_grad_ref, gain_final_grad_ref, gain_ffn_grad_ref,
):

    @pl.when(pl.program_id(0) == 0)
    def _():
        gain_final_grad_ref[...] = jnp.zeros_like(gain_final_grad_ref)
        gain_ffn_grad_ref[...] = jnp.zeros_like(gain_ffn_grad_ref)

    y = y_ref[...]
    scale = lax.rsqrt(jnp.mean(y * y, axis=-1, keepdims=True) + epsilon)
    final_back = nt(gkv_ref[0], wck_ref[...]) + nt(gkv_ref[1], wcv_ref[...])
    back, gain_grad = rms_back(y, scale, gain_of(gains_ref, GAIN_FINAL), final_back)
    gain_final_grad_ref[...] += gain_grad
    grad_y = cot_ref[...].astype(jnp.float32) + back
    eout = to_low(grad_y)
    eout_ref[...] = eout
    width = 768
    acc = None
    for c in range(win_ref.shape[1] // width):
        cols = slice(c * width, (c + 1) * width)
        epre = to_low(slope_ref[:, cols].astype(jnp.float32) * nt(eout, wout_ref[cols, :]))
        epre_ref[:, cols] = epre
        part = nt(epre, win_ref[:, cols])
        acc = part if acc is None else acc + part
    mid = mid_ref[...]
    scale = lax.rsqrt(jnp.mean(mid * mid, axis=-1, keepdims=True) + epsilon)
    back, gain_grad = rms_back(mid, scale, gain_of(gains_ref, GAIN_FFN), acc)
    gain_ffn_grad_ref[...] += gain_grad
    grad_mid = grad_y + back
    grad_mid_ref[...] = grad_mid
    emid = to_low(grad_mid)
    emid_ref[...] = emid
    att_grad_ref[...] = to_low(nt(emid, wo_ref[...]))


def qkv_back_kernel(opening, dq_ref, dk_ref, dv_ref, x_ref, grad_mid_ref, gains_ref, wq_ref, wk_ref, wv_ref, out_ref, gain_grad_ref):
    @pl.when(opening)
    def _():
        gain_grad_ref[...] = jnp.zeros_like(gain_grad_ref)

    x = x_ref[...].astype(jnp.float32)
    scale = lax.rsqrt(jnp.mean(x * x, axis=-1, keepdims=True) + epsilon)
    grad = nt(dq_ref[...], wq_ref[...]) + nt(dk_ref[...], wk_ref[...]) + nt(dv_ref[...], wv_ref[...])
    back, gain_grad = rms_back(x, scale, gain_of(gains_ref, GAIN_ATTN), grad)
    gain_grad_ref[...] += gain_grad
    out_ref[...] = grad_mid_ref[...] + back


def weight_grad_kernel(rows, pb, pa, tiles, chains, table_ref, turned_ref, *refs):
    rights = refs[: len(tiles)]
    keep_ref, send_ref = refs[-2:]
    step = pl.program_id(0)
    core = table_ref[0, 0]
    chain = chains[0]
    for place, c in enumerate(chains):
        chain = jnp.where(step == place, c, chain)
    half_rows = pa * rows

    def work(right):
        for y in range(pb // 2):
            low_part = nn(turned_ref[2 * y * half_rows : (2 * y + 1) * half_rows, :], right)
            high_part = nn(turned_ref[(2 * y + 1) * half_rows : (2 * y + 2) * half_rows, :], right)
            mine = jnp.where(core == 0, low_part, high_part)
            other = jnp.where(core == 0, high_part, low_part)
            for a in range(pa):
                slot = table_ref[chain + 1, y * pa + a]
                keep_ref[slot] = mine[a * rows : (a + 1) * rows]
                send_ref[slot] = other[a * rows : (a + 1) * rows]

    first = 0
    for right_ref, count in zip(rights, tiles):
        if len(tiles) == 1:
            work(right_ref[...])
        else:

            @pl.when((step >= first) & (step < first + count))
            def _(right_ref=right_ref):
                work(right_ref[...] if len(right_ref.shape) == 2 else right_ref[0])

        first += count


def weight_grad(table, turned, rights, pb, pa, width, chains):
    height, tokens = turned.shape
    rows = height // (pb * pa)
    arrays = [r[0] if isinstance(r, tuple) else r for r in rights]
    tiles = [a.shape[-1] // width for a in arrays]
    total = sum(tiles)
    firsts = np.cumsum([0] + tiles)[:-1]

    def spec(right, first, count):
        def column(i):
            return jnp.clip(i - int(first), 0, count - 1)

        if isinstance(right, tuple):
            return pl.BlockSpec((1, tokens, width), lambda i, *_: (right[1], 0, column(i)))
        return pl.BlockSpec((tokens, width), lambda i, *_: (0, column(i)))

    half = pb * pa // 2
    out = pl.BlockSpec((half, rows, width), lambda i, *_: (0, 0, i))
    shape = sds((half, rows, total * width), jnp.float32)
    return pl.pallas_call(
        functools.partial(weight_grad_kernel, rows, pb, pa, tiles, chains),
        grid_spec=pltpu.PrefetchScalarGridSpec(
            num_scalar_prefetch=1,
            grid=(total,),
            in_specs=[pl.BlockSpec((height, tokens), lambda i, *_: (0, 0))]
            + [spec(r, f, c) for r, f, c in zip(rights, firsts, tiles)],
            out_specs=[out, out],
        ),
        out_shape=[shape, shape],
        compiler_params=params(62),
        name="weight_grad",
    )(table, turned, *arrays)


def gains_kernel(*refs):
    for row, ref in enumerate(refs[:-1]):
        refs[-1][row] = ref[...].astype(jnp.float32)


def gains_together(*gains):
    vmem = pl.BlockSpec(memory_space=pltpu.VMEM)
    return pl.pallas_call(
        gains_kernel,
        in_specs=[vmem] * len(gains),
        out_specs=vmem,
        out_shape=sds((len(gains), D), jnp.float32),
        name="gains",
    )(*gains)


PACK = 896


def permitted_mask(question_ref, length_ref, answer_rows, passages):
    row = lax.broadcasted_iota(jnp.int32, (answer_rows, PL), 0)
    place = lax.broadcasted_iota(jnp.int32, (answer_rows, PL), 1)
    whose = row // ANS
    return jnp.concatenate(
        [(whose == question_ref[p]) & (place < length_ref[p]) for p in range(passages)], axis=1
    )


def cross_part_kernel(question_ref, length_ref, q_ref, ck_ref, cv_ref, part_ref, stats_ref, all_ref):
    pair = pl.program_id(0)
    rows = q_ref.shape[0]
    mask = permitted_mask(question_ref, length_ref, rows, ck_ref.shape[0] // PL)
    lane = lax.broadcasted_iota(jnp.int32, (rows, 128), 1)

    @pl.when(pair == 0)
    def _():
        all_ref[...] = jnp.zeros_like(all_ref)

    q = q_ref[...]
    k = ck_ref[...]
    v = cv_ref[...]
    stats = all_ref[...]
    outs = []
    for head in range(2):
        s = jnp.where(mask, 0.125 * nt(head_lanes(q, head), k), -1e9)
        top = jnp.max(s, axis=1, keepdims=True)
        e = jnp.exp(s - top)
        total = jnp.sum(e, axis=1, keepdims=True)
        outs.append(nn(to_low(e), v))
        place = 2 * pair + head
        stats = jnp.where(lane == place, top, jnp.where(lane == HEADS + place, total, stats))
    all_ref[...] = stats
    part = jnp.where(lane < HEAD, outs[0], outs[1])
    each = part_ref.shape[1]
    for r in range(part_ref.shape[0]):
        part_ref[r] = part[r * each : (r + 1) * each]
        stats_ref[r] = stats[r * each : (r + 1) * each]


def cross_part(pa, question_of, lengths, q, ck, cv):
    smem = pl.BlockSpec(memory_space=pltpu.SMEM)
    rows, tokens = q.shape[0], ck.shape[0]
    short = pl.BlockSpec((rows, 128), lambda h: (0, h))
    tall = pl.BlockSpec((tokens, 128), lambda h: (0, h))
    return pl.pallas_call(
        cross_part_kernel,
        grid=(HEADS // 2,),
        in_specs=[smem, smem, short, tall, tall],
        out_specs=[pl.BlockSpec((pa, rows // pa, 128), lambda h: (0, 0, h)), pl.BlockSpec((pa, rows // pa, 128), lambda h: (0, 0, 0))],
        out_shape=[sds((pa, rows // pa, D), jnp.float32), sds((pa, rows // pa, 128), jnp.float32)],
        scratch_shapes=[pltpu.VMEM((rows, 128), jnp.float32)],
        compiler_params=params(62),
        name="cross_part",
    )(question_of, lengths, q, ck, cv)


def over_heads(stats, rows):
    lane = lax.broadcasted_iota(jnp.int32, (rows, 128), 1)
    return jnp.concatenate(
        [jnp.where(lane < HEAD, stats[:, 2 * g : 2 * g + 1], stats[:, 2 * g + 1 : 2 * g + 2]) for g in range(HEADS // 2)],
        axis=1,
    )


def merge_kernel(pa, sums_ref, stats_ref, out_ref, part_ref, recv_ref, mine_ref, send_sem, recv_sem, send2_sem, recv2_sem):
    me = lax.axis_index("pa")
    rows = part_ref.shape[1]
    part_ref[:, :, :D] = sums_ref[...]
    part_ref[:, :, D:] = stats_ref[...]
    barrier = pltpu.get_barrier_semaphore()
    for off in range(1, pa):
        pl.semaphore_signal(barrier, inc=1, device_id={"pa": lax.rem(me + off, pa)}, device_id_type=pl.DeviceIdType.MESH)
    pl.semaphore_wait(barrier, pa - 1)

    def first(off):
        peer = lax.rem(me + off, pa)
        return pltpu.make_async_remote_copy(
            src_ref=part_ref.at[peer], dst_ref=recv_ref.at[off], send_sem=send_sem.at[off], recv_sem=recv_sem.at[off],
            device_id={"pa": peer}, device_id_type=pl.DeviceIdType.MESH,
        )

    def second(off):
        peer = lax.rem(me + off, pa)
        return pltpu.make_async_remote_copy(
            src_ref=mine_ref, dst_ref=out_ref.at[me], send_sem=send2_sem.at[off], recv_sem=recv2_sem.at[off],
            device_id={"pa": peer}, device_id_type=pl.DeviceIdType.MESH,
        )

    for off in range(1, pa):
        first(off).start()
    recv_ref[0] = part_ref[me]
    for off in range(1, pa):
        first(off).wait()
    tops = [recv_ref[i, :, D : D + 128][:, :HEADS] for i in range(pa)]
    top = tops[0]
    for t in tops[1:]:
        top = jnp.maximum(top, t)
    total = jnp.zeros((rows, HEADS), jnp.float32)
    acc = jnp.zeros((rows, D), jnp.float32)
    for i in range(pa):
        w = jnp.exp(tops[i] - top)
        total = total + w * recv_ref[i, :, D : D + 128][:, HEADS : 2 * HEADS]
        acc = acc + over_heads(w, rows) * recv_ref[i, :, :D]
    mine_ref[:, :D] = acc / over_heads(total, rows)
    lse = top + jnp.log(total)
    mine_ref[:, D:] = jnp.concatenate([lse, jnp.zeros((rows, 128 - HEADS), jnp.float32)], axis=1)
    for off in range(1, pa):
        second(off).start()
    out_ref[me] = mine_ref[...]
    for off in range(1, pa):
        second(off).wait()


def merge(part, stats, pa):
    rows = part.shape[1]
    answer_rows = pa * rows
    block = (pa, rows, PACK)
    vmem = pl.BlockSpec(memory_space=pltpu.VMEM)
    out = pl.pallas_call(
        functools.partial(merge_kernel, pa),
        in_specs=[vmem, vmem],
        out_specs=vmem,
        out_shape=sds(block, jnp.float32),
        scratch_shapes=[
            pltpu.VMEM(block, jnp.float32),
            pltpu.VMEM(block, jnp.float32),
            pltpu.VMEM((rows, PACK), jnp.float32),
            pltpu.SemaphoreType.DMA((pa,)),
            pltpu.SemaphoreType.DMA((pa,)),
            pltpu.SemaphoreType.DMA((pa,)),
            pltpu.SemaphoreType.DMA((pa,)),
        ],
        compiler_params=pltpu.CompilerParams(collective_id=0, has_side_effects=True, vmem_limit_bytes=16 * MIB),
        name="cross_merge",
    )(part, stats)
    return out.reshape(answer_rows, PACK)


def cross_back_kernel(question_ref, length_ref, q_ref, ck_ref, cv_ref, grad_ref, att_ref, lse_ref, gq_ref, gkv_ref):
    pair = pl.program_id(0)
    rows = q_ref.shape[0]
    mask = permitted_mask(question_ref, length_ref, rows, ck_ref.shape[0] // PL)
    lane = lax.broadcasted_iota(jnp.int32, (rows, 128), 1)
    q = q_ref[...]
    k = ck_ref[...]
    v = cv_ref[...]
    g = grad_ref[...]
    weighed = g.astype(jnp.float32) * att_ref[...]
    gqs = []
    scores = []
    probs = []
    for head in range(2):
        lse = jnp.sum(jnp.where(lane == 2 * pair + head, lse_ref[...], 0.0), axis=1, keepdims=True)
        s = jnp.where(mask, 0.125 * nt(head_lanes(q, head), k), -1e9)
        p = jnp.exp(s - lse)
        dp = nt(head_lanes(g, head), v)
        delta = jnp.sum(head_lanes(weighed, head), axis=1, keepdims=True)
        ds = to_low(p * (dp - delta))
        gqs.append(nn(ds, k))
        scores.append(ds)
        probs.append(to_low(p))
    gq_ref[...] = 0.125 * jnp.where(lane < HEAD, gqs[0], gqs[1])
    both_q = jnp.concatenate([head_lanes(q, 0), head_lanes(q, 1)], axis=0)
    both_g = jnp.concatenate([head_lanes(g, 0), head_lanes(g, 1)], axis=0)
    gkv_ref[0] = to_low(0.125 * product_tn(jnp.concatenate(scores, axis=0), both_q))
    gkv_ref[1] = to_low(product_tn(jnp.concatenate(probs, axis=0), both_g))


def cross_back(question_of, lengths, q, ck, cv, grad, merged):
    smem = pl.BlockSpec(memory_space=pltpu.SMEM)
    rows, tokens = q.shape[0], ck.shape[0]
    short = pl.BlockSpec((rows, 128), lambda h: (0, h))
    tall = pl.BlockSpec((tokens, 128), lambda h: (0, h))
    return pl.pallas_call(
        cross_back_kernel,
        grid=(HEADS // 2,),
        in_specs=[smem, smem, short, tall, tall, short, short, pl.BlockSpec((rows, 128), lambda h: (0, D // 128))],
        out_specs=[short, pl.BlockSpec((2, tokens, 128), lambda h: (0, 0, h))],
        out_shape=[sds((rows, D), jnp.float32), sds((2, tokens, D), jnp.bfloat16)],
        compiler_params=params(62),
        name="cross_back",
    )(question_of, lengths, q, ck, cv, grad, merged, merged)


def causal_row(length):
    table = np.zeros((128, BUCKETS), np.float32)
    for back in range(length):
        table[-back % 128, bucket_of(-back, False)] = 1.0
    return table


def in_three(values):
    high = to_low(values)
    rest = values - high.astype(jnp.float32)
    middle = to_low(rest)
    return high, middle, to_low(rest - middle.astype(jnp.float32))


def dec_pre_kernel(
    x_ref, gains_ref, bias_ref, table_ref, wq_ref, wk_ref, wv_ref, wo_ref, wcq_ref,
    low_ref, q_ref, k_ref, v_ref, probs_ref, att_ref, mid_ref, cross_low_ref, cross_q_ref,
):
    rows = x_ref.shape[0]
    base = nn(bias_ref[...], table_ref[...])
    x = x_ref[...].astype(jnp.float32)
    normed, _ = rms(x, gain_of(gains_ref, GAIN_SELF))
    low = to_low(normed)
    low_ref[...] = low
    q = to_low(0.125 * to_low(nn(low, wq_ref[...])).astype(jnp.float32))
    k = to_low(nn(low, wk_ref[...]))
    v = to_low(nn(low, wv_ref[...]))
    q_ref[...] = q
    k_ref[...] = k
    v_ref[...] = v
    i = lax.broadcasted_iota(jnp.int32, (rows, rows), 0)
    j = lax.broadcasted_iota(jnp.int32, (rows, rows), 1)
    mask = (j <= i) & (i // ANS == j // ANS)
    lane = lax.broadcasted_iota(jnp.int32, (rows, 128), 1)
    for pair in range(HEADS // 2):
        cols = slice(pair * 128, (pair + 1) * 128)
        outs = []
        for half in range(2):
            head = 2 * pair + half
            spread = jnp.broadcast_to(base[head : head + 1, :], (rows, 128))
            bias = pltpu.roll(spread, 0, 1, stride=1, stride_axis=0)[:, :rows]
            s = jnp.where(mask, nt(head_lanes(q[:, cols], half), k[:, cols]) + bias, -1e9)
            e = jnp.exp(s - jnp.max(s, axis=1, keepdims=True))
            p = e / jnp.sum(e, axis=1, keepdims=True)
            probs_ref[head] = p
            outs.append(nn(to_low(p), v[:, cols]))
        att_ref[:, cols] = to_low(jnp.where(lane < HEAD, outs[0], outs[1]))
    mid = x + nn(att_ref[...], wo_ref[...])
    mid_ref[...] = mid
    normed, _ = rms(mid, gain_of(gains_ref, GAIN_CROSS))
    low = to_low(normed)
    cross_low_ref[...] = low
    cross_q_ref[...] = to_low(nn(low, wcq_ref[...]))


def in_vmem(kernel, outs, name, *args, smem=0):
    vmem = pl.BlockSpec(memory_space=pltpu.VMEM)
    return pl.pallas_call(
        kernel,
        in_specs=[pl.BlockSpec(memory_space=pltpu.SMEM)] * smem + [vmem] * (len(args) - smem),
        out_specs=[vmem] * len(outs),
        out_shape=outs,
        compiler_params=params(62),
        name=name,
    )(*args)


def dec_pre(x, gains, bias, table, wq, wk, wv, wo, wcq):
    rows = x.shape[0]
    low = sds((rows, D), jnp.bfloat16)
    full = sds((rows, D), jnp.float32)
    outs = [low, low, low, low, sds((HEADS, rows, rows), jnp.float32), low, full, low, low]
    return in_vmem(dec_pre_kernel, outs, "dec_pre", x, gains, bias, table, wq, wk, wv, wo, wcq)


def dec_mid_kernel(
    merged_ref, mid_ref, cot_ref, gains_ref, wco_ref, win_ref, wout_ref,
    out_ref, low_ref, hidden_ref, pre_grad_ref, after_low_ref, grad_after_ref, att_grad_ref, gain_grad_ref, slope_ref,
):
    rows = mid_ref.shape[0]
    three = nn(jnp.concatenate(in_three(merged_ref[:, :D]), axis=0), wco_ref[...])
    after = mid_ref[...] + (three[:rows] + three[rows : 2 * rows] + three[2 * rows :])
    normed, scale = rms(after, gain_of(gains_ref, GAIN_DFFN))
    low = to_low(normed)
    low_ref[...] = low
    y = after
    width = 768
    chunks = [slice(c * width, (c + 1) * width) for c in range(win_ref.shape[1] // width)]
    for cols in chunks:
        hidden, slope = gelu_both(nn(low, win_ref[:, cols]))
        hidden = to_low(hidden)
        hidden_ref[:, cols] = hidden
        slope_ref[:, cols] = slope
        y = y + nn(hidden, wout_ref[cols, :])
    out_ref[...] = to_low(y)
    cot = cot_ref[...]
    acc = None
    for cols in chunks:
        pre = to_low(slope_ref[:, cols] * nt(cot, wout_ref[cols, :]))
        pre_grad_ref[:, cols] = pre
        part = nt(pre, win_ref[:, cols])
        acc = part if acc is None else acc + part
    back, gain_grad = rms_back(after, scale, gain_of(gains_ref, GAIN_DFFN), acc)
    gain_grad_ref[...] = gain_grad
    grad_after = cot.astype(jnp.float32) + back
    grad_after_ref[...] = grad_after
    after_low = to_low(grad_after)
    after_low_ref[...] = after_low
    att_grad_ref[...] = to_low(nt(after_low, wco_ref[...]))


def dec_mid_call(merged, mid, cot, gain, wco, win, wout):
    rows = mid.shape[0]
    ff = win.shape[1]
    low = sds((rows, D), jnp.bfloat16)
    full = sds((rows, D), jnp.float32)
    wide = sds((rows, ff), jnp.bfloat16)
    outs = [low, low, wide, wide, low, full, low, sds((1, D), jnp.float32)]
    vmem = pl.BlockSpec(memory_space=pltpu.VMEM)
    return pl.pallas_call(
        dec_mid_kernel,
        in_specs=[vmem] * 7,
        out_specs=[vmem] * len(outs),
        out_shape=outs,
        scratch_shapes=[pltpu.VMEM((rows, ff), jnp.float32)],
        compiler_params=params(62),
        name="dec_mid",
    )(merged, mid, cot, gain, wco, win, wout)


def dec_post_kernel(
    gq_ref, grad_after_ref, mid_ref, x_ref, q_ref, k_ref, v_ref, probs_ref, gains_ref,
    wq_ref, wk_ref, wv_ref, wo_ref, wcq_ref, after_ref,
    mid_low_ref, dq_ref, dk_ref, dv_ref, out_ref, gain_self_grad_ref, gain_cross_grad_ref, fold_ref,
):
    rows = x_ref.shape[0]
    mid = mid_ref[...]
    scale = lax.rsqrt(jnp.mean(mid * mid, axis=-1, keepdims=True) + epsilon)
    three = nt(jnp.concatenate(in_three(gq_ref[...]), axis=0), wcq_ref[...])
    back, gain_grad = rms_back(mid, scale, gain_of(gains_ref, GAIN_CROSS), three[:rows] + three[rows : 2 * rows] + three[2 * rows :])
    gain_cross_grad_ref[...] = gain_grad
    grad_mid = grad_after_ref[...] + back
    mid_low = to_low(grad_mid)
    mid_low_ref[...] = mid_low
    att_grad = to_low(nt(mid_low, wo_ref[...]))
    lane = lax.broadcasted_iota(jnp.int32, (rows, 128), 1)
    row8 = lax.broadcasted_iota(jnp.int32, (8, 128), 0)
    for pair in range(HEADS // 2):
        cols = slice(pair * 128, (pair + 1) * 128)
        q = q_ref[:, cols]
        k = k_ref[:, cols]
        v = v_ref[:, cols]
        g = att_grad[:, cols]
        dqs = []
        scores = []
        probs = []
        for half in range(2):
            head = 2 * pair + half
            p = probs_ref[head]
            dp = nt(head_lanes(g, half), v)
            ds = p * (dp - jnp.sum(p * dp, axis=1, keepdims=True))
            wide = jnp.concatenate([ds, jnp.zeros((rows, 128 - rows), jnp.float32)], axis=1)
            total = wide[0:8]
            for group in range(1, rows // 8):
                total = total + pltpu.roll(wide[group * 8 : group * 8 + 8], 128 - group * 8, 1)
            for bit in (1, 2, 4):
                total = jnp.where((row8 // bit) % 2 == 1, pltpu.roll(total, 128 - bit, 1), total)
            fold_ref[head : head + 1, :] = jnp.sum(total, axis=0, keepdims=True)
            ds = to_low(ds)
            dqs.append(nn(ds, k))
            scores.append(ds)
            probs.append(to_low(p))
        dq_ref[:, cols] = to_low(0.125 * jnp.where(lane < HEAD, dqs[0], dqs[1]))
        both_q = jnp.concatenate([head_lanes(q, 0), head_lanes(q, 1)], axis=0)
        both_g = jnp.concatenate([head_lanes(g, 0), head_lanes(g, 1)], axis=0)
        dk_ref[:, cols] = to_low(product_tn(jnp.concatenate(scores, axis=0), both_q))
        dv_ref[:, cols] = to_low(product_tn(jnp.concatenate(probs, axis=0), both_g))
    x = x_ref[...].astype(jnp.float32)
    scale = lax.rsqrt(jnp.mean(x * x, axis=-1, keepdims=True) + epsilon)
    grad = nt(dq_ref[...], wq_ref[...]) + nt(dk_ref[...], wk_ref[...]) + nt(dv_ref[...], wv_ref[...])
    back, gain_grad = rms_back(x, scale, gain_of(gains_ref, GAIN_SELF), grad)
    gain_self_grad_ref[...] = gain_grad
    out_ref[...] = grad_mid + back


def dec_post(gq, grad_after, mid, x, q, k, v, probs, gains, wq, wk, wv, wo, wcq, after):
    rows = x.shape[0]
    low = sds((rows, D), jnp.bfloat16)
    gain = sds((1, D), jnp.float32)
    outs = [low, low, low, low, sds((rows, D), jnp.float32), gain, gain, sds((HEADS, 128), jnp.float32)]
    vmem = pl.BlockSpec(memory_space=pltpu.VMEM)
    return pl.pallas_call(
        dec_post_kernel,
        in_specs=[vmem] * 14 + [pl.BlockSpec(memory_space=pl.ANY)],
        out_specs=[vmem] * len(outs),
        out_shape=outs,
        compiler_params=params(62),
        name="dec_post",
    )(gq, grad_after, mid, x, q, k, v, probs, gains, wq, wk, wv, wo, wcq, after)


def dec_weight_kernel(
    pb, pa, place_ref, low_ref, dq_ref, dk_ref, dv_ref, att_ref, mid_low_ref, cross_low_ref, gq_ref, merged_ref, after_low_ref,
    hidden_ref, cot_ref, dffn_low_ref, pre_grad_ref, keep_ref, send_ref, turned_ref, wide_ref,
):
    shards = pb * pa
    column = place_ref[0]
    core = place_ref[1]
    rows = D // shards
    depth = low_ref.shape[0]

    def own(left, scratch):
        height = left.shape[1]
        here = height // shards
        span = left.shape[0]
        scratch[:, :span] = left.astype(jnp.float32).T
        cut = [scratch[pl.ds((b * pa + column) * here, here), :span] for b in range(pb)]
        return to_low(jnp.concatenate(cut, axis=0)), here

    first = 0

    def put(values, here):
        nonlocal first
        for y in range(pb // 2):
            low_part = values[2 * y * here : (2 * y + 1) * here]
            high_part = values[(2 * y + 1) * here : (2 * y + 2) * here]
            slot = place_ref[2 + y]
            keep_ref[slot, first : first + here, :] = jnp.where(core == 0, low_part, high_part)
            send_ref[slot, first : first + here, :] = jnp.where(core == 0, high_part, low_part)
        first += here

    left, here = own(low_ref[...], turned_ref)
    for right_ref in (dq_ref, dk_ref, dv_ref):
        put(nn(left, right_ref[...]), here)
    left, here = own(att_ref[...], turned_ref)
    put(nn(left, mid_low_ref[...]), here)
    left, here = own(cross_low_ref[...], turned_ref)
    a, b, c = in_three(gq_ref[...])
    put(nn(left, a) + nn(left, b) + nn(left, c), here)
    right = after_low_ref[...]
    a, b, c = (own(part, turned_ref)[0] for part in in_three(merged_ref[:, :D]))
    put(nn(a, right) + nn(b, right) + nn(c, right), here)
    left, wide = own(hidden_ref[...], wide_ref)
    put(nn(left, cot_ref[...]), wide)
    left, here = own(dffn_low_ref[...], turned_ref)
    for c in range(pre_grad_ref.shape[1] // D):
        put(nn(left, pre_grad_ref[:, c * D : (c + 1) * D]), here)


def dec_weight_grads(pb, pa, place, *args):
    rows, ff = args[-1].shape
    shards = pb * pa
    height = (6 * D + ff + ff) // shards
    vmem = pl.BlockSpec(memory_space=pltpu.VMEM)
    return pl.pallas_call(
        functools.partial(dec_weight_kernel, pb, pa),
        in_specs=[pl.BlockSpec(memory_space=pltpu.SMEM)] + [vmem] * len(args),
        out_specs=[vmem, vmem],
        out_shape=[sds((pb // 2, height, D), jnp.float32)] * 2,
        scratch_shapes=[pltpu.VMEM((D, rows), jnp.float32), pltpu.VMEM((ff, rows), jnp.float32)],
        compiler_params=params(62),
        name="dec_weight_grads",
    )(place, *args)


def finish_kernel(pb, pa, heights, cuts, small_ref, dec_ref, enc_table_ref, dec_table_ref, *refs):
    pieces, big_ref, outs = refs[: len(cuts)], refs[len(cuts)], refs[len(cuts) + 1 :]
    outs[-1][...] = big_ref[...]

    @pl.when(pl.program_id(0) == 0)
    def _():
        finish_small(pb, pa, heights, small_ref, dec_ref, enc_table_ref, dec_table_ref, pieces, cuts, outs)


def finish_small(pb, pa, heights, small_ref, dec_ref, enc_table_ref, dec_table_ref, pieces, cuts, outs):
    shards = pb * pa
    shard = lax.axis_index("pb") * pa + lax.axis_index("pa")
    width = D // shards
    rolled = pltpu.roll(small_ref[0:8, :D], lax.rem(D - shard * width, D), 1)
    for r in range(6):
        outs[r][...] = rolled[r, :width]
    share = BUCKETS * HEADS // shards
    bucket = shard * share // HEADS
    head = lax.rem(shard * share, HEADS)

    def bias_grad(folded, table_ref, out_ref):
        table = table_ref[...]
        by_bucket = sum(nt(table, part) for part in in_three(folded))
        row = lax.broadcasted_iota(jnp.int32, by_bucket.shape, 0)
        mine = jnp.sum(jnp.where(row == bucket, by_bucket, 0.0), axis=0, keepdims=True)
        mine = jnp.concatenate([mine, jnp.zeros((1, 128 - HEADS), jnp.float32)], axis=1)
        mine = jnp.broadcast_to(mine, (8, 128))
        out_ref[...] = pltpu.roll(mine, lax.rem(128 - head, 128), 1)[0, :share]

    bias_grad(small_ref[8 : 8 + HEADS, :], enc_table_ref, outs[6])
    dec_fold = jnp.concatenate([small_ref[0:6, D : D + 128], small_ref[0:6, D + 128 : D + 256]], axis=0)
    bias_grad(dec_fold, dec_table_ref, outs[7])
    first = 0
    for number, height in enumerate(heights):
        outs[8 + number][...] = dec_ref[first : first + height]
        first += height
    at = 8 + len(heights)
    wide_ref = outs[at]
    for c in range(wide_ref.shape[1] // D):
        wide_ref[:, c * D : (c + 1) * D] = dec_ref[first : first + width]
        first += width
    for piece_ref, count in zip(pieces, cuts):
        columns = piece_ref.shape[1] // count
        for c in range(count):
            at += 1
            outs[at][...] = piece_ref[:, c * columns : (c + 1) * columns]


def finish(pb, pa, small, dec_sum, enc_table, dec_table, ff, pieces, cuts, big):
    shards = pb * pa
    width = D // shards
    share = BUCKETS * HEADS // shards
    heights = [width] * 6 + [ff // shards]
    outs = [sds((width,), jnp.float32)] * 6 + [sds((share,), jnp.float32)] * 2
    outs += [sds((h, D), jnp.float32) for h in heights] + [sds((width, ff), jnp.float32)]
    for piece, count in zip(pieces, cuts):
        outs += [sds((piece.shape[0], piece.shape[1] // count), jnp.float32)] * count
    args = [small, dec_sum, enc_table, dec_table, *pieces]
    tile = pl.BlockSpec((256, big.shape[1]), lambda i: (i, 0))
    return pl.pallas_call(
        functools.partial(finish_kernel, pb, pa, heights, cuts),
        grid=(big.shape[0] // 256,),
        in_specs=[whole(a) for a in args] + [tile],
        out_specs=[whole(o) for o in outs] + [tile],
        out_shape=outs + [sds(big.shape, big.dtype)],
        compiler_params=params(62),
        name="finish",
    )(*args, big)


def bits_of(mesh_sizes):
    pb, pa = mesh_sizes
    pb_bits = pb.bit_length() - 1
    pa_bits = pa.bit_length() - 1
    ys = [("pb", b) for b in range(1, pb_bits)]
    xs = [("pa", b) for b in range(pa_bits - 2)]
    zs = [("pa", b) for b in range(pa_bits - 2, pa_bits)]
    return xs, ys, zs


def orders_of(mesh_sizes):
    xs, ys, zs = bits_of(mesh_sizes)
    return (xs + ys + zs, ys + xs + zs, zs[:1] + xs + ys + zs[1:], zs[:1] + ys + xs + zs[1:])


def exchange_table(mesh_sizes, orders):
    pb, pa = mesh_sizes
    pb_me = lax.axis_index("pb")
    pa_me = lax.axis_index("pa")
    cells = np.arange(pb * pa // 2)
    pb_of = jnp.asarray(cells // pa * 2)
    pa_of = jnp.asarray(cells % pa)
    rows = [jnp.full((cells.size,), pb_me % 2, jnp.int32)]
    for order in orders:
        slot = jnp.zeros((cells.size,), jnp.int32)
        for axis, bit in order:
            far = ((pb_of if axis == "pb" else pa_of) >> bit) ^ ((pb_me if axis == "pb" else pa_me) >> bit)
            slot = slot * 2 + (far & 1).astype(jnp.int32)
        rows.append(slot)
    return jnp.stack(rows)


MESH = pl.DeviceIdType.MESH
LINK = 0.11
PAIR = 0.45
NEAR = ("pb", 0)


def link_of(step, sizes):
    xs, ys, zs = bits_of(sizes)
    if step == NEAR:
        return "core"
    if step in ys:
        return "y"
    if step in xs:
        return "x"
    return "z far" if step == zs[-1] else "z"


def link_time(step, megabytes, sizes, rate=None):
    if step == NEAR:
        return megabytes / PAIR
    return 2 * megabytes * (2 if step == bits_of(sizes)[2][-1] else 1) / (rate or LINK)


class Piece:
    def __init__(self, array, first, width, order, place=None, start=0.0, met=False):
        self.array, self.first, self.width, self.order = array, first, width, [NEAR] + list(order)
        self.place, self.start, self.met = place, start, met


DEPTH = 3


def block_of(piece, shapes):
    return tuple(shapes[piece.array][:2]) + (piece.width,)


def plan(pieces, shapes, sizes, rate=None):
    free, held, queues = {}, {}, {}
    pending = [(piece.start, i, "ready", 0) for i, piece in enumerate(pieces)]
    events = []

    def key_of(what, i, step):
        return ("load", block_of(pieces[i], shapes)) if what == "load" else link_of(pieces[i].order[step], sizes)

    def start(now, what, i, step, starts):
        key = key_of(what, i, step)
        if key != "core" and held.get(key, 0) >= (1 if what == "load" else DEPTH):
            queues.setdefault(key, []).append((what, i, step))
            return
        held[key] = held.get(key, 0) + 1
        half, rows = shapes[pieces[i].array][:2]
        megabytes = (half >> step) * rows * pieces[i].width * 4e-6
        begin = max(now, free.get(key, 0.0))
        if what == "load":
            free[key] = begin + 1.0 + megabytes * 0.8
            pending.append((free[key], i, "loaded", 0))
        else:
            free[key] = begin + link_time(pieces[i].order[step], megabytes, sizes, rate)
            pending.append((free[key] + 1.5, i, "arrived", step))
        starts.append((what, i, step))

    while pending:
        pending.sort()
        now, i, what, step = pending.pop(0)
        starts = []
        if what != "ready":
            key = key_of("load" if what == "loaded" else "send", i, step)
            held[key] -= 1
            if queues.get(key):
                start(now, *queues[key].pop(0), starts)
        if what == "ready":
            start(now, "load" if pieces[i].met else "send", i, 0, starts)
        elif what == "arrived" and step == 0:
            start(now, "load", i, 0, starts)
        elif what == "loaded":
            start(now + 0.5, "send", i, 1, starts)
        elif step + 1 < len(pieces[i].order):
            start(now + 0.5, "send", i, step + 1, starts)
        events.append((now, what, i, step, starts))
    return events


def partner(step):
    axis, bit = step
    me = lax.axis_index(axis)
    size = 1 << bit
    there = me + size - 2 * size * lax.rem(me // size, 2)
    return {"pb": lax.axis_index("pb"), "pa": lax.axis_index("pa"), axis: there}


def all_steps(sizes):
    xs, ys, zs = bits_of(sizes)
    return [NEAR] + xs + ys + zs


def greet(sizes):
    barrier = pltpu.get_barrier_semaphore()
    for step in all_steps(sizes):
        pl.semaphore_signal(barrier, inc=1, device_id=partner(step), device_id_type=MESH)
    pl.semaphore_wait(barrier, len(all_steps(sizes)))


class Exchange:
    def __init__(self, sizes, pieces, shapes, rate=None):
        self.sizes, self.pieces, self.shapes = sizes, pieces, shapes
        self.events = plan(pieces, shapes, sizes, rate)
        self.stages = len(all_steps(sizes))
        self.arrays = range(len(shapes))
        self.own = [a for a in self.arrays if any(p.array == a and p.place is not None for p in pieces)]
        self.block = [block_of(pieces[self.of(a)[0]], shapes) for a in self.arrays]
        self.blocks = sorted(set(self.block))
        self.before = {}
        for n, a in enumerate(self.own):
            earlier = [b for b in self.own[:n] if self.block[b] == self.block[a]]
            if earlier:
                self.before[a] = earlier[-1]

    def of(self, array):
        return [i for i, p in enumerate(self.pieces) if p.array == array]

    def scratch(self):
        out = [pltpu.VMEM(block, jnp.float32) for block in self.blocks]
        for array in self.arrays:
            half, *block = self.block[array]
            count = len(self.of(array))
            out += [
                pltpu.VMEM((count, half, *block), jnp.float32),
                pltpu.VMEM((count, half - 1, *block), jnp.float32),
            ]
        count = len(self.pieces)
        return out + [
            pltpu.SemaphoreType.DMA((count,)),
            pltpu.SemaphoreType.DMA((count,)),
            pltpu.SemaphoreType.DMA((count, self.stages)),
            pltpu.SemaphoreType.DMA((count, self.stages)),
        ]

    def bind(self, keeps, sends, nears, outs, staging, scratch):
        self.keeps, self.sends, self.nears, self.outs, self.staging = keeps, sends, nears, outs, staging
        places = dict(zip(self.blocks, scratch))
        self.loaded = [places[block] for block in self.block]
        scratch = scratch[len(self.blocks) :]
        self.kept = [scratch[2 * a] for a in self.arrays]
        recvs = [scratch[2 * a + 1] for a in self.arrays]
        self.near_sems, self.keep_sems, self.send_sems, self.recv_sems = scratch[2 * len(self.shapes) :]
        self.bufs, self.recvs = {}, {}
        for array in self.arrays:
            for number, i in enumerate(self.of(array)):
                self.bufs[i], self.recvs[i] = self.kept[array].at[number], recvs[array].at[number]

    def loads(self, i):
        piece = self.pieces[i]
        cols = pl.ds(piece.first, piece.width)
        out = [pltpu.make_async_copy(self.nears[piece.array].at[:, :, cols], self.loaded[piece.array], self.near_sems.at[i])]
        if piece.place is None:
            out.append(pltpu.make_async_copy(self.keeps[piece.array].at[:, :, cols], self.bufs[i], self.keep_sems.at[i]))
        return out

    def sizes_of(self, i, step):
        half = self.shapes[self.pieces[i].array][0]
        count = half >> step
        return count, half - 2 * count

    def copy(self, i, step):
        piece = self.pieces[i]
        count, first = self.sizes_of(i, step)
        if step == 0:
            if piece.place is None:
                source = self.sends[piece.array].at[:, :, pl.ds(piece.first, piece.width)]
            else:
                source = self.staging[piece.array].at[piece.place % 2]
            target = self.nears[piece.array].at[:, :, pl.ds(piece.first, piece.width)]
        else:
            source = self.bufs[i].at[pl.ds(count, count)]
            target = self.recvs[i].at[pl.ds(first, count)]
        return pltpu.make_async_remote_copy(
            src_ref=source, dst_ref=target, send_sem=self.send_sems.at[i, step], recv_sem=self.recv_sems.at[i, step],
            device_id=partner(piece.order[step]), device_id_type=MESH,
        )

    def free_staging(self, array, place):
        if place >= 2:
            self.copy(self.of(array)[place - 2], 0).wait_send()
        elif array in self.before:
            self.copy([i for i in self.of(self.before[array]) if self.pieces[i].place % 2 == place][-1], 0).wait_send()

    def event(self, what, i, step, starts):
        piece = self.pieces[i]
        buf = self.bufs[i]
        last = what == "arrived" and step + 1 == len(piece.order)
        count = 0
        if what == "loaded":
            for load in self.loads(i):
                load.wait()
            source, first, count = self.loaded[piece.array], 0, self.shapes[piece.array][0]
        elif what == "arrived":
            self.copy(i, step).wait_recv()
            if step > 0:
                source = self.recvs[i]
                count, first = self.sizes_of(i, step)

        def add(slot, _):
            buf[slot] = buf[slot] + source[first + slot]
            return 0

        if last:
            self.outs[piece.array][:, piece.first : piece.first + piece.width] = buf[0] + source[first]
        elif count:
            lax.fori_loop(count // 2, count, add, 0, unroll=min(4, count // 2))
        mine = [s for s in starts if s[0] == "send"]
        for _, j, k in mine:
            self.copy(j, k).start()
        if not last and count:
            lax.fori_loop(0, count // 2, add, 0, unroll=min(4, count // 2))
        for kind, j, _ in starts:
            if kind == "load":
                for load in self.loads(j):
                    load.start()

    def finish(self):
        for i, piece in enumerate(self.pieces):
            waited = piece.place is not None and (
                piece.place + 2 < len(self.of(piece.array)) or piece.array in self.before.values()
            )
            first = 1 if waited or piece.met else 0
            for step in range(first, len(piece.order)):
                self.copy(i, step).wait_send()

    def points(self, times, ready):
        out = [[] for _ in times]
        place = 0
        for when, what, i, step, starts in self.events:
            while place < len(times) - 1 and times[place] < when:
                place += 1
            if what == "ready" and i in ready:
                place = max(place, ready[i])
            out[place].append((what, i, step, starts))
        return out
class Everywhere:
    def __init__(self, steps, shape):
        self.steps = steps
        self.shape = shape

    def scratch(self):
        count = len(self.steps)
        return [
            pltpu.VMEM((count + 1,) + self.shape, jnp.float32),
            pltpu.VMEM((count,) + self.shape, jnp.float32),
            pltpu.SemaphoreType.DMA((count,)),
            pltpu.SemaphoreType.DMA((count,)),
        ]

    def bind(self, scratch):
        self.sums, self.recvs, self.send_sems, self.recv_sems = scratch

    def copy(self, k):
        return pltpu.make_async_remote_copy(
            src_ref=self.sums.at[k], dst_ref=self.recvs.at[k], send_sem=self.send_sems.at[k], recv_sem=self.recv_sems.at[k],
            device_id=partner(self.steps[k]), device_id_type=MESH,
        )

    def arrive(self, k):
        self.copy(k).wait_recv()
        self.sums[k + 1] = self.sums[k] + self.recvs[k]
        if k + 1 < len(self.steps):
            self.copy(k + 1).start()

    def finish(self):
        for k in range(len(self.steps)):
            self.copy(k).wait_send()


SMALL = (24, 1024)
ATTN_STEP = 3.6
OPENING = 7.0
TILE_US = 0.0052
BACK_STEP = 1.2


def slots_of(sizes, order):
    pb, pa = sizes
    far = {}
    for axis, bit in order:
        me = lax.rem(lax.axis_index(axis) // (1 << bit), 2)
        far[axis, bit] = (me, 1 - me)
    cells = []
    for y in range(pb // 2):
        for a in range(pa):
            slot = 0
            for axis, bit in order:
                slot = slot * 2 + far[axis, bit][(2 * y if axis == "pb" else a) >> bit & 1]
            cells.append(slot)
    return cells


def outside_pieces(orders, groups):
    pieces = []
    for number, (_, _, met, chains, width) in enumerate(groups):
        for c, chain in enumerate(chains):
            order = chain if isinstance(chain, list) else orders[chain]
            pieces.append(Piece(number, c * width, width, order, start=0.1 * number + 0.01 * c, met=met))
    return pieces


def back_host_kernel(adding, sizes, *refs):
    own, part_ref, outs, total_ref, scratch = refs[:11], refs[11], refs[12:19], refs[19], refs[20:]
    adding.bind(scratch)
    step = pl.program_id(0)
    last = pl.num_programs(0) - 1
    steps = len(adding.steps)

    @pl.when(step == 0)
    def _():
        adding.sums[0] = part_ref[...]
        greet(sizes)
        adding.copy(0).start()

    for k in range(steps - 1):

        @pl.when(step == jnp.minimum(k + 1, last))
        def _(k=k):
            adding.arrive(k)

    back_kernel(*own, *outs)

    @pl.when(step == last)
    def _():
        adding.arrive(steps - 1)
        total_ref[...] = adding.sums[steps]
        adding.finish()


def post_backward(sizes, part, gkv, y, mid, slope, cot, gains, wck, wcv, wout, win, wo):
    tokens = y.shape[0]
    tile = 256
    ff = win.shape[1]
    low = sds((tokens, D), jnp.bfloat16)
    d = rows_of(tile, D)
    f = rows_of(tile, ff)
    gain = pl.BlockSpec((1, D), lambda i: (0, 0))
    xs, _, zs = bits_of(sizes)
    adding = Everywhere(xs + zs, part.shape)

    def once(array):
        return pl.BlockSpec(array.shape, lambda i: (0,) * array.ndim, pipeline_mode=pl.Buffered(1))

    return pl.pallas_call(
        functools.partial(back_host_kernel, adding, sizes),
        grid=(tokens // tile,),
        in_specs=[pl.BlockSpec((2, tile, D), lambda i: (0, i, 0)), d, d, f, d] + [once(a) for a in (gains, wck, wcv, wout, win, wo, part)],
        out_specs=[d, f, d, d, d, gain, gain, pl.BlockSpec(part.shape, lambda i: (0, 0))],
        out_shape=[low, sds((tokens, ff), jnp.bfloat16), low, sds((tokens, D), jnp.float32), low]
        + [sds((1, D), jnp.float32)] * 2
        + [sds(part.shape, jnp.float32)],
        scratch_shapes=adding.scratch(),
        compiler_params=pltpu.CompilerParams(collective_id=3, has_side_effects=True, vmem_limit_bytes=62 * MIB),
        name="enc_post_back",
    )(gkv, y, mid, slope, cot, gains, wck, wcv, wout, win, wo, part)


class Phase:
    def __init__(self, name, first, count, us):
        self.name, self.first, self.count, self.us = name, first, count, us


def last_kernel(
    exchange, everywhere, points, orders, phases, passages, share, outside, gradients,
    lengths_ref, q_ref, k_ref, v_ref, o_ref, do_ref, lse_ref, base_ref, x_ref, grad_mid_ref, gains_ref, wq_ref, wk_ref, wv_ref,
    dec_fold_ref, *refs,
):
    refs = list(refs)

    def take(count):
        out = refs[:count]
        del refs[:count]
        return out

    gains = take(5)
    lefts = take(len(gradients))
    rights = take(len(gradients) - 1)
    keeps, others = take(len(outside)), take(len(outside))
    out_ref, small_ref = take(2)
    moved = take(len(exchange.shapes))
    nears = [other if met else take(1)[0] for other, met in zip(others, outside)] + take(len(gradients))
    strip_ref, gather_ref, dqT_ref, grads_ref, fold_ref, gain_grad_ref = take(6)
    staging = {}
    for array in exchange.own:
        staging[array] = staging[exchange.before[array]] if array in exchange.before else take(1)[0]
    everywhere.bind(take(4))
    exchange.bind(keeps, others, nears, moved, staging, refs)
    step = pl.program_id(0)
    sizes = exchange.sizes
    pb, pa = sizes

    @pl.when(step == 0)
    def _():
        greet(sizes)
        for event in points["start"][0]:
            exchange.event(*event)

    def run(place):
        for at, events in points.get(place, {}).items():
            if events:

                @pl.when(step == at)
                def _(events=events):
                    for event in events:
                        exchange.event(*event)

    def attention(phase):
        number = step - phase.first
        pair = number // passages
        passage = lax.rem(number, passages)
        place = pl.ds(pl.multiple_of(passage * PL, PL), PL), pl.ds(pl.multiple_of(pair * 128, 128), 128)
        attn_backward_kernel(
            lambda head: run(("attention", head)), passage, passages, lengths_ref, q_ref, k_ref, v_ref, o_ref, do_ref, lse_ref, base_ref,
            grads_ref.at[(0,) + place], grads_ref.at[(1,) + place], grads_ref.at[(2,) + place], fold_ref.at[pl.ds(pair, 1)],
            strip_ref, gather_ref, dqT_ref,
        )

    def gradient(phase, array, left_ref, right_ref):
        number = step - phase.first
        width = exchange.pieces[exchange.of(array)[0]].width
        if right_ref is None:
            each = D // width
            column = pl.ds(pl.multiple_of(lax.rem(number, each) * width, width), width)
            right = grads_ref[number // each, :, column]
        else:
            right = right_ref[...]
        for place in range(0 if array in exchange.before else 2, phase.count):

            @pl.when(number == place)
            def _(place=place):
                exchange.free_staging(array, place)

        chain = 0
        for place, c in enumerate(gradients[array - len(outside)][3]):
            chain = jnp.where(number == place, c, chain)
        choices = [slots_of(sizes, order) for order in orders]
        core = lax.rem(lax.axis_index("pb"), 2)
        rows = exchange.shapes[array][1]
        half_rows = pa * rows
        kept, staged = exchange.kept[array], exchange.staging[array]
        for y in range(pb // 2):
            low_part = nn(left_ref[2 * y * half_rows : (2 * y + 1) * half_rows, :], right)
            high_part = nn(left_ref[(2 * y + 1) * half_rows : (2 * y + 2) * half_rows, :], right)
            mine = jnp.where(core == 0, low_part, high_part)
            other = jnp.where(core == 0, high_part, low_part)
            for a in range(pa):
                slot = choices[0][y * pa + a]
                for c in range(1, len(orders)):
                    slot = jnp.where(chain == c, choices[c][y * pa + a], slot)
                kept[number, slot] = mine[a * rows : (a + 1) * rows]
                staged[lax.rem(number, 2), slot] = other[a * rows : (a + 1) * rows]

    def back(phase):
        height = x_ref.shape[0]
        rows = pl.ds(pl.multiple_of((step - phase.first) * height, height), height)
        qkv_back_kernel(
            step == phase.first, grads_ref.at[0, rows], grads_ref.at[1, rows], grads_ref.at[2, rows],
            x_ref, grad_mid_ref, gains_ref, wq_ref, wk_ref, wv_ref, out_ref, gain_grad_ref,
        )

    for phase in phases:

        @pl.when((step >= phase.first) & (step < phase.first + phase.count))
        def _(phase=phase):
            if phase.name == "attention":
                attention(phase)
            elif phase.name == "back":
                back(phase)
            else:
                k = phase.name
                gradient(phase, exchange.own[k], lefts[k], rights[k] if k < len(rights) else None)

    run("end")

    @pl.when(step == pl.num_programs(0) - 1)
    def _():
        first = everywhere.sums
        first[0] = jnp.zeros(SMALL, jnp.float32)
        first[0, 0:1, :D] = gain_grad_ref[...]
        for r, ref in enumerate(gains):
            first[0, r + 1 : r + 2, :D] = ref[...] if r < 2 else ref[...] * share
        for pair in range(HEADS // 2):
            first[0, 8 + 2 * pair : 10 + 2 * pair, :] = fold_ref[pair]
        for part in range(2):
            lanes = slice(D + part * 128, D + (part + 1) * 128)
            first[0, 0:6, lanes] = dec_fold_ref[6 * part : 6 * part + 6] * share
        everywhere.copy(0).start()
        left = points["rest"]
        steps = len(everywhere.steps)
        every = max(1, len(left) // (steps + 1))
        done = 0
        for n, event in enumerate(left):
            if n % every == every - 1 and done < steps:
                everywhere.arrive(done)
                done += 1
            exchange.event(*event)
        for k in range(done, steps):
            everywhere.arrive(k)
        small_ref[...] = everywhere.sums[steps]
        exchange.finish()
        everywhere.finish()


def last_part(
    sizes, orders, groups, gradients, lengths, q, k, v, o, do, lse, base, x, grad_mid, gains, wq, wk, wv, dec_fold, grads_of_gains,
):
    pb, pa = sizes
    passages = lengths.shape[0]
    tokens = x.shape[0]
    pairs = HEADS // 2
    tile_rows = 128
    half = pb * pa // 2
    shapes = [g[0].shape for g in groups]
    widths = [right.shape[1] if right is not None else 3 * D for _, right, *_ in gradients]
    shapes += [(half, left.shape[0] // (pb * pa), w) for (left, *_), w in zip(gradients, widths)]

    phases = []
    names = list(range(len(gradients) - 1)) + ["attention", len(gradients) - 1, "back"]
    step = 0
    for name in names:
        if name == "attention":
            count, us = pairs * passages, ATTN_STEP
        elif name == "back":
            count, us = tokens // tile_rows, BACK_STEP
        else:
            count, us = widths[name] // gradients[name][2], TILE_US * gradients[name][2]
        phases.append(Phase(name, step, count, us))
        step += count
    steps = step
    pieces = outside_pieces(orders, groups)
    times, labels, ready = [OPENING], [("start", 0)], {}
    now = OPENING
    for phase in phases:
        for n in range(phase.count):
            number = phase.first + n
            if phase.name == "attention":
                times += [now, now + phase.us / 2]
                labels += [(("attention", 0), number), (("attention", 1), number)]
            now += phase.us
            if phase.name != "attention" and number < steps - 1:
                times.append(now)
                labels.append(("end", number))
            if isinstance(phase.name, int):
                ready[len(pieces)] = len(times) - 1
                width = gradients[phase.name][2]
                pieces.append(Piece(len(groups) + phase.name, n * width, width, orders[gradients[phase.name][3][n]], n, now))
    exchange = Exchange(sizes, pieces, shapes)
    everywhere = Everywhere(all_steps(sizes), SMALL)
    points = {}
    found = exchange.points(times + [1e9], ready)
    for (place, number), events in zip(labels, found):
        points.setdefault(place, {})[number] = events
    points["rest"] = found[-1]
    by_name = {phase.name: phase for phase in phases}

    def at(name, i):
        phase = by_name[name]
        return jnp.clip(i - phase.first, 0, phase.count - 1)

    def pair_of(i):
        return at("attention", i) // passages

    def passage_of(i):
        return lax.rem(at("attention", i), passages)

    def once(array):
        return pl.BlockSpec(array.shape, lambda i: (0,) * array.ndim, pipeline_mode=pl.Buffered(1))

    tile = pl.BlockSpec((PL, 128), lambda i: (passage_of(i), pair_of(i)))
    rows = pl.BlockSpec((tile_rows, D), lambda i: (at("back", i), 0))
    hbm = pl.BlockSpec(memory_space=pl.ANY)
    keeps, others = [g[0] for g in groups], [g[1] for g in groups]
    outside = [g[2] for g in groups]
    lefts = [left for left, *_ in gradients]
    rights = [right for _, right, *_ in gradients[:-1]]
    right_specs = [
        pl.BlockSpec((tokens, width), lambda i, name=name: (0, at(name, i)), pipeline_mode=pl.Buffered(1)) for name, (_, _, width, _) in enumerate(gradients[:-1])
    ]
    own_shapes = shapes[len(groups) :]
    near_shapes = [s for s, met in zip(shapes, outside) if not met] + own_shapes
    return pl.pallas_call(
        functools.partial(
            last_kernel, exchange, everywhere, points, orders, phases, passages, 1.0 / pa, outside, gradients
        ),
        grid=(steps,),
        in_specs=[pl.BlockSpec(memory_space=pltpu.SMEM)]
        + [tile] * 5
        + [pl.BlockSpec((1, 1, 2, PL), lambda i: (pair_of(i), passage_of(i), 0, 0)), pl.BlockSpec((1, 2, WIDE), lambda i: (pair_of(i), 0, 0))]
        + [rows, rows]
        + [once(a) for a in (gains, wq, wk, wv, dec_fold) + tuple(grads_of_gains)]
        + [once(left) for left in lefts]
        + right_specs
        + [hbm] * (2 * len(groups)),
        out_specs=[rows, pl.BlockSpec(SMALL, lambda i: (0, 0), pipeline_mode=pl.Buffered(1))]
        + [pl.BlockSpec(s[1:], lambda i: (0, 0), pipeline_mode=pl.Buffered(1)) for s in shapes]
        + [hbm] * len(near_shapes),
        out_shape=[sds((tokens, D), jnp.float32), sds(SMALL, jnp.float32)]
        + [sds(s[1:], jnp.float32) for s in shapes]
        + [sds(s, jnp.float32) for s in near_shapes],
        scratch_shapes=[
            pltpu.VMEM((2, STRIP, WIDE), jnp.float32),
            pltpu.VMEM((2, STRIP, WIDE), jnp.float32),
            pltpu.VMEM((128, PL), jnp.bfloat16),
            pltpu.VMEM((3, tokens, D), jnp.bfloat16),
            pltpu.VMEM((pairs, 2, WIDE), jnp.float32),
            pltpu.VMEM((1, D), jnp.float32),
        ]
        + [pltpu.VMEM((2,) + exchange.block[a], jnp.float32) for a in exchange.own if a not in exchange.before]
        + everywhere.scratch()
        + exchange.scratch(),
        compiler_params=pltpu.CompilerParams(collective_id=1, has_side_effects=True, vmem_limit_bytes=63 * MIB + MIB // 2),
        name="enc_last",
    )(
        lengths, q, k, v, o, do, lse, base, x, grad_mid, gains, wq, wk, wv, dec_fold, *grads_of_gains, *lefts, *rights, *keeps, *others
    )[: 2 + len(shapes)]


def exchange_kernel(exchange, arrays, *refs):
    exchange.bind(refs[:arrays], {}, refs[arrays : 2 * arrays], refs[2 * arrays : 3 * arrays], {}, refs[3 * arrays :])
    greet(exchange.sizes)
    for _, *event in exchange.events:
        exchange.event(*event)
    exchange.finish()


def exchange_only(sizes, orders, groups):
    shapes = [g[0].shape for g in groups]
    exchange = Exchange(sizes, outside_pieces(orders, groups), shapes)
    return pl.pallas_call(
        functools.partial(exchange_kernel, exchange, len(groups)),
        in_specs=[pl.BlockSpec(memory_space=pl.ANY)] * (2 * len(groups)),
        out_specs=[pl.BlockSpec(memory_space=pltpu.VMEM)] * len(groups),
        out_shape=[sds(s[1:], jnp.float32) for s in shapes],
        scratch_shapes=exchange.scratch(),
        compiler_params=pltpu.CompilerParams(collective_id=2, has_side_effects=True, vmem_limit_bytes=63 * MIB),
        name="exchange",
    )(*[g[0] for g in groups], *[g[1] for g in groups])


def local(
    pb, pa,
    enc_in, dec_in, question_of, lengths, enc_gain_attn, enc_query, enc_key, enc_value, enc_output, enc_bias,
    enc_gain_ffn, enc_ff_in, enc_ff_out, enc_gain_final, cross_key, cross_value, dec_gain_self, dec_query, dec_key,
    dec_value, dec_output, dec_bias, dec_gain_cross, cross_query, cross_output, dec_gain_ffn, dec_ff_in, dec_ff_out,
    enc_cot, dec_cot,
):
    sizes = (pb, pa)
    orders = orders_of(sizes)
    answer_rows = dec_in.shape[0]
    gains = gains_together(enc_gain_attn, enc_gain_ffn, enc_gain_final, dec_gain_self, dec_gain_cross, dec_gain_ffn)
    table = exchange_table(sizes, orders)
    enc_table = jnp.asarray(strip_table().T, jnp.bfloat16)
    dec_table = jnp.asarray(causal_row(ANS).T, jnp.bfloat16)

    attn_turned, enc_queries, enc_keys, enc_values = qkv_forward(enc_in, gains, enc_query, enc_key, enc_value)
    enc_attended, attended_turned, enc_lse, base = attn_forward(lengths, enc_queries, enc_keys, enc_values, enc_bias.T, enc_table)
    enc_mid, ffn_turned, hidden_turned, enc_slope, enc_y, enc_out, final_turned, cross_keys, cross_values = post_forward(
        enc_in, enc_attended, gains, enc_output, enc_ff_in, enc_ff_out, cross_key, cross_value
    )

    self_low, dec_queries, dec_keys, dec_values, dec_probs, dec_attended, dec_mid, cross_low, cross_queries = dec_pre(
        dec_in, gains, dec_bias.T, dec_table, dec_query, dec_key, dec_value, dec_output, cross_query
    )

    merged = merge(*cross_part(pa, question_of, lengths, cross_queries, cross_keys, cross_values), pa)
    dec_out, dffn_low, dec_hidden, pre_grad_low, after_low, grad_after, cross_att_grad, dec_gain_ffn_grad = dec_mid_call(
        merged, dec_mid, dec_cot, gains, cross_output, dec_ff_in, dec_ff_out
    )
    query_part, grad_cross = cross_back(
        question_of, lengths, cross_queries, cross_keys, cross_values, cross_att_grad, merged
    )
    def near(terms):
        keep, send = terms
        return keep, lax.ppermute(send, "pb", [(i, i ^ 1) for i in range(pb)])

    cross_terms = near(weight_grad(table, final_turned, [(grad_cross, 0), (grad_cross, 1)], pb, pa, 256, (0, 0, 1, 1, 2, 2)))
    eout_low, epre_low, emid_low, grad_enc_mid, enc_att_grad, final_gain_grad, ffn_gain_grad, grad_cross_q = post_backward(
        sizes, query_part,
        grad_cross, enc_y, enc_mid, enc_slope, enc_cot, gains, cross_key, cross_value, enc_ff_out, enc_ff_in, enc_output,
    )
    out_terms = near(weight_grad(table, hidden_turned, [eout_low], pb, pa, 256, (0, 1, 3)))

    mid_low, grad_dq, grad_dk, grad_dv, dec_in_grad, dec_gain_self_grad, dec_gain_cross_grad, dec_fold = dec_post(
        grad_cross_q, grad_after, dec_mid, dec_in, dec_queries, dec_keys, dec_values, dec_probs, gains,
        dec_query, dec_key, dec_value, dec_output, cross_query, out_terms[0],
    )
    far = lax.axis_index("pb") // 2
    places = [lax.axis_index("pa"), lax.axis_index("pb") % 2]
    for y in range(pb // 2):
        slot = 0
        for _, bit in bits_of(sizes)[1]:
            slot = slot * 2 + ((far >> (bit - 1)) + (y >> (bit - 1))) % 2
        places.append(slot)
    dec_terms = dec_weight_grads(
        pb, pa, jnp.stack(places).astype(jnp.int32), self_low, grad_dq, grad_dk, grad_dv, dec_attended, mid_low, cross_low, grad_cross_q,
        merged, after_low, dec_hidden, dec_cot, dffn_low, pre_grad_low,
    )
    ys = bits_of(sizes)[1]
    groups = [
        cross_terms + (True, (0, 1, 2), 512),
        out_terms + (True, (0, 1, 3), 256),
        tuple(dec_terms) + (False, (ys, ys, ys), 256),
    ]
    gradients = [
        (ffn_turned, epre_low, 512, (0, 1, 2, 0, 1, 3)),
        (attended_turned, emid_low, 256, (0, 1, 2)),
        (attn_turned, None, 256, (0, 1, 2, 0, 1, 3, 0, 1, 2)),
    ]
    roomy = D // (pb * pa) % 8 == 0
    if not roomy:
        del gradients[0]
        keep, send = weight_grad(table, ffn_turned, [epre_low], pb, pa, 512, (0, 0, 1, 1, 2, 2))
        in_terms = keep, lax.ppermute(send, "pb", [(i, i ^ 1) for i in range(pb)])
    enc_in_grad, small, *summed = last_part(
        sizes, orders, groups, gradients, lengths, enc_queries, enc_keys, enc_values, enc_attended, enc_att_grad, enc_lse, base,
        enc_in, grad_enc_mid, gains, enc_query, enc_key, enc_value, dec_fold,
        (ffn_gain_grad, final_gain_grad, dec_gain_self_grad, dec_gain_cross_grad, dec_gain_ffn_grad),
    )
    if not roomy:
        summed[3:3] = exchange_only(sizes, orders, [tuple(in_terms) + (True, (0, 1, 2), 1024)])
    cross_sum, ff_out_sum, dec_sum, *summed = summed
    ends = finish(
        pb, pa, small, dec_sum, enc_table, dec_table, dec_hidden.shape[1], [cross_sum, ff_out_sum] + summed, [2, 1, 1, 1, 3], enc_in_grad
    )
    gain_grads, (enc_bias_grad, dec_bias_grad), got = ends[:6], ends[6:8], ends[8:16]
    cross_key_grad, cross_value_grad, ff_out_grad, ff_in_grad, output_grad, query_grad, key_grad, value_grad, enc_in_grad = ends[16:]

    return (
        enc_out, dec_out, enc_in_grad, dec_in_grad,
        gain_grads[0], query_grad, key_grad, value_grad, output_grad, enc_bias_grad,
        gain_grads[1], ff_in_grad, ff_out_grad, gain_grads[2], cross_key_grad, cross_value_grad,
        gain_grads[3], got[0], got[1], got[2], got[3], dec_bias_grad, gain_grads[4], got[4], got[5], gain_grads[5], got[7], got[6],
    )


def solution(mesh):
    pb, pa = mesh.shape["pb"], mesh.shape["pa"]
    rows = P(("pb", "pa"), None)
    flat = P(("pb", "pa"))
    dec = P("pb", None)
    return jax.shard_map(
        functools.partial(local, pb, pa),
        mesh=mesh,
        in_specs=(rows, dec, flat, flat) + (P(),) * 24 + (rows, dec),
        out_specs=(rows, dec, rows, dec)
        + (flat, rows, rows, rows, rows, flat, flat, rows, rows, flat, rows, rows)
        + (flat, rows, rows, rows, rows, flat, flat, rows, rows, flat, rows, rows),
        check_vma=False,
    )
```

```python
import functools
import math

import jax
import jax.numpy as jnp
import numpy as np
from jax import lax
from jax.experimental import pallas as pl
from jax.experimental.pallas import tpu as pltpu
from jax.sharding import PartitionSpec as P

D = 768
HEADS = 12
HEAD = 64
BUCKETS = 32
PL = 512
ANS = 24

far_distance = 128
epsilon = 1e-06
highest = lax.Precision.HIGHEST


def bucket_of(offset, bidirectional):
    if bidirectional:
        halves = BUCKETS // 2
        base_bucket = halves if offset > 0 else 0
        distance = abs(offset)
    else:
        halves = BUCKETS
        base_bucket = 0
        distance = max(-offset, 0)
    exact_count = halves // 2
    if distance < exact_count:
        return base_bucket + distance
    scaled = (
        math.log(distance / exact_count)
        / math.log(far_distance / exact_count)
        * (halves - exact_count)
    )
    return base_bucket + min(exact_count + int(scaled), halves - 1)


def to_low(values):
    return values.astype(jnp.bfloat16)


def product_tn(left, right):
    return lax.dot_general(
        left, right, (((0,), (0,)), ((), ())), preferred_element_type=jnp.float32
    )


STRIP = 128
WIDE = 1024


def strip_table():
    table = np.zeros((WIDE, BUCKETS), np.float32)
    for place in range(WIDE):
        if place < PL + STRIP * 3:
            offset = PL - STRIP - place
        else:
            offset = PL - STRIP + WIDE - place
        if abs(offset) < PL:
            table[place, bucket_of(offset, True)] = 1.0
    return table


def nn(left, right):
    return lax.dot_general(left, right, (((1,), (0,)), ((), ())), preferred_element_type=jnp.float32)


def head_lanes(values, head):
    lane = lax.broadcasted_iota(jnp.int32, values.shape, 1)
    keep = lane < HEAD if head == 0 else lane >= HEAD
    return jnp.where(keep, values, jnp.zeros_like(values))


def key_mask(length):
    place = lax.broadcasted_iota(jnp.int32, (PL, 1), 0)
    return jnp.where(place < length, 0.0, -1e9)


def build_strip(base_ref, strip_ref):
    for head in range(2):
        row = base_ref[0, head : head + 1, :]
        spread = jnp.broadcast_to(row, (STRIP, WIDE))
        strip_ref[head] = pltpu.roll(spread, 0, 1, stride=1, stride_axis=0)


def attn_forward_kernel(lengths_ref, q_ref, k_ref, v_ref, bias_ref, table_ref, out_ref, turned_ref, lse_ref, base_ref, rows_ref, strip_ref, score_ref):
    passage = pl.program_id(1)

    @pl.when((passage == 0) & (pl.program_id(0) == 0))
    def _():
        every = nn(bias_ref[...], table_ref[...])
        for pair in range(HEADS // 2):
            rows_ref[pair] = every[2 * pair : 2 * pair + 2]

    base_ref[...] = rows_ref[pl.ds(pl.program_id(0), 1)]

    @pl.when(passage == 0)
    def _():
        build_strip(base_ref, strip_ref)

    mask = key_mask(lengths_ref[passage])
    q_t = q_ref[...].T
    v_t = v_ref[...].T
    k = k_ref[...]
    blocks = PL // STRIP
    for head in range(2):
        k_head = head_lanes(k, head)
        top = None
        for b in range(blocks):
            rows = slice(b * STRIP, (b + 1) * STRIP)
            start = PL - STRIP - b * STRIP
            s = nn(k_head[rows], q_t) + strip_ref[head, :, start : start + PL] + mask[rows]
            score_ref[head, rows, :] = s
            here = jnp.max(s, axis=0, keepdims=True)
            top = here if top is None else jnp.maximum(top, here)
        total = None
        acc = None
        for b in range(blocks):
            rows = slice(b * STRIP, (b + 1) * STRIP)
            e = jnp.exp(score_ref[head, rows, :] - top)
            here = jnp.sum(e, axis=0, keepdims=True)
            total = here if total is None else total + here
            part = nn(v_t[head * HEAD : (head + 1) * HEAD, rows], to_low(e))
            acc = part if acc is None else acc + part
        turned_ref[head * HEAD : (head + 1) * HEAD, :] = to_low(acc * (1.0 / total))
        lse_ref[0, 0, head : head + 1, :] = top + jnp.log(total)
    out_ref[...] = turned_ref[...].T


def attn_forward(lengths, q, k, v, bias, table):
    passages = lengths.shape[0]
    pairs = HEADS // 2
    tile = pl.BlockSpec((PL, 128), lambda h, p, *_: (p, h))
    return pl.pallas_call(
        attn_forward_kernel,
        grid_spec=pltpu.PrefetchScalarGridSpec(
            num_scalar_prefetch=1,
            grid=(pairs, passages),
            in_specs=[tile, tile, tile, pl.BlockSpec(bias.shape, lambda h, p, *_: (0, 0)), pl.BlockSpec(table.shape, lambda h, p, *_: (0, 0))],
            out_specs=[
                tile,
                pl.BlockSpec((128, PL), lambda h, p, *_: (h, p)),
                pl.BlockSpec((1, 1, 2, PL), lambda h, p, *_: (h, p, 0, 0)),
                pl.BlockSpec((1, 2, WIDE), lambda h, p, *_: (h, 0, 0)),
            ],
            scratch_shapes=[
                pltpu.VMEM((pairs, 2, WIDE), jnp.float32),
                pltpu.VMEM((2, STRIP, WIDE), jnp.float32),
                pltpu.VMEM((2, PL, PL), jnp.float32),
            ],
        ),
        out_shape=[
            jax.ShapeDtypeStruct((passages * PL, D), jnp.bfloat16),
            jax.ShapeDtypeStruct((D, passages * PL), jnp.bfloat16),
            jax.ShapeDtypeStruct((pairs, passages, 2, PL), jnp.float32),
            jax.ShapeDtypeStruct((pairs, 2, WIDE), jnp.float32),
        ],
        compiler_params=pltpu.CompilerParams(vmem_limit_bytes=62 * 2**20),
        name="enc_attention",
    )(lengths, q, k, v, bias, table)


def attn_backward_kernel(
    beside, passage, passages, lengths_ref, q_ref, k_ref, v_ref, o_ref, do_ref, lse_ref, base_ref,
    dq_ref, dk_ref, dv_ref, fold_ref,
    strip_ref, gather_ref, dqT_ref,
):
    @pl.when(passage == 0)
    def _():
        build_strip(base_ref, strip_ref)
        gather_ref[...] = jnp.zeros_like(gather_ref)

    mask = key_mask(lengths_ref[passage])
    q = q_ref[...]
    k = k_ref[...]
    v = v_ref[...]
    do = do_ref[...]
    q_t = q.T
    k_t = k.T
    do_t = do.T
    o_t = o_ref[...].T
    weighed = do_t.astype(jnp.float32) * o_t.astype(jnp.float32)
    blocks = PL // STRIP
    lane = lax.broadcasted_iota(jnp.int32, (STRIP, 128), 1)
    first = lane < HEAD
    dks = []
    dvs = []
    for head in range(2):
        beside(head)
        heads = slice(head * HEAD, (head + 1) * HEAD)
        delta = jnp.sum(weighed[heads], axis=0, keepdims=True)
        lse = lse_ref[0, 0, head : head + 1, :]
        k_head = head_lanes(k, head)
        v_head = head_lanes(v, head)
        acc = None
        for b in range(blocks):
            rows = slice(b * STRIP, (b + 1) * STRIP)
            start = PL - STRIP - b * STRIP
            s = nn(k_head[rows], q_t) + strip_ref[head, :, start : start + PL] + mask[rows]
            p = jnp.exp(s - lse)
            dp = nn(v_head[rows], do_t)
            ds = p * (dp - delta)
            gather_ref[head, :, start : start + PL] += ds
            ds_low = to_low(ds)
            dv_part = nn(to_low(p), do)
            dk_part = nn(ds_low, q)
            if head == 0:
                dvs.append(dv_part)
                dks.append(dk_part)
            else:
                dv_ref[rows, :] = to_low(jnp.where(first, dvs[b], dv_part))
                dk_ref[rows, :] = to_low(jnp.where(first, dks[b], dk_part))
            part = nn(k_t[heads, rows], ds_low)
            acc = part if acc is None else acc + part
        dqT_ref[heads, :] = to_low(0.125 * acc)
    dq_ref[...] = dqT_ref[...].T

    @pl.when(passage == passages - 1)
    def _():
        row = lax.broadcasted_iota(jnp.int32, (8, WIDE), 0)
        for head in range(2):
            total = gather_ref[head, 0:8, :]
            for group in range(1, STRIP // 8):
                total = total + pltpu.roll(gather_ref[head, group * 8 : group * 8 + 8, :], WIDE - group * 8, 1)
            for bit in (1, 2, 4):
                total = jnp.where((row // bit) % 2 == 1, pltpu.roll(total, WIDE - bit, 1), total)
            fold_ref[0, head : head + 1, :] = jnp.sum(total, axis=0, keepdims=True)


MIB = 2**20


def nt(left, right):
    return lax.dot_general(left, right, (((1,), (1,)), ((), ())), preferred_element_type=jnp.float32)


def rms(values, gain):
    scale = lax.rsqrt(jnp.mean(values * values, axis=-1, keepdims=True) + epsilon)
    return values * scale * gain, scale


def rms_back(values, scale, gain, grad):
    scaled = grad * gain
    gain_grad = jnp.sum(grad * values * scale, axis=0, keepdims=True)
    inner = jnp.mean(scaled * values, axis=-1, keepdims=True)
    return scaled * scale - values * (scale * scale * scale) * inner, gain_grad


def gelu_both(v):
    c = math.sqrt(2.0 / math.pi)
    square = v * v
    t = jnp.tanh(v * (c + (c * 0.044715) * square))
    half = 0.5 + 0.5 * t
    slope = half + (half * (1.0 - t)) * v * (c + (3.0 * 0.044715 * c) * square)
    return v * half, slope


GAIN_ATTN, GAIN_FFN, GAIN_FINAL, GAIN_SELF, GAIN_CROSS, GAIN_DFFN = range(6)


def gain_of(gains_ref, which):
    return gains_ref[which : which + 1, :]


def whole(array):
    return pl.BlockSpec(array.shape, lambda *_: (0,) * array.ndim)


def rows_of(tile, width):
    return pl.BlockSpec((tile, width), lambda i: (i, 0))


def sds(shape, kind):
    return jax.ShapeDtypeStruct(shape, kind)


def params(mib):
    return pltpu.CompilerParams(vmem_limit_bytes=mib * MIB)


def qkv_kernel(x_ref, gains_ref, wq_ref, wk_ref, wv_ref, turned_ref, q_ref, k_ref, v_ref):
    normed, _ = rms(x_ref[...].astype(jnp.float32), gain_of(gains_ref, GAIN_ATTN))
    low = to_low(normed)
    turned_ref[...] = low.T
    q_ref[...] = to_low(0.125 * to_low(nn(low, wq_ref[...])).astype(jnp.float32))
    k_ref[...] = to_low(nn(low, wk_ref[...]))
    v_ref[...] = to_low(nn(low, wv_ref[...]))


def qkv_forward(x, gains, wq, wk, wv):
    tokens = x.shape[0]
    tile = 256
    big = sds((tokens, D), jnp.bfloat16)
    return pl.pallas_call(
        qkv_kernel,
        grid=(tokens // tile,),
        in_specs=[rows_of(tile, D)] + [whole(a) for a in (gains, wq, wk, wv)],
        out_specs=[pl.BlockSpec((D, tile), lambda i: (0, i))] + [rows_of(tile, D)] * 3,
        out_shape=[sds((D, tokens), jnp.bfloat16)] + [big] * 3,
        compiler_params=params(62),
        name="enc_qkv",
    )(x, gains, wq, wk, wv)


def post_kernel(
    x_ref, att_ref, gains_ref, wo_ref, win_ref, wout_ref, wck_ref, wcv_ref,
    mid_ref, ffn_turned_ref, hidden_turned_ref, slope_ref, y_ref, out_ref, final_turned_ref, ck_ref, cv_ref,
):
    mid = x_ref[...].astype(jnp.float32) + nn(att_ref[...], wo_ref[...])
    mid_ref[...] = mid
    normed, _ = rms(mid, gain_of(gains_ref, GAIN_FFN))
    low = to_low(normed)
    ffn_turned_ref[...] = low.T
    y = mid
    width = 768
    for c in range(win_ref.shape[1] // width):
        cols = slice(c * width, (c + 1) * width)
        hidden, slope = gelu_both(nn(low, win_ref[:, cols]))
        hidden = to_low(hidden)
        hidden_turned_ref[cols, :] = hidden.T
        slope_ref[:, cols] = to_low(slope)
        y = y + nn(hidden, wout_ref[cols, :])
    y_ref[...] = y
    out_ref[...] = to_low(y)
    final, _ = rms(y, gain_of(gains_ref, GAIN_FINAL))
    final = to_low(final)
    final_turned_ref[...] = final.T
    ck_ref[...] = to_low(nn(final, wck_ref[...]))
    cv_ref[...] = to_low(nn(final, wcv_ref[...]))


def post_forward(x, att, gains, wo, win, wout, wck, wcv):
    tokens = x.shape[0]
    tile = 256
    ff = win.shape[1]
    low = sds((tokens, D), jnp.bfloat16)
    wide = sds((tokens, ff), jnp.bfloat16)
    full = sds((tokens, D), jnp.float32)
    d = rows_of(tile, D)
    f = rows_of(tile, ff)
    turned = pl.BlockSpec((D, tile), lambda i: (0, i))
    flat = sds((D, tokens), jnp.bfloat16)
    return pl.pallas_call(
        post_kernel,
        grid=(tokens // tile,),
        in_specs=[d, d] + [whole(a) for a in (gains, wo, win, wout, wck, wcv)],
        out_specs=[d, turned, pl.BlockSpec((ff, tile), lambda i: (0, i)), f, d, d, turned, d, d],
        out_shape=[full, flat, sds((ff, tokens), jnp.bfloat16), wide, full, low, flat, low, low],
        compiler_params=params(62),
        name="enc_post",
    )(x, att, gains, wo, win, wout, wck, wcv)


def back_kernel(
    gkv_ref, y_ref, mid_ref, slope_ref, cot_ref, gains_ref,
    wck_ref, wcv_ref, wout_ref, win_ref, wo_ref,
    eout_ref, epre_ref, emid_ref, grad_mid_ref, att_grad_ref, gain_final_grad_ref, gain_ffn_grad_ref,
):

    @pl.when(pl.program_id(0) == 0)
    def _():
        gain_final_grad_ref[...] = jnp.zeros_like(gain_final_grad_ref)
        gain_ffn_grad_ref[...] = jnp.zeros_like(gain_ffn_grad_ref)

    y = y_ref[...]
    scale = lax.rsqrt(jnp.mean(y * y, axis=-1, keepdims=True) + epsilon)
    final_back = nt(gkv_ref[0], wck_ref[...]) + nt(gkv_ref[1], wcv_ref[...])
    back, gain_grad = rms_back(y, scale, gain_of(gains_ref, GAIN_FINAL), final_back)
    gain_final_grad_ref[...] += gain_grad
    grad_y = cot_ref[...].astype(jnp.float32) + back
    eout = to_low(grad_y)
    eout_ref[...] = eout
    width = 768
    acc = None
    for c in range(win_ref.shape[1] // width):
        cols = slice(c * width, (c + 1) * width)
        epre = to_low(slope_ref[:, cols].astype(jnp.float32) * nt(eout, wout_ref[cols, :]))
        epre_ref[:, cols] = epre
        part = nt(epre, win_ref[:, cols])
        acc = part if acc is None else acc + part
    mid = mid_ref[...]
    scale = lax.rsqrt(jnp.mean(mid * mid, axis=-1, keepdims=True) + epsilon)
    back, gain_grad = rms_back(mid, scale, gain_of(gains_ref, GAIN_FFN), acc)
    gain_ffn_grad_ref[...] += gain_grad
    grad_mid = grad_y + back
    grad_mid_ref[...] = grad_mid
    emid = to_low(grad_mid)
    emid_ref[...] = emid
    att_grad_ref[...] = to_low(nt(emid, wo_ref[...]))


def qkv_back_kernel(opening, dq_ref, dk_ref, dv_ref, x_ref, grad_mid_ref, gains_ref, wq_ref, wk_ref, wv_ref, out_ref, gain_grad_ref):
    @pl.when(opening)
    def _():
        gain_grad_ref[...] = jnp.zeros_like(gain_grad_ref)

    x = x_ref[...].astype(jnp.float32)
    scale = lax.rsqrt(jnp.mean(x * x, axis=-1, keepdims=True) + epsilon)
    grad = nt(dq_ref[...], wq_ref[...]) + nt(dk_ref[...], wk_ref[...]) + nt(dv_ref[...], wv_ref[...])
    back, gain_grad = rms_back(x, scale, gain_of(gains_ref, GAIN_ATTN), grad)
    gain_grad_ref[...] += gain_grad
    out_ref[...] = grad_mid_ref[...] + back


def weight_grad_kernel(rows, pb, pa, tiles, chains, table_ref, turned_ref, *refs):
    rights = refs[: len(tiles)]
    keep_ref, send_ref = refs[-2:]
    step = pl.program_id(0)
    core = table_ref[0, 0]
    chain = chains[0]
    for place, c in enumerate(chains):
        chain = jnp.where(step == place, c, chain)
    half_rows = pa * rows

    def work(right):
        for y in range(pb // 2):
            low_part = nn(turned_ref[2 * y * half_rows : (2 * y + 1) * half_rows, :], right)
            high_part = nn(turned_ref[(2 * y + 1) * half_rows : (2 * y + 2) * half_rows, :], right)
            mine = jnp.where(core == 0, low_part, high_part)
            other = jnp.where(core == 0, high_part, low_part)
            for a in range(pa):
                slot = table_ref[chain + 1, y * pa + a]
                keep_ref[slot] = mine[a * rows : (a + 1) * rows]
                send_ref[slot] = other[a * rows : (a + 1) * rows]

    first = 0
    for right_ref, count in zip(rights, tiles):
        if len(tiles) == 1:
            work(right_ref[...])
        else:

            @pl.when((step >= first) & (step < first + count))
            def _(right_ref=right_ref):
                work(right_ref[...] if len(right_ref.shape) == 2 else right_ref[0])

        first += count


def weight_grad(table, turned, rights, pb, pa, width, chains):
    height, tokens = turned.shape
    rows = height // (pb * pa)
    arrays = [r[0] if isinstance(r, tuple) else r for r in rights]
    tiles = [a.shape[-1] // width for a in arrays]
    total = sum(tiles)
    firsts = np.cumsum([0] + tiles)[:-1]

    def spec(right, first, count):
        def column(i):
            return jnp.clip(i - int(first), 0, count - 1)

        if isinstance(right, tuple):
            return pl.BlockSpec((1, tokens, width), lambda i, *_: (right[1], 0, column(i)))
        return pl.BlockSpec((tokens, width), lambda i, *_: (0, column(i)))

    half = pb * pa // 2
    out = pl.BlockSpec((half, rows, width), lambda i, *_: (0, 0, i))
    shape = sds((half, rows, total * width), jnp.float32)
    return pl.pallas_call(
        functools.partial(weight_grad_kernel, rows, pb, pa, tiles, chains),
        grid_spec=pltpu.PrefetchScalarGridSpec(
            num_scalar_prefetch=1,
            grid=(total,),
            in_specs=[pl.BlockSpec((height, tokens), lambda i, *_: (0, 0))]
            + [spec(r, f, c) for r, f, c in zip(rights, firsts, tiles)],
            out_specs=[out, out],
        ),
        out_shape=[shape, shape],
        compiler_params=params(62),
        name="weight_grad",
    )(table, turned, *arrays)


def gains_kernel(*refs):
    for row, ref in enumerate(refs[:-1]):
        refs[-1][row] = ref[...].astype(jnp.float32)


def gains_together(*gains):
    vmem = pl.BlockSpec(memory_space=pltpu.VMEM)
    return pl.pallas_call(
        gains_kernel,
        in_specs=[vmem] * len(gains),
        out_specs=vmem,
        out_shape=sds((len(gains), D), jnp.float32),
        name="gains",
    )(*gains)


PACK = 896


def permitted_mask(question_ref, length_ref, answer_rows, passages):
    row = lax.broadcasted_iota(jnp.int32, (answer_rows, PL), 0)
    place = lax.broadcasted_iota(jnp.int32, (answer_rows, PL), 1)
    whose = row // ANS
    return jnp.concatenate(
        [(whose == question_ref[p]) & (place < length_ref[p]) for p in range(passages)], axis=1
    )


def cross_part_kernel(question_ref, length_ref, q_ref, ck_ref, cv_ref, part_ref, stats_ref, all_ref):
    pair = pl.program_id(0)
    rows = q_ref.shape[0]
    mask = permitted_mask(question_ref, length_ref, rows, ck_ref.shape[0] // PL)
    lane = lax.broadcasted_iota(jnp.int32, (rows, 128), 1)

    @pl.when(pair == 0)
    def _():
        all_ref[...] = jnp.zeros_like(all_ref)

    q = q_ref[...]
    k = ck_ref[...]
    v = cv_ref[...]
    stats = all_ref[...]
    outs = []
    for head in range(2):
        s = jnp.where(mask, 0.125 * nt(head_lanes(q, head), k), -1e9)
        top = jnp.max(s, axis=1, keepdims=True)
        e = jnp.exp(s - top)
        total = jnp.sum(e, axis=1, keepdims=True)
        outs.append(nn(to_low(e), v))
        place = 2 * pair + head
        stats = jnp.where(lane == place, top, jnp.where(lane == HEADS + place, total, stats))
    all_ref[...] = stats
    part = jnp.where(lane < HEAD, outs[0], outs[1])
    each = part_ref.shape[1]
    for r in range(part_ref.shape[0]):
        part_ref[r] = part[r * each : (r + 1) * each]
        stats_ref[r] = stats[r * each : (r + 1) * each]


def cross_part(pa, question_of, lengths, q, ck, cv):
    smem = pl.BlockSpec(memory_space=pltpu.SMEM)
    rows, tokens = q.shape[0], ck.shape[0]
    short = pl.BlockSpec((rows, 128), lambda h: (0, h))
    tall = pl.BlockSpec((tokens, 128), lambda h: (0, h))
    return pl.pallas_call(
        cross_part_kernel,
        grid=(HEADS // 2,),
        in_specs=[smem, smem, short, tall, tall],
        out_specs=[pl.BlockSpec((pa, rows // pa, 128), lambda h: (0, 0, h)), pl.BlockSpec((pa, rows // pa, 128), lambda h: (0, 0, 0))],
        out_shape=[sds((pa, rows // pa, D), jnp.float32), sds((pa, rows // pa, 128), jnp.float32)],
        scratch_shapes=[pltpu.VMEM((rows, 128), jnp.float32)],
        compiler_params=params(62),
        name="cross_part",
    )(question_of, lengths, q, ck, cv)


def over_heads(stats, rows):
    lane = lax.broadcasted_iota(jnp.int32, (rows, 128), 1)
    return jnp.concatenate(
        [jnp.where(lane < HEAD, stats[:, 2 * g : 2 * g + 1], stats[:, 2 * g + 1 : 2 * g + 2]) for g in range(HEADS // 2)],
        axis=1,
    )


def merge_kernel(pa, sums_ref, stats_ref, out_ref, part_ref, recv_ref, mine_ref, send_sem, recv_sem, send2_sem, recv2_sem):
    me = lax.axis_index("pa")
    rows = part_ref.shape[1]
    part_ref[:, :, :D] = sums_ref[...]
    part_ref[:, :, D:] = stats_ref[...]
    barrier = pltpu.get_barrier_semaphore()
    for off in range(1, pa):
        pl.semaphore_signal(barrier, inc=1, device_id={"pa": lax.rem(me + off, pa)}, device_id_type=pl.DeviceIdType.MESH)
    pl.semaphore_wait(barrier, pa - 1)

    def first(off):
        peer = lax.rem(me + off, pa)
        return pltpu.make_async_remote_copy(
            src_ref=part_ref.at[peer], dst_ref=recv_ref.at[off], send_sem=send_sem.at[off], recv_sem=recv_sem.at[off],
            device_id={"pa": peer}, device_id_type=pl.DeviceIdType.MESH,
        )

    def second(off):
        peer = lax.rem(me + off, pa)
        return pltpu.make_async_remote_copy(
            src_ref=mine_ref, dst_ref=out_ref.at[me], send_sem=send2_sem.at[off], recv_sem=recv2_sem.at[off],
            device_id={"pa": peer}, device_id_type=pl.DeviceIdType.MESH,
        )

    for off in range(1, pa):
        first(off).start()
    recv_ref[0] = part_ref[me]
    for off in range(1, pa):
        first(off).wait()
    tops = [recv_ref[i, :, D : D + 128][:, :HEADS] for i in range(pa)]
    top = tops[0]
    for t in tops[1:]:
        top = jnp.maximum(top, t)
    total = jnp.zeros((rows, HEADS), jnp.float32)
    acc = jnp.zeros((rows, D), jnp.float32)
    for i in range(pa):
        w = jnp.exp(tops[i] - top)
        total = total + w * recv_ref[i, :, D : D + 128][:, HEADS : 2 * HEADS]
        acc = acc + over_heads(w, rows) * recv_ref[i, :, :D]
    mine_ref[:, :D] = acc / over_heads(total, rows)
    lse = top + jnp.log(total)
    mine_ref[:, D:] = jnp.concatenate([lse, jnp.zeros((rows, 128 - HEADS), jnp.float32)], axis=1)
    for off in range(1, pa):
        second(off).start()
    out_ref[me] = mine_ref[...]
    for off in range(1, pa):
        second(off).wait()


def merge(part, stats, pa):
    rows = part.shape[1]
    answer_rows = pa * rows
    block = (pa, rows, PACK)
    vmem = pl.BlockSpec(memory_space=pltpu.VMEM)
    out = pl.pallas_call(
        functools.partial(merge_kernel, pa),
        in_specs=[vmem, vmem],
        out_specs=vmem,
        out_shape=sds(block, jnp.float32),
        scratch_shapes=[
            pltpu.VMEM(block, jnp.float32),
            pltpu.VMEM(block, jnp.float32),
            pltpu.VMEM((rows, PACK), jnp.float32),
            pltpu.SemaphoreType.DMA((pa,)),
            pltpu.SemaphoreType.DMA((pa,)),
            pltpu.SemaphoreType.DMA((pa,)),
            pltpu.SemaphoreType.DMA((pa,)),
        ],
        compiler_params=pltpu.CompilerParams(collective_id=0, has_side_effects=True, vmem_limit_bytes=16 * MIB),
        name="cross_merge",
    )(part, stats)
    return out.reshape(answer_rows, PACK)


def cross_back_kernel(question_ref, length_ref, q_ref, ck_ref, cv_ref, grad_ref, att_ref, lse_ref, gq_ref, gkv_ref):
    pair = pl.program_id(0)
    rows = q_ref.shape[0]
    mask = permitted_mask(question_ref, length_ref, rows, ck_ref.shape[0] // PL)
    lane = lax.broadcasted_iota(jnp.int32, (rows, 128), 1)
    q = q_ref[...]
    k = ck_ref[...]
    v = cv_ref[...]
    g = grad_ref[...]
    weighed = g.astype(jnp.float32) * att_ref[...]
    gqs = []
    scores = []
    probs = []
    for head in range(2):
        lse = jnp.sum(jnp.where(lane == 2 * pair + head, lse_ref[...], 0.0), axis=1, keepdims=True)
        s = jnp.where(mask, 0.125 * nt(head_lanes(q, head), k), -1e9)
        p = jnp.exp(s - lse)
        dp = nt(head_lanes(g, head), v)
        delta = jnp.sum(head_lanes(weighed, head), axis=1, keepdims=True)
        ds = to_low(p * (dp - delta))
        gqs.append(nn(ds, k))
        scores.append(ds)
        probs.append(to_low(p))
    gq_ref[...] = 0.125 * jnp.where(lane < HEAD, gqs[0], gqs[1])
    both_q = jnp.concatenate([head_lanes(q, 0), head_lanes(q, 1)], axis=0)
    both_g = jnp.concatenate([head_lanes(g, 0), head_lanes(g, 1)], axis=0)
    gkv_ref[0] = to_low(0.125 * product_tn(jnp.concatenate(scores, axis=0), both_q))
    gkv_ref[1] = to_low(product_tn(jnp.concatenate(probs, axis=0), both_g))


def cross_back(question_of, lengths, q, ck, cv, grad, merged):
    smem = pl.BlockSpec(memory_space=pltpu.SMEM)
    rows, tokens = q.shape[0], ck.shape[0]
    short = pl.BlockSpec((rows, 128), lambda h: (0, h))
    tall = pl.BlockSpec((tokens, 128), lambda h: (0, h))
    return pl.pallas_call(
        cross_back_kernel,
        grid=(HEADS // 2,),
        in_specs=[smem, smem, short, tall, tall, short, short, pl.BlockSpec((rows, 128), lambda h: (0, D // 128))],
        out_specs=[short, pl.BlockSpec((2, tokens, 128), lambda h: (0, 0, h))],
        out_shape=[sds((rows, D), jnp.float32), sds((2, tokens, D), jnp.bfloat16)],
        compiler_params=params(62),
        name="cross_back",
    )(question_of, lengths, q, ck, cv, grad, merged, merged)


def causal_row(length):
    table = np.zeros((128, BUCKETS), np.float32)
    for back in range(length):
        table[-back % 128, bucket_of(-back, False)] = 1.0
    return table


def in_three(values):
    high = to_low(values)
    rest = values - high.astype(jnp.float32)
    middle = to_low(rest)
    return high, middle, to_low(rest - middle.astype(jnp.float32))


def dec_pre_kernel(
    x_ref, gains_ref, bias_ref, table_ref, wq_ref, wk_ref, wv_ref, wo_ref, wcq_ref,
    low_ref, q_ref, k_ref, v_ref, probs_ref, att_ref, mid_ref, cross_low_ref, cross_q_ref,
):
    rows = x_ref.shape[0]
    base = nn(bias_ref[...], table_ref[...])
    x = x_ref[...].astype(jnp.float32)
    normed, _ = rms(x, gain_of(gains_ref, GAIN_SELF))
    low = to_low(normed)
    low_ref[...] = low
    q = to_low(0.125 * to_low(nn(low, wq_ref[...])).astype(jnp.float32))
    k = to_low(nn(low, wk_ref[...]))
    v = to_low(nn(low, wv_ref[...]))
    q_ref[...] = q
    k_ref[...] = k
    v_ref[...] = v
    i = lax.broadcasted_iota(jnp.int32, (rows, rows), 0)
    j = lax.broadcasted_iota(jnp.int32, (rows, rows), 1)
    mask = (j <= i) & (i // ANS == j // ANS)
    lane = lax.broadcasted_iota(jnp.int32, (rows, 128), 1)
    for pair in range(HEADS // 2):
        cols = slice(pair * 128, (pair + 1) * 128)
        outs = []
        for half in range(2):
            head = 2 * pair + half
            spread = jnp.broadcast_to(base[head : head + 1, :], (rows, 128))
            bias = pltpu.roll(spread, 0, 1, stride=1, stride_axis=0)[:, :rows]
            s = jnp.where(mask, nt(head_lanes(q[:, cols], half), k[:, cols]) + bias, -1e9)
            e = jnp.exp(s - jnp.max(s, axis=1, keepdims=True))
            p = e / jnp.sum(e, axis=1, keepdims=True)
            probs_ref[head] = p
            outs.append(nn(to_low(p), v[:, cols]))
        att_ref[:, cols] = to_low(jnp.where(lane < HEAD, outs[0], outs[1]))
    mid = x + nn(att_ref[...], wo_ref[...])
    mid_ref[...] = mid
    normed, _ = rms(mid, gain_of(gains_ref, GAIN_CROSS))
    low = to_low(normed)
    cross_low_ref[...] = low
    cross_q_ref[...] = to_low(nn(low, wcq_ref[...]))


def in_vmem(kernel, outs, name, *args, smem=0):
    vmem = pl.BlockSpec(memory_space=pltpu.VMEM)
    return pl.pallas_call(
        kernel,
        in_specs=[pl.BlockSpec(memory_space=pltpu.SMEM)] * smem + [vmem] * (len(args) - smem),
        out_specs=[vmem] * len(outs),
        out_shape=outs,
        compiler_params=params(62),
        name=name,
    )(*args)


def dec_pre(x, gains, bias, table, wq, wk, wv, wo, wcq):
    rows = x.shape[0]
    low = sds((rows, D), jnp.bfloat16)
    full = sds((rows, D), jnp.float32)
    outs = [low, low, low, low, sds((HEADS, rows, rows), jnp.float32), low, full, low, low]
    return in_vmem(dec_pre_kernel, outs, "dec_pre", x, gains, bias, table, wq, wk, wv, wo, wcq)


def dec_mid_kernel(
    merged_ref, mid_ref, cot_ref, gains_ref, wco_ref, win_ref, wout_ref,
    out_ref, low_ref, hidden_ref, pre_grad_ref, after_low_ref, grad_after_ref, att_grad_ref, gain_grad_ref, slope_ref,
):
    rows = mid_ref.shape[0]
    three = nn(jnp.concatenate(in_three(merged_ref[:, :D]), axis=0), wco_ref[...])
    after = mid_ref[...] + (three[:rows] + three[rows : 2 * rows] + three[2 * rows :])
    normed, scale = rms(after, gain_of(gains_ref, GAIN_DFFN))
    low = to_low(normed)
    low_ref[...] = low
    y = after
    width = 768
    chunks = [slice(c * width, (c + 1) * width) for c in range(win_ref.shape[1] // width)]
    for cols in chunks:
        hidden, slope = gelu_both(nn(low, win_ref[:, cols]))
        hidden = to_low(hidden)
        hidden_ref[:, cols] = hidden
        slope_ref[:, cols] = slope
        y = y + nn(hidden, wout_ref[cols, :])
    out_ref[...] = to_low(y)
    cot = cot_ref[...]
    acc = None
    for cols in chunks:
        pre = to_low(slope_ref[:, cols] * nt(cot, wout_ref[cols, :]))
        pre_grad_ref[:, cols] = pre
        part = nt(pre, win_ref[:, cols])
        acc = part if acc is None else acc + part
    back, gain_grad = rms_back(after, scale, gain_of(gains_ref, GAIN_DFFN), acc)
    gain_grad_ref[...] = gain_grad
    grad_after = cot.astype(jnp.float32) + back
    grad_after_ref[...] = grad_after
    after_low = to_low(grad_after)
    after_low_ref[...] = after_low
    att_grad_ref[...] = to_low(nt(after_low, wco_ref[...]))


def dec_mid_call(merged, mid, cot, gain, wco, win, wout):
    rows = mid.shape[0]
    ff = win.shape[1]
    low = sds((rows, D), jnp.bfloat16)
    full = sds((rows, D), jnp.float32)
    wide = sds((rows, ff), jnp.bfloat16)
    outs = [low, low, wide, wide, low, full, low, sds((1, D), jnp.float32)]
    vmem = pl.BlockSpec(memory_space=pltpu.VMEM)
    return pl.pallas_call(
        dec_mid_kernel,
        in_specs=[vmem] * 7,
        out_specs=[vmem] * len(outs),
        out_shape=outs,
        scratch_shapes=[pltpu.VMEM((rows, ff), jnp.float32)],
        compiler_params=params(62),
        name="dec_mid",
    )(merged, mid, cot, gain, wco, win, wout)


def dec_post_kernel(
    gq_ref, grad_after_ref, mid_ref, x_ref, q_ref, k_ref, v_ref, probs_ref, gains_ref,
    wq_ref, wk_ref, wv_ref, wo_ref, wcq_ref, after_ref,
    mid_low_ref, dq_ref, dk_ref, dv_ref, out_ref, gain_self_grad_ref, gain_cross_grad_ref, fold_ref,
):
    rows = x_ref.shape[0]
    mid = mid_ref[...]
    scale = lax.rsqrt(jnp.mean(mid * mid, axis=-1, keepdims=True) + epsilon)
    three = nt(jnp.concatenate(in_three(gq_ref[...]), axis=0), wcq_ref[...])
    back, gain_grad = rms_back(mid, scale, gain_of(gains_ref, GAIN_CROSS), three[:rows] + three[rows : 2 * rows] + three[2 * rows :])
    gain_cross_grad_ref[...] = gain_grad
    grad_mid = grad_after_ref[...] + back
    mid_low = to_low(grad_mid)
    mid_low_ref[...] = mid_low
    att_grad = to_low(nt(mid_low, wo_ref[...]))
    lane = lax.broadcasted_iota(jnp.int32, (rows, 128), 1)
    row8 = lax.broadcasted_iota(jnp.int32, (8, 128), 0)
    for pair in range(HEADS // 2):
        cols = slice(pair * 128, (pair + 1) * 128)
        q = q_ref[:, cols]
        k = k_ref[:, cols]
        v = v_ref[:, cols]
        g = att_grad[:, cols]
        dqs = []
        scores = []
        probs = []
        for half in range(2):
            head = 2 * pair + half
            p = probs_ref[head]
            dp = nt(head_lanes(g, half), v)
            ds = p * (dp - jnp.sum(p * dp, axis=1, keepdims=True))
            wide = jnp.concatenate([ds, jnp.zeros((rows, 128 - rows), jnp.float32)], axis=1)
            total = wide[0:8]
            for group in range(1, rows // 8):
                total = total + pltpu.roll(wide[group * 8 : group * 8 + 8], 128 - group * 8, 1)
            for bit in (1, 2, 4):
                total = jnp.where((row8 // bit) % 2 == 1, pltpu.roll(total, 128 - bit, 1), total)
            fold_ref[head : head + 1, :] = jnp.sum(total, axis=0, keepdims=True)
            ds = to_low(ds)
            dqs.append(nn(ds, k))
            scores.append(ds)
            probs.append(to_low(p))
        dq_ref[:, cols] = to_low(0.125 * jnp.where(lane < HEAD, dqs[0], dqs[1]))
        both_q = jnp.concatenate([head_lanes(q, 0), head_lanes(q, 1)], axis=0)
        both_g = jnp.concatenate([head_lanes(g, 0), head_lanes(g, 1)], axis=0)
        dk_ref[:, cols] = to_low(product_tn(jnp.concatenate(scores, axis=0), both_q))
        dv_ref[:, cols] = to_low(product_tn(jnp.concatenate(probs, axis=0), both_g))
    x = x_ref[...].astype(jnp.float32)
    scale = lax.rsqrt(jnp.mean(x * x, axis=-1, keepdims=True) + epsilon)
    grad = nt(dq_ref[...], wq_ref[...]) + nt(dk_ref[...], wk_ref[...]) + nt(dv_ref[...], wv_ref[...])
    back, gain_grad = rms_back(x, scale, gain_of(gains_ref, GAIN_SELF), grad)
    gain_self_grad_ref[...] = gain_grad
    out_ref[...] = grad_mid + back


def dec_post(gq, grad_after, mid, x, q, k, v, probs, gains, wq, wk, wv, wo, wcq, after):
    rows = x.shape[0]
    low = sds((rows, D), jnp.bfloat16)
    gain = sds((1, D), jnp.float32)
    outs = [low, low, low, low, sds((rows, D), jnp.float32), gain, gain, sds((HEADS, 128), jnp.float32)]
    vmem = pl.BlockSpec(memory_space=pltpu.VMEM)
    return pl.pallas_call(
        dec_post_kernel,
        in_specs=[vmem] * 14 + [pl.BlockSpec(memory_space=pl.ANY)],
        out_specs=[vmem] * len(outs),
        out_shape=outs,
        compiler_params=params(62),
        name="dec_post",
    )(gq, grad_after, mid, x, q, k, v, probs, gains, wq, wk, wv, wo, wcq, after)


def dec_weight_kernel(
    pb, pa, place_ref, low_ref, dq_ref, dk_ref, dv_ref, att_ref, mid_low_ref, cross_low_ref, gq_ref, merged_ref, after_low_ref,
    hidden_ref, cot_ref, dffn_low_ref, pre_grad_ref, keep_ref, send_ref, turned_ref, wide_ref,
):
    shards = pb * pa
    column = place_ref[0]
    core = place_ref[1]
    rows = D // shards
    depth = low_ref.shape[0]

    def own(left, scratch):
        height = left.shape[1]
        here = height // shards
        span = left.shape[0]
        scratch[:, :span] = left.astype(jnp.float32).T
        cut = [scratch[pl.ds((b * pa + column) * here, here), :span] for b in range(pb)]
        return to_low(jnp.concatenate(cut, axis=0)), here

    first = 0

    def put(values, here):
        nonlocal first
        for y in range(pb // 2):
            low_part = values[2 * y * here : (2 * y + 1) * here]
            high_part = values[(2 * y + 1) * here : (2 * y + 2) * here]
            slot = place_ref[2 + y]
            keep_ref[slot, first : first + here, :] = jnp.where(core == 0, low_part, high_part)
            send_ref[slot, first : first + here, :] = jnp.where(core == 0, high_part, low_part)
        first += here

    left, here = own(low_ref[...], turned_ref)
    for right_ref in (dq_ref, dk_ref, dv_ref):
        put(nn(left, right_ref[...]), here)
    left, here = own(att_ref[...], turned_ref)
    put(nn(left, mid_low_ref[...]), here)
    left, here = own(cross_low_ref[...], turned_ref)
    a, b, c = in_three(gq_ref[...])
    put(nn(left, a) + nn(left, b) + nn(left, c), here)
    right = after_low_ref[...]
    a, b, c = (own(part, turned_ref)[0] for part in in_three(merged_ref[:, :D]))
    put(nn(a, right) + nn(b, right) + nn(c, right), here)
    left, wide = own(hidden_ref[...], wide_ref)
    put(nn(left, cot_ref[...]), wide)
    left, here = own(dffn_low_ref[...], turned_ref)
    for c in range(pre_grad_ref.shape[1] // D):
        put(nn(left, pre_grad_ref[:, c * D : (c + 1) * D]), here)


def dec_weight_grads(pb, pa, place, *args):
    rows, ff = args[-1].shape
    shards = pb * pa
    height = (6 * D + ff + ff) // shards
    vmem = pl.BlockSpec(memory_space=pltpu.VMEM)
    return pl.pallas_call(
        functools.partial(dec_weight_kernel, pb, pa),
        in_specs=[pl.BlockSpec(memory_space=pltpu.SMEM)] + [vmem] * len(args),
        out_specs=[vmem, vmem],
        out_shape=[sds((pb // 2, height, D), jnp.float32)] * 2,
        scratch_shapes=[pltpu.VMEM((D, rows), jnp.float32), pltpu.VMEM((ff, rows), jnp.float32)],
        compiler_params=params(62),
        name="dec_weight_grads",
    )(place, *args)


def finish_kernel(pb, pa, heights, cuts, small_ref, dec_ref, enc_table_ref, dec_table_ref, *refs):
    pieces, big_ref, outs = refs[: len(cuts)], refs[len(cuts)], refs[len(cuts) + 1 :]
    outs[-1][...] = big_ref[...]

    @pl.when(pl.program_id(0) == 0)
    def _():
        finish_small(pb, pa, heights, small_ref, dec_ref, enc_table_ref, dec_table_ref, pieces, cuts, outs)


def finish_small(pb, pa, heights, small_ref, dec_ref, enc_table_ref, dec_table_ref, pieces, cuts, outs):
    shards = pb * pa
    shard = lax.axis_index("pb") * pa + lax.axis_index("pa")
    width = D // shards
    rolled = pltpu.roll(small_ref[0:8, :D], lax.rem(D - shard * width, D), 1)
    for r in range(6):
        outs[r][...] = rolled[r, :width]
    share = BUCKETS * HEADS // shards
    bucket = shard * share // HEADS
    head = lax.rem(shard * share, HEADS)

    def bias_grad(folded, table_ref, out_ref):
        table = table_ref[...]
        by_bucket = sum(nt(table, part) for part in in_three(folded))
        row = lax.broadcasted_iota(jnp.int32, by_bucket.shape, 0)
        mine = jnp.sum(jnp.where(row == bucket, by_bucket, 0.0), axis=0, keepdims=True)
        mine = jnp.concatenate([mine, jnp.zeros((1, 128 - HEADS), jnp.float32)], axis=1)
        mine = jnp.broadcast_to(mine, (8, 128))
        out_ref[...] = pltpu.roll(mine, lax.rem(128 - head, 128), 1)[0, :share]

    bias_grad(small_ref[8 : 8 + HEADS, :], enc_table_ref, outs[6])
    dec_fold = jnp.concatenate([small_ref[0:6, D : D + 128], small_ref[0:6, D + 128 : D + 256]], axis=0)
    bias_grad(dec_fold, dec_table_ref, outs[7])
    first = 0
    for number, height in enumerate(heights):
        outs[8 + number][...] = dec_ref[first : first + height]
        first += height
    at = 8 + len(heights)
    wide_ref = outs[at]
    for c in range(wide_ref.shape[1] // D):
        wide_ref[:, c * D : (c + 1) * D] = dec_ref[first : first + width]
        first += width
    for piece_ref, count in zip(pieces, cuts):
        columns = piece_ref.shape[1] // count
        for c in range(count):
            at += 1
            outs[at][...] = piece_ref[:, c * columns : (c + 1) * columns]


def finish(pb, pa, small, dec_sum, enc_table, dec_table, ff, pieces, cuts, big):
    shards = pb * pa
    width = D // shards
    share = BUCKETS * HEADS // shards
    heights = [width] * 6 + [ff // shards]
    outs = [sds((width,), jnp.float32)] * 6 + [sds((share,), jnp.float32)] * 2
    outs += [sds((h, D), jnp.float32) for h in heights] + [sds((width, ff), jnp.float32)]
    for piece, count in zip(pieces, cuts):
        outs += [sds((piece.shape[0], piece.shape[1] // count), jnp.float32)] * count
    args = [small, dec_sum, enc_table, dec_table, *pieces]
    tile = pl.BlockSpec((256, big.shape[1]), lambda i: (i, 0))
    return pl.pallas_call(
        functools.partial(finish_kernel, pb, pa, heights, cuts),
        grid=(big.shape[0] // 256,),
        in_specs=[whole(a) for a in args] + [tile],
        out_specs=[whole(o) for o in outs] + [tile],
        out_shape=outs + [sds(big.shape, big.dtype)],
        compiler_params=params(62),
        name="finish",
    )(*args, big)


def bits_of(mesh_sizes):
    pb, pa = mesh_sizes
    pb_bits = pb.bit_length() - 1
    pa_bits = pa.bit_length() - 1
    ys = [("pb", b) for b in range(1, pb_bits)]
    xs = [("pa", b) for b in range(pa_bits - 2)]
    zs = [("pa", b) for b in range(pa_bits - 2, pa_bits)]
    return xs, ys, zs


def orders_of(mesh_sizes):
    xs, ys, zs = bits_of(mesh_sizes)
    return (xs + ys + zs, ys + xs + zs, zs[:1] + xs + ys + zs[1:], zs[:1] + ys + xs + zs[1:])


def exchange_table(mesh_sizes, orders):
    pb, pa = mesh_sizes
    pb_me = lax.axis_index("pb")
    pa_me = lax.axis_index("pa")
    cells = np.arange(pb * pa // 2)
    pb_of = jnp.asarray(cells // pa * 2)
    pa_of = jnp.asarray(cells % pa)
    rows = [jnp.full((cells.size,), pb_me % 2, jnp.int32)]
    for order in orders:
        slot = jnp.zeros((cells.size,), jnp.int32)
        for axis, bit in order:
            far = ((pb_of if axis == "pb" else pa_of) >> bit) ^ ((pb_me if axis == "pb" else pa_me) >> bit)
            slot = slot * 2 + (far & 1).astype(jnp.int32)
        rows.append(slot)
    return jnp.stack(rows)


MESH = pl.DeviceIdType.MESH
LINK = 0.11
PAIR = 0.45
NEAR = ("pb", 0)


def link_of(step, sizes):
    xs, ys, zs = bits_of(sizes)
    if step == NEAR:
        return "core"
    if step in ys:
        return "y"
    if step in xs:
        return "x"
    return "z far" if step == zs[-1] else "z"


def link_time(step, megabytes, sizes, rate=None):
    if step == NEAR:
        return megabytes / PAIR
    return 2 * megabytes * (2 if step == bits_of(sizes)[2][-1] else 1) / (rate or LINK)


class Piece:
    def __init__(self, array, first, width, order, place=None, start=0.0, met=False):
        self.array, self.first, self.width, self.order = array, first, width, [NEAR] + list(order)
        self.place, self.start, self.met = place, start, met


DEPTH = 4


def block_of(piece, shapes):
    return tuple(shapes[piece.array][:2]) + (piece.width,)


def plan(pieces, shapes, sizes, rate=None):
    free, held, queues = {}, {}, {}
    pending = [(piece.start, i, "ready", 0) for i, piece in enumerate(pieces)]
    events = []

    def key_of(what, i, step):
        return ("load", block_of(pieces[i], shapes)) if what == "load" else link_of(pieces[i].order[step], sizes)

    def start(now, what, i, step, starts):
        key = key_of(what, i, step)
        if key != "core" and held.get(key, 0) >= (1 if what == "load" else DEPTH):
            queues.setdefault(key, []).append((what, i, step))
            return
        held[key] = held.get(key, 0) + 1
        half, rows = shapes[pieces[i].array][:2]
        megabytes = (half >> step) * rows * pieces[i].width * 4e-6
        begin = max(now, free.get(key, 0.0))
        if what == "load":
            free[key] = begin + 1.0 + megabytes * 0.8
            pending.append((free[key], i, "loaded", 0))
        else:
            free[key] = begin + link_time(pieces[i].order[step], megabytes, sizes, rate)
            pending.append((free[key] + 1.5, i, "arrived", step))
        starts.append((what, i, step))

    while pending:
        pending.sort()
        now, i, what, step = pending.pop(0)
        starts = []
        if what != "ready":
            key = key_of("load" if what == "loaded" else "send", i, step)
            held[key] -= 1
            if queues.get(key):
                start(now, *queues[key].pop(0), starts)
        if what == "ready":
            start(now, "load" if pieces[i].met else "send", i, 0, starts)
        elif what == "arrived" and step == 0:
            start(now, "load", i, 0, starts)
        elif what == "loaded":
            start(now + 0.5, "send", i, 1, starts)
        elif step + 1 < len(pieces[i].order):
            start(now + 0.5, "send", i, step + 1, starts)
        events.append((now, what, i, step, starts))
    return events


def partner(step):
    axis, bit = step
    me = lax.axis_index(axis)
    size = 1 << bit
    there = me + size - 2 * size * lax.rem(me // size, 2)
    return {"pb": lax.axis_index("pb"), "pa": lax.axis_index("pa"), axis: there}


def all_steps(sizes):
    xs, ys, zs = bits_of(sizes)
    return [NEAR] + xs + ys + zs


def greet(sizes):
    barrier = pltpu.get_barrier_semaphore()
    for step in all_steps(sizes):
        pl.semaphore_signal(barrier, inc=1, device_id=partner(step), device_id_type=MESH)
    pl.semaphore_wait(barrier, len(all_steps(sizes)))


class Exchange:
    def __init__(self, sizes, pieces, shapes, rate=None):
        self.sizes, self.pieces, self.shapes = sizes, pieces, shapes
        self.events = plan(pieces, shapes, sizes, rate)
        self.stages = len(all_steps(sizes))
        self.arrays = range(len(shapes))
        self.own = [a for a in self.arrays if any(p.array == a and p.place is not None for p in pieces)]
        self.block = [block_of(pieces[self.of(a)[0]], shapes) for a in self.arrays]
        self.blocks = sorted(set(self.block))
        self.before = {}
        for n, a in enumerate(self.own):
            earlier = [b for b in self.own[:n] if self.block[b] == self.block[a]]
            if earlier:
                self.before[a] = earlier[-1]

    def of(self, array):
        return [i for i, p in enumerate(self.pieces) if p.array == array]

    def scratch(self):
        out = [pltpu.VMEM(block, jnp.float32) for block in self.blocks]
        for array in self.arrays:
            half, *block = self.block[array]
            count = len(self.of(array))
            out += [
                pltpu.VMEM((count, half, *block), jnp.float32),
                pltpu.VMEM((count, half - 1, *block), jnp.float32),
            ]
        count = len(self.pieces)
        return out + [
            pltpu.SemaphoreType.DMA((count,)),
            pltpu.SemaphoreType.DMA((count,)),
            pltpu.SemaphoreType.DMA((count, self.stages)),
            pltpu.SemaphoreType.DMA((count, self.stages)),
        ]

    def bind(self, keeps, sends, nears, outs, staging, scratch):
        self.keeps, self.sends, self.nears, self.outs, self.staging = keeps, sends, nears, outs, staging
        places = dict(zip(self.blocks, scratch))
        self.loaded = [places[block] for block in self.block]
        scratch = scratch[len(self.blocks) :]
        self.kept = [scratch[2 * a] for a in self.arrays]
        recvs = [scratch[2 * a + 1] for a in self.arrays]
        self.near_sems, self.keep_sems, self.send_sems, self.recv_sems = scratch[2 * len(self.shapes) :]
        self.bufs, self.recvs = {}, {}
        for array in self.arrays:
            for number, i in enumerate(self.of(array)):
                self.bufs[i], self.recvs[i] = self.kept[array].at[number], recvs[array].at[number]

    def loads(self, i):
        piece = self.pieces[i]
        cols = pl.ds(piece.first, piece.width)
        out = [pltpu.make_async_copy(self.nears[piece.array].at[:, :, cols], self.loaded[piece.array], self.near_sems.at[i])]
        if piece.place is None:
            out.append(pltpu.make_async_copy(self.keeps[piece.array].at[:, :, cols], self.bufs[i], self.keep_sems.at[i]))
        return out

    def sizes_of(self, i, step):
        half = self.shapes[self.pieces[i].array][0]
        count = half >> step
        return count, half - 2 * count

    def copy(self, i, step):
        piece = self.pieces[i]
        count, first = self.sizes_of(i, step)
        if step == 0:
            if piece.place is None:
                source = self.sends[piece.array].at[:, :, pl.ds(piece.first, piece.width)]
            else:
                source = self.staging[piece.array].at[piece.place % 2]
            target = self.nears[piece.array].at[:, :, pl.ds(piece.first, piece.width)]
        else:
            source = self.bufs[i].at[pl.ds(count, count)]
            target = self.recvs[i].at[pl.ds(first, count)]
        return pltpu.make_async_remote_copy(
            src_ref=source, dst_ref=target, send_sem=self.send_sems.at[i, step], recv_sem=self.recv_sems.at[i, step],
            device_id=partner(piece.order[step]), device_id_type=MESH,
        )

    def free_staging(self, array, place):
        if place >= 2:
            self.copy(self.of(array)[place - 2], 0).wait_send()
        elif array in self.before:
            self.copy([i for i in self.of(self.before[array]) if self.pieces[i].place % 2 == place][-1], 0).wait_send()

    def event(self, what, i, step, starts):
        piece = self.pieces[i]
        buf = self.bufs[i]
        last = what == "arrived" and step + 1 == len(piece.order)
        count = 0
        if what == "loaded":
            for load in self.loads(i):
                load.wait()
            source, first, count = self.loaded[piece.array], 0, self.shapes[piece.array][0]
        elif what == "arrived":
            self.copy(i, step).wait_recv()
            if step > 0:
                source = self.recvs[i]
                count, first = self.sizes_of(i, step)

        def add(slot, _):
            buf[slot] = buf[slot] + source[first + slot]
            return 0

        if last:
            self.outs[piece.array][:, piece.first : piece.first + piece.width] = buf[0] + source[first]
        elif count:
            lax.fori_loop(count // 2, count, add, 0, unroll=min(4, count // 2))
        mine = [s for s in starts if s[0] == "send"]
        for _, j, k in mine:
            self.copy(j, k).start()
        if not last and count:
            lax.fori_loop(0, count // 2, add, 0, unroll=min(4, count // 2))
        for kind, j, _ in starts:
            if kind == "load":
                for load in self.loads(j):
                    load.start()

    def finish(self):
        for i, piece in enumerate(self.pieces):
            waited = piece.place is not None and (
                piece.place + 2 < len(self.of(piece.array)) or piece.array in self.before.values()
            )
            first = 1 if waited or piece.met else 0
            for step in range(first, len(piece.order)):
                self.copy(i, step).wait_send()

    def points(self, times, ready):
        out = [[] for _ in times]
        place = 0
        for when, what, i, step, starts in self.events:
            while place < len(times) - 1 and times[place] < when:
                place += 1
            if what == "ready" and i in ready:
                place = max(place, ready[i])
            out[place].append((what, i, step, starts))
        return out
class Everywhere:
    def __init__(self, steps, shape):
        self.steps = steps
        self.shape = shape

    def scratch(self):
        count = len(self.steps)
        return [
            pltpu.VMEM((count + 1,) + self.shape, jnp.float32),
            pltpu.VMEM((count,) + self.shape, jnp.float32),
            pltpu.SemaphoreType.DMA((count,)),
            pltpu.SemaphoreType.DMA((count,)),
        ]

    def bind(self, scratch):
        self.sums, self.recvs, self.send_sems, self.recv_sems = scratch

    def copy(self, k):
        return pltpu.make_async_remote_copy(
            src_ref=self.sums.at[k], dst_ref=self.recvs.at[k], send_sem=self.send_sems.at[k], recv_sem=self.recv_sems.at[k],
            device_id=partner(self.steps[k]), device_id_type=MESH,
        )

    def arrive(self, k):
        self.copy(k).wait_recv()
        self.sums[k + 1] = self.sums[k] + self.recvs[k]
        if k + 1 < len(self.steps):
            self.copy(k + 1).start()

    def finish(self):
        for k in range(len(self.steps)):
            self.copy(k).wait_send()


SMALL = (24, 1024)
ATTN_STEP = 3.6
OPENING = 7.0
TILE_US = 0.0052
BACK_STEP = 1.2


def slots_of(sizes, order):
    pb, pa = sizes
    far = {}
    for axis, bit in order:
        me = lax.rem(lax.axis_index(axis) // (1 << bit), 2)
        far[axis, bit] = (me, 1 - me)
    cells = []
    for y in range(pb // 2):
        for a in range(pa):
            slot = 0
            for axis, bit in order:
                slot = slot * 2 + far[axis, bit][(2 * y if axis == "pb" else a) >> bit & 1]
            cells.append(slot)
    return cells


def outside_pieces(orders, groups):
    pieces = []
    for number, (_, _, met, chains, width) in enumerate(groups):
        for c, chain in enumerate(chains):
            order = chain if isinstance(chain, list) else orders[chain]
            pieces.append(Piece(number, c * width, width, order, start=0.1 * number + 0.01 * c, met=met))
    return pieces


def back_host_kernel(adding, sizes, *refs):
    own, part_ref, outs, total_ref, scratch = refs[:11], refs[11], refs[12:19], refs[19], refs[20:]
    adding.bind(scratch)
    step = pl.program_id(0)
    last = pl.num_programs(0) - 1
    steps = len(adding.steps)

    @pl.when(step == 0)
    def _():
        adding.sums[0] = part_ref[...]
        greet(sizes)
        adding.copy(0).start()

    for k in range(steps - 1):

        @pl.when(step == jnp.minimum(k + 1, last))
        def _(k=k):
            adding.arrive(k)

    back_kernel(*own, *outs)

    @pl.when(step == last)
    def _():
        adding.arrive(steps - 1)
        total_ref[...] = adding.sums[steps]
        adding.finish()


def post_backward(sizes, part, gkv, y, mid, slope, cot, gains, wck, wcv, wout, win, wo):
    tokens = y.shape[0]
    tile = 256
    ff = win.shape[1]
    low = sds((tokens, D), jnp.bfloat16)
    d = rows_of(tile, D)
    f = rows_of(tile, ff)
    gain = pl.BlockSpec((1, D), lambda i: (0, 0))
    xs, _, zs = bits_of(sizes)
    adding = Everywhere(xs + zs, part.shape)

    def once(array):
        return pl.BlockSpec(array.shape, lambda i: (0,) * array.ndim, pipeline_mode=pl.Buffered(1))

    return pl.pallas_call(
        functools.partial(back_host_kernel, adding, sizes),
        grid=(tokens // tile,),
        in_specs=[pl.BlockSpec((2, tile, D), lambda i: (0, i, 0)), d, d, f, d] + [once(a) for a in (gains, wck, wcv, wout, win, wo, part)],
        out_specs=[d, f, d, d, d, gain, gain, pl.BlockSpec(part.shape, lambda i: (0, 0))],
        out_shape=[low, sds((tokens, ff), jnp.bfloat16), low, sds((tokens, D), jnp.float32), low]
        + [sds((1, D), jnp.float32)] * 2
        + [sds(part.shape, jnp.float32)],
        scratch_shapes=adding.scratch(),
        compiler_params=pltpu.CompilerParams(collective_id=3, has_side_effects=True, vmem_limit_bytes=62 * MIB),
        name="enc_post_back",
    )(gkv, y, mid, slope, cot, gains, wck, wcv, wout, win, wo, part)


class Phase:
    def __init__(self, name, first, count, us):
        self.name, self.first, self.count, self.us = name, first, count, us


def last_kernel(
    exchange, everywhere, points, orders, phases, passages, share, outside, gradients,
    lengths_ref, q_ref, k_ref, v_ref, o_ref, do_ref, lse_ref, base_ref, x_ref, grad_mid_ref, gains_ref, wq_ref, wk_ref, wv_ref,
    dec_fold_ref, *refs,
):
    refs = list(refs)

    def take(count):
        out = refs[:count]
        del refs[:count]
        return out

    gains = take(5)
    lefts = take(len(gradients))
    rights = take(len(gradients) - 1)
    keeps, others = take(len(outside)), take(len(outside))
    out_ref, small_ref = take(2)
    moved = take(len(exchange.shapes))
    nears = [other if met else take(1)[0] for other, met in zip(others, outside)] + take(len(gradients))
    strip_ref, gather_ref, dqT_ref, grads_ref, fold_ref, gain_grad_ref = take(6)
    staging = {}
    for array in exchange.own:
        staging[array] = staging[exchange.before[array]] if array in exchange.before else take(1)[0]
    everywhere.bind(take(4))
    exchange.bind(keeps, others, nears, moved, staging, refs)
    step = pl.program_id(0)
    sizes = exchange.sizes
    pb, pa = sizes

    @pl.when(step == 0)
    def _():
        greet(sizes)
        for event in points["start"][0]:
            exchange.event(*event)

    def run(place):
        for at, events in points.get(place, {}).items():
            if events:

                @pl.when(step == at)
                def _(events=events):
                    for event in events:
                        exchange.event(*event)

    def attention(phase):
        number = step - phase.first
        pair = number // passages
        passage = lax.rem(number, passages)
        place = pl.ds(pl.multiple_of(passage * PL, PL), PL), pl.ds(pl.multiple_of(pair * 128, 128), 128)
        attn_backward_kernel(
            lambda head: run(("attention", head)), passage, passages, lengths_ref, q_ref, k_ref, v_ref, o_ref, do_ref, lse_ref, base_ref,
            grads_ref.at[(0,) + place], grads_ref.at[(1,) + place], grads_ref.at[(2,) + place], fold_ref.at[pl.ds(pair, 1)],
            strip_ref, gather_ref, dqT_ref,
        )

    def gradient(phase, array, left_ref, right_ref):
        number = step - phase.first
        width = exchange.pieces[exchange.of(array)[0]].width
        if right_ref is None:
            each = D // width
            column = pl.ds(pl.multiple_of(lax.rem(number, each) * width, width), width)
            right = grads_ref[number // each, :, column]
        else:
            right = right_ref[...]
        for place in range(0 if array in exchange.before else 2, phase.count):

            @pl.when(number == place)
            def _(place=place):
                exchange.free_staging(array, place)

        chain = 0
        for place, c in enumerate(gradients[array - len(outside)][3]):
            chain = jnp.where(number == place, c, chain)
        choices = [slots_of(sizes, order) for order in orders]
        core = lax.rem(lax.axis_index("pb"), 2)
        rows = exchange.shapes[array][1]
        half_rows = pa * rows
        kept, staged = exchange.kept[array], exchange.staging[array]
        for y in range(pb // 2):
            low_part = nn(left_ref[2 * y * half_rows : (2 * y + 1) * half_rows, :], right)
            high_part = nn(left_ref[(2 * y + 1) * half_rows : (2 * y + 2) * half_rows, :], right)
            mine = jnp.where(core == 0, low_part, high_part)
            other = jnp.where(core == 0, high_part, low_part)
            for a in range(pa):
                slot = choices[0][y * pa + a]
                for c in range(1, len(orders)):
                    slot = jnp.where(chain == c, choices[c][y * pa + a], slot)
                kept[number, slot] = mine[a * rows : (a + 1) * rows]
                staged[lax.rem(number, 2), slot] = other[a * rows : (a + 1) * rows]

    def back(phase):
        height = x_ref.shape[0]
        rows = pl.ds(pl.multiple_of((step - phase.first) * height, height), height)
        qkv_back_kernel(
            step == phase.first, grads_ref.at[0, rows], grads_ref.at[1, rows], grads_ref.at[2, rows],
            x_ref, grad_mid_ref, gains_ref, wq_ref, wk_ref, wv_ref, out_ref, gain_grad_ref,
        )

    for phase in phases:

        @pl.when((step >= phase.first) & (step < phase.first + phase.count))
        def _(phase=phase):
            if phase.name == "attention":
                attention(phase)
            elif phase.name == "back":
                back(phase)
            else:
                k = phase.name
                gradient(phase, exchange.own[k], lefts[k], rights[k] if k < len(rights) else None)

    run("end")

    @pl.when(step == pl.num_programs(0) - 1)
    def _():
        first = everywhere.sums
        first[0] = jnp.zeros(SMALL, jnp.float32)
        first[0, 0:1, :D] = gain_grad_ref[...]
        for r, ref in enumerate(gains):
            first[0, r + 1 : r + 2, :D] = ref[...] if r < 2 else ref[...] * share
        for pair in range(HEADS // 2):
            first[0, 8 + 2 * pair : 10 + 2 * pair, :] = fold_ref[pair]
        for part in range(2):
            lanes = slice(D + part * 128, D + (part + 1) * 128)
            first[0, 0:6, lanes] = dec_fold_ref[6 * part : 6 * part + 6] * share
        everywhere.copy(0).start()
        left = points["rest"]
        steps = len(everywhere.steps)
        every = max(1, len(left) // (steps + 1))
        done = 0
        for n, event in enumerate(left):
            if n % every == every - 1 and done < steps:
                everywhere.arrive(done)
                done += 1
            exchange.event(*event)
        for k in range(done, steps):
            everywhere.arrive(k)
        small_ref[...] = everywhere.sums[steps]
        exchange.finish()
        everywhere.finish()


def last_part(
    sizes, orders, groups, gradients, lengths, q, k, v, o, do, lse, base, x, grad_mid, gains, wq, wk, wv, dec_fold, grads_of_gains,
):
    pb, pa = sizes
    passages = lengths.shape[0]
    tokens = x.shape[0]
    pairs = HEADS // 2
    tile_rows = 128
    half = pb * pa // 2
    shapes = [g[0].shape for g in groups]
    widths = [right.shape[1] if right is not None else 3 * D for _, right, *_ in gradients]
    shapes += [(half, left.shape[0] // (pb * pa), w) for (left, *_), w in zip(gradients, widths)]

    phases = []
    names = list(range(len(gradients) - 1)) + ["attention", len(gradients) - 1, "back"]
    step = 0
    for name in names:
        if name == "attention":
            count, us = pairs * passages, ATTN_STEP
        elif name == "back":
            count, us = tokens // tile_rows, BACK_STEP
        else:
            count, us = widths[name] // gradients[name][2], TILE_US * gradients[name][2]
        phases.append(Phase(name, step, count, us))
        step += count
    steps = step
    pieces = outside_pieces(orders, groups)
    times, labels, ready = [OPENING], [("start", 0)], {}
    now = OPENING
    for phase in phases:
        for n in range(phase.count):
            number = phase.first + n
            if phase.name == "attention":
                times += [now, now + phase.us / 2]
                labels += [(("attention", 0), number), (("attention", 1), number)]
            now += phase.us
            if phase.name != "attention" and number < steps - 1:
                times.append(now)
                labels.append(("end", number))
            if isinstance(phase.name, int):
                ready[len(pieces)] = len(times) - 1
                width = gradients[phase.name][2]
                pieces.append(Piece(len(groups) + phase.name, n * width, width, orders[gradients[phase.name][3][n]], n, now))
    exchange = Exchange(sizes, pieces, shapes)
    everywhere = Everywhere(all_steps(sizes), SMALL)
    points = {}
    found = exchange.points(times + [1e9], ready)
    for (place, number), events in zip(labels, found):
        points.setdefault(place, {})[number] = events
    points["rest"] = found[-1]
    by_name = {phase.name: phase for phase in phases}

    def at(name, i):
        phase = by_name[name]
        return jnp.clip(i - phase.first, 0, phase.count - 1)

    def pair_of(i):
        return at("attention", i) // passages

    def passage_of(i):
        return lax.rem(at("attention", i), passages)

    def once(array):
        return pl.BlockSpec(array.shape, lambda i: (0,) * array.ndim, pipeline_mode=pl.Buffered(1))

    tile = pl.BlockSpec((PL, 128), lambda i: (passage_of(i), pair_of(i)))
    rows = pl.BlockSpec((tile_rows, D), lambda i: (at("back", i), 0))
    hbm = pl.BlockSpec(memory_space=pl.ANY)
    keeps, others = [g[0] for g in groups], [g[1] for g in groups]
    outside = [g[2] for g in groups]
    lefts = [left for left, *_ in gradients]
    rights = [right for _, right, *_ in gradients[:-1]]
    right_specs = [
        pl.BlockSpec((tokens, width), lambda i, name=name: (0, at(name, i)), pipeline_mode=pl.Buffered(1)) for name, (_, _, width, _) in enumerate(gradients[:-1])
    ]
    own_shapes = shapes[len(groups) :]
    near_shapes = [s for s, met in zip(shapes, outside) if not met] + own_shapes
    return pl.pallas_call(
        functools.partial(
            last_kernel, exchange, everywhere, points, orders, phases, passages, 1.0 / pa, outside, gradients
        ),
        grid=(steps,),
        in_specs=[pl.BlockSpec(memory_space=pltpu.SMEM)]
        + [tile] * 5
        + [pl.BlockSpec((1, 1, 2, PL), lambda i: (pair_of(i), passage_of(i), 0, 0)), pl.BlockSpec((1, 2, WIDE), lambda i: (pair_of(i), 0, 0))]
        + [rows, rows]
        + [once(a) for a in (gains, wq, wk, wv, dec_fold) + tuple(grads_of_gains)]
        + [once(left) for left in lefts]
        + right_specs
        + [hbm] * (2 * len(groups)),
        out_specs=[rows, pl.BlockSpec(SMALL, lambda i: (0, 0), pipeline_mode=pl.Buffered(1))]
        + [pl.BlockSpec(s[1:], lambda i: (0, 0), pipeline_mode=pl.Buffered(1)) for s in shapes]
        + [hbm] * len(near_shapes),
        out_shape=[sds((tokens, D), jnp.float32), sds(SMALL, jnp.float32)]
        + [sds(s[1:], jnp.float32) for s in shapes]
        + [sds(s, jnp.float32) for s in near_shapes],
        scratch_shapes=[
            pltpu.VMEM((2, STRIP, WIDE), jnp.float32),
            pltpu.VMEM((2, STRIP, WIDE), jnp.float32),
            pltpu.VMEM((128, PL), jnp.bfloat16),
            pltpu.VMEM((3, tokens, D), jnp.bfloat16),
            pltpu.VMEM((pairs, 2, WIDE), jnp.float32),
            pltpu.VMEM((1, D), jnp.float32),
        ]
        + [pltpu.VMEM((2,) + exchange.block[a], jnp.float32) for a in exchange.own if a not in exchange.before]
        + everywhere.scratch()
        + exchange.scratch(),
        compiler_params=pltpu.CompilerParams(collective_id=1, has_side_effects=True, vmem_limit_bytes=63 * MIB + MIB // 2),
        name="enc_last",
    )(
        lengths, q, k, v, o, do, lse, base, x, grad_mid, gains, wq, wk, wv, dec_fold, *grads_of_gains, *lefts, *rights, *keeps, *others
    )[: 2 + len(shapes)]


def exchange_kernel(exchange, arrays, *refs):
    exchange.bind(refs[:arrays], {}, refs[arrays : 2 * arrays], refs[2 * arrays : 3 * arrays], {}, refs[3 * arrays :])
    greet(exchange.sizes)
    for _, *event in exchange.events:
        exchange.event(*event)
    exchange.finish()


def exchange_only(sizes, orders, groups):
    shapes = [g[0].shape for g in groups]
    exchange = Exchange(sizes, outside_pieces(orders, groups), shapes)
    return pl.pallas_call(
        functools.partial(exchange_kernel, exchange, len(groups)),
        in_specs=[pl.BlockSpec(memory_space=pl.ANY)] * (2 * len(groups)),
        out_specs=[pl.BlockSpec(memory_space=pltpu.VMEM)] * len(groups),
        out_shape=[sds(s[1:], jnp.float32) for s in shapes],
        scratch_shapes=exchange.scratch(),
        compiler_params=pltpu.CompilerParams(collective_id=2, has_side_effects=True, vmem_limit_bytes=63 * MIB),
        name="exchange",
    )(*[g[0] for g in groups], *[g[1] for g in groups])


def local(
    pb, pa,
    enc_in, dec_in, question_of, lengths, enc_gain_attn, enc_query, enc_key, enc_value, enc_output, enc_bias,
    enc_gain_ffn, enc_ff_in, enc_ff_out, enc_gain_final, cross_key, cross_value, dec_gain_self, dec_query, dec_key,
    dec_value, dec_output, dec_bias, dec_gain_cross, cross_query, cross_output, dec_gain_ffn, dec_ff_in, dec_ff_out,
    enc_cot, dec_cot,
):
    sizes = (pb, pa)
    orders = orders_of(sizes)
    answer_rows = dec_in.shape[0]
    gains = gains_together(enc_gain_attn, enc_gain_ffn, enc_gain_final, dec_gain_self, dec_gain_cross, dec_gain_ffn)
    table = exchange_table(sizes, orders)
    enc_table = jnp.asarray(strip_table().T, jnp.bfloat16)
    dec_table = jnp.asarray(causal_row(ANS).T, jnp.bfloat16)

    attn_turned, enc_queries, enc_keys, enc_values = qkv_forward(enc_in, gains, enc_query, enc_key, enc_value)
    enc_attended, attended_turned, enc_lse, base = attn_forward(lengths, enc_queries, enc_keys, enc_values, enc_bias.T, enc_table)
    enc_mid, ffn_turned, hidden_turned, enc_slope, enc_y, enc_out, final_turned, cross_keys, cross_values = post_forward(
        enc_in, enc_attended, gains, enc_output, enc_ff_in, enc_ff_out, cross_key, cross_value
    )

    self_low, dec_queries, dec_keys, dec_values, dec_probs, dec_attended, dec_mid, cross_low, cross_queries = dec_pre(
        dec_in, gains, dec_bias.T, dec_table, dec_query, dec_key, dec_value, dec_output, cross_query
    )

    merged = merge(*cross_part(pa, question_of, lengths, cross_queries, cross_keys, cross_values), pa)
    dec_out, dffn_low, dec_hidden, pre_grad_low, after_low, grad_after, cross_att_grad, dec_gain_ffn_grad = dec_mid_call(
        merged, dec_mid, dec_cot, gains, cross_output, dec_ff_in, dec_ff_out
    )
    query_part, grad_cross = cross_back(
        question_of, lengths, cross_queries, cross_keys, cross_values, cross_att_grad, merged
    )
    def near(terms):
        keep, send = terms
        return keep, lax.ppermute(send, "pb", [(i, i ^ 1) for i in range(pb)])

    cross_terms = near(weight_grad(table, final_turned, [(grad_cross, 0), (grad_cross, 1)], pb, pa, 256, (0, 0, 1, 1, 2, 2)))
    eout_low, epre_low, emid_low, grad_enc_mid, enc_att_grad, final_gain_grad, ffn_gain_grad, grad_cross_q = post_backward(
        sizes, query_part,
        grad_cross, enc_y, enc_mid, enc_slope, enc_cot, gains, cross_key, cross_value, enc_ff_out, enc_ff_in, enc_output,
    )
    out_terms = near(weight_grad(table, hidden_turned, [eout_low], pb, pa, 256, (0, 1, 3)))

    mid_low, grad_dq, grad_dk, grad_dv, dec_in_grad, dec_gain_self_grad, dec_gain_cross_grad, dec_fold = dec_post(
        grad_cross_q, grad_after, dec_mid, dec_in, dec_queries, dec_keys, dec_values, dec_probs, gains,
        dec_query, dec_key, dec_value, dec_output, cross_query, out_terms[0],
    )
    far = lax.axis_index("pb") // 2
    places = [lax.axis_index("pa"), lax.axis_index("pb") % 2]
    for y in range(pb // 2):
        slot = 0
        for _, bit in bits_of(sizes)[1]:
            slot = slot * 2 + ((far >> (bit - 1)) + (y >> (bit - 1))) % 2
        places.append(slot)
    dec_terms = dec_weight_grads(
        pb, pa, jnp.stack(places).astype(jnp.int32), self_low, grad_dq, grad_dk, grad_dv, dec_attended, mid_low, cross_low, grad_cross_q,
        merged, after_low, dec_hidden, dec_cot, dffn_low, pre_grad_low,
    )
    ys = bits_of(sizes)[1]
    groups = [
        cross_terms + (True, (0, 1, 2), 512),
        out_terms + (True, (0, 1, 3), 256),
        tuple(dec_terms) + (False, (ys, ys, ys), 256),
    ]
    gradients = [
        (ffn_turned, epre_low, 512, (0, 1, 2, 0, 1, 3)),
        (attended_turned, emid_low, 256, (0, 1, 2)),
        (attn_turned, None, 256, (0, 1, 2, 0, 1, 3, 0, 1, 2)),
    ]
    roomy = D // (pb * pa) % 8 == 0
    if not roomy:
        del gradients[0]
        keep, send = weight_grad(table, ffn_turned, [epre_low], pb, pa, 512, (0, 0, 1, 1, 2, 2))
        in_terms = keep, lax.ppermute(send, "pb", [(i, i ^ 1) for i in range(pb)])
    enc_in_grad, small, *summed = last_part(
        sizes, orders, groups, gradients, lengths, enc_queries, enc_keys, enc_values, enc_attended, enc_att_grad, enc_lse, base,
        enc_in, grad_enc_mid, gains, enc_query, enc_key, enc_value, dec_fold,
        (ffn_gain_grad, final_gain_grad, dec_gain_self_grad, dec_gain_cross_grad, dec_gain_ffn_grad),
    )
    if not roomy:
        summed[3:3] = exchange_only(sizes, orders, [tuple(in_terms) + (True, (0, 1, 2), 1024)])
    cross_sum, ff_out_sum, dec_sum, *summed = summed
    ends = finish(
        pb, pa, small, dec_sum, enc_table, dec_table, dec_hidden.shape[1], [cross_sum, ff_out_sum] + summed, [2, 1, 1, 1, 3], enc_in_grad
    )
    gain_grads, (enc_bias_grad, dec_bias_grad), got = ends[:6], ends[6:8], ends[8:16]
    cross_key_grad, cross_value_grad, ff_out_grad, ff_in_grad, output_grad, query_grad, key_grad, value_grad, enc_in_grad = ends[16:]

    return (
        enc_out, dec_out, enc_in_grad, dec_in_grad,
        gain_grads[0], query_grad, key_grad, value_grad, output_grad, enc_bias_grad,
        gain_grads[1], ff_in_grad, ff_out_grad, gain_grads[2], cross_key_grad, cross_value_grad,
        gain_grads[3], got[0], got[1], got[2], got[3], dec_bias_grad, gain_grads[4], got[4], got[5], gain_grads[5], got[7], got[6],
    )


def solution(mesh):
    pb, pa = mesh.shape["pb"], mesh.shape["pa"]
    rows = P(("pb", "pa"), None)
    flat = P(("pb", "pa"))
    dec = P("pb", None)
    return jax.shard_map(
        functools.partial(local, pb, pa),
        mesh=mesh,
        in_specs=(rows, dec, flat, flat) + (P(),) * 24 + (rows, dec),
        out_specs=(rows, dec, rows, dec)
        + (flat, rows, rows, rows, rows, flat, flat, rows, rows, flat, rows, rows)
        + (flat, rows, rows, rows, rows, flat, flat, rows, rows, flat, rows, rows),
        check_vma=False,
    )
```
